32 devices in a mesh: groups: 2 (over y), region: 4 (over z), feat: 2 (over x), sub: 2 (over core).
Axes of the slice: x: 2, y: 2, z: 4, core: 2. Of those that a mesh axis runs over, the one named last changes fastest.
Arguments:
- node_latent: bfloat16 [6144, 512], P(('groups', 'region', 'feat')), parts along dimension 0, may hold values from -6 to 6
- edge_latent: bfloat16 [49152, 512], P(('groups', 'region', 'feat', 'sub')), parts along dimension 0, may hold values from -6 to 6
- edge_source: int32 [49152], P(('groups', 'region', 'feat', 'sub')), parts along dimension 0, may hold values from 0 to 527, as said below
- receivers: int32 [49152], P(('groups', 'region', 'feat', 'sub')), parts along dimension 0, may hold values from 0 to 383
- near_rows: int32 [16, 4, 32], P(('groups', 'region', 'feat')), parts along dimension 0, may hold values from 0 to 383
- far_rows: int32 [16, 8, 2], P(('groups', 'region', 'feat')), parts along dimension 0, may hold values from 0 to 383
- edge_in_weight: bfloat16 [3, 512, 512], P(None, ('feat', 'sub')), may hold values from -0.15625 to 0.15625
- edge_out_weight: bfloat16 [512, 512], P(('feat', 'sub')), may hold values from -0.25 to 0.25
- node_in_weight: bfloat16 [2, 512, 512], P(None, ('feat', 'sub')), may hold values from -0.1875 to 0.1875
- node_out_weight: bfloat16 [512, 512], P(('feat', 'sub')), may hold values from -0.25 to 0.25
- edge_in_bias: float32 [512], replicated, may hold values from -4 to 4
- edge_out_bias: float32 [512], replicated, may hold values from -4 to 4
- edge_gain: float32 [512], replicated, may hold values from 0.5 to 1.5
- edge_offset: float32 [512], replicated, may hold values from -3 to 3
- node_in_bias: float32 [512], replicated, may hold values from -4 to 4
- node_out_bias: float32 [512], replicated, may hold values from -4 to 4
- node_gain: float32 [512], replicated, may hold values from 0.5 to 1.5
- node_offset: float32 [512], replicated, may hold values from -3 to 3
Outputs:
- edge_new: bfloat16 [49152, 512], P(('groups', 'region', 'feat', 'sub')), parts along dimension 0
- node_new: bfloat16 [6144, 512], P(('groups', 'region', 'feat')), parts along dimension 0
The draws below stay inside these ranges and needn't reach their ends.
There are 2 independent parts, one for each index of `groups`. The reference program is written for one: setup_inputs(seed, part) draws one part's arguments, and reference() takes and returns one part's arrays. A program takes and returns all parts, laid end to end along the dimension named above; an argument that names none is the same for every part. Nothing has to cross between parts.
Inputs may be any that keep to these rules, and one draw needn't show every extreme that they name: `edge_source`: each partition's block of 3072 edges holds every halo slot value 384 to 527 at least once; the other values of the block are local nodes.
All inputs are finite; a program needn't handle non-finite values.
Results may differ from the reference program's by a relative error of at most 0.0051.
Values may be sent and summed in bfloat16 or wider, within the bound.
No kernel may reach another device: no remote copies, remote signals or barrier semaphores. Data moves between devices by JAX's collectives and lax.ppermute only.
A program may use at most 64 MiB of HBM per device.

```python
import jax
import jax.numpy as jnp
from jax import lax

D = 512
H = 512
NODE_DEV = 384
DEGREE = 8
NEAR_CAP = 32
FAR_CAP = 2
PARTS_SIZE = 8
SLOTS = 144
NODES = 3072
EDGES = 24576


def draw_edge_source(key, part):
    key = jax.random.fold_in(key, 7)
    block = DEGREE * NODE_DEV
    slot_ids = NODE_DEV + jnp.arange(SLOTS, dtype=jnp.int32)
    part_keys = jax.random.split(key, PARTS_SIZE)

    def one_block(part_key):
        first_key, second_key = jax.random.split(part_key)
        local_ids = jax.random.randint(first_key, (block - SLOTS,), 0, NODE_DEV, dtype=jnp.int32)
        return jax.random.permutation(second_key, jnp.concatenate([slot_ids, local_ids]))
    return jax.vmap(one_block)(part_keys).reshape(PARTS_SIZE * block)


def place_ends(values, key, low, top_value):
    longest = values.shape.index(max(values.shape))
    spots = []
    for shift in (0, 1):
        where = [jax.random.randint(jax.random.fold_in(key, axis), (), 0, length) for axis, length in enumerate(values.shape)]
        where[longest] = (where[longest] + shift) % values.shape[longest]
        spots.append(tuple(where))
    return values.at[spots[0]].set(low).at[spots[1]].set(top_value)


def shard_levels(stream_key, dims, cuts, low, largest):
    def one(position, parts):
        draws = jax.random.uniform(jax.random.fold_in(jax.random.fold_in(stream_key, 6), position), (parts,), jnp.float32, low / len(cuts), largest / len(cuts))
        return jnp.repeat(jnp.exp(draws), dims[position] // parts).reshape((-1,) + (1,) * (len(dims) - position - 1))

    level = one(*cuts[0])
    for cut in cuts[1:]:
        level = level * one(*cut)
    return level


def normal_values(stream_key, extent, deviation, most, cuts=(), kind=jnp.bfloat16):
    loudness = shard_levels(stream_key, extent, cuts, -0.22, 0.18) if cuts else 1.0
    entries = jax.random.normal(stream_key, extent, jnp.float32) * deviation * loudness
    return jnp.minimum(jnp.maximum(entries, -most), most).astype(kind)


def setup_inputs(seed: int = 0, part: int = 0) -> dict:
    keys = jax.random.split(jax.random.key(seed), 19)
    own_keys = jax.random.split(jax.random.fold_in(keys[18], part), 19)
    node_latent = normal_values(own_keys[0], (NODES, D), 1.0, 6.0, ((0, 8),))
    edge_latent = normal_values(own_keys[1], (EDGES, D), 1.0, 6.0, ((0, 16),))
    edge_source = draw_edge_source(jax.random.fold_in(jax.random.fold_in(keys[18], part), 71), part)
    receivers = place_ends(jax.random.randint(own_keys[3], (EDGES,), 0, NODE_DEV), jax.random.fold_in(own_keys[3], 1), 0, NODE_DEV - 1).astype(jnp.int32)
    near_rows = place_ends(jax.random.randint(own_keys[4], (PARTS_SIZE, 4, NEAR_CAP), 0, NODE_DEV), jax.random.fold_in(own_keys[4], 1), 0, NODE_DEV - 1).astype(jnp.int32)
    far_rows = place_ends(jax.random.randint(own_keys[5], (PARTS_SIZE, PARTS_SIZE, FAR_CAP), 0, NODE_DEV), jax.random.fold_in(own_keys[5], 1), 0, NODE_DEV - 1).astype(jnp.int32)
    edge_in_weight = normal_values(keys[6], (3, D, H), (3 * D) ** -0.5, 0.15625, ((1, 4),))
    edge_out_weight = normal_values(keys[7], (H, D), H ** -0.5, 0.25, ((0, 4),))
    node_in_weight = normal_values(keys[8], (2, D, H), (2 * D) ** -0.5, 0.1875, ((1, 4),))
    node_out_weight = normal_values(keys[9], (H, D), H ** -0.5, 0.25, ((0, 4),))
    edge_in_bias = normal_values(keys[10], (H,), 1.0, 4.0, (), jnp.float32)
    edge_out_bias = normal_values(keys[11], (D,), 1.0, 4.0, (), jnp.float32)
    edge_gain = jnp.clip(1.0 + 0.1 * jax.random.normal(keys[12], (D,), jnp.float32), 0.5, 1.5)
    edge_offset = normal_values(keys[13], (D,), 0.5, 3.0, (), jnp.float32)
    node_in_bias = normal_values(keys[14], (H,), 1.0, 4.0, (), jnp.float32)
    node_out_bias = normal_values(keys[15], (D,), 1.0, 4.0, (), jnp.float32)
    node_gain = jnp.clip(1.0 + 0.1 * jax.random.normal(keys[16], (D,), jnp.float32), 0.5, 1.5)
    node_offset = normal_values(keys[17], (D,), 0.5, 3.0, (), jnp.float32)
    return dict(node_latent=node_latent, edge_latent=edge_latent, edge_source=edge_source, receivers=receivers, near_rows=near_rows, far_rows=far_rows, edge_in_weight=edge_in_weight, edge_out_weight=edge_out_weight, node_in_weight=node_in_weight, node_out_weight=node_out_weight, edge_in_bias=edge_in_bias, edge_out_bias=edge_out_bias, edge_gain=edge_gain, edge_offset=edge_offset, node_in_bias=node_in_bias, node_out_bias=node_out_bias, node_gain=node_gain, node_offset=node_offset)


near_offsets = (1, 2, -1, -2)

def layer_norm(values, gain, offset):
    average = lax.optimization_barrier(jnp.mean(values, axis=-1, keepdims=True))
    centred = values - average
    spread = lax.optimization_barrier(jnp.mean(centred * centred, axis=-1, keepdims=True))
    return centred * lax.rsqrt(spread + 1e-05) * gain + offset

def node_update(latent, summed, node_in, node_out, in_bias, out_bias, gain, offset):
    preact = jnp.dot(latent, node_in[0], preferred_element_type=jnp.float32)
    preact = preact + jnp.dot(summed.astype(jnp.bfloat16), node_in[1], preferred_element_type=jnp.float32) + in_bias
    hidden = jax.nn.silu(preact).astype(jnp.bfloat16)
    output = jnp.dot(hidden, node_out, preferred_element_type=jnp.float32) + out_bias
    return (latent.astype(jnp.float32) + layer_norm(output, gain, offset)).astype(jnp.bfloat16)

def reference(node_latent, edge_latent, edge_source, receivers, near_rows, far_rows, edge_in_weight, edge_out_weight, node_in_weight, node_out_weight, edge_in_bias, edge_out_bias, edge_gain, edge_offset, node_in_bias, node_out_bias, node_gain, node_offset):
    sender_proj = jnp.dot(node_latent, edge_in_weight[1], preferred_element_type=jnp.float32).astype(jnp.bfloat16)
    recv_proj = jnp.dot(node_latent, edge_in_weight[2], preferred_element_type=jnp.float32)
    by_part = sender_proj.reshape(PARTS_SIZE, NODE_DEV, H)
    block = DEGREE * NODE_DEV
    every_part = jnp.arange(PARTS_SIZE, dtype=jnp.int32)

    def one_part(inputs):
        part_index, edges, anchor, targets, latent, projected = inputs
        pieces = [by_part[part_index]]
        for which, offset in enumerate(near_offsets):
            source_part = (part_index - offset) % PARTS_SIZE
            pieces.append(jnp.take(by_part[source_part], near_rows[source_part, which], axis=0))
        far_ids = far_rows[:, part_index, :]
        pieces.append(by_part[every_part[:, None], far_ids].reshape(PARTS_SIZE * FAR_CAP, H))
        source_table = jnp.concatenate(pieces, axis=0)
        preact = jnp.dot(edges, edge_in_weight[0], preferred_element_type=jnp.float32)
        preact = preact + jnp.take(source_table, anchor, axis=0).astype(jnp.float32)
        preact = preact + jnp.take(projected, targets, axis=0) + edge_in_bias
        hidden = jax.nn.silu(preact).astype(jnp.bfloat16)
        output = jnp.dot(hidden, edge_out_weight, preferred_element_type=jnp.float32) + edge_out_bias
        edge_new = (edges.astype(jnp.float32) + layer_norm(output, edge_gain, edge_offset)).astype(jnp.bfloat16)
        summed = jax.ops.segment_sum(edge_new.astype(jnp.float32), targets, num_segments=NODE_DEV)
        node_new = node_update(latent, summed, node_in_weight, node_out_weight, node_in_bias, node_out_bias, node_gain, node_offset)
        return (edge_new, node_new)
    edge_new, node_new = lax.map(one_part, (every_part, edge_latent.reshape(PARTS_SIZE, block, D), edge_source.reshape(PARTS_SIZE, block), receivers.reshape(PARTS_SIZE, block), node_latent.reshape(PARTS_SIZE, NODE_DEV, D), recv_proj.reshape(PARTS_SIZE, NODE_DEV, H)))
    return (edge_new.reshape(EDGES, D), node_new.reshape(NODES, D))
```

```python
import functools

import jax
import jax.numpy as jnp
from jax import lax
from jax.experimental import pallas as pl
from jax.experimental.pallas import tpu as pltpu
from jax.sharding import PartitionSpec as P

near_offsets = (1, 2, -1, -2)
tile_rows = 16
lanes = 128
direct_parts = 8
bf16 = jnp.bfloat16
f32 = jnp.float32
vmem = pl.BlockSpec(memory_space=pltpu.VMEM)
smem = pl.BlockSpec(memory_space=pltpu.SMEM)


def wrap(value, count):
    return jnp.where(value < 0, value + count, value)


def as_columns(row):
    return jnp.transpose(jnp.broadcast_to(row, (lanes, row.shape[1])))


def one_hot(columns, width):
    place = lax.broadcasted_iota(jnp.int32, columns.shape, 1)
    return jnp.concatenate(
        [
            jnp.where(columns == place + start, 1.0, 0.0).astype(bf16)
            for start in range(0, width, lanes)
        ],
        axis=1,
    )


def silu(values):
    half = 0.5 * values
    return half + half * jnp.tanh(half)


def layer_norm(values, gain, offset):
    average = jnp.mean(values, axis=-1, keepdims=True)
    centred = values - average
    spread = jnp.mean(centred * centred, axis=-1, keepdims=True)
    return centred * lax.rsqrt(spread + 1e-05) * gain + offset


def pick_kernel(part_count, near_cap, far_cap, far_ref, near_ref, latent_ref, *out_refs):
    me = lax.axis_index("region") * lax.axis_size("feat") + lax.axis_index("feat")
    near = near_ref[...]
    row = jnp.concatenate([near[which : which + 1] for which in range(len(near_offsets))], axis=1)
    near_columns = as_columns(row)
    far_columns = jnp.full((part_count * tile_rows, lanes), -1, jnp.int32)
    row_place = lax.broadcasted_iota(jnp.int32, far_columns.shape, 0)
    for shift in range(part_count):
        target = lax.rem(me + shift, part_count)
        for slot in range(far_cap):
            far_columns = jnp.where(
                row_place == shift * tile_rows + slot,
                far_ref[target * far_cap + slot],
                far_columns,
            )
    hot = one_hot(jnp.concatenate([near_columns, far_columns], axis=0), latent_ref.shape[0])
    picked = jnp.dot(hot, latent_ref[...], preferred_element_type=f32).astype(bf16)
    far_start = len(near_offsets) * near_cap
    for shift in range(part_count):
        far = picked[far_start + shift * tile_rows : far_start + (shift + 1) * tile_rows]
        which = near_shift(shift, part_count)
        if which is None:
            out_refs[shift][...] = far
        else:
            out_refs[shift][:near_cap] = picked[which * near_cap : (which + 1) * near_cap]
            out_refs[shift][near_cap:] = far


def near_shift(shift, part_count):
    for which, offset in enumerate(near_offsets):
        if offset % part_count == shift:
            return which
    return None


def exchange_direct(node_latent, near_rows, far_rows, part_count):
    near_cap, far_cap = near_rows.shape[2], far_rows.shape[2]
    width = node_latent.shape[1]
    shapes = []
    for shift in range(part_count):
        rows = tile_rows if near_shift(shift, part_count) is None else near_cap + tile_rows
        shapes.append(jax.ShapeDtypeStruct((rows, width), bf16))
    blocks = pl.pallas_call(
        functools.partial(pick_kernel, part_count, near_cap, far_cap),
        out_shape=shapes,
        in_specs=[smem, vmem, vmem],
        out_specs=[vmem] * part_count,
        name="pick_halo",
    )(far_rows.reshape(-1), near_rows[0], node_latent)
    got = [blocks[0]]
    for shift in range(1, part_count):
        pairs = [(part, (part + shift) % part_count) for part in range(part_count)]
        got.append(lax.ppermute(blocks[shift], ("region", "feat"), pairs))
    return got


def exchange_all(node_latent, near_rows, far_rows, part_count):
    near_send = jnp.take(node_latent, near_rows[0], axis=0, mode="clip")
    far_send = jnp.take(node_latent, far_rows[0], axis=0, mode="clip")
    got = []
    for which, offset in enumerate(near_offsets):
        pairs = [(part, (part + offset) % part_count) for part in range(part_count)]
        got.append(lax.ppermute(near_send[which], ("region", "feat"), pairs))
    far = lax.all_to_all(far_send, ("region", "feat"), split_axis=0, concat_axis=0, tiled=True)
    got.append(far.reshape(-1, far.shape[2]))
    return got


def gather_kernel(
    part_count, near_cap, far_cap, by_shift, source_ref, receiver_ref, latent_ref, *refs
):
    got_refs, out_ref, table = refs[:-2], refs[-2], refs[-1]
    node_count, width = latent_ref.shape
    far_start = node_count + len(near_offsets) * near_cap

    @pl.when(pl.program_id(0) == 0)
    def _():
        table[:node_count] = latent_ref[...]
        if by_shift:
            for shift in range(part_count):
                which = near_shift(shift, part_count)
                start = 0
                if which is not None:
                    start = near_cap
                    place = node_count + which * near_cap
                    table[place : place + near_cap] = got_refs[shift][:near_cap]
                place = far_start + shift * tile_rows
                table[place : place + tile_rows] = got_refs[shift][start : start + tile_rows]
            used = far_start + part_count * tile_rows
        else:
            for which in range(len(near_offsets)):
                place = node_count + which * near_cap
                table[place : place + near_cap] = got_refs[which][...]
            used = far_start + got_refs[-1].shape[0]
            table[far_start:used] = got_refs[-1][...]
        if used < table.shape[0]:
            table[used:] = jnp.zeros((table.shape[0] - used, width), bf16)

    source = source_ref[0]
    if by_shift:
        me = lax.axis_index("region") * lax.axis_size("feat") + lax.axis_index("feat")
        far = source - far_start
        part = lax.div(far, far_cap)
        slot = far - part * far_cap
        shifted = far_start + wrap(me - part, part_count) * tile_rows + slot
        source = jnp.where(far >= 0, shifted, source)
    sent = one_hot(as_columns(source), table.shape[0])
    out_ref[:, :width] = jnp.dot(sent, table[...], preferred_element_type=f32).astype(bf16)
    received = one_hot(as_columns(receiver_ref[0]), node_count)
    out_ref[:, width:] = jnp.dot(
        received, latent_ref[...], preferred_element_type=f32
    ).astype(bf16)


def place_rows(whole, pieces, order):
    for piece, owner in zip(pieces, order):
        rows = piece.shape[-2]
        spot = pl.ds(pl.multiple_of(owner * rows, rows), rows)
        if len(whole.shape) == 3:
            whole[:, spot, :] = piece[...]
        else:
            whole[spot, :] = piece[...]


def owners():
    feat, feats = lax.axis_index("feat"), lax.axis_size("feat")
    sub, subs = lax.axis_index("sub"), lax.axis_size("sub")
    order = []
    for turn in range(subs):
        for shift in range(feats):
            order.append(
                wrap(feat - shift, feats) * subs + wrap(sub - turn, subs)
            )
    return order


def gather_rows(weight):
    feats, subs = lax.axis_size("feat"), lax.axis_size("sub")
    own = [weight]
    for shift in range(1, feats):
        own.append(lax.ppermute(weight, "feat", [(at, (at + shift) % feats) for at in range(feats)]))
    pieces = list(own)
    for turn in range(1, subs):
        pairs = [(at, (at + turn) % subs) for at in range(subs)]
        pieces += [lax.ppermute(piece, "sub", pairs) for piece in own]
    return pieces


def edge_kernel(pieces_count, *refs):
    edge_ref, gathered_ref, receiver_ref = refs[:3]
    in_pieces = refs[3 : 3 + pieces_count]
    out_pieces = refs[3 + pieces_count : 3 + 2 * pieces_count]
    in_bias, out_bias, gain, offset, new_ref, sum_ref, in_weight, out_weight, total = refs[
        3 + 2 * pieces_count :
    ]
    width = edge_ref.shape[1]
    step = pl.program_id(0)

    @pl.when(step == 0)
    def _():
        order = owners()
        place_rows(in_weight, in_pieces, order)
        place_rows(out_weight, out_pieces, order)

    edges = edge_ref[...]
    preact = jnp.dot(edges, in_weight[0], preferred_element_type=f32)
    preact += jnp.dot(gathered_ref[:, :width], in_weight[1], preferred_element_type=f32)
    preact += jnp.dot(gathered_ref[:, width:], in_weight[2], preferred_element_type=f32)
    hidden = silu(preact + in_bias[...]).astype(bf16)
    output = jnp.dot(hidden, out_weight[...], preferred_element_type=f32) + out_bias[...]
    edge_new = (edges.astype(f32) + layer_norm(output, gain[...], offset[...])).astype(bf16)
    new_ref[...] = edge_new
    receiver = receiver_ref[0]
    node_place = lax.broadcasted_iota(jnp.int32, (total.shape[0], receiver.shape[1]), 0)
    hot = jnp.where(node_place == receiver, 1.0, 0.0).astype(bf16)
    part = jnp.dot(hot, edge_new, preferred_element_type=f32)

    @pl.when(step == 0)
    def _():
        total[...] = part

    @pl.when(step > 0)
    def _():
        total[...] += part

    @pl.when(step == pl.num_programs(0) - 1)
    def _():
        sum_ref[...] = total[...].astype(bf16)


def node_kernel(pieces_count, *refs):
    latent_ref, own_ref, other_ref = refs[:3]
    in_pieces = refs[3 : 3 + pieces_count]
    out_pieces = refs[3 + pieces_count : 3 + 2 * pieces_count]
    in_bias, out_bias, gain, offset, new_ref, in_weight, out_weight = refs[3 + 2 * pieces_count :]
    order = owners()
    place_rows(in_weight, in_pieces, order)
    place_rows(out_weight, out_pieces, order)
    latent = latent_ref[...]
    summed = (own_ref[...].astype(f32) + other_ref[...].astype(f32)).astype(bf16)
    preact = jnp.dot(latent, in_weight[0], preferred_element_type=f32)
    preact += jnp.dot(summed, in_weight[1], preferred_element_type=f32)
    hidden = silu(preact + in_bias[...]).astype(bf16)
    output = jnp.dot(hidden, out_weight[...], preferred_element_type=f32) + out_bias[...]
    new_ref[...] = (
        latent.astype(f32) + layer_norm(output, gain[...], offset[...])
    ).astype(bf16)


def shards(
    node_latent,
    edge_latent,
    edge_source,
    receivers,
    near_rows,
    far_rows,
    edge_in_weight,
    edge_out_weight,
    node_in_weight,
    node_out_weight,
    edge_in_bias,
    edge_out_bias,
    edge_gain,
    edge_offset,
    node_in_bias,
    node_out_bias,
    node_gain,
    node_offset,
):
    node_count, width = node_latent.shape
    edge_count = edge_latent.shape[0]
    near_cap, far_cap = near_rows.shape[2], far_rows.shape[2]
    part_count = far_rows.shape[1]
    block = 512
    steps = edge_count // block

    edge_in = gather_rows(edge_in_weight)
    edge_out = gather_rows(edge_out_weight)
    node_in = gather_rows(node_in_weight)
    node_out = gather_rows(node_out_weight)
    pieces_count = len(edge_in)

    by_shift = part_count <= direct_parts
    exchange = exchange_direct if by_shift else exchange_all
    got = exchange(node_latent, near_rows, far_rows, part_count)
    far_space = part_count * tile_rows if by_shift else got[-1].shape[0]
    table_rows = node_count + len(near_offsets) * near_cap + far_space
    table_rows = -(-table_rows // lanes) * lanes

    source_blocks = edge_source.reshape(steps, 1, block)
    receiver_blocks = receivers.reshape(steps, 1, block)
    index_spec = pl.BlockSpec((1, 1, block), lambda step: (step, 0, 0))

    def whole(array):
        return pl.BlockSpec(array.shape, lambda step: (0,) * array.ndim)

    gathered = pl.pallas_call(
        functools.partial(gather_kernel, part_count, near_cap, far_cap, by_shift),
        grid=(steps,),
        out_shape=jax.ShapeDtypeStruct((edge_count, 2 * width), bf16),
        in_specs=[index_spec, index_spec, whole(node_latent)] + [whole(rows) for rows in got],
        out_specs=pl.BlockSpec((block, 2 * width), lambda step: (step, 0)),
        scratch_shapes=[pltpu.VMEM((table_rows, width), bf16)],
        cost_estimate=pl.CostEstimate(
            flops=2 * edge_count * width * (table_rows + node_count),
            bytes_accessed=4 * edge_count * width,
            transcendentals=0,
        ),
        name="gather_latents",
    )(source_blocks, receiver_blocks, node_latent, *got)

    rows = [value.reshape(1, -1) for value in (edge_in_bias, edge_out_bias, edge_gain, edge_offset)]
    edge_new, partial_sums = pl.pallas_call(
        functools.partial(edge_kernel, pieces_count),
        grid=(steps,),
        out_shape=[
            jax.ShapeDtypeStruct((edge_count, width), bf16),
            jax.ShapeDtypeStruct((node_count, width), bf16),
        ],
        in_specs=[
            pl.BlockSpec((block, width), lambda step: (step, 0)),
            pl.BlockSpec((block, 2 * width), lambda step: (step, 0)),
            index_spec,
        ]
        + [whole(piece) for piece in edge_in + edge_out]
        + [whole(row) for row in rows],
        out_specs=[
            pl.BlockSpec((block, width), lambda step: (step, 0)),
            pl.BlockSpec((node_count, width), lambda step: (0, 0)),
        ],
        scratch_shapes=[
            pltpu.VMEM((3, pieces_count * edge_in_weight.shape[1], width), bf16),
            pltpu.VMEM((pieces_count * edge_out_weight.shape[0], width), bf16),
            pltpu.VMEM((node_count, width), f32),
        ],
        compiler_params=pltpu.CompilerParams(vmem_limit_bytes=40 << 20),
        cost_estimate=pl.CostEstimate(
            flops=2 * edge_count * width * (4 * width + node_count),
            bytes_accessed=8 * edge_count * width,
            transcendentals=edge_count * width,
        ),
        name="edge_update",
    )(edge_latent, gathered, receiver_blocks, *edge_in, *edge_out, *rows)

    subs = lax.axis_size("sub")
    other_sums = lax.ppermute(partial_sums, "sub", [(at, (at + 1) % subs) for at in range(subs)])

    rows = [value.reshape(1, -1) for value in (node_in_bias, node_out_bias, node_gain, node_offset)]
    node_new = pl.pallas_call(
        functools.partial(node_kernel, pieces_count),
        out_shape=jax.ShapeDtypeStruct((node_count, width), bf16),
        in_specs=[vmem] * (3 + 2 * pieces_count + 4),
        out_specs=vmem,
        scratch_shapes=[
            pltpu.VMEM((2, pieces_count * node_in_weight.shape[1], width), bf16),
            pltpu.VMEM((pieces_count * node_out_weight.shape[0], width), bf16),
        ],
        compiler_params=pltpu.CompilerParams(vmem_limit_bytes=40 << 20),
        cost_estimate=pl.CostEstimate(
            flops=2 * node_count * width * 3 * width,
            bytes_accessed=10 * node_count * width,
            transcendentals=node_count * width,
        ),
        name="node_update",
    )(node_latent, partial_sums, other_sums, *node_in, *node_out, *rows)
    return (edge_new, node_new)


def solution(mesh):
    return jax.shard_map(
        shards,
        mesh=mesh,
        in_specs=(
            P(("groups", "region", "feat"), None),
            P(("groups", "region", "feat", "sub"), None),
            P(("groups", "region", "feat", "sub")),
            P(("groups", "region", "feat", "sub")),
            P(("groups", "region", "feat"), None, None),
            P(("groups", "region", "feat"), None, None),
            P(None, ("feat", "sub"), None),
            P(("feat", "sub"), None),
            P(None, ("feat", "sub"), None),
            P(("feat", "sub"), None),
            P(),
            P(),
            P(),
            P(),
            P(),
            P(),
            P(),
            P(),
        ),
        out_specs=(
            P(("groups", "region", "feat", "sub"), None),
            P(("groups", "region", "feat"), None),
        ),
        check_vma=False,
    )
```

```python
import functools

import jax
import jax.numpy as jnp
from jax import lax
from jax.experimental import pallas as pl
from jax.experimental.pallas import tpu as pltpu
from jax.sharding import PartitionSpec as P

near_offsets = (1, 2, -1, -2)
tile_rows = 16
lanes = 128
padded_parts = 8
bf16 = jnp.bfloat16
f32 = jnp.float32
vmem = pl.BlockSpec(memory_space=pltpu.VMEM)
smem = pl.BlockSpec(memory_space=pltpu.SMEM)


def wrap(value, count):
    return jnp.where(value < 0, value + count, value)


def as_columns(row):
    return jnp.transpose(jnp.broadcast_to(row, (lanes, row.shape[1])))


def one_hot(columns, width):
    place = lax.broadcasted_iota(jnp.int32, columns.shape, 1)
    return jnp.concatenate(
        [
            jnp.where(columns == place + start, 1.0, 0.0).astype(bf16)
            for start in range(0, width, lanes)
        ],
        axis=1,
    )


def silu(values):
    half = 0.5 * values
    return half + half * jnp.tanh(half)


def layer_norm(values, gain, offset):
    average = jnp.mean(values, axis=-1, keepdims=True)
    centred = values - average
    spread = jnp.mean(centred * centred, axis=-1, keepdims=True)
    return centred * lax.rsqrt(spread + 1e-05) * gain + offset


def my_part():
    return lax.axis_index("region") * lax.axis_size("feat") + lax.axis_index("feat")


def pick_kernel(part_count, near_cap, far_cap, far_ref, near_ref, latent_ref, out_ref):
    me = my_part()
    near = near_ref[0]
    row = jnp.concatenate([near[which : which + 1] for which in range(len(near_offsets))], axis=1)
    columns = [as_columns(row)]
    tile_place = lax.broadcasted_iota(jnp.int32, (tile_rows, lanes), 0)
    far = [as_columns(far_ref[0, slot : slot + 1]) for slot in range(far_cap)]
    for part in range(part_count):
        tile = jnp.full((tile_rows, lanes), -1, jnp.int32)
        for slot in range(far_cap):
            tile = jnp.where(tile_place == slot, far[slot][part : part + 1], tile)
        columns.append(tile)
    hot = one_hot(jnp.concatenate(columns, axis=0), latent_ref.shape[0])
    picked = jnp.dot(hot, latent_ref[...], preferred_element_type=f32).astype(bf16)
    for which, offset in enumerate(near_offsets):
        target = lax.rem(me + (offset + part_count), part_count)
        out_ref[target, :near_cap] = picked[which * near_cap : (which + 1) * near_cap]
    far_start = len(near_offsets) * near_cap
    for part in range(part_count):
        out_ref[part, near_cap:] = picked[
            far_start + part * tile_rows : far_start + (part + 1) * tile_rows
        ]


def exchange_padded(node_latent, near_rows, far_rows, part_count):
    near_cap, far_cap = near_rows.shape[2], far_rows.shape[2]
    block = (part_count, near_cap + tile_rows, node_latent.shape[1])
    blocks = pl.pallas_call(
        functools.partial(pick_kernel, part_count, near_cap, far_cap),
        out_shape=jax.ShapeDtypeStruct(block, bf16),
        in_specs=[vmem, vmem, vmem],
        out_specs=vmem,
        name="pick_halo",
    )(jnp.transpose(far_rows, (0, 2, 1)), near_rows, node_latent)
    return [
        lax.all_to_all(blocks, ("region", "feat"), split_axis=0, concat_axis=0, tiled=True)
    ]


def exchange_all(node_latent, near_rows, far_rows, part_count):
    near_send = jnp.take(node_latent, near_rows[0], axis=0, mode="clip")
    far_send = jnp.take(node_latent, far_rows[0], axis=0, mode="clip")
    got = []
    for which, offset in enumerate(near_offsets):
        pairs = [(part, (part + offset) % part_count) for part in range(part_count)]
        got.append(lax.ppermute(near_send[which], ("region", "feat"), pairs))
    far = lax.all_to_all(far_send, ("region", "feat"), split_axis=0, concat_axis=0, tiled=True)
    got.append(far.reshape(-1, far.shape[2]))
    return got


def gather_kernel(
    part_count, near_cap, far_cap, padded, source_ref, receiver_ref, latent_ref, *refs
):
    got_refs, out_ref, table = refs[:-2], refs[-2], refs[-1]
    node_count, width = latent_ref.shape
    far_start = node_count + len(near_offsets) * near_cap

    @pl.when(pl.program_id(0) == 0)
    def _():
        table[:node_count] = latent_ref[...]
        for which, offset in enumerate(near_offsets):
            place = node_count + which * near_cap
            if padded:
                origin = lax.rem(my_part() + (part_count - offset), part_count)
                table[place : place + near_cap] = got_refs[0][origin, :near_cap]
            else:
                table[place : place + near_cap] = got_refs[which][...]
        if padded:
            for part in range(part_count):
                place = far_start + part * tile_rows
                table[place : place + tile_rows] = got_refs[0][part, near_cap:]
            used = far_start + part_count * tile_rows
        else:
            used = far_start + got_refs[-1].shape[0]
            table[far_start:used] = got_refs[-1][...]
        if used < table.shape[0]:
            table[used:] = jnp.zeros((table.shape[0] - used, width), bf16)

    source = source_ref[0]
    if padded:
        far = source - far_start
        part = lax.div(far, far_cap)
        spread = far_start + part * (tile_rows - far_cap) + far
        source = jnp.where(far >= 0, spread, source)
    sent = one_hot(as_columns(source), table.shape[0])
    out_ref[:, :width] = jnp.dot(sent, table[...], preferred_element_type=f32).astype(bf16)
    received = one_hot(as_columns(receiver_ref[0]), node_count)
    out_ref[:, width:] = jnp.dot(
        received, latent_ref[...], preferred_element_type=f32
    ).astype(bf16)


def place_rows(whole, pieces, order):
    for piece, owner in zip(pieces, order):
        rows = piece.shape[-2]
        spot = pl.ds(pl.multiple_of(owner * rows, rows), rows)
        if len(whole.shape) == 3:
            whole[:, spot, :] = piece[...]
        else:
            whole[spot, :] = piece[...]


def owners():
    feat, feats = lax.axis_index("feat"), lax.axis_size("feat")
    sub, subs = lax.axis_index("sub"), lax.axis_size("sub")
    own = [(0, turn) for turn in range(subs)]
    rest = [(shift, turn) for turn in range(subs) for shift in range(1, feats)]
    return [
        wrap(feat - shift, feats) * subs + wrap(sub - turn, subs) for shift, turn in own + rest
    ]


def from_feats(weight):
    feats = lax.axis_size("feat")
    return [
        lax.ppermute(weight, "feat", [(at, (at + shift) % feats) for at in range(feats)])
        for shift in range(1, feats)
    ]


def from_subs(pieces):
    subs = lax.axis_size("sub")
    return [
        lax.ppermute(piece, "sub", [(at, (at + turn) % subs) for at in range(subs)])
        for turn in range(1, subs)
        for piece in pieces
    ]


def edge_kernel(pieces_count, *refs):
    edge_ref, gathered_ref, receiver_ref = refs[:3]
    in_pieces = refs[3 : 3 + pieces_count]
    out_pieces = refs[3 + pieces_count : 3 + 2 * pieces_count]
    in_bias, out_bias, gain, offset, new_ref, sum_ref, in_weight, out_weight, total = refs[
        3 + 2 * pieces_count :
    ]
    width = edge_ref.shape[1]
    step = pl.program_id(0)

    @pl.when(step == 0)
    def _():
        order = owners()
        place_rows(in_weight, in_pieces, order)
        place_rows(out_weight, out_pieces, order)

    edges = edge_ref[...]
    preact = jnp.dot(edges, in_weight[0], preferred_element_type=f32)
    preact += jnp.dot(gathered_ref[:, :width], in_weight[1], preferred_element_type=f32)
    preact += jnp.dot(gathered_ref[:, width:], in_weight[2], preferred_element_type=f32)
    hidden = silu(preact + in_bias[...]).astype(bf16)
    output = jnp.dot(hidden, out_weight[...], preferred_element_type=f32) + out_bias[...]
    edge_new = (edges.astype(f32) + layer_norm(output, gain[...], offset[...])).astype(bf16)
    new_ref[...] = edge_new
    receiver = receiver_ref[0]
    node_place = lax.broadcasted_iota(jnp.int32, (total.shape[0], receiver.shape[1]), 0)
    hot = jnp.where(node_place == receiver, 1.0, 0.0).astype(bf16)
    part = jnp.dot(hot, edge_new, preferred_element_type=f32)

    @pl.when(step == 0)
    def _():
        total[...] = part

    @pl.when(step > 0)
    def _():
        total[...] += part

    @pl.when(step == pl.num_programs(0) - 1)
    def _():
        sum_ref[...] = total[...].astype(bf16)


def node_kernel(pieces_count, *refs):
    latent_ref, own_ref, other_ref = refs[:3]
    in_pieces = refs[3 : 3 + pieces_count]
    out_pieces = refs[3 + pieces_count : 3 + 2 * pieces_count]
    in_bias, out_bias, gain, offset, new_ref, in_weight, out_weight = refs[3 + 2 * pieces_count :]
    order = owners()
    place_rows(in_weight, in_pieces, order)
    place_rows(out_weight, out_pieces, order)
    latent = latent_ref[...]
    summed = (own_ref[...].astype(f32) + other_ref[...].astype(f32)).astype(bf16)
    preact = jnp.dot(latent, in_weight[0], preferred_element_type=f32)
    preact += jnp.dot(summed, in_weight[1], preferred_element_type=f32)
    hidden = silu(preact + in_bias[...]).astype(bf16)
    output = jnp.dot(hidden, out_weight[...], preferred_element_type=f32) + out_bias[...]
    new_ref[...] = (
        latent.astype(f32) + layer_norm(output, gain[...], offset[...])
    ).astype(bf16)


def shards(
    node_latent,
    edge_latent,
    edge_source,
    receivers,
    near_rows,
    far_rows,
    edge_in_weight,
    edge_out_weight,
    node_in_weight,
    node_out_weight,
    edge_in_bias,
    edge_out_bias,
    edge_gain,
    edge_offset,
    node_in_bias,
    node_out_bias,
    node_gain,
    node_offset,
):
    node_count, width = node_latent.shape
    edge_count = edge_latent.shape[0]
    near_cap, far_cap = near_rows.shape[2], far_rows.shape[2]
    part_count = far_rows.shape[1]
    block = 512
    steps = edge_count // block

    far_edge = [from_feats(edge_in_weight), from_feats(edge_out_weight)]
    near_edge = [from_subs([edge_in_weight]), from_subs([edge_out_weight])]

    padded = part_count <= padded_parts
    exchange = exchange_padded if padded else exchange_all
    got = exchange(node_latent, near_rows, far_rows, part_count)
    far_space = part_count * tile_rows if padded else got[-1].shape[0]
    table_rows = node_count + len(near_offsets) * near_cap + far_space
    table_rows = -(-table_rows // lanes) * lanes

    source_blocks = edge_source.reshape(steps, 1, block)
    receiver_blocks = receivers.reshape(steps, 1, block)
    index_spec = pl.BlockSpec((1, 1, block), lambda step: (step, 0, 0))

    def whole(array):
        return pl.BlockSpec(array.shape, lambda step: (0,) * array.ndim)

    gathered = pl.pallas_call(
        functools.partial(gather_kernel, part_count, near_cap, far_cap, padded),
        grid=(steps,),
        out_shape=jax.ShapeDtypeStruct((edge_count, 2 * width), bf16),
        in_specs=[index_spec, index_spec, whole(node_latent)] + [whole(rows) for rows in got],
        out_specs=pl.BlockSpec((block, 2 * width), lambda step: (step, 0)),
        scratch_shapes=[pltpu.VMEM((table_rows, width), bf16)],
        cost_estimate=pl.CostEstimate(
            flops=2 * edge_count * width * (table_rows + node_count),
            bytes_accessed=4 * edge_count * width,
            transcendentals=0,
        ),
        name="gather_latents",
    )(source_blocks, receiver_blocks, node_latent, *got)

    far_edge, gathered, node_in_weight, node_out_weight = lax.optimization_barrier(
        (far_edge, gathered, node_in_weight, node_out_weight)
    )
    edge_in, edge_out = [
        [weight] + near + far + from_subs(far)
        for weight, near, far in zip((edge_in_weight, edge_out_weight), near_edge, far_edge)
    ]
    far_node = [from_feats(node_in_weight), from_feats(node_out_weight)]
    node_in, node_out = [
        [weight] + from_subs([weight]) + far + from_subs(far)
        for weight, far in zip((node_in_weight, node_out_weight), far_node)
    ]
    pieces_count = len(edge_in)

    rows = [value.reshape(1, -1) for value in (edge_in_bias, edge_out_bias, edge_gain, edge_offset)]
    edge_new, partial_sums = pl.pallas_call(
        functools.partial(edge_kernel, pieces_count),
        grid=(steps,),
        out_shape=[
            jax.ShapeDtypeStruct((edge_count, width), bf16),
            jax.ShapeDtypeStruct((node_count, width), bf16),
        ],
        in_specs=[
            pl.BlockSpec((block, width), lambda step: (step, 0)),
            pl.BlockSpec((block, 2 * width), lambda step: (step, 0)),
            index_spec,
        ]
        + [whole(piece) for piece in edge_in + edge_out]
        + [whole(row) for row in rows],
        out_specs=[
            pl.BlockSpec((block, width), lambda step: (step, 0)),
            pl.BlockSpec((node_count, width), lambda step: (0, 0)),
        ],
        scratch_shapes=[
            pltpu.VMEM((3, pieces_count * edge_in_weight.shape[1], width), bf16),
            pltpu.VMEM((pieces_count * edge_out_weight.shape[0], width), bf16),
            pltpu.VMEM((node_count, width), f32),
        ],
        compiler_params=pltpu.CompilerParams(vmem_limit_bytes=40 << 20),
        cost_estimate=pl.CostEstimate(
            flops=2 * edge_count * width * (4 * width + node_count),
            bytes_accessed=8 * edge_count * width,
            transcendentals=edge_count * width,
        ),
        name="edge_update",
    )(edge_latent, gathered, receiver_blocks, *edge_in, *edge_out, *rows)

    subs = lax.axis_size("sub")
    other_sums = lax.ppermute(partial_sums, "sub", [(at, (at + 1) % subs) for at in range(subs)])

    rows = [value.reshape(1, -1) for value in (node_in_bias, node_out_bias, node_gain, node_offset)]
    node_new = pl.pallas_call(
        functools.partial(node_kernel, pieces_count),
        out_shape=jax.ShapeDtypeStruct((node_count, width), bf16),
        in_specs=[vmem] * (3 + 2 * pieces_count + 4),
        out_specs=vmem,
        scratch_shapes=[
            pltpu.VMEM((2, pieces_count * node_in_weight.shape[1], width), bf16),
            pltpu.VMEM((pieces_count * node_out_weight.shape[0], width), bf16),
        ],
        compiler_params=pltpu.CompilerParams(vmem_limit_bytes=40 << 20),
        cost_estimate=pl.CostEstimate(
            flops=2 * node_count * width * 3 * width,
            bytes_accessed=10 * node_count * width,
            transcendentals=node_count * width,
        ),
        name="node_update",
    )(node_latent, partial_sums, other_sums, *node_in, *node_out, *rows)
    return (edge_new, node_new)


def solution(mesh):
    return jax.shard_map(
        shards,
        mesh=mesh,
        in_specs=(
            P(("groups", "region", "feat"), None),
            P(("groups", "region", "feat", "sub"), None),
            P(("groups", "region", "feat", "sub")),
            P(("groups", "region", "feat", "sub")),
            P(("groups", "region", "feat"), None, None),
            P(("groups", "region", "feat"), None, None),
            P(None, ("feat", "sub"), None),
            P(("feat", "sub"), None),
            P(None, ("feat", "sub"), None),
            P(("feat", "sub"), None),
            P(),
            P(),
            P(),
            P(),
            P(),
            P(),
            P(),
            P(),
        ),
        out_specs=(
            P(("groups", "region", "feat", "sub"), None),
            P(("groups", "region", "feat"), None),
        ),
        check_vma=False,
    )
```

```python
import functools

import jax
import jax.numpy as jnp
from jax import lax
from jax.experimental import pallas as pl
from jax.experimental.pallas import tpu as pltpu
from jax.sharding import PartitionSpec as P

near_offsets = (1, 2, -1, -2)
tile_rows = 16
lanes = 128
padded_parts = 8
grant = 56 << 20
bf16 = jnp.bfloat16
f32 = jnp.float32
vmem = pl.BlockSpec(memory_space=pltpu.VMEM)


def wrap(value, count):
    return jnp.where(value < 0, value + count, value)


def as_columns(row):
    return jnp.transpose(jnp.broadcast_to(row, (lanes, row.shape[1])))


def one_hot(columns, width):
    place = lax.broadcasted_iota(jnp.int32, columns.shape, 1)
    return jnp.concatenate(
        [
            jnp.where(columns == place + start, 1.0, 0.0).astype(bf16)
            for start in range(0, width, lanes)
        ],
        axis=1,
    )


def silu(values):
    half = 0.5 * values
    return half + half * jnp.tanh(half)


def layer_norm(values, gain, offset):
    average = jnp.mean(values, axis=-1, keepdims=True)
    centred = values - average
    spread = jnp.mean(centred * centred, axis=-1, keepdims=True)
    return centred * lax.rsqrt(spread + 1e-05) * gain + offset


def my_part():
    return lax.axis_index("region") * lax.axis_size("feat") + lax.axis_index("feat")


def pick_kernel(part_count, near_cap, far_cap, far_ref, near_ref, latent_ref, out_ref):
    me = my_part()
    near = near_ref[0]
    row = jnp.concatenate([near[which : which + 1] for which in range(len(near_offsets))], axis=1)
    columns = [as_columns(row)]
    tile_place = lax.broadcasted_iota(jnp.int32, (tile_rows, lanes), 0)
    far = [as_columns(far_ref[0, slot : slot + 1]) for slot in range(far_cap)]
    for part in range(part_count):
        tile = jnp.full((tile_rows, lanes), -1, jnp.int32)
        for slot in range(far_cap):
            tile = jnp.where(tile_place == slot, far[slot][part : part + 1], tile)
        columns.append(tile)
    hot = one_hot(jnp.concatenate(columns, axis=0), latent_ref.shape[0])
    picked = jnp.dot(hot, latent_ref[...], preferred_element_type=f32).astype(bf16)
    for which, offset in enumerate(near_offsets):
        target = lax.rem(me + (offset + part_count), part_count)
        out_ref[target, :near_cap] = picked[which * near_cap : (which + 1) * near_cap]
    far_start = len(near_offsets) * near_cap
    for part in range(part_count):
        out_ref[part, near_cap:] = picked[
            far_start + part * tile_rows : far_start + (part + 1) * tile_rows
        ]


def exchange_padded(node_latent, near_rows, far_rows, part_count):
    near_cap, far_cap = near_rows.shape[2], far_rows.shape[2]
    block = (part_count, near_cap + tile_rows, node_latent.shape[1])
    blocks = pl.pallas_call(
        functools.partial(pick_kernel, part_count, near_cap, far_cap),
        out_shape=jax.ShapeDtypeStruct(block, bf16),
        in_specs=[vmem, vmem, vmem],
        out_specs=vmem,
        cost_estimate=pl.CostEstimate(flops=0, bytes_accessed=0, transcendentals=0),
        name="pick_halo",
    )(jnp.transpose(far_rows, (0, 2, 1)), near_rows, node_latent)
    return [
        lax.all_to_all(blocks, ("region", "feat"), split_axis=0, concat_axis=0, tiled=True)
    ]


def exchange_all(node_latent, near_rows, far_rows, part_count):
    near_send = jnp.take(node_latent, near_rows[0], axis=0, mode="clip")
    far_send = jnp.take(node_latent, far_rows[0], axis=0, mode="clip")
    got = []
    for which, offset in enumerate(near_offsets):
        pairs = [(part, (part + offset) % part_count) for part in range(part_count)]
        got.append(lax.ppermute(near_send[which], ("region", "feat"), pairs))
    far = lax.all_to_all(far_send, ("region", "feat"), split_axis=0, concat_axis=0, tiled=True)
    got.append(far.reshape(-1, far.shape[2]))
    return got


def gather_kernel(
    node_count,
    near_cap,
    far_cap,
    far_stride,
    halo_space,
    source_ref,
    receiver_ref,
    latent_ref,
    node_in_ref,
    node_out_ref,
    out_ref,
    pack_ref,
    sems,
):
    width = latent_ref.shape[1]
    halo_start = 2 * width
    count = node_in_ref.shape[0]
    copies = [
        pltpu.make_async_copy(node_in_ref, pack_ref.at[pl.ds(0, count)], sems.at[0]),
        pltpu.make_async_copy(node_out_ref, pack_ref.at[count], sems.at[1]),
    ]

    @pl.when(pl.program_id(0) == 0)
    def _():
        for copy in copies:
            copy.start()

    columns = as_columns(source_ref[0])
    latent = latent_ref[...]
    sent = one_hot(columns, node_count)
    out_ref[:, :width] = jnp.dot(sent, latent, preferred_element_type=f32).astype(bf16)
    received = one_hot(as_columns(receiver_ref[0]), node_count)
    out_ref[:, width:halo_start] = jnp.dot(
        received, latent, preferred_element_type=f32
    ).astype(bf16)
    slot = columns - node_count
    far = slot - len(near_offsets) * near_cap
    part = lax.div(far, far_cap)
    slot = jnp.where(far >= 0, slot + part * (far_stride - far_cap), slot)
    out_ref[:, halo_start:] = one_hot(slot, halo_space)

    @pl.when(pl.program_id(0) == pl.num_programs(0) - 1)
    def _():
        for copy in copies:
            copy.wait()


def place_halo(table, part_count, near_cap, padded, got_refs):
    far_start = len(near_offsets) * near_cap
    for which, offset in enumerate(near_offsets):
        place = which * near_cap
        if padded:
            origin = lax.rem(my_part() + (part_count - offset), part_count)
            table[place : place + near_cap] = got_refs[0][origin, :near_cap]
        else:
            table[place : place + near_cap] = got_refs[which][...]
    if padded:
        for part in range(part_count):
            place = far_start + part * tile_rows
            table[place : place + tile_rows] = got_refs[0][part, near_cap:]
        used = far_start + part_count * tile_rows
    else:
        used = far_start + got_refs[-1].shape[0]
        table[far_start:used] = got_refs[-1][...]
    if used < table.shape[0]:
        table[used:] = jnp.zeros((table.shape[0] - used, table.shape[1]), bf16)


def place_rows(whole, start, piece, owner):
    rows = piece.shape[0]
    whole[pl.ds(pl.multiple_of(start + owner * rows, rows), rows), :] = piece


def owners():
    feat, feats = lax.axis_index("feat"), lax.axis_size("feat")
    sub, subs = lax.axis_index("sub"), lax.axis_size("sub")
    own = [(0, turn) for turn in range(subs)]
    rest = [(shift, turn) for turn in range(subs) for shift in range(1, feats)]
    return [
        wrap(feat - shift, feats) * subs + wrap(sub - turn, subs) for shift, turn in own + rest
    ]


def from_feats(weight):
    feats = lax.axis_size("feat")
    return [
        lax.ppermute(weight, "feat", [(at, (at + shift) % feats) for at in range(feats)])
        for shift in range(1, feats)
    ]


def from_subs(pieces):
    subs = lax.axis_size("sub")
    return [
        lax.ppermute(piece, "sub", [(at, (at + turn) % subs) for at in range(subs)])
        for turn in range(1, subs)
        for piece in pieces
    ]


def edge_kernel(pieces_count, got_count, part_count, near_cap, padded, *refs):
    edge_ref, gathered_ref, receiver_ref = refs[:3]
    got_refs = refs[3 : 3 + got_count]
    in_pieces = refs[3 + got_count : 3 + got_count + pieces_count]
    out_pieces = refs[3 + got_count + pieces_count : 3 + got_count + 2 * pieces_count]
    in_bias, out_bias, gain, offset, new_ref, sum_ref, in_weight, out_weight, halo, total = refs[
        3 + got_count + 2 * pieces_count :
    ]
    width = edge_ref.shape[1]
    step = pl.program_id(0)

    @pl.when(step == 0)
    def _():
        for in_piece, out_piece, owner in zip(in_pieces, out_pieces, owners()):
            for which in range(in_piece.shape[0]):
                place_rows(in_weight, which * width, in_piece[which], owner)
            place_rows(out_weight, 0, out_piece[...], owner)
        place_halo(halo, part_count, near_cap, padded, got_refs)
        in_weight[3 * width :] = jnp.dot(
            halo[...], in_weight[width : 2 * width], preferred_element_type=f32
        ).astype(bf16)

    edges = edge_ref[...]
    preact = jnp.dot(
        jnp.concatenate([edges, gathered_ref[...]], axis=1),
        in_weight[...],
        preferred_element_type=f32,
    )
    hidden = silu(preact + in_bias[...]).astype(bf16)
    output = jnp.dot(hidden, out_weight[...], preferred_element_type=f32) + out_bias[...]
    edge_new = (edges.astype(f32) + layer_norm(output, gain[...], offset[...])).astype(bf16)
    new_ref[...] = edge_new
    receiver = receiver_ref[0]
    node_place = lax.broadcasted_iota(jnp.int32, (total.shape[0], receiver.shape[1]), 0)
    hot = jnp.where(node_place == receiver, 1.0, 0.0).astype(bf16)
    part = jnp.dot(hot, edge_new, preferred_element_type=f32)

    @pl.when(step == 0)
    def _():
        total[...] = part

    @pl.when(step > 0)
    def _():
        total[...] += part

    @pl.when(step == pl.num_programs(0) - 1)
    def _():
        sum_ref[...] = total[...].astype(bf16)


def node_kernel(pieces_count, *refs):
    latent_ref, own_ref, other_ref = refs[:3]
    pieces = refs[3 : 3 + pieces_count]
    in_bias, out_bias, gain, offset, new_ref, weights = refs[3 + pieces_count :]
    width = latent_ref.shape[1]
    for piece, owner in zip(pieces, owners()):
        for which in range(piece.shape[0]):
            place_rows(weights, which * width, piece[which], owner)
    latent = latent_ref[...]
    summed = (own_ref[...].astype(f32) + other_ref[...].astype(f32)).astype(bf16)
    preact = jnp.dot(
        jnp.concatenate([latent, summed], axis=1),
        weights[: 2 * width],
        preferred_element_type=f32,
    )
    hidden = silu(preact + in_bias[...]).astype(bf16)
    output = jnp.dot(hidden, weights[2 * width :], preferred_element_type=f32) + out_bias[...]
    new_ref[...] = (
        latent.astype(f32) + layer_norm(output, gain[...], offset[...])
    ).astype(bf16)


def shards(
    node_latent,
    edge_latent,
    edge_source,
    receivers,
    near_rows,
    far_rows,
    edge_in_weight,
    edge_out_weight,
    node_in_weight,
    node_out_weight,
    edge_in_bias,
    edge_out_bias,
    edge_gain,
    edge_offset,
    node_in_bias,
    node_out_bias,
    node_gain,
    node_offset,
):
    node_count, width = node_latent.shape
    edge_count = edge_latent.shape[0]
    near_cap, far_cap = near_rows.shape[2], far_rows.shape[2]
    part_count = far_rows.shape[1]
    block = 512
    steps = edge_count // block

    far_edge = [from_feats(edge_in_weight), from_feats(edge_out_weight)]
    near_edge = [from_subs([edge_in_weight]), from_subs([edge_out_weight])]

    padded = part_count <= padded_parts
    exchange = exchange_padded if padded else exchange_all
    got = exchange(node_latent, near_rows, far_rows, part_count)
    far_stride = tile_rows if padded else far_cap
    halo_space = len(near_offsets) * near_cap + part_count * far_stride
    halo_space = -(-halo_space // lanes) * lanes

    source_blocks = edge_source.reshape(steps, 1, block)
    receiver_blocks = receivers.reshape(steps, 1, block)
    index_spec = pl.BlockSpec((1, 1, block), lambda step: (step, 0, 0))

    def whole(array):
        return pl.BlockSpec(array.shape, lambda step: (0,) * array.ndim)

    hbm = pl.BlockSpec(memory_space=pl.ANY)
    gathered_width = 2 * width + halo_space
    gathered, node_weight = pl.pallas_call(
        functools.partial(
            gather_kernel, node_count, near_cap, far_cap, far_stride, halo_space
        ),
        grid=(steps,),
        out_shape=[
            jax.ShapeDtypeStruct((edge_count, gathered_width), bf16),
            jax.ShapeDtypeStruct((node_in_weight.shape[0] + 1,) + node_out_weight.shape, bf16),
        ],
        in_specs=[index_spec, index_spec, whole(node_latent), hbm, hbm],
        out_specs=[pl.BlockSpec((block, gathered_width), lambda step: (step, 0)), hbm],
        scratch_shapes=[pltpu.SemaphoreType.DMA((2,))],
        compiler_params=pltpu.CompilerParams(vmem_limit_bytes=grant),
        cost_estimate=pl.CostEstimate(flops=0, bytes_accessed=0, transcendentals=0),
        name="gather_latents",
    )(source_blocks, receiver_blocks, node_latent, node_in_weight, node_out_weight)

    far_edge, gathered, node_weight = lax.optimization_barrier(
        (far_edge, gathered, node_weight)
    )
    edge_in, edge_out = [
        [weight] + near + far + from_subs(far)
        for weight, near, far in zip((edge_in_weight, edge_out_weight), near_edge, far_edge)
    ]
    far_node = from_feats(node_weight)
    node_pieces = [node_weight] + from_subs([node_weight]) + far_node + from_subs(far_node)
    pieces_count = len(edge_in)

    rows = [value.reshape(1, -1) for value in (edge_in_bias, edge_out_bias, edge_gain, edge_offset)]
    edge_new, partial_sums = pl.pallas_call(
        functools.partial(edge_kernel, pieces_count, len(got), part_count, near_cap, padded),
        grid=(steps,),
        out_shape=[
            jax.ShapeDtypeStruct((edge_count, width), bf16),
            jax.ShapeDtypeStruct((node_count, width), bf16),
        ],
        in_specs=[
            pl.BlockSpec((block, width), lambda step: (step, 0)),
            pl.BlockSpec((block, gathered_width), lambda step: (step, 0)),
            index_spec,
        ]
        + [whole(rows) for rows in got]
        + [whole(piece) for piece in edge_in + edge_out]
        + [whole(row) for row in rows],
        out_specs=[
            pl.BlockSpec((block, width), lambda step: (step, 0)),
            pl.BlockSpec((node_count, width), lambda step: (0, 0)),
        ],
        scratch_shapes=[
            pltpu.VMEM((3 * width + halo_space, width), bf16),
            pltpu.VMEM((width, width), bf16),
            pltpu.VMEM((halo_space, width), bf16),
            pltpu.VMEM((node_count, width), f32),
        ],
        compiler_params=pltpu.CompilerParams(vmem_limit_bytes=grant),
        cost_estimate=pl.CostEstimate(
            flops=2 * edge_count * width * (4 * width + node_count),
            bytes_accessed=8 * edge_count * width,
            transcendentals=edge_count * width,
        ),
        name="edge_update",
    )(edge_latent, gathered, receiver_blocks, *got, *edge_in, *edge_out, *rows)

    subs = lax.axis_size("sub")
    other_sums = lax.ppermute(partial_sums, "sub", [(at, (at + 1) % subs) for at in range(subs)])

    rows = [value.reshape(1, -1) for value in (node_in_bias, node_out_bias, node_gain, node_offset)]
    node_new = pl.pallas_call(
        functools.partial(node_kernel, pieces_count),
        out_shape=jax.ShapeDtypeStruct((node_count, width), bf16),
        in_specs=[vmem] * (3 + pieces_count + 4),
        out_specs=vmem,
        scratch_shapes=[
            pltpu.VMEM((3 * width, width), bf16),
        ],
        compiler_params=pltpu.CompilerParams(vmem_limit_bytes=grant),
        cost_estimate=pl.CostEstimate(
            flops=2 * node_count * width * 3 * width,
            bytes_accessed=10 * node_count * width,
            transcendentals=node_count * width,
        ),
        name="node_update",
    )(node_latent, partial_sums, other_sums, *node_pieces, *rows)
    return (edge_new, node_new)


def solution(mesh):
    return jax.shard_map(
        shards,
        mesh=mesh,
        in_specs=(
            P(("groups", "region", "feat"), None),
            P(("groups", "region", "feat", "sub"), None),
            P(("groups", "region", "feat", "sub")),
            P(("groups", "region", "feat", "sub")),
            P(("groups", "region", "feat"), None, None),
            P(("groups", "region", "feat"), None, None),
            P(None, ("feat", "sub"), None),
            P(("feat", "sub"), None),
            P(None, ("feat", "sub"), None),
            P(("feat", "sub"), None),
            P(),
            P(),
            P(),
            P(),
            P(),
            P(),
            P(),
            P(),
        ),
        out_specs=(
            P(("groups", "region", "feat", "sub"), None),
            P(("groups", "region", "feat"), None),
        ),
        check_vma=False,
    )
```

```python
import functools

import jax
import jax.numpy as jnp
from jax import lax
from jax.experimental import pallas as pl
from jax.experimental.pallas import tpu as pltpu
from jax.sharding import PartitionSpec as P

near_offsets = (1, 2, -1, -2)
tile_rows = 16
lanes = 128
padded_parts = 8
grant = 24 << 20
bf16 = jnp.bfloat16
f32 = jnp.float32
vmem = pl.BlockSpec(memory_space=pltpu.VMEM)


def wrap(value, count):
    return jnp.where(value < 0, value + count, value)


def as_columns(row):
    return jnp.transpose(jnp.broadcast_to(row, (lanes, row.shape[1])))


def one_hot(columns, width):
    place = lax.broadcasted_iota(jnp.int32, columns.shape, 1)
    return jnp.concatenate(
        [
            jnp.where(columns == place + start, 1.0, 0.0).astype(bf16)
            for start in range(0, width, lanes)
        ],
        axis=1,
    )


def silu(values):
    half = 0.5 * values
    return half + half * jnp.tanh(half)


def layer_norm(values, gain, offset):
    average = jnp.mean(values, axis=-1, keepdims=True)
    centred = values - average
    spread = jnp.mean(centred * centred, axis=-1, keepdims=True)
    return centred * lax.rsqrt(spread + 1e-05) * gain + offset


def my_part():
    return lax.axis_index("region") * lax.axis_size("feat") + lax.axis_index("feat")


def pick_kernel(part_count, near_cap, far_cap, far_ref, near_ref, latent_ref, out_ref):
    me = my_part()
    near = near_ref[0]
    row = jnp.concatenate([near[which : which + 1] for which in range(len(near_offsets))], axis=1)
    columns = [as_columns(row)]
    tile_place = lax.broadcasted_iota(jnp.int32, (tile_rows, lanes), 0)
    far = [as_columns(far_ref[0, slot : slot + 1]) for slot in range(far_cap)]
    for part in range(part_count):
        tile = jnp.full((tile_rows, lanes), -1, jnp.int32)
        for slot in range(far_cap):
            tile = jnp.where(tile_place == slot, far[slot][part : part + 1], tile)
        columns.append(tile)
    hot = one_hot(jnp.concatenate(columns, axis=0), latent_ref.shape[0])
    picked = jnp.dot(hot, latent_ref[...], preferred_element_type=f32).astype(bf16)
    for which, offset in enumerate(near_offsets):
        target = lax.rem(me + (offset + part_count), part_count)
        out_ref[target, :near_cap] = picked[which * near_cap : (which + 1) * near_cap]
    far_start = len(near_offsets) * near_cap
    for part in range(part_count):
        out_ref[part, near_cap:] = picked[
            far_start + part * tile_rows : far_start + (part + 1) * tile_rows
        ]


def exchange_padded(node_latent, near_rows, far_rows, part_count):
    near_cap, far_cap = near_rows.shape[2], far_rows.shape[2]
    block = (part_count, near_cap + tile_rows, node_latent.shape[1])
    blocks = pl.pallas_call(
        functools.partial(pick_kernel, part_count, near_cap, far_cap),
        out_shape=jax.ShapeDtypeStruct(block, bf16),
        in_specs=[vmem, vmem, vmem],
        out_specs=vmem,
        compiler_params=pltpu.CompilerParams(vmem_limit_bytes=grant),
        cost_estimate=pl.CostEstimate(flops=0, bytes_accessed=0, transcendentals=0),
        name="pick_halo",
    )(jnp.transpose(far_rows, (0, 2, 1)), near_rows, node_latent)
    return [
        lax.all_to_all(blocks, ("region", "feat"), split_axis=0, concat_axis=0, tiled=True)
    ]


def exchange_all(node_latent, near_rows, far_rows, part_count):
    near_send = jnp.take(node_latent, near_rows[0], axis=0, mode="clip")
    far_send = jnp.take(node_latent, far_rows[0], axis=0, mode="clip")
    got = []
    for which, offset in enumerate(near_offsets):
        pairs = [(part, (part + offset) % part_count) for part in range(part_count)]
        got.append(lax.ppermute(near_send[which], ("region", "feat"), pairs))
    far = lax.all_to_all(far_send, ("region", "feat"), split_axis=0, concat_axis=0, tiled=True)
    got.append(far.reshape(-1, far.shape[2]))
    return got


def gather_kernel(
    node_count,
    near_cap,
    far_cap,
    far_stride,
    halo_space,
    source_ref,
    receiver_ref,
    latent_ref,
    node_in_ref,
    node_out_ref,
    out_ref,
    pack_ref,
):
    width = latent_ref.shape[1]
    halo_start = 2 * width
    count = node_in_ref.shape[0]

    @pl.when(pl.program_id(0) == 0)
    def _():
        pack_ref[:count] = node_in_ref[...]
        pack_ref[count] = node_out_ref[...]

    source = source_ref[0]
    far = source - (node_count + len(near_offsets) * near_cap)
    spread = source + lax.div(far, far_cap) * (far_stride - far_cap)
    columns = as_columns(jnp.where(far >= 0, spread, source))
    latent = latent_ref[...]
    sent = one_hot(columns, node_count)
    out_ref[:, :width] = jnp.dot(sent, latent, preferred_element_type=f32).astype(bf16)
    received = one_hot(as_columns(receiver_ref[0]), node_count)
    out_ref[:, width:halo_start] = jnp.dot(
        received, latent, preferred_element_type=f32
    ).astype(bf16)
    out_ref[:, halo_start:] = one_hot(columns - node_count, halo_space)


def place_halo(table, part_count, near_cap, padded, got_refs):
    far_start = len(near_offsets) * near_cap
    for which, offset in enumerate(near_offsets):
        place = which * near_cap
        if padded:
            origin = lax.rem(my_part() + (part_count - offset), part_count)
            table[place : place + near_cap] = got_refs[0][origin, :near_cap]
        else:
            table[place : place + near_cap] = got_refs[which][...]
    if padded:
        for part in range(part_count):
            place = far_start + part * tile_rows
            table[place : place + tile_rows] = got_refs[0][part, near_cap:]
        used = far_start + part_count * tile_rows
    else:
        used = far_start + got_refs[-1].shape[0]
        table[far_start:used] = got_refs[-1][...]
    if used < table.shape[0]:
        table[used:] = jnp.zeros((table.shape[0] - used, table.shape[1]), bf16)


def place_rows(whole, start, piece, owner):
    rows = piece.shape[0]
    whole[pl.ds(pl.multiple_of(start + owner * rows, rows), rows), :] = piece


def owners():
    feat, feats = lax.axis_index("feat"), lax.axis_size("feat")
    sub, subs = lax.axis_index("sub"), lax.axis_size("sub")
    own = [(0, turn) for turn in range(subs)]
    rest = [(shift, turn) for turn in range(subs) for shift in range(1, feats)]
    return [
        wrap(feat - shift, feats) * subs + wrap(sub - turn, subs) for shift, turn in own + rest
    ]


def from_feats(weight):
    feats = lax.axis_size("feat")
    return [
        lax.ppermute(weight, "feat", [(at, (at + shift) % feats) for at in range(feats)])
        for shift in range(1, feats)
    ]


def from_subs(pieces):
    subs = lax.axis_size("sub")
    return [
        lax.ppermute(piece, "sub", [(at, (at + turn) % subs) for at in range(subs)])
        for turn in range(1, subs)
        for piece in pieces
    ]


def edge_kernel(pieces_count, got_count, part_count, near_cap, padded, *refs):
    edge_ref, gathered_ref, receiver_ref = refs[:3]
    got_refs = refs[3 : 3 + got_count]
    in_pieces = refs[3 + got_count : 3 + got_count + pieces_count]
    out_pieces = refs[3 + got_count + pieces_count : 3 + got_count + 2 * pieces_count]
    in_bias, out_bias, gain, offset, new_ref, sum_ref, in_weight, out_weight, halo, total = refs[
        3 + got_count + 2 * pieces_count :
    ]
    width = edge_ref.shape[1]
    step = pl.program_id(0)

    @pl.when(step == 0)
    def _():
        for in_piece, out_piece, owner in zip(in_pieces, out_pieces, owners()):
            for which in range(in_piece.shape[0]):
                place_rows(in_weight, which * width, in_piece[which], owner)
            place_rows(out_weight, 0, out_piece[...], owner)
        place_halo(halo, part_count, near_cap, padded, got_refs)
        in_weight[3 * width :] = jnp.dot(
            halo[...], in_weight[width : 2 * width], preferred_element_type=f32
        ).astype(bf16)

    edges = edge_ref[...]
    preact = jnp.dot(
        jnp.concatenate([edges, gathered_ref[...]], axis=1),
        in_weight[...],
        preferred_element_type=f32,
    )
    hidden = silu(preact + in_bias[...]).astype(bf16)
    output = jnp.dot(hidden, out_weight[...], preferred_element_type=f32) + out_bias[...]
    edge_new = (edges.astype(f32) + layer_norm(output, gain[...], offset[...])).astype(bf16)
    new_ref[...] = edge_new
    receiver = receiver_ref[0]
    node_place = lax.broadcasted_iota(jnp.int32, (total.shape[0], receiver.shape[1]), 0)
    hot = jnp.where(node_place == receiver, 1.0, 0.0).astype(bf16)
    part = jnp.dot(hot, edge_new, preferred_element_type=f32)

    @pl.when(step == 0)
    def _():
        total[...] = part

    @pl.when(step > 0)
    def _():
        total[...] += part

    @pl.when(step == pl.num_programs(0) - 1)
    def _():
        sum_ref[...] = total[...].astype(bf16)


def node_kernel(pieces_count, *refs):
    latent_ref, own_ref, other_ref = refs[:3]
    pieces = refs[3 : 3 + pieces_count]
    in_bias, out_bias, gain, offset, new_ref, weights = refs[3 + pieces_count :]
    width = latent_ref.shape[1]
    for piece, owner in zip(pieces, owners()):
        for which in range(piece.shape[0]):
            place_rows(weights, which * width, piece[which], owner)
    latent = latent_ref[...]
    summed = (own_ref[...].astype(f32) + other_ref[...].astype(f32)).astype(bf16)
    preact = jnp.dot(
        jnp.concatenate([latent, summed], axis=1),
        weights[: 2 * width],
        preferred_element_type=f32,
    )
    hidden = silu(preact + in_bias[...]).astype(bf16)
    output = jnp.dot(hidden, weights[2 * width :], preferred_element_type=f32) + out_bias[...]
    new_ref[...] = (
        latent.astype(f32) + layer_norm(output, gain[...], offset[...])
    ).astype(bf16)


def shards(
    node_latent,
    edge_latent,
    edge_source,
    receivers,
    near_rows,
    far_rows,
    edge_in_weight,
    edge_out_weight,
    node_in_weight,
    node_out_weight,
    edge_in_bias,
    edge_out_bias,
    edge_gain,
    edge_offset,
    node_in_bias,
    node_out_bias,
    node_gain,
    node_offset,
):
    node_count, width = node_latent.shape
    edge_count = edge_latent.shape[0]
    near_cap, far_cap = near_rows.shape[2], far_rows.shape[2]
    part_count = far_rows.shape[1]
    block = 512
    steps = edge_count // block

    far_edge = [from_feats(edge_in_weight), from_feats(edge_out_weight)]
    near_edge = [from_subs([edge_in_weight]), from_subs([edge_out_weight])]

    padded = part_count <= padded_parts
    exchange = exchange_padded if padded else exchange_all
    got = exchange(node_latent, near_rows, far_rows, part_count)
    far_stride = tile_rows if padded else far_cap
    halo_space = len(near_offsets) * near_cap + part_count * far_stride
    halo_space = -(-halo_space // lanes) * lanes

    source_blocks = edge_source.reshape(steps, 1, block)
    receiver_blocks = receivers.reshape(steps, 1, block)
    index_spec = pl.BlockSpec((1, 1, block), lambda step: (step, 0, 0))

    def whole(array):
        return pl.BlockSpec(array.shape, lambda step: (0,) * array.ndim)

    pack_shape = (node_in_weight.shape[0] + 1,) + node_out_weight.shape
    gathered_width = 2 * width + halo_space
    gathered, node_weight = pl.pallas_call(
        functools.partial(
            gather_kernel, node_count, near_cap, far_cap, far_stride, halo_space
        ),
        grid=(steps,),
        out_shape=[
            jax.ShapeDtypeStruct((edge_count, gathered_width), bf16),
            jax.ShapeDtypeStruct(pack_shape, bf16),
        ],
        in_specs=[index_spec, index_spec]
        + [whole(array) for array in (node_latent, node_in_weight, node_out_weight)],
        out_specs=[
            pl.BlockSpec((block, gathered_width), lambda step: (step, 0)),
            pl.BlockSpec(pack_shape, lambda step: (0, 0, 0)),
        ],
        compiler_params=pltpu.CompilerParams(vmem_limit_bytes=grant),
        cost_estimate=pl.CostEstimate(flops=0, bytes_accessed=0, transcendentals=0),
        name="gather_latents",
    )(source_blocks, receiver_blocks, node_latent, node_in_weight, node_out_weight)

    far_edge, gathered, node_weight = lax.optimization_barrier(
        (far_edge, gathered, node_weight)
    )
    edge_in, edge_out = [
        [weight] + near + far + from_subs(far)
        for weight, near, far in zip((edge_in_weight, edge_out_weight), near_edge, far_edge)
    ]
    far_node = from_feats(node_weight)
    node_pieces = [node_weight] + from_subs([node_weight]) + far_node + from_subs(far_node)
    pieces_count = len(edge_in)

    rows = [value.reshape(1, -1) for value in (edge_in_bias, edge_out_bias, edge_gain, edge_offset)]
    edge_new, partial_sums = pl.pallas_call(
        functools.partial(edge_kernel, pieces_count, len(got), part_count, near_cap, padded),
        grid=(steps,),
        out_shape=[
            jax.ShapeDtypeStruct((edge_count, width), bf16),
            jax.ShapeDtypeStruct((node_count, width), bf16),
        ],
        in_specs=[
            pl.BlockSpec((block, width), lambda step: (step, 0)),
            pl.BlockSpec((block, gathered_width), lambda step: (step, 0)),
            index_spec,
        ]
        + [whole(rows) for rows in got]
        + [whole(piece) for piece in edge_in + edge_out]
        + [whole(row) for row in rows],
        out_specs=[
            pl.BlockSpec((block, width), lambda step: (step, 0)),
            pl.BlockSpec((node_count, width), lambda step: (0, 0)),
        ],
        scratch_shapes=[
            pltpu.VMEM((3 * width + halo_space, width), bf16),
            pltpu.VMEM((width, width), bf16),
            pltpu.VMEM((halo_space, width), bf16),
            pltpu.VMEM((node_count, width), f32),
        ],
        compiler_params=pltpu.CompilerParams(vmem_limit_bytes=grant),
        cost_estimate=pl.CostEstimate(
            flops=2 * edge_count * width * (4 * width + node_count),
            bytes_accessed=8 * edge_count * width,
            transcendentals=edge_count * width,
        ),
        name="edge_update",
    )(edge_latent, gathered, receiver_blocks, *got, *edge_in, *edge_out, *rows)

    subs = lax.axis_size("sub")
    other_sums = lax.ppermute(partial_sums, "sub", [(at, (at + 1) % subs) for at in range(subs)])

    rows = [value.reshape(1, -1) for value in (node_in_bias, node_out_bias, node_gain, node_offset)]
    node_new = pl.pallas_call(
        functools.partial(node_kernel, pieces_count),
        out_shape=jax.ShapeDtypeStruct((node_count, width), bf16),
        in_specs=[vmem] * (3 + pieces_count + 4),
        out_specs=vmem,
        scratch_shapes=[
            pltpu.VMEM((3 * width, width), bf16),
        ],
        compiler_params=pltpu.CompilerParams(vmem_limit_bytes=grant),
        cost_estimate=pl.CostEstimate(
            flops=2 * node_count * width * 3 * width,
            bytes_accessed=10 * node_count * width,
            transcendentals=node_count * width,
        ),
        name="node_update",
    )(node_latent, partial_sums, other_sums, *node_pieces, *rows)
    return (edge_new, node_new)


def solution(mesh):
    return jax.shard_map(
        shards,
        mesh=mesh,
        in_specs=(
            P(("groups", "region", "feat"), None),
            P(("groups", "region", "feat", "sub"), None),
            P(("groups", "region", "feat", "sub")),
            P(("groups", "region", "feat", "sub")),
            P(("groups", "region", "feat"), None, None),
            P(("groups", "region", "feat"), None, None),
            P(None, ("feat", "sub"), None),
            P(("feat", "sub"), None),
            P(None, ("feat", "sub"), None),
            P(("feat", "sub"), None),
            P(),
            P(),
            P(),
            P(),
            P(),
            P(),
            P(),
            P(),
        ),
        out_specs=(
            P(("groups", "region", "feat", "sub"), None),
            P(("groups", "region", "feat"), None),
        ),
        check_vma=False,
    )
```

```python
import functools

import jax
import jax.numpy as jnp
from jax import lax
from jax.experimental import pallas as pl
from jax.experimental.pallas import tpu as pltpu
from jax.sharding import PartitionSpec as P

near_offsets = (1, 2, -1, -2)
tile_rows = 16
lanes = 128
padded_parts = 8
grant = 32 << 20
bf16 = jnp.bfloat16
f32 = jnp.float32
vmem = pl.BlockSpec(memory_space=pltpu.VMEM)


def in_hbm(array):
    return pltpu.with_memory_space_constraint(array, pltpu.HBM)


def wrap(value, count):
    return jnp.where(value < 0, value + count, value)


def as_columns(rows):
    return jnp.concatenate(
        [
            jnp.transpose(jnp.broadcast_to(rows[at : at + 1], (lanes, rows.shape[1])))
            for at in range(rows.shape[0])
        ],
        axis=0,
    )


def one_hot(columns, width):
    place = lax.broadcasted_iota(jnp.int32, columns.shape, 1)
    return jnp.concatenate(
        [
            jnp.where(columns == place + start, 1.0, 0.0).astype(bf16)
            for start in range(0, width, lanes)
        ],
        axis=1,
    )


def silu(values):
    half = 0.5 * values
    return half + half * jnp.tanh(half)


def layer_norm(values, gain, offset):
    average = jnp.mean(values, axis=-1, keepdims=True)
    centred = values - average
    spread = jnp.mean(centred * centred, axis=-1, keepdims=True)
    return centred * lax.rsqrt(spread + 1e-05) * gain + offset


def my_part():
    return lax.axis_index("region") * lax.axis_size("feat") + lax.axis_index("feat")


def pick_kernel(part_count, near_cap, far_cap, far_ref, near_ref, latent_ref, out_ref):
    me = my_part()
    columns = [as_columns(near_ref[0])]
    tile_place = lax.broadcasted_iota(jnp.int32, (tile_rows, lanes), 0)
    far = [as_columns(far_ref[0, slot : slot + 1]) for slot in range(far_cap)]
    for part in range(part_count):
        tile = jnp.full((tile_rows, lanes), -1, jnp.int32)
        for slot in range(far_cap):
            tile = jnp.where(tile_place == slot, far[slot][part : part + 1], tile)
        columns.append(tile)
    hot = one_hot(jnp.concatenate(columns, axis=0), latent_ref.shape[0])
    picked = jnp.dot(hot, latent_ref[...], preferred_element_type=f32).astype(bf16)
    for which, offset in enumerate(near_offsets):
        target = lax.rem(me + (offset + part_count), part_count)
        out_ref[target, :near_cap] = picked[which * near_cap : (which + 1) * near_cap]
    far_start = len(near_offsets) * near_cap
    for part in range(part_count):
        out_ref[part, near_cap:] = picked[
            far_start + part * tile_rows : far_start + (part + 1) * tile_rows
        ]


def exchange_padded(node_latent, near_rows, far_rows, part_count):
    near_cap, far_cap = near_rows.shape[2], far_rows.shape[2]
    block = (part_count, near_cap + tile_rows, node_latent.shape[1])
    blocks = pl.pallas_call(
        functools.partial(pick_kernel, part_count, near_cap, far_cap),
        out_shape=pltpu.HBM(block, bf16),
        in_specs=[vmem, vmem, vmem],
        out_specs=vmem,
        compiler_params=pltpu.CompilerParams(vmem_limit_bytes=grant),
        cost_estimate=pl.CostEstimate(flops=0, bytes_accessed=0, transcendentals=0),
        name="pick_halo",
    )(in_hbm(jnp.transpose(far_rows, (0, 2, 1))), in_hbm(near_rows), in_hbm(node_latent))
    return [
        lax.all_to_all(blocks, ("region", "feat"), split_axis=0, concat_axis=0, tiled=True)
    ]


def exchange_all(node_latent, near_rows, far_rows, part_count):
    near_send = jnp.take(node_latent, near_rows[0], axis=0, mode="clip")
    far_send = jnp.take(node_latent, far_rows[0], axis=0, mode="clip")
    got = []
    for which, offset in enumerate(near_offsets):
        pairs = [(part, (part + offset) % part_count) for part in range(part_count)]
        got.append(lax.ppermute(near_send[which], ("region", "feat"), pairs))
    far = lax.all_to_all(far_send, ("region", "feat"), split_axis=0, concat_axis=0, tiled=True)
    got.append(far.reshape(-1, far.shape[2]))
    return got


def gather_kernel(
    node_count,
    near_cap,
    far_cap,
    far_stride,
    halo_space,
    source_ref,
    receiver_ref,
    latent_ref,
    node_in_ref,
    node_out_ref,
    out_ref,
    pack_ref,
):
    width = latent_ref.shape[1]
    halo_start = 2 * width
    count = node_in_ref.shape[0]

    @pl.when(pl.program_id(0) == 0)
    def _():
        pack_ref[:count] = node_in_ref[...]
        pack_ref[count] = node_out_ref[...]

    index_rows = out_ref.shape[0] // lanes
    here = pl.ds(pl.program_id(0) * index_rows, index_rows)
    source = source_ref[here]
    far = source - (node_count + len(near_offsets) * near_cap)
    spread = source + lax.div(far, far_cap) * (far_stride - far_cap)
    columns = as_columns(jnp.where(far >= 0, spread, source))
    latent = latent_ref[...]
    sent = one_hot(columns, node_count)
    out_ref[:, :width] = jnp.dot(sent, latent, preferred_element_type=f32).astype(bf16)
    received = one_hot(as_columns(receiver_ref[here]), node_count)
    out_ref[:, width:halo_start] = jnp.dot(
        received, latent, preferred_element_type=f32
    ).astype(bf16)
    out_ref[:, halo_start:] = one_hot(columns - node_count, halo_space)


def halo_parts(part_count, near_cap, padded, got_refs):
    far_start = len(near_offsets) * near_cap
    parts = []
    for which, offset in enumerate(near_offsets):
        if padded:
            origin = lax.rem(my_part() + (part_count - offset), part_count)
            near = got_refs[0].at[origin, pl.ds(0, near_cap)]
        else:
            near = got_refs[which]
        parts.append((near, pl.ds(which * near_cap, near_cap)))
    if padded:
        for part in range(part_count):
            rows = pl.ds(far_start + part * tile_rows, tile_rows)
            parts.append((got_refs[0].at[part, pl.ds(near_cap, tile_rows)], rows))
    else:
        parts.append((got_refs[-1], pl.ds(far_start, got_refs[-1].shape[0])))
    return parts


def place_rows(whole, start, piece, owner):
    rows = piece.shape[0]
    whole[pl.ds(pl.multiple_of(start + owner * rows, rows), rows), :] = piece


def owners():
    feat, feats = lax.axis_index("feat"), lax.axis_size("feat")
    sub, subs = lax.axis_index("sub"), lax.axis_size("sub")
    own = [(0, turn) for turn in range(subs)]
    rest = [(shift, turn) for turn in range(subs) for shift in range(1, feats)]
    return [
        wrap(feat - shift, feats) * subs + wrap(sub - turn, subs) for shift, turn in own + rest
    ]


def from_feats(weight):
    feats = lax.axis_size("feat")
    return [
        lax.ppermute(weight, "feat", [(at, (at + shift) % feats) for at in range(feats)])
        for shift in range(1, feats)
    ]


def from_subs(pieces):
    subs = lax.axis_size("sub")
    return [
        lax.ppermute(piece, "sub", [(at, (at + turn) % subs) for at in range(subs)])
        for turn in range(1, subs)
        for piece in pieces
    ]


def edge_kernel(pieces_count, got_count, part_count, near_cap, padded, block, *refs):
    edge_hbm, gathered_hbm, receiver_hbm = refs[:3]
    got_refs = refs[3 : 3 + got_count]
    refs = refs[3 + got_count :]
    in_pieces, out_pieces = refs[:pieces_count], refs[pieces_count : 2 * pieces_count]
    row_refs = refs[2 * pieces_count : 2 * pieces_count + 4]
    new_hbm, sum_ref = refs[2 * pieces_count + 4 : 2 * pieces_count + 6]
    known, in_weight, out_weight, halo, receiver_ref, rows, new_ref, total, sems = refs[
        2 * pieces_count + 6 :
    ]
    edge_count, width = edge_hbm.shape
    blocks = edge_count // block
    taken = []

    def start(source, target):
        copy = pltpu.make_async_copy(source, target, sems.at[len(taken)])
        copy.start()
        taken.append(copy)
        return copy

    order = owners()
    first, later, last = [], [], []
    for which in (1, 0, 2):
        for piece, owner in zip(in_pieces, order):
            count = piece.shape[1]
            spot = pl.ds(pl.multiple_of(which * width + owner * count, count), count)
            target = first if which == 1 else later
            target.append(start(piece.at[which], in_weight.at[spot]))
        if which == 1:
            for source, spot in halo_parts(part_count, near_cap, padded, got_refs):
                first.append(start(source, halo.at[spot]))
    known_copies = []
    for at in range(blocks):
        spot = pl.ds(at * block, block)
        known_copies.append(
            [
                start(edge_hbm.at[spot], known.at[spot, pl.ds(0, width)]),
                start(
                    gathered_hbm.at[spot],
                    known.at[spot, pl.ds(width, known.shape[1] - width)],
                ),
            ]
        )
        if at == 0:
            for row_ref, row in zip(row_refs, rows):
                last.append(start(row_ref, row))
            for piece, owner in zip(out_pieces, order):
                count = piece.shape[0]
                spot = pl.ds(pl.multiple_of(owner * count, count), count)
                last.append(start(piece, out_weight.at[spot]))
            last.append(start(receiver_hbm, receiver_ref))
    in_bias, out_bias, gain, offset = rows

    used = len(near_offsets) * near_cap + (
        part_count * tile_rows if padded else got_refs[-1].shape[0]
    )
    if used < halo.shape[0]:
        halo[used:] = jnp.zeros((halo.shape[0] - used, width), bf16)
    for copy in first:
        copy.wait()
    in_weight[3 * width :] = jnp.dot(
        halo[...], in_weight[width : 2 * width], preferred_element_type=f32
    ).astype(bf16)
    for copy in later:
        copy.wait()

    def first_dot(at):
        for copy in known_copies[at]:
            copy.wait()
        return jnp.dot(
            known[at * block : (at + 1) * block], in_weight[...], preferred_element_type=f32
        )

    preact = first_dot(0)
    for copy in last:
        copy.wait()
    out_copies = []
    for at in range(blocks):
        spot = pl.ds(at * block, block)
        following = first_dot(at + 1) if at + 1 < blocks else None
        hidden = silu(preact + in_bias[...]).astype(bf16)
        output = jnp.dot(hidden, out_weight[...], preferred_element_type=f32) + out_bias[...]
        edges = known[spot, :width].astype(f32)
        edge_new = (edges + layer_norm(output, gain[...], offset[...])).astype(bf16)
        new_ref[spot] = edge_new
        out_copies.append(start(new_ref.at[spot], new_hbm.at[spot]))
        index_rows = block // lanes
        receiver = jnp.concatenate(
            [receiver_ref[at * index_rows + row][None] for row in range(index_rows)], axis=1
        )
        node_place = lax.broadcasted_iota(jnp.int32, (total.shape[0], block), 0)
        hot = jnp.where(node_place == receiver, 1.0, 0.0).astype(bf16)
        part = jnp.dot(hot, edge_new, preferred_element_type=f32)
        if at > 0:
            part += total[...]
        if at + 1 < blocks:
            total[...] = part
        else:
            sum_ref[...] = part.astype(bf16)
        preact = following
    for copy in out_copies:
        copy.wait()


def node_kernel(pieces_count, *refs):
    latent_ref, own_ref, other_ref = refs[:3]
    pieces = refs[3 : 3 + pieces_count]
    in_bias, out_bias, gain, offset, new_ref, weights = refs[3 + pieces_count :]
    width = latent_ref.shape[1]
    for piece, owner in zip(pieces, owners()):
        for which in range(piece.shape[0]):
            place_rows(weights, which * width, piece[which], owner)
    latent = latent_ref[...]
    summed = (own_ref[...].astype(f32) + other_ref[...].astype(f32)).astype(bf16)
    preact = jnp.dot(
        jnp.concatenate([latent, summed], axis=1),
        weights[: 2 * width],
        preferred_element_type=f32,
    )
    hidden = silu(preact + in_bias[...]).astype(bf16)
    output = jnp.dot(hidden, weights[2 * width :], preferred_element_type=f32) + out_bias[...]
    new_ref[...] = (
        latent.astype(f32) + layer_norm(output, gain[...], offset[...])
    ).astype(bf16)


def shards(
    node_latent,
    edge_latent,
    edge_source,
    receivers,
    near_rows,
    far_rows,
    edge_in_weight,
    edge_out_weight,
    node_in_weight,
    node_out_weight,
    edge_in_bias,
    edge_out_bias,
    edge_gain,
    edge_offset,
    node_in_bias,
    node_out_bias,
    node_gain,
    node_offset,
):
    node_count, width = node_latent.shape
    edge_count = edge_latent.shape[0]
    near_cap, far_cap = near_rows.shape[2], far_rows.shape[2]
    part_count = far_rows.shape[1]
    block = 512
    steps = edge_count // block

    far_edge = [from_feats(edge_in_weight), from_feats(edge_out_weight)]
    near_edge = [from_subs([edge_in_weight]), from_subs([edge_out_weight])]

    padded = part_count <= padded_parts
    exchange = exchange_padded if padded else exchange_all
    got = exchange(node_latent, near_rows, far_rows, part_count)
    far_stride = tile_rows if padded else far_cap
    halo_space = len(near_offsets) * near_cap + part_count * far_stride
    halo_space = -(-halo_space // lanes) * lanes

    source_rows = in_hbm(edge_source.reshape(-1, lanes))
    receiver_rows = in_hbm(receivers.reshape(-1, lanes))

    def whole(array):
        return pl.BlockSpec(array.shape, lambda step: (0,) * array.ndim)

    pack_shape = (node_in_weight.shape[0] + 1,) + node_out_weight.shape
    gathered_width = 2 * width + halo_space
    gathered, node_weight = pl.pallas_call(
        functools.partial(
            gather_kernel, node_count, near_cap, far_cap, far_stride, halo_space
        ),
        grid=(steps,),
        out_shape=[
            pltpu.HBM((edge_count, gathered_width), bf16),
            pltpu.HBM(pack_shape, bf16),
        ],
        in_specs=[
            whole(array)
            for array in (source_rows, receiver_rows, node_latent, node_in_weight, node_out_weight)
        ],
        out_specs=[
            pl.BlockSpec((block, gathered_width), lambda step: (step, 0)),
            pl.BlockSpec(pack_shape, lambda step: (0, 0, 0)),
        ],
        compiler_params=pltpu.CompilerParams(vmem_limit_bytes=grant),
        cost_estimate=pl.CostEstimate(flops=0, bytes_accessed=0, transcendentals=0),
        name="gather_latents",
    )(
        source_rows,
        receiver_rows,
        in_hbm(node_latent),
        in_hbm(node_in_weight),
        in_hbm(node_out_weight),
    )

    far_edge, gathered, node_weight = lax.optimization_barrier(
        (far_edge, gathered, node_weight)
    )
    edge_in, edge_out = [
        [weight] + near + far + from_subs(far)
        for weight, near, far in zip((edge_in_weight, edge_out_weight), near_edge, far_edge)
    ]
    far_node = from_feats(node_weight)
    node_pieces = [node_weight] + from_subs([node_weight]) + far_node + from_subs(far_node)
    pieces_count = len(edge_in)

    rows = [value.reshape(1, -1) for value in (edge_in_bias, edge_out_bias, edge_gain, edge_offset)]
    hbm = pl.BlockSpec(memory_space=pltpu.HBM)
    edge_operands = [edge_latent, gathered, receivers.reshape(-1, lanes)]
    edge_operands += got + edge_in + edge_out + rows
    known_width = 3 * width + halo_space
    copy_count = 3 * pieces_count + 4 + part_count + 3 * steps + 4 + pieces_count + 1
    edge_new, partial_sums = pl.pallas_call(
        functools.partial(
            edge_kernel, pieces_count, len(got), part_count, near_cap, padded, block
        ),
        out_shape=[
            pltpu.HBM((edge_count, width), bf16),
            jax.ShapeDtypeStruct((node_count, width), bf16),
        ],
        in_specs=[hbm] * len(edge_operands),
        out_specs=[hbm, vmem],
        scratch_shapes=[
            pltpu.VMEM((edge_count, known_width), bf16),
            pltpu.VMEM((known_width, width), bf16),
            pltpu.VMEM((width, width), bf16),
            pltpu.VMEM((halo_space, width), bf16),
            pltpu.VMEM((edge_count // lanes, lanes), jnp.int32),
            [pltpu.VMEM((1, width), f32)] * 4,
            pltpu.VMEM((edge_count, width), bf16),
            pltpu.VMEM((node_count, width), f32),
            pltpu.SemaphoreType.DMA((copy_count,)),
        ],
        compiler_params=pltpu.CompilerParams(vmem_limit_bytes=grant),
        cost_estimate=pl.CostEstimate(
            flops=2 * edge_count * width * (4 * width + node_count),
            bytes_accessed=8 * edge_count * width,
            transcendentals=edge_count * width,
        ),
        name="edge_update",
    )(*[in_hbm(operand) for operand in edge_operands])

    subs = lax.axis_size("sub")
    other_sums = lax.ppermute(partial_sums, "sub", [(at, (at + 1) % subs) for at in range(subs)])

    rows = [value.reshape(1, -1) for value in (node_in_bias, node_out_bias, node_gain, node_offset)]
    node_new = pl.pallas_call(
        functools.partial(node_kernel, pieces_count),
        out_shape=jax.ShapeDtypeStruct((node_count, width), bf16),
        in_specs=[vmem] * (3 + pieces_count + 4),
        out_specs=vmem,
        scratch_shapes=[
            pltpu.VMEM((3 * width, width), bf16),
        ],
        compiler_params=pltpu.CompilerParams(vmem_limit_bytes=grant),
        cost_estimate=pl.CostEstimate(
            flops=2 * node_count * width * 3 * width,
            bytes_accessed=10 * node_count * width,
            transcendentals=node_count * width,
        ),
        name="node_update",
    )(node_latent, partial_sums, other_sums, *node_pieces, *rows)
    return (edge_new, node_new)


def solution(mesh):
    return jax.shard_map(
        shards,
        mesh=mesh,
        in_specs=(
            P(("groups", "region", "feat"), None),
            P(("groups", "region", "feat", "sub"), None),
            P(("groups", "region", "feat", "sub")),
            P(("groups", "region", "feat", "sub")),
            P(("groups", "region", "feat"), None, None),
            P(("groups", "region", "feat"), None, None),
            P(None, ("feat", "sub"), None),
            P(("feat", "sub"), None),
            P(None, ("feat", "sub"), None),
            P(("feat", "sub"), None),
            P(),
            P(),
            P(),
            P(),
            P(),
            P(),
            P(),
            P(),
        ),
        out_specs=(
            P(("groups", "region", "feat", "sub"), None),
            P(("groups", "region", "feat"), None),
        ),
        check_vma=False,
    )
```

```python
import functools

import jax
import jax.numpy as jnp
from jax import lax
from jax.experimental import pallas as pl
from jax.experimental.pallas import tpu as pltpu
from jax.sharding import PartitionSpec as P

near_offsets = (1, 2, -1, -2)
tile_rows = 16
lanes = 128
few_parts = 8
grant = 32 << 20
bf16 = jnp.bfloat16
f32 = jnp.float32
vmem = pl.BlockSpec(memory_space=pltpu.VMEM)


def in_hbm(array):
    return pltpu.with_memory_space_constraint(array, pltpu.HBM)


def in_vmem(array):
    return pltpu.with_memory_space_constraint(array, pltpu.VMEM)


def wrap(value, count):
    return jnp.where(value < 0, value + count, value)


def as_columns(rows):
    return jnp.concatenate(
        [
            jnp.transpose(jnp.broadcast_to(rows[at : at + 1], (lanes, rows.shape[1])))
            for at in range(rows.shape[0])
        ],
        axis=0,
    )


def one_hot(columns, width):
    place = lax.broadcasted_iota(jnp.int32, columns.shape, 1)
    return jnp.concatenate(
        [
            jnp.where(columns == place + start, 1.0, 0.0).astype(bf16)
            for start in range(0, width, lanes)
        ],
        axis=1,
    )


def silu(values):
    half = 0.5 * values
    return half + half * jnp.tanh(half)


def layer_norm(values, gain, offset):
    average = jnp.mean(values, axis=-1, keepdims=True)
    centred = values - average
    spread = jnp.mean(centred * centred, axis=-1, keepdims=True)
    return centred * lax.rsqrt(spread + 1e-05) * gain + offset


def my_part():
    return lax.axis_index("region") * lax.axis_size("feat") + lax.axis_index("feat")


def pick_kernel(part_count, near_cap, far_cap, far_ref, near_ref, latent_ref, out_ref, picked):
    me, sub, subs = my_part(), lax.axis_index("sub"), lax.axis_size("sub")
    half = near_cap // subs
    columns = [as_columns(near_ref[0])]
    tile_place = lax.broadcasted_iota(jnp.int32, (tile_rows, lanes), 0)
    far = as_columns(far_ref[0, 0:1])
    for slot in range(1, far_cap):
        far = jnp.where(sub == slot, as_columns(far_ref[0, slot : slot + 1]), far)
    for part in range(part_count):
        columns.append(jnp.where(tile_place == 0, far[part : part + 1], -1))
    hot = one_hot(jnp.concatenate(columns, axis=0), latent_ref.shape[0])
    picked[...] = jnp.dot(hot, latent_ref[...], preferred_element_type=f32).astype(bf16)
    for which, offset in enumerate(near_offsets):
        target = lax.rem(me + (offset + part_count), part_count)
        start = pl.multiple_of(which * near_cap + sub * half, half)
        out_ref[target, :half] = picked[pl.ds(start, half)]
    far_start = len(near_offsets) * near_cap
    for part in range(part_count):
        spot = far_start + part * tile_rows
        out_ref[part, half:] = picked[spot : spot + tile_rows][:1]


def exchange_halves(node_latent, near_rows, far_rows, part_count):
    near_cap, far_cap = near_rows.shape[2], far_rows.shape[2]
    subs = lax.axis_size("sub")
    width = node_latent.shape[1]
    block = (part_count, near_cap // subs + 1, width)
    picks = len(near_offsets) * near_cap + part_count * tile_rows
    blocks = pl.pallas_call(
        functools.partial(pick_kernel, part_count, near_cap, far_cap),
        out_shape=pltpu.HBM(block, bf16),
        in_specs=[vmem, vmem, vmem],
        out_specs=vmem,
        scratch_shapes=[pltpu.VMEM((picks, width), bf16)],
        compiler_params=pltpu.CompilerParams(vmem_limit_bytes=grant),
        cost_estimate=pl.CostEstimate(flops=0, bytes_accessed=0, transcendentals=0),
        name="pick_halo",
    )(in_hbm(jnp.transpose(far_rows, (0, 2, 1))), in_hbm(near_rows), in_hbm(node_latent))
    own = lax.all_to_all(blocks, ("region", "feat"), split_axis=0, concat_axis=0, tiled=True)
    return blocks, [own] + from_subs([own])


def exchange_all(node_latent, near_rows, far_rows, part_count):
    near_send = jnp.take(node_latent, near_rows[0], axis=0, mode="clip")
    far_send = jnp.take(node_latent, far_rows[0], axis=0, mode="clip")
    got = []
    for which, offset in enumerate(near_offsets):
        pairs = [(part, (part + offset) % part_count) for part in range(part_count)]
        got.append(lax.ppermute(near_send[which], ("region", "feat"), pairs))
    far = lax.all_to_all(far_send, ("region", "feat"), split_axis=0, concat_axis=0, tiled=True)
    got.append(far.reshape(-1, far.shape[2]))
    return far_send, got


def gather_kernel(
    node_count,
    near_cap,
    far_cap,
    halved,
    halo_space,
    source_ref,
    receiver_ref,
    latent_ref,
    node_in_ref,
    node_out_ref,
    out_ref,
    pack_ref,
):
    width = latent_ref.shape[1]
    halo_start = 2 * width
    count = node_in_ref.shape[0]

    @pl.when(pl.program_id(0) == 0)
    def _():
        pack_ref[:count] = node_in_ref[...]
        pack_ref[count] = node_out_ref[...]

    index_rows = out_ref.shape[0] // lanes
    here = pl.ds(pl.program_id(0) * index_rows, index_rows)
    source = source_ref[here]
    if halved:
        far = source - (node_count + len(near_offsets) * near_cap)
        slot = lax.rem(far, far_cap)
        turned = wrap(slot - lax.axis_index("sub"), far_cap)
        source = jnp.where(far >= 0, source - slot + turned, source)
    columns = as_columns(source)
    latent = latent_ref[...]
    sent = one_hot(columns, node_count)
    out_ref[:, :width] = jnp.dot(sent, latent, preferred_element_type=f32).astype(bf16)
    received = one_hot(as_columns(receiver_ref[here]), node_count)
    out_ref[:, width:halo_start] = jnp.dot(
        received, latent, preferred_element_type=f32
    ).astype(bf16)
    out_ref[:, halo_start:] = one_hot(columns - node_count, halo_space)


def place_halo(halo, part_count, near_cap, halved, got):
    subs = lax.axis_size("sub")
    far_start = len(near_offsets) * near_cap
    used = far_start
    if halved:
        half = near_cap // subs
        for which, offset in enumerate(near_offsets):
            origin = lax.rem(my_part() + (part_count - offset), part_count)
            for turn in range(subs):
                owner = wrap(lax.axis_index("sub") - turn, subs)
                start = pl.multiple_of(which * near_cap + owner * half, half)
                halo[pl.ds(start, half)] = got[turn][origin, :half]
        far = [got[turn][part, half:] for part in range(part_count) for turn in range(subs)]
        used += len(far)
        halo[far_start:used] = jnp.concatenate(
            [row.astype(f32) for row in far], axis=0
        ).astype(bf16)
    else:
        for rows in got:
            start = used - far_start if rows is not got[-1] else far_start
            halo[start : start + rows.shape[0]] = rows[...]
            used += rows.shape[0]
        used -= far_start
    if used < halo.shape[0]:
        halo[used:] = jnp.zeros((halo.shape[0] - used, halo.shape[1]), bf16)


def place_rows(whole, start, piece, owner):
    rows = piece.shape[0]
    whole[pl.ds(pl.multiple_of(start + owner * rows, rows), rows), :] = piece


def owners():
    feat, feats = lax.axis_index("feat"), lax.axis_size("feat")
    sub, subs = lax.axis_index("sub"), lax.axis_size("sub")
    own = [(0, turn) for turn in range(subs)]
    rest = [(shift, turn) for turn in range(subs) for shift in range(1, feats)]
    return [
        wrap(feat - shift, feats) * subs + wrap(sub - turn, subs) for shift, turn in own + rest
    ]


def from_feats(weight):
    feats = lax.axis_size("feat")
    return [
        lax.ppermute(weight, "feat", [(at, (at + shift) % feats) for at in range(feats)])
        for shift in range(1, feats)
    ]


def from_subs(pieces):
    subs = lax.axis_size("sub")
    return [
        lax.ppermute(piece, "sub", [(at, (at + turn) % subs) for at in range(subs)])
        for turn in range(1, subs)
        for piece in pieces
    ]


def edge_kernel(pieces_count, got_count, part_count, near_cap, halved, block, *refs):
    edge_hbm, gathered_hbm, receiver_hbm = refs[:3]
    got_refs = refs[3 : 3 + got_count]
    refs = refs[3 + got_count :]
    in_pieces, out_pieces = refs[:pieces_count], refs[pieces_count : 2 * pieces_count]
    row_refs = refs[2 * pieces_count : 2 * pieces_count + 4]
    new_hbm, sum_ref = refs[2 * pieces_count + 4 : 2 * pieces_count + 6]
    known, in_weight, out_weight, halo, got, receiver_ref, rows, new_ref, total, sems = refs[
        2 * pieces_count + 6 :
    ]
    edge_count, width = edge_hbm.shape
    blocks = edge_count // block
    taken = []

    def start(source, target):
        copy = pltpu.make_async_copy(source, target, sems.at[len(taken)])
        copy.start()
        taken.append(copy)
        return copy

    order = owners()
    first, later, last = [], [], []
    for which in (1, 0, 2):
        for piece, owner in zip(in_pieces, order):
            count = piece.shape[1]
            spot = pl.ds(pl.multiple_of(which * width + owner * count, count), count)
            target = first if which == 1 else later
            target.append(start(piece.at[which], in_weight.at[spot]))
        if which == 1:
            first += [start(source, target) for source, target in zip(got_refs, got)]
    known_copies = []
    for at in range(blocks):
        spot = pl.ds(at * block, block)
        known_copies.append(
            [
                start(edge_hbm.at[spot], known.at[spot, pl.ds(0, width)]),
                start(
                    gathered_hbm.at[spot],
                    known.at[spot, pl.ds(width, known.shape[1] - width)],
                ),
            ]
        )
        if at == 0:
            for row_ref, row in zip(row_refs, rows):
                last.append(start(row_ref, row))
            for piece, owner in zip(out_pieces, order):
                count = piece.shape[0]
                spot = pl.ds(pl.multiple_of(owner * count, count), count)
                last.append(start(piece, out_weight.at[spot]))
            last.append(start(receiver_hbm, receiver_ref))
    in_bias, out_bias, gain, offset = rows

    for copy in first:
        copy.wait()
    place_halo(halo, part_count, near_cap, halved, got)
    in_weight[3 * width :] = jnp.dot(
        halo[...], in_weight[width : 2 * width], preferred_element_type=f32
    ).astype(bf16)
    for copy in later:
        copy.wait()

    def first_dot(at):
        for copy in known_copies[at]:
            copy.wait()
        return jnp.dot(
            known[at * block : (at + 1) * block], in_weight[...], preferred_element_type=f32
        )

    preact = first_dot(0)
    for copy in last:
        copy.wait()
    out_copies = []
    for at in range(blocks):
        spot = pl.ds(at * block, block)
        following = first_dot(at + 1) if at + 1 < blocks else None
        hidden = silu(preact + in_bias[...]).astype(bf16)
        output = jnp.dot(hidden, out_weight[...], preferred_element_type=f32) + out_bias[...]
        edges = known[spot, :width].astype(f32)
        edge_new = (edges + layer_norm(output, gain[...], offset[...])).astype(bf16)
        new_ref[spot] = edge_new
        out_copies.append(start(new_ref.at[spot], new_hbm.at[spot]))
        index_rows = block // lanes
        receiver = jnp.concatenate(
            [receiver_ref[at * index_rows + row][None] for row in range(index_rows)], axis=1
        )
        node_place = lax.broadcasted_iota(jnp.int32, (total.shape[0], block), 0)
        hot = jnp.where(node_place == receiver, 1.0, 0.0).astype(bf16)
        part = jnp.dot(hot, edge_new, preferred_element_type=f32)
        if at > 0:
            part += total[...]
        if at + 1 < blocks:
            total[...] = part
        else:
            sum_ref[...] = part.astype(bf16)
        preact = following
    for copy in out_copies:
        copy.wait()


def node_kernel(pieces_count, *refs):
    latent_ref, own_ref, other_ref = refs[:3]
    pieces = refs[3 : 3 + pieces_count]
    in_bias, out_bias, gain, offset, new_ref, weights = refs[3 + pieces_count :]
    width = latent_ref.shape[1]
    for piece, owner in zip(pieces, owners()):
        for which in range(piece.shape[0]):
            place_rows(weights, which * width, piece[which], owner)
    latent = latent_ref[...]
    summed = (own_ref[...].astype(f32) + other_ref[...].astype(f32)).astype(bf16)
    preact = jnp.dot(
        jnp.concatenate([latent, summed], axis=1),
        weights[: 2 * width],
        preferred_element_type=f32,
    )
    hidden = silu(preact + in_bias[...]).astype(bf16)
    output = jnp.dot(hidden, weights[2 * width :], preferred_element_type=f32) + out_bias[...]
    new_ref[...] = (
        latent.astype(f32) + layer_norm(output, gain[...], offset[...])
    ).astype(bf16)


def shards(
    node_latent,
    edge_latent,
    edge_source,
    receivers,
    near_rows,
    far_rows,
    edge_in_weight,
    edge_out_weight,
    node_in_weight,
    node_out_weight,
    edge_in_bias,
    edge_out_bias,
    edge_gain,
    edge_offset,
    node_in_bias,
    node_out_bias,
    node_gain,
    node_offset,
):
    node_count, width = node_latent.shape
    edge_count = edge_latent.shape[0]
    near_cap, far_cap = near_rows.shape[2], far_rows.shape[2]
    part_count = far_rows.shape[1]
    block = 512
    steps = edge_count // block

    far_edge = [from_feats(edge_in_weight), from_feats(edge_out_weight)]
    near_edge = [from_subs([edge_in_weight]), from_subs([edge_out_weight])]

    subs = lax.axis_size("sub")
    halved = part_count <= few_parts and far_cap == subs and near_cap % (tile_rows * subs) == 0
    exchange = exchange_halves if halved else exchange_all
    sent, got = exchange(node_latent, near_rows, far_rows, part_count)
    halo_space = len(near_offsets) * near_cap + part_count * far_cap
    halo_space = -(-halo_space // lanes) * lanes

    source_rows = in_hbm(edge_source.reshape(-1, lanes))
    receiver_rows = in_hbm(receivers.reshape(-1, lanes))

    def whole(array):
        return pl.BlockSpec(array.shape, lambda step: (0,) * array.ndim)

    pack_shape = (node_in_weight.shape[0] + 1,) + node_out_weight.shape
    gathered_width = 2 * width + halo_space
    far_edge[1], sent, latent_after = lax.optimization_barrier((far_edge[1], sent, node_latent))
    gather_block = block // 2
    gathered, node_weight = pl.pallas_call(
        functools.partial(
            gather_kernel, node_count, near_cap, far_cap, halved, halo_space
        ),
        grid=(edge_count // gather_block,),
        out_shape=[
            pltpu.HBM((edge_count, gathered_width), bf16),
            pltpu.HBM(pack_shape, bf16),
        ],
        in_specs=[
            whole(array)
            for array in (source_rows, receiver_rows, node_latent, node_in_weight, node_out_weight)
        ],
        out_specs=[
            pl.BlockSpec((gather_block, gathered_width), lambda step: (step, 0)),
            pl.BlockSpec(pack_shape, lambda step: (0, 0, 0)),
        ],
        compiler_params=pltpu.CompilerParams(vmem_limit_bytes=grant),
        cost_estimate=pl.CostEstimate(flops=0, bytes_accessed=0, transcendentals=0),
        name="gather_latents",
    )(
        source_rows,
        receiver_rows,
        in_hbm(latent_after),
        in_hbm(node_in_weight),
        in_hbm(node_out_weight),
    )

    far_edge, gathered, node_weight = lax.optimization_barrier(
        (far_edge, gathered, node_weight)
    )
    edge_in, edge_out = [
        [weight] + near + far + from_subs(far)
        for weight, near, far in zip((edge_in_weight, edge_out_weight), near_edge, far_edge)
    ]
    far_node = from_feats(node_weight)
    node_pieces = [node_weight] + from_subs([node_weight]) + far_node + from_subs(far_node)
    pieces_count = len(edge_in)

    rows = [value.reshape(1, -1) for value in (edge_in_bias, edge_out_bias, edge_gain, edge_offset)]
    hbm = pl.BlockSpec(memory_space=pltpu.HBM)
    anywhere = pl.BlockSpec(memory_space=pl.ANY)
    edge_operands = [in_hbm(edge_latent), in_hbm(gathered), in_hbm(receivers.reshape(-1, lanes))]
    edge_operands += [in_vmem(blocks) for blocks in got]
    for pieces in (edge_in, edge_out):
        edge_operands += [in_hbm(pieces[0])] + [in_vmem(piece) for piece in pieces[1:]]
    edge_operands += [in_hbm(row) for row in rows]
    known_width = 3 * width + halo_space
    copy_count = 3 * pieces_count + len(got) + 3 * steps + 4 + pieces_count + 1
    edge_new, partial_sums = pl.pallas_call(
        functools.partial(
            edge_kernel, pieces_count, len(got), part_count, near_cap, halved, block
        ),
        out_shape=[
            pltpu.HBM((edge_count, width), bf16),
            jax.ShapeDtypeStruct((node_count, width), bf16),
        ],
        in_specs=[anywhere] * len(edge_operands),
        out_specs=[hbm, vmem],
        scratch_shapes=[
            pltpu.VMEM((edge_count, known_width), bf16),
            pltpu.VMEM((known_width, width), bf16),
            pltpu.VMEM((width, width), bf16),
            pltpu.VMEM((halo_space, width), bf16),
            [pltpu.VMEM(rows.shape, bf16) for rows in got],
            pltpu.VMEM((edge_count // lanes, lanes), jnp.int32),
            [pltpu.VMEM((1, width), f32)] * 4,
            pltpu.VMEM((edge_count, width), bf16),
            pltpu.VMEM((node_count, width), f32),
            pltpu.SemaphoreType.DMA((copy_count,)),
        ],
        compiler_params=pltpu.CompilerParams(vmem_limit_bytes=grant),
        cost_estimate=pl.CostEstimate(
            flops=2 * edge_count * width * (4 * width + node_count),
            bytes_accessed=8 * edge_count * width,
            transcendentals=edge_count * width,
        ),
        name="edge_update",
    )(*edge_operands)

    subs = lax.axis_size("sub")
    other_sums = lax.ppermute(partial_sums, "sub", [(at, (at + 1) % subs) for at in range(subs)])

    rows = [value.reshape(1, -1) for value in (node_in_bias, node_out_bias, node_gain, node_offset)]
    node_new = pl.pallas_call(
        functools.partial(node_kernel, pieces_count),
        out_shape=jax.ShapeDtypeStruct((node_count, width), bf16),
        in_specs=[vmem] * (3 + pieces_count + 4),
        out_specs=vmem,
        scratch_shapes=[
            pltpu.VMEM((3 * width, width), bf16),
        ],
        compiler_params=pltpu.CompilerParams(vmem_limit_bytes=grant),
        cost_estimate=pl.CostEstimate(
            flops=2 * node_count * width * 3 * width,
            bytes_accessed=10 * node_count * width,
            transcendentals=node_count * width,
        ),
        name="node_update",
    )(node_latent, partial_sums, other_sums, *node_pieces, *rows)
    return (edge_new, node_new)


def solution(mesh):
    return jax.shard_map(
        shards,
        mesh=mesh,
        in_specs=(
            P(("groups", "region", "feat"), None),
            P(("groups", "region", "feat", "sub"), None),
            P(("groups", "region", "feat", "sub")),
            P(("groups", "region", "feat", "sub")),
            P(("groups", "region", "feat"), None, None),
            P(("groups", "region", "feat"), None, None),
            P(None, ("feat", "sub"), None),
            P(("feat", "sub"), None),
            P(None, ("feat", "sub"), None),
            P(("feat", "sub"), None),
            P(),
            P(),
            P(),
            P(),
            P(),
            P(),
            P(),
            P(),
        ),
        out_specs=(
            P(("groups", "region", "feat", "sub"), None),
            P(("groups", "region", "feat"), None),
        ),
        check_vma=False,
    )
```

```python
import functools

import jax
import jax.numpy as jnp
from jax import lax
from jax.experimental import pallas as pl
from jax.experimental.pallas import tpu as pltpu
from jax.sharding import PartitionSpec as P

near_offsets = (1, 2, -1, -2)
tile_rows = 16
lanes = 128
few_parts = 8
grant = 32 << 20
bf16 = jnp.bfloat16
f32 = jnp.float32
vmem = pl.BlockSpec(memory_space=pltpu.VMEM)


def in_hbm(array):
    return pltpu.with_memory_space_constraint(array, pltpu.HBM)


def in_vmem(array):
    return pltpu.with_memory_space_constraint(array, pltpu.VMEM)


def wrap(value, count):
    return jnp.where(value < 0, value + count, value)


def as_columns(rows):
    return jnp.concatenate(
        [
            jnp.transpose(jnp.broadcast_to(rows[at : at + 1], (lanes, rows.shape[1])))
            for at in range(rows.shape[0])
        ],
        axis=0,
    )


def one_hot(columns, width):
    place = lax.broadcasted_iota(jnp.int32, columns.shape, 1)
    return jnp.concatenate(
        [
            jnp.where(columns == place + start, 1.0, 0.0).astype(bf16)
            for start in range(0, width, lanes)
        ],
        axis=1,
    )


def silu(values):
    half = 0.5 * values
    return half + half * jnp.tanh(half)


def layer_norm(values, gain, offset):
    average = jnp.mean(values, axis=-1, keepdims=True)
    centred = values - average
    spread = jnp.mean(centred * centred, axis=-1, keepdims=True)
    return centred * lax.rsqrt(spread + 1e-05) * gain + offset


def my_part():
    return lax.axis_index("region") * lax.axis_size("feat") + lax.axis_index("feat")


def pick_kernel(part_count, near_cap, far_cap, far_ref, near_ref, latent_ref, out_ref, picked):
    me, sub, subs = my_part(), lax.axis_index("sub"), lax.axis_size("sub")
    half = near_cap // subs
    columns = [as_columns(near_ref[0])]
    tile_place = lax.broadcasted_iota(jnp.int32, (tile_rows, lanes), 0)
    far = as_columns(far_ref[0, 0:1])
    for slot in range(1, far_cap):
        far = jnp.where(sub == slot, as_columns(far_ref[0, slot : slot + 1]), far)
    for part in range(part_count):
        columns.append(jnp.where(tile_place == 0, far[part : part + 1], -1))
    hot = one_hot(jnp.concatenate(columns, axis=0), latent_ref.shape[0])
    picked[...] = jnp.dot(hot, latent_ref[...], preferred_element_type=f32).astype(bf16)
    for which, offset in enumerate(near_offsets):
        target = lax.rem(me + (offset + part_count), part_count)
        start = pl.multiple_of(which * near_cap + sub * half, half)
        out_ref[target, :half] = picked[pl.ds(start, half)]
    far_start = len(near_offsets) * near_cap
    for part in range(part_count):
        spot = far_start + part * tile_rows
        out_ref[part, half:] = picked[spot : spot + tile_rows][:1]


def exchange_halves(node_latent, near_rows, far_rows, part_count):
    near_cap, far_cap = near_rows.shape[2], far_rows.shape[2]
    subs = lax.axis_size("sub")
    width = node_latent.shape[1]
    block = (part_count, near_cap // subs + 1, width)
    picks = len(near_offsets) * near_cap + part_count * tile_rows
    blocks = pl.pallas_call(
        functools.partial(pick_kernel, part_count, near_cap, far_cap),
        out_shape=pltpu.HBM(block, bf16),
        in_specs=[vmem, vmem, vmem],
        out_specs=vmem,
        scratch_shapes=[pltpu.VMEM((picks, width), bf16)],
        compiler_params=pltpu.CompilerParams(vmem_limit_bytes=grant),
        cost_estimate=pl.CostEstimate(flops=0, bytes_accessed=0, transcendentals=0),
        name="pick_halo",
    )(in_hbm(jnp.transpose(far_rows, (0, 2, 1))), in_hbm(near_rows), in_hbm(node_latent))
    own = lax.all_to_all(blocks, ("region", "feat"), split_axis=0, concat_axis=0, tiled=True)
    return [own] + from_subs([own])


def exchange_all(node_latent, near_rows, far_rows, part_count):
    near_send = jnp.take(node_latent, near_rows[0], axis=0, mode="clip")
    far_send = jnp.take(node_latent, far_rows[0], axis=0, mode="clip")
    got = []
    for which, offset in enumerate(near_offsets):
        pairs = [(part, (part + offset) % part_count) for part in range(part_count)]
        got.append(lax.ppermute(near_send[which], ("region", "feat"), pairs))
    far = lax.all_to_all(far_send, ("region", "feat"), split_axis=0, concat_axis=0, tiled=True)
    got.append(far.reshape(-1, far.shape[2]))
    return got


def gather_kernel(
    node_count,
    near_cap,
    far_cap,
    halved,
    halo_space,
    source_ref,
    receiver_ref,
    latent_ref,
    node_in_ref,
    node_out_ref,
    out_ref,
    pack_ref,
):
    width = latent_ref.shape[1]
    halo_start = 2 * width
    count = node_in_ref.shape[0]

    @pl.when(pl.program_id(0) == 0)
    def _():
        pack_ref[:count] = node_in_ref[...]
        pack_ref[count] = node_out_ref[...]

    index_rows = out_ref.shape[0] // lanes
    here = pl.ds(pl.program_id(0) * index_rows, index_rows)
    source = source_ref[here]
    if halved:
        far = source - (node_count + len(near_offsets) * near_cap)
        slot = lax.rem(far, far_cap)
        turned = wrap(slot - lax.axis_index("sub"), far_cap)
        source = jnp.where(far >= 0, source - slot + turned, source)
    columns = as_columns(source)
    latent = latent_ref[...]
    sent = one_hot(columns, node_count)
    out_ref[:, :width] = jnp.dot(sent, latent, preferred_element_type=f32).astype(bf16)
    received = one_hot(as_columns(receiver_ref[here]), node_count)
    out_ref[:, width:halo_start] = jnp.dot(
        received, latent, preferred_element_type=f32
    ).astype(bf16)
    out_ref[:, halo_start:] = one_hot(columns - node_count, halo_space)


def place_halo(halo, part_count, near_cap, halved, got):
    subs = lax.axis_size("sub")
    far_start = len(near_offsets) * near_cap
    used = far_start
    if halved:
        half = near_cap // subs
        for which, offset in enumerate(near_offsets):
            origin = lax.rem(my_part() + (part_count - offset), part_count)
            for turn in range(subs):
                owner = wrap(lax.axis_index("sub") - turn, subs)
                start = pl.multiple_of(which * near_cap + owner * half, half)
                halo[pl.ds(start, half)] = got[turn][origin, :half]
        far = [got[turn][part, half:] for part in range(part_count) for turn in range(subs)]
        used += len(far)
        halo[far_start:used] = jnp.concatenate(
            [row.astype(f32) for row in far], axis=0
        ).astype(bf16)
    else:
        for rows in got:
            start = used - far_start if rows is not got[-1] else far_start
            halo[start : start + rows.shape[0]] = rows[...]
            used += rows.shape[0]
        used -= far_start
    if used < halo.shape[0]:
        halo[used:] = jnp.zeros((halo.shape[0] - used, halo.shape[1]), bf16)


def place_rows(whole, start, piece, owner):
    rows = piece.shape[0]
    whole[pl.ds(pl.multiple_of(start + owner * rows, rows), rows), :] = piece


def owners():
    feat, feats = lax.axis_index("feat"), lax.axis_size("feat")
    sub, subs = lax.axis_index("sub"), lax.axis_size("sub")
    own = [(0, turn) for turn in range(subs)]
    rest = [(shift, turn) for turn in range(subs) for shift in range(1, feats)]
    return [
        wrap(feat - shift, feats) * subs + wrap(sub - turn, subs) for shift, turn in own + rest
    ]


def from_feats(weight):
    feats = lax.axis_size("feat")
    return [
        lax.ppermute(weight, "feat", [(at, (at + shift) % feats) for at in range(feats)])
        for shift in range(1, feats)
    ]


def from_subs(pieces):
    subs = lax.axis_size("sub")
    return [
        lax.ppermute(piece, "sub", [(at, (at + turn) % subs) for at in range(subs)])
        for turn in range(1, subs)
        for piece in pieces
    ]


def edge_kernel(pieces_count, got_count, part_count, near_cap, halved, block, *refs):
    edge_hbm, gathered_hbm, receiver_hbm = refs[:3]
    got_refs = refs[3 : 3 + got_count]
    refs = refs[3 + got_count :]
    in_pieces, out_pieces = refs[:pieces_count], refs[pieces_count : 2 * pieces_count]
    row_refs = refs[2 * pieces_count : 2 * pieces_count + 4]
    new_hbm, sum_ref = refs[2 * pieces_count + 4 : 2 * pieces_count + 6]
    known, in_weight, out_weight, halo, got, receiver_ref, rows, new_ref, total, sems = refs[
        2 * pieces_count + 6 :
    ]
    edge_count, width = edge_hbm.shape
    blocks = edge_count // block
    taken = []

    def start(source, target):
        copy = pltpu.make_async_copy(source, target, sems.at[len(taken)])
        copy.start()
        taken.append(copy)
        return copy

    order = owners()
    first, later, last = [], [], []
    for which in (1, 0, 2):
        for piece, owner in zip(in_pieces, order):
            count = piece.shape[1]
            spot = pl.ds(pl.multiple_of(which * width + owner * count, count), count)
            target = first if which == 1 else later
            target.append(start(piece.at[which], in_weight.at[spot]))
        if which == 1:
            first += [start(source, target) for source, target in zip(got_refs, got)]
    known_copies = []
    for at in range(blocks):
        spot = pl.ds(at * block, block)
        known_copies.append(
            [
                start(edge_hbm.at[spot], known.at[spot, pl.ds(0, width)]),
                start(
                    gathered_hbm.at[spot],
                    known.at[spot, pl.ds(width, known.shape[1] - width)],
                ),
            ]
        )
        if at == 0:
            for row_ref, row in zip(row_refs, rows):
                last.append(start(row_ref, row))
            for piece, owner in zip(out_pieces, order):
                count = piece.shape[0]
                spot = pl.ds(pl.multiple_of(owner * count, count), count)
                last.append(start(piece, out_weight.at[spot]))
            last.append(start(receiver_hbm, receiver_ref))
    in_bias, out_bias, gain, offset = rows

    for copy in first:
        copy.wait()
    place_halo(halo, part_count, near_cap, halved, got)
    in_weight[3 * width :] = jnp.dot(
        halo[...], in_weight[width : 2 * width], preferred_element_type=f32
    ).astype(bf16)
    for copy in later:
        copy.wait()

    def first_dot(at):
        for copy in known_copies[at]:
            copy.wait()
        return jnp.dot(
            known[at * block : (at + 1) * block], in_weight[...], preferred_element_type=f32
        )

    preact = first_dot(0)
    for copy in last:
        copy.wait()
    out_copies = []
    for at in range(blocks):
        spot = pl.ds(at * block, block)
        following = first_dot(at + 1) if at + 1 < blocks else None
        hidden = silu(preact + in_bias[...]).astype(bf16)
        output = jnp.dot(hidden, out_weight[...], preferred_element_type=f32) + out_bias[...]
        edges = known[spot, :width].astype(f32)
        edge_new = (edges + layer_norm(output, gain[...], offset[...])).astype(bf16)
        new_ref[spot] = edge_new
        out_copies.append(start(new_ref.at[spot], new_hbm.at[spot]))
        index_rows = block // lanes
        receiver = jnp.concatenate(
            [receiver_ref[at * index_rows + row][None] for row in range(index_rows)], axis=1
        )
        node_place = lax.broadcasted_iota(jnp.int32, (total.shape[0], block), 0)
        hot = jnp.where(node_place == receiver, 1.0, 0.0).astype(bf16)
        part = jnp.dot(hot, edge_new, preferred_element_type=f32)
        if at > 0:
            part += total[...]
        if at + 1 < blocks:
            total[...] = part
        else:
            sum_ref[...] = part.astype(bf16)
        preact = following
    for copy in out_copies:
        copy.wait()


def node_kernel(pieces_count, *refs):
    latent_ref, own_ref, other_ref = refs[:3]
    pieces = refs[3 : 3 + pieces_count]
    in_bias, out_bias, gain, offset, new_ref, weights = refs[3 + pieces_count :]
    width = latent_ref.shape[1]
    for piece, owner in zip(pieces, owners()):
        for which in range(piece.shape[0]):
            place_rows(weights, which * width, piece[which], owner)
    latent = latent_ref[...]
    summed = (own_ref[...].astype(f32) + other_ref[...].astype(f32)).astype(bf16)
    preact = jnp.dot(
        jnp.concatenate([latent, summed], axis=1),
        weights[: 2 * width],
        preferred_element_type=f32,
    )
    hidden = silu(preact + in_bias[...]).astype(bf16)
    output = jnp.dot(hidden, weights[2 * width :], preferred_element_type=f32) + out_bias[...]
    new_ref[...] = (
        latent.astype(f32) + layer_norm(output, gain[...], offset[...])
    ).astype(bf16)


def shards(
    node_latent,
    edge_latent,
    edge_source,
    receivers,
    near_rows,
    far_rows,
    edge_in_weight,
    edge_out_weight,
    node_in_weight,
    node_out_weight,
    edge_in_bias,
    edge_out_bias,
    edge_gain,
    edge_offset,
    node_in_bias,
    node_out_bias,
    node_gain,
    node_offset,
):
    node_count, width = node_latent.shape
    edge_count = edge_latent.shape[0]
    near_cap, far_cap = near_rows.shape[2], far_rows.shape[2]
    part_count = far_rows.shape[1]
    block = 256
    steps = edge_count // block

    far_edge = [from_feats(edge_in_weight), from_feats(edge_out_weight)]
    near_edge = [from_subs([edge_in_weight]), from_subs([edge_out_weight])]

    subs = lax.axis_size("sub")
    halved = part_count <= few_parts and far_cap == subs and near_cap % (tile_rows * subs) == 0
    exchange = exchange_halves if halved else exchange_all
    got = exchange(node_latent, near_rows, far_rows, part_count)
    halo_space = len(near_offsets) * near_cap + part_count * far_cap
    halo_space = -(-halo_space // lanes) * lanes

    source_rows = in_hbm(edge_source.reshape(-1, lanes))
    receiver_rows = in_hbm(receivers.reshape(-1, lanes))

    def whole(array):
        return pl.BlockSpec(array.shape, lambda step: (0,) * array.ndim)

    pack_shape = (node_in_weight.shape[0] + 1,) + node_out_weight.shape
    gathered_width = 2 * width + halo_space
    gather_block = edge_count // 3
    gathered, node_weight = pl.pallas_call(
        functools.partial(
            gather_kernel, node_count, near_cap, far_cap, halved, halo_space
        ),
        grid=(edge_count // gather_block,),
        out_shape=[
            pltpu.HBM((edge_count, gathered_width), bf16),
            pltpu.HBM(pack_shape, bf16),
        ],
        in_specs=[
            whole(array)
            for array in (source_rows, receiver_rows, node_latent, node_in_weight, node_out_weight)
        ],
        out_specs=[
            pl.BlockSpec((gather_block, gathered_width), lambda step: (step, 0)),
            pl.BlockSpec(pack_shape, lambda step: (0, 0, 0)),
        ],
        compiler_params=pltpu.CompilerParams(vmem_limit_bytes=grant),
        cost_estimate=pl.CostEstimate(flops=0, bytes_accessed=0, transcendentals=0),
        name="gather_latents",
    )(
        source_rows,
        receiver_rows,
        in_hbm(node_latent),
        in_hbm(node_in_weight),
        in_hbm(node_out_weight),
    )

    far_edge, gathered, node_weight = lax.optimization_barrier(
        (far_edge, gathered, node_weight)
    )
    edge_in, edge_out = [
        [weight] + near + far + from_subs(far)
        for weight, near, far in zip((edge_in_weight, edge_out_weight), near_edge, far_edge)
    ]
    far_node = from_feats(node_weight)
    node_pieces = [node_weight] + from_subs([node_weight]) + far_node + from_subs(far_node)
    pieces_count = len(edge_in)

    rows = [value.reshape(1, -1) for value in (edge_in_bias, edge_out_bias, edge_gain, edge_offset)]
    hbm = pl.BlockSpec(memory_space=pltpu.HBM)
    anywhere = pl.BlockSpec(memory_space=pl.ANY)
    edge_operands = [in_hbm(edge_latent), in_hbm(gathered), in_hbm(receivers.reshape(-1, lanes))]
    edge_operands += [in_vmem(blocks) for blocks in got]
    for pieces in (edge_in, edge_out):
        edge_operands += [in_hbm(pieces[0])] + [in_vmem(piece) for piece in pieces[1:]]
    edge_operands += [in_hbm(row) for row in rows]
    known_width = 3 * width + halo_space
    copy_count = 3 * pieces_count + len(got) + 3 * steps + 4 + pieces_count + 1
    edge_new, partial_sums = pl.pallas_call(
        functools.partial(
            edge_kernel, pieces_count, len(got), part_count, near_cap, halved, block
        ),
        out_shape=[
            pltpu.HBM((edge_count, width), bf16),
            jax.ShapeDtypeStruct((node_count, width), bf16),
        ],
        in_specs=[anywhere] * len(edge_operands),
        out_specs=[hbm, vmem],
        scratch_shapes=[
            pltpu.VMEM((edge_count, known_width), bf16),
            pltpu.VMEM((known_width, width), bf16),
            pltpu.VMEM((width, width), bf16),
            pltpu.VMEM((halo_space, width), bf16),
            [pltpu.VMEM(rows.shape, bf16) for rows in got],
            pltpu.VMEM((edge_count // lanes, lanes), jnp.int32),
            [pltpu.VMEM((1, width), f32)] * 4,
            pltpu.VMEM((edge_count, width), bf16),
            pltpu.VMEM((node_count, width), f32),
            pltpu.SemaphoreType.DMA((copy_count,)),
        ],
        compiler_params=pltpu.CompilerParams(vmem_limit_bytes=grant),
        cost_estimate=pl.CostEstimate(
            flops=2 * edge_count * width * (4 * width + node_count),
            bytes_accessed=8 * edge_count * width,
            transcendentals=edge_count * width,
        ),
        name="edge_update",
    )(*edge_operands)

    subs = lax.axis_size("sub")
    other_sums = lax.ppermute(partial_sums, "sub", [(at, (at + 1) % subs) for at in range(subs)])

    rows = [value.reshape(1, -1) for value in (node_in_bias, node_out_bias, node_gain, node_offset)]
    node_new = pl.pallas_call(
        functools.partial(node_kernel, pieces_count),
        out_shape=jax.ShapeDtypeStruct((node_count, width), bf16),
        in_specs=[vmem] * (3 + pieces_count + 4),
        out_specs=vmem,
        scratch_shapes=[
            pltpu.VMEM((3 * width, width), bf16),
        ],
        compiler_params=pltpu.CompilerParams(vmem_limit_bytes=grant),
        cost_estimate=pl.CostEstimate(
            flops=2 * node_count * width * 3 * width,
            bytes_accessed=10 * node_count * width,
            transcendentals=node_count * width,
        ),
        name="node_update",
    )(node_latent, partial_sums, other_sums, *node_pieces, *rows)
    return (edge_new, node_new)


def solution(mesh):
    return jax.shard_map(
        shards,
        mesh=mesh,
        in_specs=(
            P(("groups", "region", "feat"), None),
            P(("groups", "region", "feat", "sub"), None),
            P(("groups", "region", "feat", "sub")),
            P(("groups", "region", "feat", "sub")),
            P(("groups", "region", "feat"), None, None),
            P(("groups", "region", "feat"), None, None),
            P(None, ("feat", "sub"), None),
            P(("feat", "sub"), None),
            P(None, ("feat", "sub"), None),
            P(("feat", "sub"), None),
            P(),
            P(),
            P(),
            P(),
            P(),
            P(),
            P(),
            P(),
        ),
        out_specs=(
            P(("groups", "region", "feat", "sub"), None),
            P(("groups", "region", "feat"), None),
        ),
        check_vma=False,
    )
```

```python
import functools

import jax
import jax.numpy as jnp
from jax import lax
from jax.experimental import pallas as pl
from jax.experimental.pallas import tpu as pltpu
from jax.sharding import PartitionSpec as P

near_offsets = (1, 2, -1, -2)
tile_rows = 16
lanes = 128
few_parts = 8
grant = 32 << 20
bf16 = jnp.bfloat16
f32 = jnp.float32
vmem = pl.BlockSpec(memory_space=pltpu.VMEM)


def in_hbm(array):
    return pltpu.with_memory_space_constraint(array, pltpu.HBM)


def in_vmem(array):
    return pltpu.with_memory_space_constraint(array, pltpu.VMEM)


def wrap(value, count):
    return jnp.where(value < 0, value + count, value)


def as_columns(rows):
    return jnp.concatenate(
        [
            jnp.transpose(jnp.broadcast_to(rows[at : at + 1], (lanes, rows.shape[1])))
            for at in range(rows.shape[0])
        ],
        axis=0,
    )


def one_hot(columns, width):
    place = lax.broadcasted_iota(jnp.int32, columns.shape, 1)
    return jnp.concatenate(
        [
            jnp.where(columns == place + start, 1.0, 0.0).astype(bf16)
            for start in range(0, width, lanes)
        ],
        axis=1,
    )


def silu(values):
    half = 0.5 * values
    return half + half * jnp.tanh(half)


def layer_norm(values, gain, offset):
    average = jnp.mean(values, axis=-1, keepdims=True)
    centred = values - average
    spread = jnp.mean(centred * centred, axis=-1, keepdims=True)
    return centred * lax.rsqrt(spread + 1e-05) * gain + offset


def my_part():
    return lax.axis_index("region") * lax.axis_size("feat") + lax.axis_index("feat")


def pick_kernel(part_count, near_cap, far_cap, far_ref, near_ref, latent_ref, out_ref, picked):
    me, sub, subs = my_part(), lax.axis_index("sub"), lax.axis_size("sub")
    half = near_cap // subs
    columns = [as_columns(near_ref[0])]
    tile_place = lax.broadcasted_iota(jnp.int32, (tile_rows, lanes), 0)
    far = as_columns(far_ref[0, 0:1])
    for slot in range(1, far_cap):
        far = jnp.where(sub == slot, as_columns(far_ref[0, slot : slot + 1]), far)
    for part in range(part_count):
        columns.append(jnp.where(tile_place == 0, far[part : part + 1], -1))
    hot = one_hot(jnp.concatenate(columns, axis=0), latent_ref.shape[0])
    picked[...] = jnp.dot(hot, latent_ref[...], preferred_element_type=f32).astype(bf16)
    for which, offset in enumerate(near_offsets):
        target = lax.rem(me + (offset + part_count), part_count)
        start = pl.multiple_of(which * near_cap + sub * half, half)
        out_ref[target, :half] = picked[pl.ds(start, half)]
    far_start = len(near_offsets) * near_cap
    for part in range(part_count):
        spot = far_start + part * tile_rows
        out_ref[part, half:] = picked[spot : spot + tile_rows][:1]


def exchange_halves(node_latent, near_rows, far_rows, part_count):
    near_cap, far_cap = near_rows.shape[2], far_rows.shape[2]
    subs = lax.axis_size("sub")
    width = node_latent.shape[1]
    block = (part_count, near_cap // subs + 1, width)
    picks = len(near_offsets) * near_cap + part_count * tile_rows
    blocks = pl.pallas_call(
        functools.partial(pick_kernel, part_count, near_cap, far_cap),
        out_shape=pltpu.HBM(block, bf16),
        in_specs=[vmem, vmem, vmem],
        out_specs=vmem,
        scratch_shapes=[pltpu.VMEM((picks, width), bf16)],
        compiler_params=pltpu.CompilerParams(vmem_limit_bytes=grant),
        cost_estimate=pl.CostEstimate(flops=0, bytes_accessed=0, transcendentals=0),
        name="pick_halo",
    )(in_hbm(jnp.transpose(far_rows, (0, 2, 1))), in_hbm(near_rows), in_hbm(node_latent))
    own = lax.all_to_all(blocks, ("region", "feat"), split_axis=0, concat_axis=0, tiled=True)
    return [own]


def exchange_all(node_latent, near_rows, far_rows, part_count):
    near_send = jnp.take(node_latent, near_rows[0], axis=0, mode="clip")
    far_send = jnp.take(node_latent, far_rows[0], axis=0, mode="clip")
    got = []
    for which, offset in enumerate(near_offsets):
        pairs = [(part, (part + offset) % part_count) for part in range(part_count)]
        got.append(lax.ppermute(near_send[which], ("region", "feat"), pairs))
    far = lax.all_to_all(far_send, ("region", "feat"), split_axis=0, concat_axis=0, tiled=True)
    got.append(far.reshape(-1, far.shape[2]))
    return got


def gather_kernel(
    node_count,
    near_cap,
    far_cap,
    halved,
    halo_space,
    source_ref,
    receiver_ref,
    latent_ref,
    node_in_ref,
    node_out_ref,
    out_ref,
    pack_ref,
):
    width = latent_ref.shape[1]
    halo_start = 2 * width
    count = node_in_ref.shape[0]

    @pl.when(pl.program_id(0) == 0)
    def _():
        pack_ref[:count] = node_in_ref[...]
        pack_ref[count] = node_out_ref[...]

    index_rows = out_ref.shape[0] // lanes
    here = pl.ds(pl.program_id(0) * index_rows, index_rows)
    source = source_ref[here]
    if halved:
        far = source - (node_count + len(near_offsets) * near_cap)
        slot = lax.rem(far, far_cap)
        turned = wrap(slot - lax.axis_index("sub"), far_cap)
        source = jnp.where(far >= 0, source - slot + turned, source)
    columns = as_columns(source)
    latent = latent_ref[...]
    sent = one_hot(columns, node_count)
    out_ref[:, :width] = jnp.dot(sent, latent, preferred_element_type=f32).astype(bf16)
    received = one_hot(as_columns(receiver_ref[here]), node_count)
    out_ref[:, width:halo_start] = jnp.dot(
        received, latent, preferred_element_type=f32
    ).astype(bf16)
    out_ref[:, halo_start:] = one_hot(columns - node_count, halo_space)


def place_halo(halo, part_count, near_cap, halved, got):
    subs = lax.axis_size("sub")
    far_start = len(near_offsets) * near_cap
    used = far_start
    if halved:
        half = near_cap // subs
        for which, offset in enumerate(near_offsets):
            origin = lax.rem(my_part() + (part_count - offset), part_count)
            for turn in range(subs):
                owner = wrap(lax.axis_index("sub") - turn, subs)
                start = pl.multiple_of(which * near_cap + owner * half, half)
                halo[pl.ds(start, half)] = got[turn][origin, :half]
        far = [got[turn][part, half:] for part in range(part_count) for turn in range(subs)]
        used += len(far)
        halo[far_start:used] = jnp.concatenate(
            [row.astype(f32) for row in far], axis=0
        ).astype(bf16)
    else:
        for rows in got:
            start = used - far_start if rows is not got[-1] else far_start
            halo[start : start + rows.shape[0]] = rows[...]
            used += rows.shape[0]
        used -= far_start
    if used < halo.shape[0]:
        halo[used:] = jnp.zeros((halo.shape[0] - used, halo.shape[1]), bf16)


def place_rows(whole, start, piece, owner):
    rows = piece.shape[0]
    whole[pl.ds(pl.multiple_of(start + owner * rows, rows), rows), :] = piece


def owners():
    feat, feats = lax.axis_index("feat"), lax.axis_size("feat")
    sub, subs = lax.axis_index("sub"), lax.axis_size("sub")
    own = [(0, turn) for turn in range(subs)]
    rest = [(shift, turn) for turn in range(subs) for shift in range(1, feats)]
    return [
        wrap(feat - shift, feats) * subs + wrap(sub - turn, subs) for shift, turn in own + rest
    ]


def from_feats(weight):
    feats = lax.axis_size("feat")
    return [
        lax.ppermute(weight, "feat", [(at, (at + shift) % feats) for at in range(feats)])
        for shift in range(1, feats)
    ]


def from_subs(pieces):
    subs = lax.axis_size("sub")
    return [
        lax.ppermute(piece, "sub", [(at, (at + turn) % subs) for at in range(subs)])
        for turn in range(1, subs)
        for piece in pieces
    ]


def edge_kernel(pieces_count, got_count, part_count, near_cap, halved, block, *refs):
    edge_hbm, gathered_hbm, receiver_hbm = refs[:3]
    got_refs = refs[3 : 3 + got_count]
    refs = refs[3 + got_count :]
    in_pieces, out_pieces = refs[:pieces_count], refs[pieces_count : 2 * pieces_count]
    row_refs = refs[2 * pieces_count : 2 * pieces_count + 4]
    new_hbm, sum_ref = refs[2 * pieces_count + 4 : 2 * pieces_count + 6]
    known, in_weight, out_weight, halo, receiver_ref, rows, new_ref, total, sems = refs[
        2 * pieces_count + 6 :
    ]
    edge_count, width = edge_hbm.shape
    blocks = edge_count // block
    taken = []

    def start(source, target):
        copy = pltpu.make_async_copy(source, target, sems.at[len(taken)])
        copy.start()
        taken.append(copy)
        return copy

    order = owners()
    first, later, last = [], [], []
    for which in (1, 0, 2):
        count = in_pieces[0].shape[1]
        spot = pl.ds(pl.multiple_of(which * width + order[0] * count, count), count)
        target = first if which == 1 else later
        target.append(start(in_pieces[0].at[which], in_weight.at[spot]))
    known_copies = []
    for at in range(blocks):
        spot = pl.ds(at * block, block)
        known_copies.append(
            [
                start(edge_hbm.at[spot], known.at[spot, pl.ds(0, width)]),
                start(
                    gathered_hbm.at[spot],
                    known.at[spot, pl.ds(width, known.shape[1] - width)],
                ),
            ]
        )
        if at == 0:
            for row_ref, row in zip(row_refs, rows):
                last.append(start(row_ref, row))
            count = out_pieces[0].shape[0]
            spot = pl.ds(pl.multiple_of(order[0] * count, count), count)
            last.append(start(out_pieces[0], out_weight.at[spot]))
            last.append(start(receiver_hbm, receiver_ref))
    in_bias, out_bias, gain, offset = rows

    place_halo(halo, part_count, near_cap, halved, got_refs)
    for which in (1, 0, 2):
        for piece, owner in zip(in_pieces[1:], order[1:]):
            place_rows(in_weight, which * width, piece[which], owner)
    for piece, owner in zip(out_pieces[1:], order[1:]):
        place_rows(out_weight, 0, piece[...], owner)
    for copy in first:
        copy.wait()
    in_weight[3 * width :] = jnp.dot(
        halo[...], in_weight[width : 2 * width], preferred_element_type=f32
    ).astype(bf16)
    for copy in later:
        copy.wait()

    def first_dot(at):
        for copy in known_copies[at]:
            copy.wait()
        return jnp.dot(
            known[at * block : (at + 1) * block], in_weight[...], preferred_element_type=f32
        )

    preact = first_dot(0)
    for copy in last:
        copy.wait()
    out_copies = []
    for at in range(blocks):
        spot = pl.ds(at * block, block)
        following = first_dot(at + 1) if at + 1 < blocks else None
        hidden = silu(preact + in_bias[...]).astype(bf16)
        output = jnp.dot(hidden, out_weight[...], preferred_element_type=f32) + out_bias[...]
        edges = known[spot, :width].astype(f32)
        edge_new = (edges + layer_norm(output, gain[...], offset[...])).astype(bf16)
        new_ref[spot] = edge_new
        out_copies.append(start(new_ref.at[spot], new_hbm.at[spot]))
        index_rows = block // lanes
        receiver = jnp.concatenate(
            [receiver_ref[at * index_rows + row][None] for row in range(index_rows)], axis=1
        )
        node_place = lax.broadcasted_iota(jnp.int32, (total.shape[0], block), 0)
        hot = jnp.where(node_place == receiver, 1.0, 0.0).astype(bf16)
        part = jnp.dot(hot, edge_new, preferred_element_type=f32)
        if at > 0:
            part += total[...]
        if at + 1 < blocks:
            total[...] = part
        else:
            sum_ref[...] = part.astype(bf16)
        preact = following
    for copy in out_copies:
        copy.wait()


def node_kernel(pieces_count, *refs):
    latent_ref, own_ref, other_ref = refs[:3]
    pieces = refs[3 : 3 + pieces_count]
    in_bias, out_bias, gain, offset, new_ref, weights = refs[3 + pieces_count :]
    width = latent_ref.shape[1]
    for piece, owner in zip(pieces, owners()):
        for which in range(piece.shape[0]):
            place_rows(weights, which * width, piece[which], owner)
    latent = latent_ref[...]
    summed = (own_ref[...].astype(f32) + other_ref[...].astype(f32)).astype(bf16)
    preact = jnp.dot(
        jnp.concatenate([latent, summed], axis=1),
        weights[: 2 * width],
        preferred_element_type=f32,
    )
    hidden = silu(preact + in_bias[...]).astype(bf16)
    output = jnp.dot(hidden, weights[2 * width :], preferred_element_type=f32) + out_bias[...]
    new_ref[...] = (
        latent.astype(f32) + layer_norm(output, gain[...], offset[...])
    ).astype(bf16)


def shards(
    node_latent,
    edge_latent,
    edge_source,
    receivers,
    near_rows,
    far_rows,
    edge_in_weight,
    edge_out_weight,
    node_in_weight,
    node_out_weight,
    edge_in_bias,
    edge_out_bias,
    edge_gain,
    edge_offset,
    node_in_bias,
    node_out_bias,
    node_gain,
    node_offset,
):
    node_count, width = node_latent.shape
    edge_count = edge_latent.shape[0]
    near_cap, far_cap = near_rows.shape[2], far_rows.shape[2]
    part_count = far_rows.shape[1]
    block = edge_count // 2
    steps = edge_count // block

    far_edge = [from_feats(edge_in_weight), from_feats(edge_out_weight)]
    near_edge = [from_subs([edge_in_weight]), from_subs([edge_out_weight])]

    subs = lax.axis_size("sub")
    halved = part_count <= few_parts and far_cap == subs and near_cap % (tile_rows * subs) == 0
    exchange = exchange_halves if halved else exchange_all
    got = exchange(node_latent, near_rows, far_rows, part_count)
    halo_space = len(near_offsets) * near_cap + part_count * far_cap
    halo_space = -(-halo_space // lanes) * lanes

    source_rows = in_hbm(edge_source.reshape(-1, lanes))
    receiver_rows = in_hbm(receivers.reshape(-1, lanes))

    def whole(array):
        return pl.BlockSpec(array.shape, lambda step: (0,) * array.ndim)

    pack_shape = (node_in_weight.shape[0] + 1,) + node_out_weight.shape
    gathered_width = 2 * width + halo_space
    gather_block = edge_count // 3
    gathered, node_weight = pl.pallas_call(
        functools.partial(
            gather_kernel, node_count, near_cap, far_cap, halved, halo_space
        ),
        grid=(edge_count // gather_block,),
        out_shape=[
            pltpu.HBM((edge_count, gathered_width), bf16),
            pltpu.HBM(pack_shape, bf16),
        ],
        in_specs=[
            whole(array)
            for array in (source_rows, receiver_rows, node_latent, node_in_weight, node_out_weight)
        ],
        out_specs=[
            pl.BlockSpec((gather_block, gathered_width), lambda step: (step, 0)),
            pl.BlockSpec(pack_shape, lambda step: (0, 0, 0)),
        ],
        compiler_params=pltpu.CompilerParams(vmem_limit_bytes=grant),
        cost_estimate=pl.CostEstimate(flops=0, bytes_accessed=0, transcendentals=0),
        name="gather_latents",
    )(
        source_rows,
        receiver_rows,
        in_hbm(node_latent),
        in_hbm(node_in_weight),
        in_hbm(node_out_weight),
    )

    far_edge, got, gathered, node_weight = lax.optimization_barrier(
        (far_edge, got, gathered, node_weight)
    )
    if halved:
        got = got + from_subs(got)
    edge_in, edge_out = [
        [weight] + near + far + from_subs(far)
        for weight, near, far in zip((edge_in_weight, edge_out_weight), near_edge, far_edge)
    ]
    far_node = from_feats(node_weight)
    node_pieces = [node_weight] + from_subs([node_weight]) + far_node + from_subs(far_node)
    pieces_count = len(edge_in)

    rows = [value.reshape(1, -1) for value in (edge_in_bias, edge_out_bias, edge_gain, edge_offset)]
    hbm = pl.BlockSpec(memory_space=pltpu.HBM)
    edge_operands = [in_hbm(edge_latent), in_hbm(gathered), in_hbm(receivers.reshape(-1, lanes))]
    edge_operands += [in_vmem(blocks) for blocks in got]
    edge_specs = [hbm] * 3 + [vmem] * len(got)
    for pieces in (edge_in, edge_out):
        edge_operands += [in_hbm(pieces[0])] + [in_vmem(piece) for piece in pieces[1:]]
        edge_specs += [hbm] + [vmem] * (pieces_count - 1)
    edge_operands += [in_hbm(row) for row in rows]
    edge_specs += [hbm] * len(rows)
    known_width = 3 * width + halo_space
    copy_count = 3 + 3 * steps + 4 + 1 + 1
    edge_new, partial_sums = pl.pallas_call(
        functools.partial(
            edge_kernel, pieces_count, len(got), part_count, near_cap, halved, block
        ),
        out_shape=[
            pltpu.HBM((edge_count, width), bf16),
            jax.ShapeDtypeStruct((node_count, width), bf16),
        ],
        in_specs=edge_specs,
        out_specs=[hbm, vmem],
        scratch_shapes=[
            pltpu.VMEM((edge_count, known_width), bf16),
            pltpu.VMEM((known_width, width), bf16),
            pltpu.VMEM((width, width), bf16),
            pltpu.VMEM((halo_space, width), bf16),
            pltpu.VMEM((edge_count // lanes, lanes), jnp.int32),
            [pltpu.VMEM((1, width), f32)] * 4,
            pltpu.VMEM((edge_count, width), bf16),
            pltpu.VMEM((node_count, width), f32),
            pltpu.SemaphoreType.DMA((copy_count,)),
        ],
        compiler_params=pltpu.CompilerParams(vmem_limit_bytes=grant),
        cost_estimate=pl.CostEstimate(
            flops=2 * edge_count * width * (4 * width + node_count),
            bytes_accessed=8 * edge_count * width,
            transcendentals=edge_count * width,
        ),
        name="edge_update",
    )(*edge_operands)

    subs = lax.axis_size("sub")
    other_sums = lax.ppermute(partial_sums, "sub", [(at, (at + 1) % subs) for at in range(subs)])

    rows = [value.reshape(1, -1) for value in (node_in_bias, node_out_bias, node_gain, node_offset)]
    node_new = pl.pallas_call(
        functools.partial(node_kernel, pieces_count),
        out_shape=jax.ShapeDtypeStruct((node_count, width), bf16),
        in_specs=[vmem] * (3 + pieces_count + 4),
        out_specs=vmem,
        scratch_shapes=[
            pltpu.VMEM((3 * width, width), bf16),
        ],
        compiler_params=pltpu.CompilerParams(vmem_limit_bytes=grant),
        cost_estimate=pl.CostEstimate(
            flops=2 * node_count * width * 3 * width,
            bytes_accessed=10 * node_count * width,
            transcendentals=node_count * width,
        ),
        name="node_update",
    )(node_latent, partial_sums, other_sums, *node_pieces, *rows)
    return (edge_new, node_new)


def solution(mesh):
    return jax.shard_map(
        shards,
        mesh=mesh,
        in_specs=(
            P(("groups", "region", "feat"), None),
            P(("groups", "region", "feat", "sub"), None),
            P(("groups", "region", "feat", "sub")),
            P(("groups", "region", "feat", "sub")),
            P(("groups", "region", "feat"), None, None),
            P(("groups", "region", "feat"), None, None),
            P(None, ("feat", "sub"), None),
            P(("feat", "sub"), None),
            P(None, ("feat", "sub"), None),
            P(("feat", "sub"), None),
            P(),
            P(),
            P(),
            P(),
            P(),
            P(),
            P(),
            P(),
        ),
        out_specs=(
            P(("groups", "region", "feat", "sub"), None),
            P(("groups", "region", "feat"), None),
        ),
        check_vma=False,
    )
```

```python
import functools

import jax
import jax.numpy as jnp
from jax import lax
from jax.experimental import pallas as pl
from jax.experimental.pallas import tpu as pltpu
from jax.sharding import PartitionSpec as P

near_offsets = (1, 2, -1, -2)
tile_rows = 16
lanes = 128
few_parts = 8
grant = 32 << 20
chunk_rows = 64
bf16 = jnp.bfloat16
f32 = jnp.float32
vmem = pl.BlockSpec(memory_space=pltpu.VMEM)
hbm = pl.BlockSpec(memory_space=pltpu.HBM)


def in_hbm(array):
    return pltpu.with_memory_space_constraint(array, pltpu.HBM)


def in_vmem(array):
    return pltpu.with_memory_space_constraint(array, pltpu.VMEM)


def wrap(value, count):
    return jnp.where(value < 0, value + count, value)


def as_columns(rows):
    return jnp.concatenate(
        [
            jnp.transpose(jnp.broadcast_to(rows[at : at + 1], (lanes, rows.shape[1])))
            for at in range(rows.shape[0])
        ],
        axis=0,
    )


def one_hot(columns, width):
    place = lax.broadcasted_iota(jnp.int32, columns.shape, 1)
    return jnp.concatenate(
        [
            jnp.where(columns == place + start, 1.0, 0.0).astype(bf16)
            for start in range(0, width, lanes)
        ],
        axis=1,
    )


def silu(values):
    half = 0.5 * values
    return half + half * jnp.tanh(half)


def layer_norm(values, gain, offset):
    average = jnp.mean(values, axis=-1, keepdims=True)
    centred = values - average
    spread = jnp.mean(centred * centred, axis=-1, keepdims=True)
    return centred * lax.rsqrt(spread + 1e-05) * gain + offset


def my_part():
    return lax.axis_index("region") * lax.axis_size("feat") + lax.axis_index("feat")


def pick_kernel(part_count, near_cap, far_cap, far_ref, near_ref, latent_ref, out_ref, picked):
    me, sub, subs = my_part(), lax.axis_index("sub"), lax.axis_size("sub")
    half = near_cap // subs
    columns = [as_columns(near_ref[0])]
    tile_place = lax.broadcasted_iota(jnp.int32, (tile_rows, lanes), 0)
    far = as_columns(far_ref[0, 0:1])
    for slot in range(1, far_cap):
        far = jnp.where(sub == slot, as_columns(far_ref[0, slot : slot + 1]), far)
    for part in range(part_count):
        columns.append(jnp.where(tile_place == 0, far[part : part + 1], -1))
    hot = one_hot(jnp.concatenate(columns, axis=0), latent_ref.shape[0])
    picked[...] = jnp.dot(hot, latent_ref[...], preferred_element_type=f32).astype(bf16)
    for which, offset in enumerate(near_offsets):
        target = lax.rem(me + (offset + part_count), part_count)
        start = pl.multiple_of(which * near_cap + sub * half, half)
        out_ref[target, :half] = picked[pl.ds(start, half)]
    far_start = len(near_offsets) * near_cap
    for part in range(part_count):
        spot = far_start + part * tile_rows
        out_ref[part, half:] = picked[spot : spot + tile_rows][:1]


def exchange_halves(node_latent, near_rows, far_rows, part_count):
    near_cap, far_cap = near_rows.shape[2], far_rows.shape[2]
    subs = lax.axis_size("sub")
    width = node_latent.shape[1]
    block = (part_count, near_cap // subs + 1, width)
    picks = len(near_offsets) * near_cap + part_count * tile_rows
    blocks = pl.pallas_call(
        functools.partial(pick_kernel, part_count, near_cap, far_cap),
        out_shape=pltpu.HBM(block, bf16),
        in_specs=[vmem, vmem, vmem],
        out_specs=vmem,
        scratch_shapes=[pltpu.VMEM((picks, width), bf16)],
        compiler_params=pltpu.CompilerParams(vmem_limit_bytes=grant),
        cost_estimate=pl.CostEstimate(flops=0, bytes_accessed=0, transcendentals=0),
        name="pick_halo",
    )(in_hbm(jnp.transpose(far_rows, (0, 2, 1))), in_hbm(near_rows), in_hbm(node_latent))
    own = lax.all_to_all(blocks, ("region", "feat"), split_axis=0, concat_axis=0, tiled=True)
    return [own]


def exchange_all(node_latent, near_rows, far_rows, part_count):
    near_send = jnp.take(node_latent, near_rows[0], axis=0, mode="clip")
    far_send = jnp.take(node_latent, far_rows[0], axis=0, mode="clip")
    got = []
    for which, offset in enumerate(near_offsets):
        pairs = [(part, (part + offset) % part_count) for part in range(part_count)]
        got.append(lax.ppermute(near_send[which], ("region", "feat"), pairs))
    far = lax.all_to_all(far_send, ("region", "feat"), split_axis=0, concat_axis=0, tiled=True)
    got.append(far.reshape(-1, far.shape[2]))
    return got


def gather_kernel(
    near_cap,
    far_cap,
    halved,
    block,
    source_ref,
    receiver_ref,
    latent_ref,
    node_in_ref,
    node_out_ref,
    edge_hbm,
    known,
    to_node,
    pack_ref,
    sem,
):
    node_count, width = latent_ref.shape
    edge_count = known.shape[0]
    copy = pltpu.make_async_copy(edge_hbm, known.at[:, pl.ds(0, width)], sem)
    copy.start()
    count = node_in_ref.shape[0]
    pack_ref[:count] = node_in_ref[...]
    pack_ref[count] = node_out_ref[...]
    latent = latent_ref[...]
    index_rows = block // lanes
    node_place = lax.broadcasted_iota(jnp.int32, (node_count, lanes), 0)
    for at in range(edge_count // block):
        spot = slice(at * block, (at + 1) * block)
        here = slice(at * index_rows, (at + 1) * index_rows)
        source, receiver = source_ref[here], receiver_ref[here]
        if halved:
            far = source - (node_count + len(near_offsets) * near_cap)
            slot = lax.rem(far, far_cap)
            turned = wrap(slot - lax.axis_index("sub"), far_cap)
            source = jnp.where(far >= 0, source - slot + turned, source)
        columns = as_columns(source)
        sent = one_hot(columns, node_count)
        known[spot, width : 2 * width] = jnp.dot(
            sent, latent, preferred_element_type=f32
        ).astype(bf16)
        received = one_hot(as_columns(receiver), node_count)
        known[spot, 2 * width : 3 * width] = jnp.dot(
            received, latent, preferred_element_type=f32
        ).astype(bf16)
        known[spot, 3 * width :] = one_hot(columns - node_count, known.shape[1] - 3 * width)
        for row in range(index_rows):
            start = at * block + row * lanes
            to_node[:, start : start + lanes] = jnp.where(
                node_place == receiver[row : row + 1], 1.0, 0.0
            ).astype(bf16)
    copy.wait()


def place_halo(halo, part_count, near_cap, halved, got):
    subs = lax.axis_size("sub")
    far_start = len(near_offsets) * near_cap
    used = far_start
    if halved:
        half = near_cap // subs
        for which, offset in enumerate(near_offsets):
            origin = lax.rem(my_part() + (part_count - offset), part_count)
            for turn in range(subs):
                owner = wrap(lax.axis_index("sub") - turn, subs)
                start = pl.multiple_of(which * near_cap + owner * half, half)
                halo[pl.ds(start, half)] = got[turn][origin, :half]
        far = [got[turn][part, half:] for part in range(part_count) for turn in range(subs)]
        used += len(far)
        halo[far_start:used] = jnp.concatenate(
            [row.astype(f32) for row in far], axis=0
        ).astype(bf16)
    else:
        for rows in got:
            start = used - far_start if rows is not got[-1] else far_start
            halo[start : start + rows.shape[0]] = rows[...]
            used += rows.shape[0]
        used -= far_start
    if used < halo.shape[0]:
        halo[used:] = jnp.zeros((halo.shape[0] - used, halo.shape[1]), bf16)


def place_rows(whole, start, piece, owner):
    rows = piece.shape[0]
    whole[pl.ds(pl.multiple_of(start + owner * rows, rows), rows), :] = piece


def owners():
    feat, feats = lax.axis_index("feat"), lax.axis_size("feat")
    sub, subs = lax.axis_index("sub"), lax.axis_size("sub")
    own = [(0, turn) for turn in range(subs)]
    rest = [(shift, turn) for turn in range(subs) for shift in range(1, feats)]
    return [
        wrap(feat - shift, feats) * subs + wrap(sub - turn, subs) for shift, turn in own + rest
    ]


def from_feats(weight):
    feats = lax.axis_size("feat")
    return [
        lax.ppermute(weight, "feat", [(at, (at + shift) % feats) for at in range(feats)])
        for shift in range(1, feats)
    ]


def from_subs(pieces):
    subs = lax.axis_size("sub")
    return [
        lax.ppermute(piece, "sub", [(at, (at + turn) % subs) for at in range(subs)])
        for turn in range(1, subs)
        for piece in pieces
    ]


def edge_kernel(pieces_count, got_count, part_count, near_cap, halved, block, *refs):
    known, to_node = refs[:2]
    got_refs = refs[2 : 2 + got_count]
    refs = refs[2 + got_count :]
    in_pieces, out_pieces = refs[:pieces_count], refs[pieces_count : 2 * pieces_count]
    row_refs = refs[2 * pieces_count : 2 * pieces_count + 4]
    new_hbm, sum_ref = refs[2 * pieces_count + 4 : 2 * pieces_count + 6]
    in_weight, out_weight, halo, rows, preact, hidden, output, new_ref, total, sems = refs[
        2 * pieces_count + 6 :
    ]
    edge_count, width = new_hbm.shape
    blocks = edge_count // block
    taken = []

    def start(source, target):
        copy = pltpu.make_async_copy(source, target, sems.at[len(taken)])
        copy.start()
        taken.append(copy)
        return copy

    order = owners()
    first, later = [], []
    for which in (1, 0, 2):
        count = in_pieces[0].shape[1]
        spot = pl.ds(pl.multiple_of(which * width + order[0] * count, count), count)
        target = first if which == 1 else later
        target.append(start(in_pieces[0].at[which], in_weight.at[spot]))
    for row_ref, row in zip(row_refs, rows):
        later.append(start(row_ref, row))
    count = out_pieces[0].shape[0]
    spot = pl.ds(pl.multiple_of(order[0] * count, count), count)
    later.append(start(out_pieces[0], out_weight.at[spot]))
    in_bias, out_bias, gain, offset = rows

    place_halo(halo, part_count, near_cap, halved, got_refs)
    for which in (1, 0, 2):
        for piece, owner in zip(in_pieces[1:], order[1:]):
            place_rows(in_weight, which * width, piece[which], owner)
    for piece, owner in zip(out_pieces[1:], order[1:]):
        place_rows(out_weight, 0, piece[...], owner)
    for copy in first:
        copy.wait()
    in_weight[3 * width :] = jnp.dot(
        halo[...], in_weight[width : 2 * width], preferred_element_type=f32
    ).astype(bf16)
    for copy in later:
        copy.wait()

    def in_dot(at):
        preact[at][...] = jnp.dot(
            known[at * block : (at + 1) * block], in_weight[...], preferred_element_type=f32
        )

    def activate(at):
        for start_row in range(0, block, chunk_rows):
            here = slice(start_row, start_row + chunk_rows)
            hidden[at][here] = silu(preact[at][here] + in_bias[...]).astype(bf16)

    def out_dot(at):
        output[at][...] = jnp.dot(
            hidden[at][...], out_weight[...], preferred_element_type=f32
        )

    def normalise(at):
        for start_row in range(0, block, chunk_rows):
            here = slice(start_row, start_row + chunk_rows)
            there = slice(at * block + start_row, at * block + start_row + chunk_rows)
            normed = layer_norm(output[at][here] + out_bias[...], gain[...], offset[...])
            new_ref[there] = (known[there, :width].astype(f32) + normed).astype(bf16)
        spot = pl.ds(at * block, block)
        taken.append(None)
        copy = pltpu.make_async_copy(new_ref.at[spot], new_hbm.at[spot], sems.at[len(taken) - 1])
        copy.start()
        return copy

    def sum_dot(at):
        spot = slice(at * block, (at + 1) * block)
        part = jnp.dot(to_node[:, spot], new_ref[spot], preferred_element_type=f32)
        if at > 0:
            part += total[...]
        if at + 1 < blocks:
            total[...] = part
        else:
            sum_ref[...] = part.astype(bf16)

    out_copies = []
    in_dot(0)
    for at in range(blocks):
        if at + 1 < blocks:
            in_dot(at + 1)
        activate(at)
        out_dot(at)
        if at > 0:
            sum_dot(at - 1)
        out_copies.append(normalise(at))
    sum_dot(blocks - 1)
    for copy in out_copies:
        copy.wait()


def node_kernel(pieces_count, *refs):
    latent_ref, own_ref, other_ref = refs[:3]
    pieces = refs[3 : 3 + pieces_count]
    in_bias, out_bias, gain, offset, new_ref, weights = refs[3 + pieces_count :]
    width = latent_ref.shape[1]
    for piece, owner in zip(pieces, owners()):
        for which in range(piece.shape[0]):
            place_rows(weights, which * width, piece[which], owner)
    latent = latent_ref[...]
    summed = (own_ref[...].astype(f32) + other_ref[...].astype(f32)).astype(bf16)
    preact = jnp.dot(
        jnp.concatenate([latent, summed], axis=1),
        weights[: 2 * width],
        preferred_element_type=f32,
    )
    hidden = silu(preact + in_bias[...]).astype(bf16)
    output = jnp.dot(hidden, weights[2 * width :], preferred_element_type=f32) + out_bias[...]
    new_ref[...] = (
        latent.astype(f32) + layer_norm(output, gain[...], offset[...])
    ).astype(bf16)


def shards(
    node_latent,
    edge_latent,
    edge_source,
    receivers,
    near_rows,
    far_rows,
    edge_in_weight,
    edge_out_weight,
    node_in_weight,
    node_out_weight,
    edge_in_bias,
    edge_out_bias,
    edge_gain,
    edge_offset,
    node_in_bias,
    node_out_bias,
    node_gain,
    node_offset,
):
    node_count, width = node_latent.shape
    edge_count = edge_latent.shape[0]
    near_cap, far_cap = near_rows.shape[2], far_rows.shape[2]
    part_count = far_rows.shape[1]
    block = edge_count // 2
    steps = edge_count // block

    far_edge = [from_feats(edge_in_weight), from_feats(edge_out_weight)]
    near_edge = [from_subs([edge_in_weight]), from_subs([edge_out_weight])]

    subs = lax.axis_size("sub")
    halved = part_count <= few_parts and far_cap == subs and near_cap % (tile_rows * subs) == 0
    exchange = exchange_halves if halved else exchange_all
    got = exchange(node_latent, near_rows, far_rows, part_count)
    halo_space = len(near_offsets) * near_cap + part_count * far_cap
    halo_space = -(-halo_space // lanes) * lanes

    source_rows = in_hbm(edge_source.reshape(-1, lanes))
    receiver_rows = in_hbm(receivers.reshape(-1, lanes))

    pack_shape = (node_in_weight.shape[0] + 1,) + node_out_weight.shape
    known_width = 3 * width + halo_space
    known, to_node, node_weight = pl.pallas_call(
        functools.partial(gather_kernel, near_cap, far_cap, halved, 512),
        out_shape=[
            pltpu.VMEM((edge_count, known_width), bf16),
            pltpu.VMEM((node_count, edge_count), bf16),
            pltpu.VMEM(pack_shape, bf16),
        ],
        in_specs=[vmem] * 5 + [hbm],
        out_specs=[vmem] * 3,
        scratch_shapes=[pltpu.SemaphoreType.DMA],
        compiler_params=pltpu.CompilerParams(vmem_limit_bytes=grant),
        cost_estimate=pl.CostEstimate(flops=0, bytes_accessed=0, transcendentals=0),
        name="gather_latents",
    )(
        source_rows,
        receiver_rows,
        in_hbm(node_latent),
        in_hbm(node_in_weight),
        in_hbm(node_out_weight),
        in_hbm(edge_latent),
    )

    far_edge, got, known, to_node, node_weight = lax.optimization_barrier(
        (far_edge, got, known, to_node, node_weight)
    )
    if halved:
        got = got + from_subs(got)
    edge_in, edge_out = [
        [weight] + near + far + from_subs(far)
        for weight, near, far in zip((edge_in_weight, edge_out_weight), near_edge, far_edge)
    ]
    far_node = from_feats(node_weight)
    node_pieces = [node_weight] + from_subs([node_weight]) + far_node + from_subs(far_node)
    pieces_count = len(edge_in)

    rows = [value.reshape(1, -1) for value in (edge_in_bias, edge_out_bias, edge_gain, edge_offset)]
    edge_operands = [in_vmem(known), in_vmem(to_node)] + [in_vmem(blocks) for blocks in got]
    edge_specs = [vmem] * len(edge_operands)
    for pieces in (edge_in, edge_out):
        edge_operands += [in_hbm(pieces[0])] + [in_vmem(piece) for piece in pieces[1:]]
        edge_specs += [hbm] + [vmem] * (pieces_count - 1)
    edge_operands += [in_hbm(row) for row in rows]
    edge_specs += [hbm] * len(rows)
    copy_count = 3 + 4 + 1 + steps
    edge_new, partial_sums = pl.pallas_call(
        functools.partial(
            edge_kernel, pieces_count, len(got), part_count, near_cap, halved, block
        ),
        out_shape=[
            pltpu.HBM((edge_count, width), bf16),
            jax.ShapeDtypeStruct((node_count, width), bf16),
        ],
        in_specs=edge_specs,
        out_specs=[hbm, vmem],
        scratch_shapes=[
            pltpu.VMEM((known_width, width), bf16),
            pltpu.VMEM((width, width), bf16),
            pltpu.VMEM((halo_space, width), bf16),
            [pltpu.VMEM((1, width), f32)] * 4,
            [pltpu.VMEM((block, width), f32)] * steps,
            [pltpu.VMEM((block, width), bf16)] * steps,
            [pltpu.VMEM((block, width), f32)] * steps,
            pltpu.VMEM((edge_count, width), bf16),
            pltpu.VMEM((node_count, width), f32),
            pltpu.SemaphoreType.DMA((copy_count,)),
        ],
        compiler_params=pltpu.CompilerParams(vmem_limit_bytes=grant),
        cost_estimate=pl.CostEstimate(
            flops=2 * edge_count * width * (4 * width + node_count),
            bytes_accessed=8 * edge_count * width,
            transcendentals=edge_count * width,
        ),
        name="edge_update",
    )(*edge_operands)

    subs = lax.axis_size("sub")
    other_sums = lax.ppermute(partial_sums, "sub", [(at, (at + 1) % subs) for at in range(subs)])

    rows = [value.reshape(1, -1) for value in (node_in_bias, node_out_bias, node_gain, node_offset)]
    node_new = pl.pallas_call(
        functools.partial(node_kernel, pieces_count),
        out_shape=jax.ShapeDtypeStruct((node_count, width), bf16),
        in_specs=[vmem] * (3 + pieces_count + 4),
        out_specs=vmem,
        scratch_shapes=[
            pltpu.VMEM((3 * width, width), bf16),
        ],
        compiler_params=pltpu.CompilerParams(vmem_limit_bytes=grant),
        cost_estimate=pl.CostEstimate(
            flops=2 * node_count * width * 3 * width,
            bytes_accessed=10 * node_count * width,
            transcendentals=node_count * width,
        ),
        name="node_update",
    )(node_latent, partial_sums, other_sums, *node_pieces, *rows)
    return (edge_new, node_new)


def solution(mesh):
    return jax.shard_map(
        shards,
        mesh=mesh,
        in_specs=(
            P(("groups", "region", "feat"), None),
            P(("groups", "region", "feat", "sub"), None),
            P(("groups", "region", "feat", "sub")),
            P(("groups", "region", "feat", "sub")),
            P(("groups", "region", "feat"), None, None),
            P(("groups", "region", "feat"), None, None),
            P(None, ("feat", "sub"), None),
            P(("feat", "sub"), None),
            P(None, ("feat", "sub"), None),
            P(("feat", "sub"), None),
            P(),
            P(),
            P(),
            P(),
            P(),
            P(),
            P(),
            P(),
        ),
        out_specs=(
            P(("groups", "region", "feat", "sub"), None),
            P(("groups", "region", "feat"), None),
        ),
        check_vma=False,
    )
```

```python
import functools

import jax
import jax.numpy as jnp
from jax import lax
from jax.experimental import pallas as pl
from jax.experimental.pallas import tpu as pltpu
from jax.sharding import PartitionSpec as P

near_offsets = (1, 2, -1, -2)
tile_rows = 16
lanes = 128
few_parts = 8
grant = 32 << 20
chunk_rows = 64
bf16 = jnp.bfloat16
f32 = jnp.float32
vmem = pl.BlockSpec(memory_space=pltpu.VMEM)
hbm = pl.BlockSpec(memory_space=pltpu.HBM)


def in_hbm(array):
    return pltpu.with_memory_space_constraint(array, pltpu.HBM)


def in_vmem(array):
    return pltpu.with_memory_space_constraint(array, pltpu.VMEM)


def wrap(value, count):
    return jnp.where(value < 0, value + count, value)


def as_columns(rows):
    return jnp.concatenate(
        [
            jnp.transpose(jnp.broadcast_to(rows[at : at + 1], (lanes, rows.shape[1])))
            for at in range(rows.shape[0])
        ],
        axis=0,
    )


def one_hot(columns, width):
    place = lax.broadcasted_iota(jnp.int32, columns.shape, 1)
    return jnp.concatenate(
        [
            jnp.where(columns == place + start, 1.0, 0.0).astype(bf16)
            for start in range(0, width, lanes)
        ],
        axis=1,
    )


def silu(values):
    half = 0.5 * values
    return half + half * jnp.tanh(half)


def layer_norm(values, gain, offset):
    average = jnp.mean(values, axis=-1, keepdims=True)
    centred = values - average
    spread = jnp.mean(centred * centred, axis=-1, keepdims=True)
    return centred * lax.rsqrt(spread + 1e-05) * gain + offset


def my_part():
    return lax.axis_index("region") * lax.axis_size("feat") + lax.axis_index("feat")


def pick_kernel(part_count, near_cap, far_cap, far_ref, near_ref, latent_ref, out_ref, picked):
    me, sub, subs = my_part(), lax.axis_index("sub"), lax.axis_size("sub")
    half = near_cap // subs
    columns = [as_columns(near_ref[0])]
    tile_place = lax.broadcasted_iota(jnp.int32, (tile_rows, lanes), 0)
    far = as_columns(far_ref[0, 0:1])
    for slot in range(1, far_cap):
        far = jnp.where(sub == slot, as_columns(far_ref[0, slot : slot + 1]), far)
    for part in range(part_count):
        columns.append(jnp.where(tile_place == 0, far[part : part + 1], -1))
    hot = one_hot(jnp.concatenate(columns, axis=0), latent_ref.shape[0])
    picked[...] = jnp.dot(hot, latent_ref[...], preferred_element_type=f32).astype(bf16)
    for which, offset in enumerate(near_offsets):
        target = lax.rem(me + (offset + part_count), part_count)
        start = pl.multiple_of(which * near_cap + sub * half, half)
        out_ref[target, :half] = picked[pl.ds(start, half)]
    far_start = len(near_offsets) * near_cap
    for part in range(part_count):
        spot = far_start + part * tile_rows
        out_ref[part, half:] = picked[spot : spot + tile_rows][:1]


def exchange_halves(node_latent, near_rows, far_rows, part_count):
    near_cap, far_cap = near_rows.shape[2], far_rows.shape[2]
    subs = lax.axis_size("sub")
    width = node_latent.shape[1]
    block = (part_count, near_cap // subs + 1, width)
    picks = len(near_offsets) * near_cap + part_count * tile_rows
    blocks = pl.pallas_call(
        functools.partial(pick_kernel, part_count, near_cap, far_cap),
        out_shape=pltpu.HBM(block, bf16),
        in_specs=[vmem, vmem, vmem],
        out_specs=vmem,
        scratch_shapes=[pltpu.VMEM((picks, width), bf16)],
        compiler_params=pltpu.CompilerParams(vmem_limit_bytes=grant),
        cost_estimate=pl.CostEstimate(flops=0, bytes_accessed=0, transcendentals=0),
        name="pick_halo",
    )(in_hbm(jnp.transpose(far_rows, (0, 2, 1))), in_hbm(near_rows), in_hbm(node_latent))
    own = lax.all_to_all(blocks, ("region", "feat"), split_axis=0, concat_axis=0, tiled=True)
    return [own]


def exchange_all(node_latent, near_rows, far_rows, part_count):
    near_send = jnp.take(node_latent, near_rows[0], axis=0, mode="clip")
    far_send = jnp.take(node_latent, far_rows[0], axis=0, mode="clip")
    got = []
    for which, offset in enumerate(near_offsets):
        pairs = [(part, (part + offset) % part_count) for part in range(part_count)]
        got.append(lax.ppermute(near_send[which], ("region", "feat"), pairs))
    far = lax.all_to_all(far_send, ("region", "feat"), split_axis=0, concat_axis=0, tiled=True)
    got.append(far.reshape(-1, far.shape[2]))
    return got


def gather_kernel(
    near_cap,
    far_cap,
    halved,
    block,
    source_ref,
    receiver_ref,
    latent_ref,
    node_in_ref,
    node_out_ref,
    gathered_hbm,
    to_node,
    pack_ref,
    gathered,
    sems,
):
    node_count, width = latent_ref.shape
    edge_count = gathered.shape[0]
    copies = []
    count = node_in_ref.shape[0]
    pack_ref[:count] = node_in_ref[...]
    pack_ref[count] = node_out_ref[...]
    latent = latent_ref[...]
    index_rows = block // lanes
    node_place = lax.broadcasted_iota(jnp.int32, (node_count, lanes), 0)
    for at in range(edge_count // block):
        spot = slice(at * block, (at + 1) * block)
        here = slice(at * index_rows, (at + 1) * index_rows)
        source, receiver = source_ref[here], receiver_ref[here]
        if halved:
            far = source - (node_count + len(near_offsets) * near_cap)
            slot = lax.rem(far, far_cap)
            turned = wrap(slot - lax.axis_index("sub"), far_cap)
            source = jnp.where(far >= 0, source - slot + turned, source)
        columns = as_columns(source)
        sent = one_hot(columns, node_count)
        gathered[spot, :width] = jnp.dot(
            sent, latent, preferred_element_type=f32
        ).astype(bf16)
        received = one_hot(as_columns(receiver), node_count)
        gathered[spot, width : 2 * width] = jnp.dot(
            received, latent, preferred_element_type=f32
        ).astype(bf16)
        gathered[spot, 2 * width :] = one_hot(
            columns - node_count, gathered.shape[1] - 2 * width
        )
        rows = pl.ds(at * block, block)
        copies.append(
            pltpu.make_async_copy(gathered.at[rows], gathered_hbm.at[rows], sems.at[at])
        )
        copies[-1].start()
        for row in range(index_rows):
            start = at * block + row * lanes
            to_node[:, start : start + lanes] = jnp.where(
                node_place == receiver[row : row + 1], 1.0, 0.0
            ).astype(bf16)
    for copy in copies:
        copy.wait()


def place_halo(halo, part_count, near_cap, halved, got):
    subs = lax.axis_size("sub")
    far_start = len(near_offsets) * near_cap
    used = far_start
    if halved:
        half = near_cap // subs
        for which, offset in enumerate(near_offsets):
            origin = lax.rem(my_part() + (part_count - offset), part_count)
            for turn in range(subs):
                owner = wrap(lax.axis_index("sub") - turn, subs)
                start = pl.multiple_of(which * near_cap + owner * half, half)
                halo[pl.ds(start, half)] = got[turn][origin, :half]
        far = [got[turn][part, half:] for part in range(part_count) for turn in range(subs)]
        used += len(far)
        halo[far_start:used] = jnp.concatenate(
            [row.astype(f32) for row in far], axis=0
        ).astype(bf16)
    else:
        for rows in got:
            start = used - far_start if rows is not got[-1] else far_start
            halo[start : start + rows.shape[0]] = rows[...]
            used += rows.shape[0]
        used -= far_start
    if used < halo.shape[0]:
        halo[used:] = jnp.zeros((halo.shape[0] - used, halo.shape[1]), bf16)


def place_rows(whole, start, piece, owner):
    rows = piece.shape[0]
    whole[pl.ds(pl.multiple_of(start + owner * rows, rows), rows), :] = piece


def owners():
    feat, feats = lax.axis_index("feat"), lax.axis_size("feat")
    sub, subs = lax.axis_index("sub"), lax.axis_size("sub")
    own = [(0, turn) for turn in range(subs)]
    rest = [(shift, turn) for turn in range(subs) for shift in range(1, feats)]
    return [
        wrap(feat - shift, feats) * subs + wrap(sub - turn, subs) for shift, turn in own + rest
    ]


def from_feats(weight):
    feats = lax.axis_size("feat")
    return [
        lax.ppermute(weight, "feat", [(at, (at + shift) % feats) for at in range(feats)])
        for shift in range(1, feats)
    ]


def from_subs(pieces):
    subs = lax.axis_size("sub")
    return [
        lax.ppermute(piece, "sub", [(at, (at + turn) % subs) for at in range(subs)])
        for turn in range(1, subs)
        for piece in pieces
    ]


def edge_kernel(pieces_count, got_count, part_count, near_cap, halved, block, *refs):
    edge_hbm, gathered_hbm, to_node = refs[:3]
    got_refs = refs[3 : 3 + got_count]
    refs = refs[3 + got_count :]
    in_pieces, out_pieces = refs[:pieces_count], refs[pieces_count : 2 * pieces_count]
    row_refs = refs[2 * pieces_count : 2 * pieces_count + 4]
    new_hbm, sum_ref = refs[2 * pieces_count + 4 : 2 * pieces_count + 6]
    known, in_weight, out_weight, halo, rows, preact, hidden, output, new_ref, total, sems = refs[
        2 * pieces_count + 6 :
    ]
    edge_count, width = new_hbm.shape
    blocks = edge_count // block
    taken = []

    def start(source, target):
        copy = pltpu.make_async_copy(source, target, sems.at[len(taken)])
        copy.start()
        taken.append(copy)
        return copy

    order = owners()
    first, later = [], []
    for which in (1, 0, 2):
        count = in_pieces[0].shape[1]
        spot = pl.ds(pl.multiple_of(which * width + order[0] * count, count), count)
        target = first if which == 1 else later
        target.append(start(in_pieces[0].at[which], in_weight.at[spot]))
    for row_ref, row in zip(row_refs, rows):
        later.append(start(row_ref, row))
    count = out_pieces[0].shape[0]
    spot = pl.ds(pl.multiple_of(order[0] * count, count), count)
    later.append(start(out_pieces[0], out_weight.at[spot]))
    in_bias, out_bias, gain, offset = rows
    known_copies = []
    for at in range(blocks):
        spot = pl.ds(at * block, block)
        others = pl.ds(width, known.shape[1] - width)
        known_copies.append(
            [
                start(edge_hbm.at[spot], known.at[spot, pl.ds(0, width)]),
                start(gathered_hbm.at[spot], known.at[spot, others]),
            ]
        )

    place_halo(halo, part_count, near_cap, halved, got_refs)
    for which in (1, 0, 2):
        for piece, owner in zip(in_pieces[1:], order[1:]):
            place_rows(in_weight, which * width, piece[which], owner)
    for piece, owner in zip(out_pieces[1:], order[1:]):
        place_rows(out_weight, 0, piece[...], owner)
    for copy in first:
        copy.wait()
    in_weight[3 * width :] = jnp.dot(
        halo[...], in_weight[width : 2 * width], preferred_element_type=f32
    ).astype(bf16)
    for copy in later:
        copy.wait()

    def in_dot(at):
        for copy in known_copies[at]:
            copy.wait()
        preact[at][...] = jnp.dot(
            known[at * block : (at + 1) * block], in_weight[...], preferred_element_type=f32
        )

    def activate(at):
        for start_row in range(0, block, chunk_rows):
            here = slice(start_row, start_row + chunk_rows)
            hidden[at][here] = silu(preact[at][here] + in_bias[...]).astype(bf16)

    def out_dot(at):
        output[at][...] = jnp.dot(
            hidden[at][...], out_weight[...], preferred_element_type=f32
        )

    def normalise(at):
        for start_row in range(0, block, chunk_rows):
            here = slice(start_row, start_row + chunk_rows)
            there = slice(at * block + start_row, at * block + start_row + chunk_rows)
            normed = layer_norm(output[at][here] + out_bias[...], gain[...], offset[...])
            new_ref[there] = (known[there, :width].astype(f32) + normed).astype(bf16)
        spot = pl.ds(at * block, block)
        return start(new_ref.at[spot], new_hbm.at[spot])

    def sum_dot(at):
        spot = slice(at * block, (at + 1) * block)
        part = jnp.dot(to_node[:, spot], new_ref[spot], preferred_element_type=f32)
        if at > 0:
            part += total[...]
        if at + 1 < blocks:
            total[...] = part
        else:
            sum_ref[...] = part.astype(bf16)

    out_copies = []
    in_dot(0)
    for at in range(blocks):
        if at + 1 < blocks:
            in_dot(at + 1)
        activate(at)
        out_dot(at)
        if at > 0:
            sum_dot(at - 1)
        out_copies.append(normalise(at))
    sum_dot(blocks - 1)
    for copy in out_copies:
        copy.wait()


def node_kernel(pieces_count, *refs):
    latent_ref, own_ref, other_ref = refs[:3]
    pieces = refs[3 : 3 + pieces_count]
    in_bias, out_bias, gain, offset, new_ref, weights = refs[3 + pieces_count :]
    width = latent_ref.shape[1]
    for piece, owner in zip(pieces, owners()):
        for which in range(piece.shape[0]):
            place_rows(weights, which * width, piece[which], owner)
    latent = latent_ref[...]
    summed = (own_ref[...].astype(f32) + other_ref[...].astype(f32)).astype(bf16)
    preact = jnp.dot(
        jnp.concatenate([latent, summed], axis=1),
        weights[: 2 * width],
        preferred_element_type=f32,
    )
    hidden = silu(preact + in_bias[...]).astype(bf16)
    output = jnp.dot(hidden, weights[2 * width :], preferred_element_type=f32) + out_bias[...]
    new_ref[...] = (
        latent.astype(f32) + layer_norm(output, gain[...], offset[...])
    ).astype(bf16)


def shards(
    node_latent,
    edge_latent,
    edge_source,
    receivers,
    near_rows,
    far_rows,
    edge_in_weight,
    edge_out_weight,
    node_in_weight,
    node_out_weight,
    edge_in_bias,
    edge_out_bias,
    edge_gain,
    edge_offset,
    node_in_bias,
    node_out_bias,
    node_gain,
    node_offset,
):
    node_count, width = node_latent.shape
    edge_count = edge_latent.shape[0]
    near_cap, far_cap = near_rows.shape[2], far_rows.shape[2]
    part_count = far_rows.shape[1]
    block = edge_count // 2
    steps = edge_count // block

    far_edge = [from_feats(edge_in_weight), from_feats(edge_out_weight)]
    near_edge = [from_subs([edge_in_weight]), from_subs([edge_out_weight])]

    subs = lax.axis_size("sub")
    halved = part_count <= few_parts and far_cap == subs and near_cap % (tile_rows * subs) == 0
    exchange = exchange_halves if halved else exchange_all
    got = exchange(node_latent, near_rows, far_rows, part_count)
    halo_space = len(near_offsets) * near_cap + part_count * far_cap
    halo_space = -(-halo_space // lanes) * lanes

    source_rows = in_hbm(edge_source.reshape(-1, lanes))
    receiver_rows = in_hbm(receivers.reshape(-1, lanes))

    pack_shape = (node_in_weight.shape[0] + 1,) + node_out_weight.shape
    gathered_width = 2 * width + halo_space
    gather_block = 512
    gathered, to_node, node_weight = pl.pallas_call(
        functools.partial(gather_kernel, near_cap, far_cap, halved, gather_block),
        out_shape=[
            pltpu.HBM((edge_count, gathered_width), bf16),
            pltpu.VMEM((node_count, edge_count), bf16),
            pltpu.VMEM(pack_shape, bf16),
        ],
        in_specs=[vmem] * 5,
        out_specs=[hbm, vmem, vmem],
        scratch_shapes=[
            pltpu.VMEM((edge_count, gathered_width), bf16),
            pltpu.SemaphoreType.DMA((edge_count // gather_block,)),
        ],
        compiler_params=pltpu.CompilerParams(vmem_limit_bytes=grant),
        cost_estimate=pl.CostEstimate(flops=0, bytes_accessed=0, transcendentals=0),
        name="gather_latents",
    )(
        source_rows,
        receiver_rows,
        in_hbm(node_latent),
        in_hbm(node_in_weight),
        in_hbm(node_out_weight),
    )

    far_edge[0], got, gathered, to_node = lax.optimization_barrier(
        (far_edge[0], got, gathered, to_node)
    )
    far_edge[1], to_node, node_weight = lax.optimization_barrier(
        (far_edge[1], to_node, node_weight)
    )
    if halved:
        got = got + from_subs(got)
    edge_in, edge_out = [
        [weight] + near + far + from_subs(far)
        for weight, near, far in zip((edge_in_weight, edge_out_weight), near_edge, far_edge)
    ]
    far_node = from_feats(node_weight)
    node_pieces = [node_weight] + from_subs([node_weight]) + far_node + from_subs(far_node)
    pieces_count = len(edge_in)

    rows = [value.reshape(1, -1) for value in (edge_in_bias, edge_out_bias, edge_gain, edge_offset)]
    edge_operands = [in_hbm(edge_latent), in_hbm(gathered), in_vmem(to_node)]
    edge_operands += [in_vmem(blocks) for blocks in got]
    edge_specs = [hbm] * 2 + [vmem] * (1 + len(got))
    for pieces in (edge_in, edge_out):
        edge_operands += [in_hbm(pieces[0])] + [in_vmem(piece) for piece in pieces[1:]]
        edge_specs += [hbm] + [vmem] * (pieces_count - 1)
    edge_operands += [in_hbm(row) for row in rows]
    edge_specs += [hbm] * len(rows)
    known_width = width + gathered_width
    copy_count = 3 + 4 + 1 + 3 * steps
    edge_new, partial_sums = pl.pallas_call(
        functools.partial(
            edge_kernel, pieces_count, len(got), part_count, near_cap, halved, block
        ),
        out_shape=[
            pltpu.HBM((edge_count, width), bf16),
            jax.ShapeDtypeStruct((node_count, width), bf16),
        ],
        in_specs=edge_specs,
        out_specs=[hbm, vmem],
        scratch_shapes=[
            pltpu.VMEM((edge_count, known_width), bf16),
            pltpu.VMEM((known_width, width), bf16),
            pltpu.VMEM((width, width), bf16),
            pltpu.VMEM((halo_space, width), bf16),
            [pltpu.VMEM((1, width), f32)] * 4,
            [pltpu.VMEM((block, width), f32)] * steps,
            [pltpu.VMEM((block, width), bf16)] * steps,
            [pltpu.VMEM((block, width), f32)] * steps,
            pltpu.VMEM((edge_count, width), bf16),
            pltpu.VMEM((node_count, width), f32),
            pltpu.SemaphoreType.DMA((copy_count,)),
        ],
        compiler_params=pltpu.CompilerParams(vmem_limit_bytes=grant),
        cost_estimate=pl.CostEstimate(
            flops=2 * edge_count * width * (4 * width + node_count),
            bytes_accessed=8 * edge_count * width,
            transcendentals=edge_count * width,
        ),
        name="edge_update",
    )(*edge_operands)

    subs = lax.axis_size("sub")
    other_sums = lax.ppermute(partial_sums, "sub", [(at, (at + 1) % subs) for at in range(subs)])

    rows = [value.reshape(1, -1) for value in (node_in_bias, node_out_bias, node_gain, node_offset)]
    node_new = pl.pallas_call(
        functools.partial(node_kernel, pieces_count),
        out_shape=jax.ShapeDtypeStruct((node_count, width), bf16),
        in_specs=[vmem] * (3 + pieces_count + 4),
        out_specs=vmem,
        scratch_shapes=[
            pltpu.VMEM((3 * width, width), bf16),
        ],
        compiler_params=pltpu.CompilerParams(vmem_limit_bytes=grant),
        cost_estimate=pl.CostEstimate(
            flops=2 * node_count * width * 3 * width,
            bytes_accessed=10 * node_count * width,
            transcendentals=node_count * width,
        ),
        name="node_update",
    )(node_latent, partial_sums, other_sums, *node_pieces, *rows)
    return (edge_new, node_new)


def solution(mesh):
    return jax.shard_map(
        shards,
        mesh=mesh,
        in_specs=(
            P(("groups", "region", "feat"), None),
            P(("groups", "region", "feat", "sub"), None),
            P(("groups", "region", "feat", "sub")),
            P(("groups", "region", "feat", "sub")),
            P(("groups", "region", "feat"), None, None),
            P(("groups", "region", "feat"), None, None),
            P(None, ("feat", "sub"), None),
            P(("feat", "sub"), None),
            P(None, ("feat", "sub"), None),
            P(("feat", "sub"), None),
            P(),
            P(),
            P(),
            P(),
            P(),
            P(),
            P(),
            P(),
        ),
        out_specs=(
            P(("groups", "region", "feat", "sub"), None),
            P(("groups", "region", "feat"), None),
        ),
        check_vma=False,
    )
```

```python
import functools

import jax
import jax.numpy as jnp
from jax import lax
from jax.experimental import pallas as pl
from jax.experimental.pallas import tpu as pltpu
from jax.sharding import PartitionSpec as P

near_offsets = (1, 2, -1, -2)
tile_rows = 16
lanes = 128
few_parts = 8
grant = 32 << 20
chunk_rows = 64
bf16 = jnp.bfloat16
f32 = jnp.float32
vmem = pl.BlockSpec(memory_space=pltpu.VMEM)
hbm = pl.BlockSpec(memory_space=pltpu.HBM)


def in_hbm(array):
    return pltpu.with_memory_space_constraint(array, pltpu.HBM)


def in_vmem(array):
    return pltpu.with_memory_space_constraint(array, pltpu.VMEM)


def wrap(value, count):
    return jnp.where(value < 0, value + count, value)


def as_columns(rows):
    return jnp.concatenate(
        [
            jnp.transpose(jnp.broadcast_to(rows[at : at + 1], (lanes, rows.shape[1])))
            for at in range(rows.shape[0])
        ],
        axis=0,
    )


def one_hot(columns, width):
    place = lax.broadcasted_iota(jnp.int32, columns.shape, 1)
    return jnp.concatenate(
        [
            jnp.where(columns == place + start, 1.0, 0.0).astype(bf16)
            for start in range(0, width, lanes)
        ],
        axis=1,
    )


def silu(values):
    half = 0.5 * values
    return half + half * jnp.tanh(half)


def layer_norm(values, gain, offset):
    average = jnp.mean(values, axis=-1, keepdims=True)
    centred = values - average
    spread = jnp.mean(centred * centred, axis=-1, keepdims=True)
    return centred * lax.rsqrt(spread + 1e-05) * gain + offset


def my_part():
    return lax.axis_index("region") * lax.axis_size("feat") + lax.axis_index("feat")


def pick_kernel(part_count, near_cap, far_cap, far_ref, near_ref, latent_ref, out_ref, picked):
    me, sub, subs = my_part(), lax.axis_index("sub"), lax.axis_size("sub")
    half = near_cap // subs
    columns = [as_columns(near_ref[0])]
    tile_place = lax.broadcasted_iota(jnp.int32, (tile_rows, lanes), 0)
    far = as_columns(far_ref[0, 0:1])
    for slot in range(1, far_cap):
        far = jnp.where(sub == slot, as_columns(far_ref[0, slot : slot + 1]), far)
    for part in range(part_count):
        columns.append(jnp.where(tile_place == 0, far[part : part + 1], -1))
    hot = one_hot(jnp.concatenate(columns, axis=0), latent_ref.shape[0])
    picked[...] = jnp.dot(hot, latent_ref[...], preferred_element_type=f32).astype(bf16)
    for which, offset in enumerate(near_offsets):
        target = lax.rem(me + (offset + part_count), part_count)
        start = pl.multiple_of(which * near_cap + sub * half, half)
        out_ref[target, :half] = picked[pl.ds(start, half)]
    far_start = len(near_offsets) * near_cap
    for part in range(part_count):
        spot = far_start + part * tile_rows
        out_ref[part, half:] = picked[spot : spot + tile_rows][:1]


def exchange_halves(node_latent, near_rows, far_rows, part_count):
    near_cap, far_cap = near_rows.shape[2], far_rows.shape[2]
    subs = lax.axis_size("sub")
    width = node_latent.shape[1]
    block = (part_count, near_cap // subs + 1, width)
    picks = len(near_offsets) * near_cap + part_count * tile_rows
    blocks = pl.pallas_call(
        functools.partial(pick_kernel, part_count, near_cap, far_cap),
        out_shape=pltpu.HBM(block, bf16),
        in_specs=[vmem, vmem, vmem],
        out_specs=vmem,
        scratch_shapes=[pltpu.VMEM((picks, width), bf16)],
        compiler_params=pltpu.CompilerParams(vmem_limit_bytes=grant),
        cost_estimate=pl.CostEstimate(flops=0, bytes_accessed=0, transcendentals=0),
        name="pick_halo",
    )(in_hbm(jnp.transpose(far_rows, (0, 2, 1))), in_hbm(near_rows), in_hbm(node_latent))
    own = lax.all_to_all(blocks, ("region", "feat"), split_axis=0, concat_axis=0, tiled=True)
    return [own]


def exchange_all(node_latent, near_rows, far_rows, part_count):
    near_send = jnp.take(node_latent, near_rows[0], axis=0, mode="clip")
    far_send = jnp.take(node_latent, far_rows[0], axis=0, mode="clip")
    got = []
    for which, offset in enumerate(near_offsets):
        pairs = [(part, (part + offset) % part_count) for part in range(part_count)]
        got.append(lax.ppermute(near_send[which], ("region", "feat"), pairs))
    far = lax.all_to_all(far_send, ("region", "feat"), split_axis=0, concat_axis=0, tiled=True)
    got.append(far.reshape(-1, far.shape[2]))
    return got


def gather_kernel(
    near_cap,
    far_cap,
    halved,
    source_ref,
    receiver_ref,
    latent_ref,
    node_in_ref,
    node_out_ref,
    edge_hbm,
    known,
    gathered_hbm,
    to_node_hbm,
    pack_ref,
    gathered,
    to_node,
    sems,
):
    node_count, width = latent_ref.shape
    first = known.shape[0]
    edge_count = first + gathered.shape[0]
    block = first // 2
    copies = []

    def start(source, target):
        copies.append(pltpu.make_async_copy(source, target, sems.at[len(copies)]))
        copies[-1].start()

    start(edge_hbm.at[pl.ds(0, first)], known.at[:, pl.ds(0, width)])
    count = node_in_ref.shape[0]
    pack_ref[:count] = node_in_ref[...]
    pack_ref[count] = node_out_ref[...]
    latent = latent_ref[...]
    node_place = lax.broadcasted_iota(jnp.int32, (node_count, lanes), 0)
    for row in range(edge_count // lanes):
        to_node[:, row * lanes : (row + 1) * lanes] = jnp.where(
            node_place == receiver_ref[row : row + 1], 1.0, 0.0
        ).astype(bf16)
    start(to_node, to_node_hbm)

    def gather(at, target, rows, begin):
        here = slice(at * (block // lanes), (at + 1) * (block // lanes))
        source = source_ref[here]
        if halved:
            far = source - (node_count + len(near_offsets) * near_cap)
            slot = lax.rem(far, far_cap)
            turned = wrap(slot - lax.axis_index("sub"), far_cap)
            source = jnp.where(far >= 0, source - slot + turned, source)
        columns = as_columns(source)
        sent = one_hot(columns, node_count)
        target[rows, begin : begin + width] = jnp.dot(
            sent, latent, preferred_element_type=f32
        ).astype(bf16)
        received = one_hot(as_columns(receiver_ref[here]), node_count)
        target[rows, begin + width : begin + 2 * width] = jnp.dot(
            received, latent, preferred_element_type=f32
        ).astype(bf16)
        slots = target.shape[1] - begin - 2 * width
        target[rows, begin + 2 * width :] = one_hot(columns - node_count, slots)

    for at in range(first // block, edge_count // block):
        begin = at * block - first
        gather(at, gathered, slice(begin, begin + block), 0)
        rows = pl.ds(begin, block)
        start(gathered.at[rows], gathered_hbm.at[rows])
    for at in range(first // block):
        gather(at, known, slice(at * block, (at + 1) * block), width)
    for copy in copies:
        copy.wait()


def place_halo(halo, part_count, near_cap, halved, got):
    subs = lax.axis_size("sub")
    far_start = len(near_offsets) * near_cap
    used = far_start
    if halved:
        half = near_cap // subs
        for which, offset in enumerate(near_offsets):
            origin = lax.rem(my_part() + (part_count - offset), part_count)
            for turn in range(subs):
                owner = wrap(lax.axis_index("sub") - turn, subs)
                start = pl.multiple_of(which * near_cap + owner * half, half)
                halo[pl.ds(start, half)] = got[turn][origin, :half]
        far = [got[turn][part, half:] for part in range(part_count) for turn in range(subs)]
        used += len(far)
        halo[far_start:used] = jnp.concatenate(
            [row.astype(f32) for row in far], axis=0
        ).astype(bf16)
    else:
        for rows in got:
            start = used - far_start if rows is not got[-1] else far_start
            halo[start : start + rows.shape[0]] = rows[...]
            used += rows.shape[0]
        used -= far_start
    if used < halo.shape[0]:
        halo[used:] = jnp.zeros((halo.shape[0] - used, halo.shape[1]), bf16)


def place_rows(whole, start, piece, owner):
    rows = piece.shape[0]
    whole[pl.ds(pl.multiple_of(start + owner * rows, rows), rows), :] = piece


def owners():
    feat, feats = lax.axis_index("feat"), lax.axis_size("feat")
    sub, subs = lax.axis_index("sub"), lax.axis_size("sub")
    own = [(0, turn) for turn in range(subs)]
    rest = [(shift, turn) for turn in range(subs) for shift in range(1, feats)]
    return [
        wrap(feat - shift, feats) * subs + wrap(sub - turn, subs) for shift, turn in own + rest
    ]


def from_feats(weight):
    feats = lax.axis_size("feat")
    return [
        lax.ppermute(weight, "feat", [(at, (at + shift) % feats) for at in range(feats)])
        for shift in range(1, feats)
    ]


def from_subs(pieces):
    subs = lax.axis_size("sub")
    return [
        lax.ppermute(piece, "sub", [(at, (at + turn) % subs) for at in range(subs)])
        for turn in range(1, subs)
        for piece in pieces
    ]


def edge_kernel(pieces_count, got_count, part_count, near_cap, halved, block, *refs):
    edge_hbm, gathered_hbm, to_node_hbm, known_first = refs[:4]
    got_refs = refs[4 : 4 + got_count]
    refs = refs[4 + got_count :]
    in_pieces, out_pieces = refs[:pieces_count], refs[pieces_count : 2 * pieces_count]
    row_refs = refs[2 * pieces_count : 2 * pieces_count + 4]
    new_hbm, sum_ref = refs[2 * pieces_count + 4 : 2 * pieces_count + 6]
    known_rest, to_node, in_weight, out_weight, halo, rows, preact, hidden, output, new_ref, total, sems = (
        refs[2 * pieces_count + 6 :]
    )
    edge_count, width = new_hbm.shape
    blocks = edge_count // block
    taken = []

    def start(source, target):
        copy = pltpu.make_async_copy(source, target, sems.at[len(taken)])
        copy.start()
        taken.append(copy)
        return copy

    order = owners()
    first, later = [], []
    for which in (1, 0, 2):
        count = in_pieces[0].shape[1]
        spot = pl.ds(pl.multiple_of(which * width + order[0] * count, count), count)
        target = first if which == 1 else later
        target.append(start(in_pieces[0].at[which], in_weight.at[spot]))
    for row_ref, row in zip(row_refs, rows):
        later.append(start(row_ref, row))
    count = out_pieces[0].shape[0]
    spot = pl.ds(pl.multiple_of(order[0] * count, count), count)
    later.append(start(out_pieces[0], out_weight.at[spot]))
    in_bias, out_bias, gain, offset = rows
    rest = edge_count - block
    known_copies = [
        start(edge_hbm.at[pl.ds(block, rest)], known_rest.at[:, pl.ds(0, width)]),
        start(gathered_hbm, known_rest.at[:, pl.ds(width, known_rest.shape[1] - width)]),
    ]
    to_node_copy = start(to_node_hbm, to_node)

    def known(at):
        return known_first if at == 0 else known_rest.at[pl.ds((at - 1) * block, block)]

    place_halo(halo, part_count, near_cap, halved, got_refs)
    for which in (1, 0, 2):
        for piece, owner in zip(in_pieces[1:], order[1:]):
            place_rows(in_weight, which * width, piece[which], owner)
    for piece, owner in zip(out_pieces[1:], order[1:]):
        place_rows(out_weight, 0, piece[...], owner)
    for copy in first:
        copy.wait()
    in_weight[3 * width :] = jnp.dot(
        halo[...], in_weight[width : 2 * width], preferred_element_type=f32
    ).astype(bf16)
    for copy in later:
        copy.wait()

    def in_dot(at):
        if at == 1:
            for copy in known_copies:
                copy.wait()
        preact[at][...] = jnp.dot(
            known(at)[...], in_weight[...], preferred_element_type=f32
        )

    def activate(at):
        for start_row in range(0, block, chunk_rows):
            here = slice(start_row, start_row + chunk_rows)
            hidden[at][here] = silu(preact[at][here] + in_bias[...]).astype(bf16)

    def out_dot(at):
        output[at][...] = jnp.dot(
            hidden[at][...], out_weight[...], preferred_element_type=f32
        )

    def normalise(at):
        for start_row in range(0, block, chunk_rows):
            here = slice(start_row, start_row + chunk_rows)
            there = slice(at * block + start_row, at * block + start_row + chunk_rows)
            normed = layer_norm(output[at][here] + out_bias[...], gain[...], offset[...])
            edges = known(at)[here, :width].astype(f32)
            new_ref[there] = (edges + normed).astype(bf16)
        spot = pl.ds(at * block, block)
        return start(new_ref.at[spot], new_hbm.at[spot])

    def sum_dot(at):
        if at == 0:
            to_node_copy.wait()
        spot = slice(at * block, (at + 1) * block)
        part = jnp.dot(to_node[:, spot], new_ref[spot], preferred_element_type=f32)
        if at > 0:
            part += total[...]
        if at + 1 < blocks:
            total[...] = part
        else:
            sum_ref[...] = part.astype(bf16)

    out_copies = []
    in_dot(0)
    for at in range(blocks):
        if at + 1 < blocks:
            in_dot(at + 1)
        activate(at)
        out_dot(at)
        if at > 0:
            sum_dot(at - 1)
        out_copies.append(normalise(at))
    sum_dot(blocks - 1)
    for copy in out_copies:
        copy.wait()


def node_kernel(pieces_count, *refs):
    latent_ref, own_ref, other_ref = refs[:3]
    pieces = refs[3 : 3 + pieces_count]
    in_bias, out_bias, gain, offset, new_ref, weights = refs[3 + pieces_count :]
    width = latent_ref.shape[1]
    for piece, owner in zip(pieces, owners()):
        for which in range(piece.shape[0]):
            place_rows(weights, which * width, piece[which], owner)
    latent = latent_ref[...]
    summed = (own_ref[...].astype(f32) + other_ref[...].astype(f32)).astype(bf16)
    preact = jnp.dot(
        jnp.concatenate([latent, summed], axis=1),
        weights[: 2 * width],
        preferred_element_type=f32,
    )
    hidden = silu(preact + in_bias[...]).astype(bf16)
    output = jnp.dot(hidden, weights[2 * width :], preferred_element_type=f32) + out_bias[...]
    new_ref[...] = (
        latent.astype(f32) + layer_norm(output, gain[...], offset[...])
    ).astype(bf16)


def shards(
    node_latent,
    edge_latent,
    edge_source,
    receivers,
    near_rows,
    far_rows,
    edge_in_weight,
    edge_out_weight,
    node_in_weight,
    node_out_weight,
    edge_in_bias,
    edge_out_bias,
    edge_gain,
    edge_offset,
    node_in_bias,
    node_out_bias,
    node_gain,
    node_offset,
):
    node_count, width = node_latent.shape
    edge_count = edge_latent.shape[0]
    near_cap, far_cap = near_rows.shape[2], far_rows.shape[2]
    part_count = far_rows.shape[1]
    block = edge_count // 2
    steps = edge_count // block

    far_edge = [from_feats(edge_in_weight), from_feats(edge_out_weight)]
    near_edge = [from_subs([edge_in_weight]), from_subs([edge_out_weight])]

    subs = lax.axis_size("sub")
    halved = part_count <= few_parts and far_cap == subs and near_cap % (tile_rows * subs) == 0
    exchange = exchange_halves if halved else exchange_all
    got = exchange(node_latent, near_rows, far_rows, part_count)
    halo_space = len(near_offsets) * near_cap + part_count * far_cap
    halo_space = -(-halo_space // lanes) * lanes

    source_rows = in_hbm(edge_source.reshape(-1, lanes))
    receiver_rows = in_hbm(receivers.reshape(-1, lanes))

    pack_shape = (node_in_weight.shape[0] + 1,) + node_out_weight.shape
    gathered_width = 2 * width + halo_space
    known_width = width + gathered_width
    rest = edge_count - block
    known, gathered, to_node, node_weight = pl.pallas_call(
        functools.partial(gather_kernel, near_cap, far_cap, halved),
        out_shape=[
            pltpu.VMEM((block, known_width), bf16),
            pltpu.HBM((rest, gathered_width), bf16),
            pltpu.HBM((node_count, edge_count), bf16),
            pltpu.VMEM(pack_shape, bf16),
        ],
        in_specs=[vmem] * 5 + [hbm],
        out_specs=[vmem, hbm, hbm, vmem],
        scratch_shapes=[
            pltpu.VMEM((rest, gathered_width), bf16),
            pltpu.VMEM((node_count, edge_count), bf16),
            pltpu.SemaphoreType.DMA((2 + 2 * (steps - 1),)),
        ],
        compiler_params=pltpu.CompilerParams(vmem_limit_bytes=grant),
        cost_estimate=pl.CostEstimate(flops=0, bytes_accessed=0, transcendentals=0),
        name="gather_latents",
    )(
        source_rows,
        receiver_rows,
        in_hbm(node_latent),
        in_hbm(node_in_weight),
        in_hbm(node_out_weight),
        in_hbm(edge_latent),
    )

    far_edge, got, known, gathered, to_node, node_weight = lax.optimization_barrier(
        (far_edge, got, known, gathered, to_node, node_weight)
    )
    if halved:
        got = got + from_subs(got)
    edge_in, edge_out = [
        [weight] + near + far + from_subs(far)
        for weight, near, far in zip((edge_in_weight, edge_out_weight), near_edge, far_edge)
    ]
    far_node = from_feats(node_weight)
    node_pieces = [node_weight] + from_subs([node_weight]) + far_node + from_subs(far_node)
    pieces_count = len(edge_in)

    rows = [value.reshape(1, -1) for value in (edge_in_bias, edge_out_bias, edge_gain, edge_offset)]
    edge_operands = [in_hbm(edge_latent), in_hbm(gathered), in_hbm(to_node), in_vmem(known)]
    edge_operands += [in_vmem(blocks) for blocks in got]
    edge_specs = [hbm] * 3 + [vmem] * (1 + len(got))
    for pieces in (edge_in, edge_out):
        edge_operands += [in_hbm(pieces[0])] + [in_vmem(piece) for piece in pieces[1:]]
        edge_specs += [hbm] + [vmem] * (pieces_count - 1)
    edge_operands += [in_hbm(row) for row in rows]
    edge_specs += [hbm] * len(rows)
    copy_count = 3 + 4 + 1 + 2 + 1 + steps
    edge_new, partial_sums = pl.pallas_call(
        functools.partial(
            edge_kernel, pieces_count, len(got), part_count, near_cap, halved, block
        ),
        out_shape=[
            pltpu.HBM((edge_count, width), bf16),
            jax.ShapeDtypeStruct((node_count, width), bf16),
        ],
        in_specs=edge_specs,
        out_specs=[hbm, vmem],
        scratch_shapes=[
            pltpu.VMEM((rest, known_width), bf16),
            pltpu.VMEM((node_count, edge_count), bf16),
            pltpu.VMEM((known_width, width), bf16),
            pltpu.VMEM((width, width), bf16),
            pltpu.VMEM((halo_space, width), bf16),
            [pltpu.VMEM((1, width), f32)] * 4,
            [pltpu.VMEM((block, width), f32)] * steps,
            [pltpu.VMEM((block, width), bf16)] * steps,
            [pltpu.VMEM((block, width), f32)] * steps,
            pltpu.VMEM((edge_count, width), bf16),
            pltpu.VMEM((node_count, width), f32),
            pltpu.SemaphoreType.DMA((copy_count,)),
        ],
        compiler_params=pltpu.CompilerParams(vmem_limit_bytes=grant),
        cost_estimate=pl.CostEstimate(
            flops=2 * edge_count * width * (4 * width + node_count),
            bytes_accessed=8 * edge_count * width,
            transcendentals=edge_count * width,
        ),
        name="edge_update",
    )(*edge_operands)

    subs = lax.axis_size("sub")
    other_sums = lax.ppermute(partial_sums, "sub", [(at, (at + 1) % subs) for at in range(subs)])

    rows = [value.reshape(1, -1) for value in (node_in_bias, node_out_bias, node_gain, node_offset)]
    node_new = pl.pallas_call(
        functools.partial(node_kernel, pieces_count),
        out_shape=jax.ShapeDtypeStruct((node_count, width), bf16),
        in_specs=[vmem] * (3 + pieces_count + 4),
        out_specs=vmem,
        scratch_shapes=[
            pltpu.VMEM((3 * width, width), bf16),
        ],
        compiler_params=pltpu.CompilerParams(vmem_limit_bytes=grant),
        cost_estimate=pl.CostEstimate(
            flops=2 * node_count * width * 3 * width,
            bytes_accessed=10 * node_count * width,
            transcendentals=node_count * width,
        ),
        name="node_update",
    )(node_latent, partial_sums, other_sums, *node_pieces, *rows)
    return (edge_new, node_new)


def solution(mesh):
    return jax.shard_map(
        shards,
        mesh=mesh,
        in_specs=(
            P(("groups", "region", "feat"), None),
            P(("groups", "region", "feat", "sub"), None),
            P(("groups", "region", "feat", "sub")),
            P(("groups", "region", "feat", "sub")),
            P(("groups", "region", "feat"), None, None),
            P(("groups", "region", "feat"), None, None),
            P(None, ("feat", "sub"), None),
            P(("feat", "sub"), None),
            P(None, ("feat", "sub"), None),
            P(("feat", "sub"), None),
            P(),
            P(),
            P(),
            P(),
            P(),
            P(),
            P(),
            P(),
        ),
        out_specs=(
            P(("groups", "region", "feat", "sub"), None),
            P(("groups", "region", "feat"), None),
        ),
        check_vma=False,
    )
```

```python
import functools

import jax
import jax.numpy as jnp
from jax import lax
from jax.experimental import pallas as pl
from jax.experimental.pallas import tpu as pltpu
from jax.sharding import PartitionSpec as P

near_offsets = (1, 2, -1, -2)
tile_rows = 16
lanes = 128
few_parts = 8
grant = 32 << 20
chunk_rows = 64
bf16 = jnp.bfloat16
f32 = jnp.float32
vmem = pl.BlockSpec(memory_space=pltpu.VMEM)
hbm = pl.BlockSpec(memory_space=pltpu.HBM)


def in_hbm(array):
    return pltpu.with_memory_space_constraint(array, pltpu.HBM)


def in_vmem(array):
    return pltpu.with_memory_space_constraint(array, pltpu.VMEM)


def wrap(value, count):
    return jnp.where(value < 0, value + count, value)


def as_columns(rows):
    return jnp.concatenate(
        [
            jnp.transpose(jnp.broadcast_to(rows[at : at + 1], (lanes, rows.shape[1])))
            for at in range(rows.shape[0])
        ],
        axis=0,
    )


def one_hot(columns, width):
    place = lax.broadcasted_iota(jnp.int32, columns.shape, 1)
    return jnp.concatenate(
        [
            jnp.where(columns == place + start, 1.0, 0.0).astype(bf16)
            for start in range(0, width, lanes)
        ],
        axis=1,
    )


def silu(values):
    half = 0.5 * values
    return half + half * jnp.tanh(half)


def layer_norm(values, gain, offset):
    average = jnp.mean(values, axis=-1, keepdims=True)
    centred = values - average
    spread = jnp.mean(centred * centred, axis=-1, keepdims=True)
    return centred * lax.rsqrt(spread + 1e-05) * gain + offset


def my_part():
    return lax.axis_index("region") * lax.axis_size("feat") + lax.axis_index("feat")


def pick_kernel(part_count, near_cap, far_cap, far_ref, near_ref, latent_ref, out_ref, picked):
    me, sub, subs = my_part(), lax.axis_index("sub"), lax.axis_size("sub")
    half = near_cap // subs
    columns = [as_columns(near_ref[0])]
    tile_place = lax.broadcasted_iota(jnp.int32, (tile_rows, lanes), 0)
    far = as_columns(far_ref[0, 0:1])
    for slot in range(1, far_cap):
        far = jnp.where(sub == slot, as_columns(far_ref[0, slot : slot + 1]), far)
    for part in range(part_count):
        columns.append(jnp.where(tile_place == 0, far[part : part + 1], -1))
    hot = one_hot(jnp.concatenate(columns, axis=0), latent_ref.shape[0])
    picked[...] = jnp.dot(hot, latent_ref[...], preferred_element_type=f32).astype(bf16)
    for which, offset in enumerate(near_offsets):
        target = lax.rem(me + (offset + part_count), part_count)
        start = pl.multiple_of(which * near_cap + sub * half, half)
        out_ref[target, :half] = picked[pl.ds(start, half)]
    far_start = len(near_offsets) * near_cap
    for part in range(part_count):
        spot = far_start + part * tile_rows
        out_ref[part, half:] = picked[spot : spot + tile_rows][:1]


def exchange_halves(node_latent, near_rows, far_rows, part_count):
    near_cap, far_cap = near_rows.shape[2], far_rows.shape[2]
    subs = lax.axis_size("sub")
    width = node_latent.shape[1]
    block = (part_count, near_cap // subs + 1, width)
    picks = len(near_offsets) * near_cap + part_count * tile_rows
    blocks = pl.pallas_call(
        functools.partial(pick_kernel, part_count, near_cap, far_cap),
        out_shape=pltpu.HBM(block, bf16),
        in_specs=[vmem, vmem, vmem],
        out_specs=vmem,
        scratch_shapes=[pltpu.VMEM((picks, width), bf16)],
        compiler_params=pltpu.CompilerParams(vmem_limit_bytes=grant),
        cost_estimate=pl.CostEstimate(flops=0, bytes_accessed=0, transcendentals=0),
        name="pick_halo",
    )(in_hbm(jnp.transpose(far_rows, (0, 2, 1))), in_hbm(near_rows), in_hbm(node_latent))
    own = lax.all_to_all(blocks, ("region", "feat"), split_axis=0, concat_axis=0, tiled=True)
    return [own]


def exchange_all(node_latent, near_rows, far_rows, part_count):
    near_send = jnp.take(node_latent, near_rows[0], axis=0, mode="clip")
    far_send = jnp.take(node_latent, far_rows[0], axis=0, mode="clip")
    got = []
    for which, offset in enumerate(near_offsets):
        pairs = [(part, (part + offset) % part_count) for part in range(part_count)]
        got.append(lax.ppermute(near_send[which], ("region", "feat"), pairs))
    far = lax.all_to_all(far_send, ("region", "feat"), split_axis=0, concat_axis=0, tiled=True)
    got.append(far.reshape(-1, far.shape[2]))
    return got


def gather_kernel(
    near_cap,
    far_cap,
    halved,
    source_ref,
    receiver_ref,
    latent_ref,
    node_in_ref,
    node_out_ref,
    edge_hbm,
    known,
    gathered_hbm,
    pack_ref,
    gathered,
    sems,
):
    node_count, width = latent_ref.shape
    first = known.shape[0]
    edge_count = first + gathered.shape[0]
    block = first // 2
    copies = []

    def start(source, target):
        copies.append(pltpu.make_async_copy(source, target, sems.at[len(copies)]))
        copies[-1].start()

    start(edge_hbm.at[pl.ds(0, first)], known.at[:, pl.ds(0, width)])
    count = node_in_ref.shape[0]
    pack_ref[:count] = node_in_ref[...]
    pack_ref[count] = node_out_ref[...]
    latent = latent_ref[...]

    def gather(at, target, rows, begin):
        here = slice(at * (block // lanes), (at + 1) * (block // lanes))
        source = source_ref[here]
        if halved:
            far = source - (node_count + len(near_offsets) * near_cap)
            slot = lax.rem(far, far_cap)
            turned = wrap(slot - lax.axis_index("sub"), far_cap)
            source = jnp.where(far >= 0, source - slot + turned, source)
        columns = as_columns(source)
        sent = one_hot(columns, node_count)
        target[rows, begin : begin + width] = jnp.dot(
            sent, latent, preferred_element_type=f32
        ).astype(bf16)
        received = one_hot(as_columns(receiver_ref[here]), node_count)
        target[rows, begin + width : begin + 2 * width] = jnp.dot(
            received, latent, preferred_element_type=f32
        ).astype(bf16)
        slots = target.shape[1] - begin - 2 * width
        target[rows, begin + 2 * width :] = one_hot(columns - node_count, slots)

    for at in range(first // block, edge_count // block):
        begin = at * block - first
        gather(at, gathered, slice(begin, begin + block), 0)
        rows = pl.ds(begin, block)
        start(gathered.at[rows], gathered_hbm.at[rows])
    for at in range(first // block):
        gather(at, known, slice(at * block, (at + 1) * block), width)
    for copy in copies:
        copy.wait()


def place_halo(halo, part_count, near_cap, halved, got):
    subs = lax.axis_size("sub")
    far_start = len(near_offsets) * near_cap
    used = far_start
    if halved:
        half = near_cap // subs
        for which, offset in enumerate(near_offsets):
            origin = lax.rem(my_part() + (part_count - offset), part_count)
            for turn in range(subs):
                owner = wrap(lax.axis_index("sub") - turn, subs)
                start = pl.multiple_of(which * near_cap + owner * half, half)
                halo[pl.ds(start, half)] = got[turn][origin, :half]
        far = [got[turn][part, half:] for part in range(part_count) for turn in range(subs)]
        used += len(far)
        halo[far_start:used] = jnp.concatenate(
            [row.astype(f32) for row in far], axis=0
        ).astype(bf16)
    else:
        for rows in got:
            start = used - far_start if rows is not got[-1] else far_start
            halo[start : start + rows.shape[0]] = rows[...]
            used += rows.shape[0]
        used -= far_start
    if used < halo.shape[0]:
        halo[used:] = jnp.zeros((halo.shape[0] - used, halo.shape[1]), bf16)


def place_rows(whole, start, piece, owner):
    rows = piece.shape[0]
    whole[pl.ds(pl.multiple_of(start + owner * rows, rows), rows), :] = piece


def owners():
    feat, feats = lax.axis_index("feat"), lax.axis_size("feat")
    sub, subs = lax.axis_index("sub"), lax.axis_size("sub")
    own = [(0, turn) for turn in range(subs)]
    rest = [(shift, turn) for turn in range(subs) for shift in range(1, feats)]
    return [
        wrap(feat - shift, feats) * subs + wrap(sub - turn, subs) for shift, turn in own + rest
    ]


def from_feats(weight):
    feats = lax.axis_size("feat")
    return [
        lax.ppermute(weight, "feat", [(at, (at + shift) % feats) for at in range(feats)])
        for shift in range(1, feats)
    ]


def from_subs(pieces):
    subs = lax.axis_size("sub")
    return [
        lax.ppermute(piece, "sub", [(at, (at + turn) % subs) for at in range(subs)])
        for turn in range(1, subs)
        for piece in pieces
    ]


def edge_kernel(pieces_count, got_count, part_count, near_cap, halved, block, *refs):
    edge_hbm, gathered_hbm, receiver_ref, known_first = refs[:4]
    got_refs = refs[4 : 4 + got_count]
    refs = refs[4 + got_count :]
    in_pieces, out_pieces = refs[:pieces_count], refs[pieces_count : 2 * pieces_count]
    row_refs = refs[2 * pieces_count : 2 * pieces_count + 4]
    new_hbm, sum_ref = refs[2 * pieces_count + 4 : 2 * pieces_count + 6]
    known_rest, to_node, in_weight, out_weight, halo, rows, preact, hidden, output, new_ref, total, sems = (
        refs[2 * pieces_count + 6 :]
    )
    edge_count, width = new_hbm.shape
    blocks = edge_count // block
    taken = []

    def start(source, target):
        copy = pltpu.make_async_copy(source, target, sems.at[len(taken)])
        copy.start()
        taken.append(copy)
        return copy

    order = owners()
    first, later = [], []
    for which in (1, 0, 2):
        count = in_pieces[0].shape[1]
        spot = pl.ds(pl.multiple_of(which * width + order[0] * count, count), count)
        target = first if which == 1 else later
        target.append(start(in_pieces[0].at[which], in_weight.at[spot]))
    for row_ref, row in zip(row_refs, rows):
        later.append(start(row_ref, row))
    count = out_pieces[0].shape[0]
    spot = pl.ds(pl.multiple_of(order[0] * count, count), count)
    later.append(start(out_pieces[0], out_weight.at[spot]))
    in_bias, out_bias, gain, offset = rows
    rest = edge_count - block
    known_copies = [
        start(edge_hbm.at[pl.ds(block, rest)], known_rest.at[:, pl.ds(0, width)]),
        start(gathered_hbm, known_rest.at[:, pl.ds(width, known_rest.shape[1] - width)]),
    ]

    def known(at):
        return known_first if at == 0 else known_rest.at[pl.ds((at - 1) * block, block)]

    place_halo(halo, part_count, near_cap, halved, got_refs)
    for which in (1, 0, 2):
        for piece, owner in zip(in_pieces[1:], order[1:]):
            place_rows(in_weight, which * width, piece[which], owner)
    for piece, owner in zip(out_pieces[1:], order[1:]):
        place_rows(out_weight, 0, piece[...], owner)
    for copy in first:
        copy.wait()
    in_weight[3 * width :] = jnp.dot(
        halo[...], in_weight[width : 2 * width], preferred_element_type=f32
    ).astype(bf16)
    for copy in later:
        copy.wait()

    def in_dot(at):
        if at == 1:
            for copy in known_copies:
                copy.wait()
        preact[at][...] = jnp.dot(
            known(at)[...], in_weight[...], preferred_element_type=f32
        )

    def activate(at):
        for start_row in range(0, block, chunk_rows):
            here = slice(start_row, start_row + chunk_rows)
            hidden[at][here] = silu(preact[at][here] + in_bias[...]).astype(bf16)

    def out_dot(at):
        output[at][...] = jnp.dot(
            hidden[at][...], out_weight[...], preferred_element_type=f32
        )

    def normalise(at):
        for start_row in range(0, block, chunk_rows):
            here = slice(start_row, start_row + chunk_rows)
            there = slice(at * block + start_row, at * block + start_row + chunk_rows)
            normed = layer_norm(output[at][here] + out_bias[...], gain[...], offset[...])
            edges = known(at)[here, :width].astype(f32)
            new_ref[there] = (edges + normed).astype(bf16)
        spot = pl.ds(at * block, block)
        return start(new_ref.at[spot], new_hbm.at[spot])

    def sum_dot(at):
        spot = slice(at * block, (at + 1) * block)
        part = jnp.dot(to_node[:, spot], new_ref[spot], preferred_element_type=f32)
        if at > 0:
            part += total[...]
        if at + 1 < blocks:
            total[...] = part
        else:
            sum_ref[...] = part.astype(bf16)

    in_dot(0)
    node_place = lax.broadcasted_iota(jnp.int32, (to_node.shape[0], lanes), 0)
    for row in range(edge_count // lanes):
        to_node[:, row * lanes : (row + 1) * lanes] = jnp.where(
            node_place == receiver_ref[row : row + 1], 1.0, 0.0
        ).astype(bf16)
    for at in range(1, blocks):
        in_dot(at)
        activate(at - 1)
    out_dot(0)
    activate(blocks - 1)
    for at in range(1, blocks):
        out_dot(at)
    out_copies = []
    for at in range(blocks):
        out_copies.append(normalise(at))
        if at > 0:
            sum_dot(at - 1)
    sum_dot(blocks - 1)
    for copy in out_copies:
        copy.wait()


def node_kernel(pieces_count, *refs):
    latent_ref, own_ref, other_ref = refs[:3]
    pieces = refs[3 : 3 + pieces_count]
    in_bias, out_bias, gain, offset, new_ref, weights = refs[3 + pieces_count :]
    width = latent_ref.shape[1]
    for piece, owner in zip(pieces, owners()):
        for which in range(piece.shape[0]):
            place_rows(weights, which * width, piece[which], owner)
    latent = latent_ref[...]
    summed = (own_ref[...].astype(f32) + other_ref[...].astype(f32)).astype(bf16)
    preact = jnp.dot(
        jnp.concatenate([latent, summed], axis=1),
        weights[: 2 * width],
        preferred_element_type=f32,
    )
    hidden = silu(preact + in_bias[...]).astype(bf16)
    output = jnp.dot(hidden, weights[2 * width :], preferred_element_type=f32) + out_bias[...]
    new_ref[...] = (
        latent.astype(f32) + layer_norm(output, gain[...], offset[...])
    ).astype(bf16)


def shards(
    node_latent,
    edge_latent,
    edge_source,
    receivers,
    near_rows,
    far_rows,
    edge_in_weight,
    edge_out_weight,
    node_in_weight,
    node_out_weight,
    edge_in_bias,
    edge_out_bias,
    edge_gain,
    edge_offset,
    node_in_bias,
    node_out_bias,
    node_gain,
    node_offset,
):
    node_count, width = node_latent.shape
    edge_count = edge_latent.shape[0]
    near_cap, far_cap = near_rows.shape[2], far_rows.shape[2]
    part_count = far_rows.shape[1]
    block = edge_count // 2
    steps = edge_count // block

    far_edge = [from_feats(edge_in_weight), from_feats(edge_out_weight)]
    near_edge = [from_subs([edge_in_weight]), from_subs([edge_out_weight])]

    subs = lax.axis_size("sub")
    halved = part_count <= few_parts and far_cap == subs and near_cap % (tile_rows * subs) == 0
    exchange = exchange_halves if halved else exchange_all
    got = exchange(node_latent, near_rows, far_rows, part_count)
    halo_space = len(near_offsets) * near_cap + part_count * far_cap
    halo_space = -(-halo_space // lanes) * lanes

    source_rows = in_hbm(edge_source.reshape(-1, lanes))
    receiver_rows = in_hbm(receivers.reshape(-1, lanes))

    pack_shape = (node_in_weight.shape[0] + 1,) + node_out_weight.shape
    gathered_width = 2 * width + halo_space
    known_width = width + gathered_width
    rest = edge_count - block
    known, gathered, node_weight = pl.pallas_call(
        functools.partial(gather_kernel, near_cap, far_cap, halved),
        out_shape=[
            pltpu.VMEM((block, known_width), bf16),
            pltpu.HBM((rest, gathered_width), bf16),
            pltpu.VMEM(pack_shape, bf16),
        ],
        in_specs=[vmem] * 5 + [hbm],
        out_specs=[vmem, hbm, vmem],
        scratch_shapes=[
            pltpu.VMEM((rest, gathered_width), bf16),
            pltpu.SemaphoreType.DMA((1 + 2 * (steps - 1),)),
        ],
        compiler_params=pltpu.CompilerParams(vmem_limit_bytes=grant),
        cost_estimate=pl.CostEstimate(flops=0, bytes_accessed=0, transcendentals=0),
        name="gather_latents",
    )(
        source_rows,
        receiver_rows,
        in_hbm(node_latent),
        in_hbm(node_in_weight),
        in_hbm(node_out_weight),
        in_hbm(edge_latent),
    )

    far_edge, got, known, gathered, node_weight = lax.optimization_barrier(
        (far_edge, got, known, gathered, node_weight)
    )
    if halved:
        got = got + from_subs(got)
    edge_in, edge_out = [
        [weight] + near + far + from_subs(far)
        for weight, near, far in zip((edge_in_weight, edge_out_weight), near_edge, far_edge)
    ]
    far_node = from_feats(node_weight)
    node_pieces = [node_weight] + from_subs([node_weight]) + far_node + from_subs(far_node)
    pieces_count = len(edge_in)

    rows = [value.reshape(1, -1) for value in (edge_in_bias, edge_out_bias, edge_gain, edge_offset)]
    edge_operands = [in_hbm(edge_latent), in_hbm(gathered), receiver_rows, in_vmem(known)]
    edge_operands += [in_vmem(blocks) for blocks in got]
    edge_specs = [hbm] * 2 + [vmem] * (2 + len(got))
    for pieces in (edge_in, edge_out):
        edge_operands += [in_hbm(pieces[0])] + [in_vmem(piece) for piece in pieces[1:]]
        edge_specs += [hbm] + [vmem] * (pieces_count - 1)
    edge_operands += [in_hbm(row) for row in rows]
    edge_specs += [hbm] * len(rows)
    copy_count = 3 + 4 + 1 + 2 + steps
    edge_new, partial_sums = pl.pallas_call(
        functools.partial(
            edge_kernel, pieces_count, len(got), part_count, near_cap, halved, block
        ),
        out_shape=[
            pltpu.HBM((edge_count, width), bf16),
            jax.ShapeDtypeStruct((node_count, width), bf16),
        ],
        in_specs=edge_specs,
        out_specs=[hbm, vmem],
        scratch_shapes=[
            pltpu.VMEM((rest, known_width), bf16),
            pltpu.VMEM((node_count, edge_count), bf16),
            pltpu.VMEM((known_width, width), bf16),
            pltpu.VMEM((width, width), bf16),
            pltpu.VMEM((halo_space, width), bf16),
            [pltpu.VMEM((1, width), f32)] * 4,
            [pltpu.VMEM((block, width), f32)] * steps,
            [pltpu.VMEM((block, width), bf16)] * steps,
            [pltpu.VMEM((block, width), f32)] * steps,
            pltpu.VMEM((edge_count, width), bf16),
            pltpu.VMEM((node_count, width), f32),
            pltpu.SemaphoreType.DMA((copy_count,)),
        ],
        compiler_params=pltpu.CompilerParams(vmem_limit_bytes=grant),
        cost_estimate=pl.CostEstimate(
            flops=2 * edge_count * width * (4 * width + node_count),
            bytes_accessed=8 * edge_count * width,
            transcendentals=edge_count * width,
        ),
        name="edge_update",
    )(*edge_operands)

    subs = lax.axis_size("sub")
    other_sums = lax.ppermute(partial_sums, "sub", [(at, (at + 1) % subs) for at in range(subs)])

    rows = [value.reshape(1, -1) for value in (node_in_bias, node_out_bias, node_gain, node_offset)]
    node_new = pl.pallas_call(
        functools.partial(node_kernel, pieces_count),
        out_shape=jax.ShapeDtypeStruct((node_count, width), bf16),
        in_specs=[vmem] * (3 + pieces_count + 4),
        out_specs=vmem,
        scratch_shapes=[
            pltpu.VMEM((3 * width, width), bf16),
        ],
        compiler_params=pltpu.CompilerParams(vmem_limit_bytes=grant),
        cost_estimate=pl.CostEstimate(
            flops=2 * node_count * width * 3 * width,
            bytes_accessed=10 * node_count * width,
            transcendentals=node_count * width,
        ),
        name="node_update",
    )(node_latent, partial_sums, other_sums, *node_pieces, *rows)
    return (edge_new, node_new)


def solution(mesh):
    return jax.shard_map(
        shards,
        mesh=mesh,
        in_specs=(
            P(("groups", "region", "feat"), None),
            P(("groups", "region", "feat", "sub"), None),
            P(("groups", "region", "feat", "sub")),
            P(("groups", "region", "feat", "sub")),
            P(("groups", "region", "feat"), None, None),
            P(("groups", "region", "feat"), None, None),
            P(None, ("feat", "sub"), None),
            P(("feat", "sub"), None),
            P(None, ("feat", "sub"), None),
            P(("feat", "sub"), None),
            P(),
            P(),
            P(),
            P(),
            P(),
            P(),
            P(),
            P(),
        ),
        out_specs=(
            P(("groups", "region", "feat", "sub"), None),
            P(("groups", "region", "feat"), None),
        ),
        check_vma=False,
    )
```

```python
import functools

import jax
import jax.numpy as jnp
from jax import lax
from jax.experimental import pallas as pl
from jax.experimental.pallas import tpu as pltpu
from jax.sharding import PartitionSpec as P

near_offsets = (1, 2, -1, -2)
tile_rows = 16
lanes = 128
few_parts = 8
grant = 32 << 20
chunk_rows = 64
bf16 = jnp.bfloat16
f32 = jnp.float32
vmem = pl.BlockSpec(memory_space=pltpu.VMEM)
hbm = pl.BlockSpec(memory_space=pltpu.HBM)


def in_hbm(array):
    return pltpu.with_memory_space_constraint(array, pltpu.HBM)


def in_vmem(array):
    return pltpu.with_memory_space_constraint(array, pltpu.VMEM)


def wrap(value, count):
    return jnp.where(value < 0, value + count, value)


def as_columns(rows):
    return jnp.concatenate(
        [
            jnp.transpose(jnp.broadcast_to(rows[at : at + 1], (lanes, rows.shape[1])))
            for at in range(rows.shape[0])
        ],
        axis=0,
    )


def one_hot(columns, width):
    place = lax.broadcasted_iota(jnp.int32, columns.shape, 1)
    return jnp.concatenate(
        [
            jnp.where(columns == place + start, 1.0, 0.0).astype(bf16)
            for start in range(0, width, lanes)
        ],
        axis=1,
    )


def silu(values):
    half = 0.5 * values
    return half + half * jnp.tanh(half)


def layer_norm(values, gain, offset):
    average = jnp.mean(values, axis=-1, keepdims=True)
    centred = values - average
    spread = jnp.mean(centred * centred, axis=-1, keepdims=True)
    return centred * lax.rsqrt(spread + 1e-05) * gain + offset


def my_part():
    return lax.axis_index("region") * lax.axis_size("feat") + lax.axis_index("feat")


def pick_kernel(part_count, near_cap, far_cap, far_ref, near_ref, latent_ref, out_ref, picked):
    me, sub, subs = my_part(), lax.axis_index("sub"), lax.axis_size("sub")
    half = near_cap // subs
    columns = [as_columns(near_ref[0])]
    tile_place = lax.broadcasted_iota(jnp.int32, (tile_rows, lanes), 0)
    far = as_columns(far_ref[0, 0:1])
    for slot in range(1, far_cap):
        far = jnp.where(sub == slot, as_columns(far_ref[0, slot : slot + 1]), far)
    for part in range(part_count):
        columns.append(jnp.where(tile_place == 0, far[part : part + 1], -1))
    hot = one_hot(jnp.concatenate(columns, axis=0), latent_ref.shape[0])
    picked[...] = jnp.dot(hot, latent_ref[...], preferred_element_type=f32).astype(bf16)
    for which, offset in enumerate(near_offsets):
        target = lax.rem(me + (offset + part_count), part_count)
        start = pl.multiple_of(which * near_cap + sub * half, half)
        out_ref[target, :half] = picked[pl.ds(start, half)]
    far_start = len(near_offsets) * near_cap
    for part in range(part_count):
        spot = far_start + part * tile_rows
        out_ref[part, half:] = picked[spot : spot + tile_rows][:1]


def exchange_halves(node_latent, near_rows, far_rows, part_count):
    near_cap, far_cap = near_rows.shape[2], far_rows.shape[2]
    subs = lax.axis_size("sub")
    width = node_latent.shape[1]
    block = (part_count, near_cap // subs + 1, width)
    picks = len(near_offsets) * near_cap + part_count * tile_rows
    blocks = pl.pallas_call(
        functools.partial(pick_kernel, part_count, near_cap, far_cap),
        out_shape=pltpu.HBM(block, bf16),
        in_specs=[vmem, vmem, vmem],
        out_specs=vmem,
        scratch_shapes=[pltpu.VMEM((picks, width), bf16)],
        compiler_params=pltpu.CompilerParams(vmem_limit_bytes=grant),
        cost_estimate=pl.CostEstimate(flops=0, bytes_accessed=0, transcendentals=0),
        name="pick_halo",
    )(in_hbm(jnp.transpose(far_rows, (0, 2, 1))), in_hbm(near_rows), in_hbm(node_latent))
    own = lax.all_to_all(blocks, ("region", "feat"), split_axis=0, concat_axis=0, tiled=True)
    return [own]


def exchange_all(node_latent, near_rows, far_rows, part_count):
    near_send = jnp.take(node_latent, near_rows[0], axis=0, mode="clip")
    far_send = jnp.take(node_latent, far_rows[0], axis=0, mode="clip")
    got = []
    for which, offset in enumerate(near_offsets):
        pairs = [(part, (part + offset) % part_count) for part in range(part_count)]
        got.append(lax.ppermute(near_send[which], ("region", "feat"), pairs))
    far = lax.all_to_all(far_send, ("region", "feat"), split_axis=0, concat_axis=0, tiled=True)
    got.append(far.reshape(-1, far.shape[2]))
    return got


def gather_kernel(
    near_cap,
    far_cap,
    halved,
    source_ref,
    receiver_ref,
    latent_ref,
    node_in_ref,
    node_out_ref,
    edge_hbm,
    known,
    gathered_hbm,
    pack_ref,
    gathered,
    sems,
):
    node_count, width = latent_ref.shape
    first = known.shape[0]
    edge_count = first + gathered.shape[0]
    block = first // 2
    copies = []

    def start(source, target):
        copies.append(pltpu.make_async_copy(source, target, sems.at[len(copies)]))
        copies[-1].start()

    start(edge_hbm.at[pl.ds(0, first)], known.at[:, pl.ds(0, width)])
    count = node_in_ref.shape[0]
    pack_ref[:count] = node_in_ref[...]
    pack_ref[count] = node_out_ref[...]
    latent = latent_ref[...]

    def gather(at, target, rows, begin):
        here = slice(at * (block // lanes), (at + 1) * (block // lanes))
        source = source_ref[here]
        if halved:
            far = source - (node_count + len(near_offsets) * near_cap)
            slot = lax.rem(far, far_cap)
            turned = wrap(slot - lax.axis_index("sub"), far_cap)
            source = jnp.where(far >= 0, source - slot + turned, source)
        columns = as_columns(source)
        sent = one_hot(columns, node_count)
        target[rows, begin : begin + width] = jnp.dot(
            sent, latent, preferred_element_type=f32
        ).astype(bf16)
        received = one_hot(as_columns(receiver_ref[here]), node_count)
        target[rows, begin + width : begin + 2 * width] = jnp.dot(
            received, latent, preferred_element_type=f32
        ).astype(bf16)
        slots = target.shape[1] - begin - 2 * width
        target[rows, begin + 2 * width :] = one_hot(columns - node_count, slots)

    for at in range(first // block, edge_count // block):
        begin = at * block - first
        gather(at, gathered, slice(begin, begin + block), 0)
        rows = pl.ds(begin, block)
        start(gathered.at[rows], gathered_hbm.at[rows])
    for at in range(first // block):
        gather(at, known, slice(at * block, (at + 1) * block), width)
    for copy in copies:
        copy.wait()


def place_halo(halo, part_count, near_cap, halved, got):
    subs = lax.axis_size("sub")
    far_start = len(near_offsets) * near_cap
    used = far_start
    if halved:
        half = near_cap // subs
        for which, offset in enumerate(near_offsets):
            origin = lax.rem(my_part() + (part_count - offset), part_count)
            for turn in range(subs):
                owner = wrap(lax.axis_index("sub") - turn, subs)
                start = pl.multiple_of(which * near_cap + owner * half, half)
                halo[pl.ds(start, half)] = got[turn][origin, :half]
        far = [got[turn][part, half:] for part in range(part_count) for turn in range(subs)]
        used += len(far)
        halo[far_start:used] = jnp.concatenate(
            [row.astype(f32) for row in far], axis=0
        ).astype(bf16)
    else:
        for rows in got:
            start = used - far_start if rows is not got[-1] else far_start
            halo[start : start + rows.shape[0]] = rows[...]
            used += rows.shape[0]
        used -= far_start
    if used < halo.shape[0]:
        halo[used:] = jnp.zeros((halo.shape[0] - used, halo.shape[1]), bf16)


def place_rows(whole, start, piece, owner):
    rows = piece.shape[0]
    whole[pl.ds(pl.multiple_of(start + owner * rows, rows), rows), :] = piece


def owners():
    feat, feats = lax.axis_index("feat"), lax.axis_size("feat")
    sub, subs = lax.axis_index("sub"), lax.axis_size("sub")
    own = [(0, turn) for turn in range(subs)]
    rest = [(shift, turn) for turn in range(subs) for shift in range(1, feats)]
    return [
        wrap(feat - shift, feats) * subs + wrap(sub - turn, subs) for shift, turn in own + rest
    ]


def from_feats(weight):
    feats = lax.axis_size("feat")
    return [
        lax.ppermute(weight, "feat", [(at, (at + shift) % feats) for at in range(feats)])
        for shift in range(1, feats)
    ]


def from_subs(pieces):
    subs = lax.axis_size("sub")
    return [
        lax.ppermute(piece, "sub", [(at, (at + turn) % subs) for at in range(subs)])
        for turn in range(1, subs)
        for piece in pieces
    ]


def edge_kernel(pieces_count, got_count, part_count, near_cap, halved, block, *refs):
    edge_hbm, gathered_hbm, receiver_ref, known_first = refs[:4]
    got_refs = refs[4 : 4 + got_count]
    refs = refs[4 + got_count :]
    in_pieces, out_pieces = refs[:pieces_count], refs[pieces_count : 2 * pieces_count]
    row_refs = refs[2 * pieces_count : 2 * pieces_count + 4]
    new_hbm, sum_ref = refs[2 * pieces_count + 4 : 2 * pieces_count + 6]
    known_rest, to_node, in_weight, out_weight, halo, rows, preact, hidden, output, new_ref, total, sems = (
        refs[2 * pieces_count + 6 :]
    )
    edge_count, width = new_hbm.shape
    blocks = edge_count // block
    taken = []

    def start(source, target):
        copy = pltpu.make_async_copy(source, target, sems.at[len(taken)])
        copy.start()
        taken.append(copy)
        return copy

    order = owners()
    first, later = [], []
    for which in (1, 0, 2):
        count = in_pieces[0].shape[1]
        spot = pl.ds(pl.multiple_of(which * width + order[0] * count, count), count)
        target = first if which == 1 else later
        target.append(start(in_pieces[0].at[which], in_weight.at[spot]))
    for row_ref, row in zip(row_refs, rows):
        later.append(start(row_ref, row))
    count = out_pieces[0].shape[0]
    spot = pl.ds(pl.multiple_of(order[0] * count, count), count)
    later.append(start(out_pieces[0], out_weight.at[spot]))
    in_bias, out_bias, gain, offset = rows
    rest = edge_count - block
    known_copies = [
        start(edge_hbm.at[pl.ds(block, rest)], known_rest.at[:, pl.ds(0, width)]),
        start(gathered_hbm, known_rest.at[:, pl.ds(width, known_rest.shape[1] - width)]),
    ]

    def known(at):
        return known_first if at == 0 else known_rest.at[pl.ds((at - 1) * block, block)]

    node_place = lax.broadcasted_iota(jnp.int32, (to_node.shape[0], lanes), 0)
    for row in range(edge_count // lanes):
        to_node[:, row * lanes : (row + 1) * lanes] = jnp.where(
            node_place == receiver_ref[row : row + 1], 1.0, 0.0
        ).astype(bf16)
    place_halo(halo, part_count, near_cap, halved, got_refs)
    for which in (1, 0, 2):
        for piece, owner in zip(in_pieces[1:], order[1:]):
            place_rows(in_weight, which * width, piece[which], owner)
    for piece, owner in zip(out_pieces[1:], order[1:]):
        place_rows(out_weight, 0, piece[...], owner)
    for copy in first:
        copy.wait()
    in_weight[3 * width :] = jnp.dot(
        halo[...], in_weight[width : 2 * width], preferred_element_type=f32
    ).astype(bf16)
    for copy in later:
        copy.wait()

    def in_dot(at):
        if at == 1:
            for copy in known_copies:
                copy.wait()
        preact[at][...] = jnp.dot(
            known(at)[...], in_weight[...], preferred_element_type=f32
        )

    def activate(at):
        for start_row in range(0, block, chunk_rows):
            here = slice(start_row, start_row + chunk_rows)
            hidden[at][here] = silu(preact[at][here] + in_bias[...]).astype(bf16)

    def out_dot(at):
        output[at][...] = jnp.dot(
            hidden[at][...], out_weight[...], preferred_element_type=f32
        )

    def normalise(at):
        for start_row in range(0, block, chunk_rows):
            here = slice(start_row, start_row + chunk_rows)
            there = slice(at * block + start_row, at * block + start_row + chunk_rows)
            normed = layer_norm(output[at][here] + out_bias[...], gain[...], offset[...])
            edges = known(at)[here, :width].astype(f32)
            new_ref[there] = (edges + normed).astype(bf16)
        spot = pl.ds(at * block, block)
        return start(new_ref.at[spot], new_hbm.at[spot])

    def sum_dot(at):
        spot = slice(at * block, (at + 1) * block)
        part = jnp.dot(to_node[:, spot], new_ref[spot], preferred_element_type=f32)
        if at > 0:
            part += total[...]
        if at + 1 < blocks:
            total[...] = part
        else:
            sum_ref[...] = part.astype(bf16)

    out_copies = []
    in_dot(0)
    for at in range(blocks):
        if at + 1 < blocks:
            in_dot(at + 1)
        activate(at)
        out_dot(at)
        if at > 0:
            sum_dot(at - 1)
        out_copies.append(normalise(at))
    sum_dot(blocks - 1)
    for copy in out_copies:
        copy.wait()


def node_kernel(pieces_count, *refs):
    latent_ref, own_ref, other_ref = refs[:3]
    pieces = refs[3 : 3 + pieces_count]
    in_bias, out_bias, gain, offset, new_ref, weights = refs[3 + pieces_count :]
    width = latent_ref.shape[1]
    for piece, owner in zip(pieces, owners()):
        for which in range(piece.shape[0]):
            place_rows(weights, which * width, piece[which], owner)
    latent = latent_ref[...]
    summed = (own_ref[...].astype(f32) + other_ref[...].astype(f32)).astype(bf16)
    preact = jnp.dot(
        jnp.concatenate([latent, summed], axis=1),
        weights[: 2 * width],
        preferred_element_type=f32,
    )
    hidden = silu(preact + in_bias[...]).astype(bf16)
    output = jnp.dot(hidden, weights[2 * width :], preferred_element_type=f32) + out_bias[...]
    new_ref[...] = (
        latent.astype(f32) + layer_norm(output, gain[...], offset[...])
    ).astype(bf16)


def shards(
    node_latent,
    edge_latent,
    edge_source,
    receivers,
    near_rows,
    far_rows,
    edge_in_weight,
    edge_out_weight,
    node_in_weight,
    node_out_weight,
    edge_in_bias,
    edge_out_bias,
    edge_gain,
    edge_offset,
    node_in_bias,
    node_out_bias,
    node_gain,
    node_offset,
):
    node_count, width = node_latent.shape
    edge_count = edge_latent.shape[0]
    near_cap, far_cap = near_rows.shape[2], far_rows.shape[2]
    part_count = far_rows.shape[1]
    block = edge_count // 2
    steps = edge_count // block

    far_edge = [from_feats(edge_in_weight), from_feats(edge_out_weight)]
    near_edge = [from_subs([edge_in_weight]), from_subs([edge_out_weight])]

    subs = lax.axis_size("sub")
    halved = part_count <= few_parts and far_cap == subs and near_cap % (tile_rows * subs) == 0
    exchange = exchange_halves if halved else exchange_all
    got = exchange(node_latent, near_rows, far_rows, part_count)
    halo_space = len(near_offsets) * near_cap + part_count * far_cap
    halo_space = -(-halo_space // lanes) * lanes

    source_rows = in_hbm(edge_source.reshape(-1, lanes))
    receiver_rows = in_hbm(receivers.reshape(-1, lanes))

    pack_shape = (node_in_weight.shape[0] + 1,) + node_out_weight.shape
    gathered_width = 2 * width + halo_space
    known_width = width + gathered_width
    rest = edge_count - block
    known, gathered, node_weight = pl.pallas_call(
        functools.partial(gather_kernel, near_cap, far_cap, halved),
        out_shape=[
            pltpu.VMEM((block, known_width), bf16),
            pltpu.HBM((rest, gathered_width), bf16),
            pltpu.VMEM(pack_shape, bf16),
        ],
        in_specs=[vmem] * 5 + [hbm],
        out_specs=[vmem, hbm, vmem],
        scratch_shapes=[
            pltpu.VMEM((rest, gathered_width), bf16),
            pltpu.SemaphoreType.DMA((1 + 2 * (steps - 1),)),
        ],
        compiler_params=pltpu.CompilerParams(vmem_limit_bytes=grant),
        cost_estimate=pl.CostEstimate(flops=0, bytes_accessed=0, transcendentals=0),
        name="gather_latents",
    )(
        source_rows,
        receiver_rows,
        in_hbm(node_latent),
        in_hbm(node_in_weight),
        in_hbm(node_out_weight),
        in_hbm(edge_latent),
    )

    far_edge, got, known, gathered, node_weight = lax.optimization_barrier(
        (far_edge, got, known, gathered, node_weight)
    )
    if halved:
        got = got + from_subs(got)
    edge_in, edge_out = [
        [weight] + near + far + from_subs(far)
        for weight, near, far in zip((edge_in_weight, edge_out_weight), near_edge, far_edge)
    ]
    far_node = from_feats(node_weight)
    node_pieces = [node_weight] + from_subs([node_weight]) + far_node + from_subs(far_node)
    pieces_count = len(edge_in)

    rows = [value.reshape(1, -1) for value in (edge_in_bias, edge_out_bias, edge_gain, edge_offset)]
    edge_operands = [in_hbm(edge_latent), in_hbm(gathered), receiver_rows, in_vmem(known)]
    edge_operands += [in_vmem(blocks) for blocks in got]
    edge_specs = [hbm] * 2 + [vmem] * (2 + len(got))
    for pieces in (edge_in, edge_out):
        edge_operands += [in_hbm(pieces[0])] + [in_vmem(piece) for piece in pieces[1:]]
        edge_specs += [hbm] + [vmem] * (pieces_count - 1)
    edge_operands += [in_hbm(row) for row in rows]
    edge_specs += [hbm] * len(rows)
    copy_count = 3 + 4 + 1 + 2 + steps
    edge_new, partial_sums = pl.pallas_call(
        functools.partial(
            edge_kernel, pieces_count, len(got), part_count, near_cap, halved, block
        ),
        out_shape=[
            pltpu.HBM((edge_count, width), bf16),
            jax.ShapeDtypeStruct((node_count, width), bf16),
        ],
        in_specs=edge_specs,
        out_specs=[hbm, vmem],
        scratch_shapes=[
            pltpu.VMEM((rest, known_width), bf16),
            pltpu.VMEM((node_count, edge_count), bf16),
            pltpu.VMEM((known_width, width), bf16),
            pltpu.VMEM((width, width), bf16),
            pltpu.VMEM((halo_space, width), bf16),
            [pltpu.VMEM((1, width), f32)] * 4,
            [pltpu.VMEM((block, width), f32)] * steps,
            [pltpu.VMEM((block, width), bf16)] * steps,
            [pltpu.VMEM((block, width), f32)] * steps,
            pltpu.VMEM((edge_count, width), bf16),
            pltpu.VMEM((node_count, width), f32),
            pltpu.SemaphoreType.DMA((copy_count,)),
        ],
        compiler_params=pltpu.CompilerParams(vmem_limit_bytes=grant),
        cost_estimate=pl.CostEstimate(
            flops=2 * edge_count * width * (4 * width + node_count),
            bytes_accessed=8 * edge_count * width,
            transcendentals=edge_count * width,
        ),
        name="edge_update",
    )(*edge_operands)

    subs = lax.axis_size("sub")
    other_sums = lax.ppermute(partial_sums, "sub", [(at, (at + 1) % subs) for at in range(subs)])

    rows = [value.reshape(1, -1) for value in (node_in_bias, node_out_bias, node_gain, node_offset)]
    node_new = pl.pallas_call(
        functools.partial(node_kernel, pieces_count),
        out_shape=jax.ShapeDtypeStruct((node_count, width), bf16),
        in_specs=[vmem] * (3 + pieces_count + 4),
        out_specs=vmem,
        scratch_shapes=[
            pltpu.VMEM((3 * width, width), bf16),
        ],
        compiler_params=pltpu.CompilerParams(vmem_limit_bytes=grant),
        cost_estimate=pl.CostEstimate(
            flops=2 * node_count * width * 3 * width,
            bytes_accessed=10 * node_count * width,
            transcendentals=node_count * width,
        ),
        name="node_update",
    )(node_latent, partial_sums, other_sums, *node_pieces, *rows)
    return (edge_new, node_new)


def solution(mesh):
    return jax.shard_map(
        shards,
        mesh=mesh,
        in_specs=(
            P(("groups", "region", "feat"), None),
            P(("groups", "region", "feat", "sub"), None),
            P(("groups", "region", "feat", "sub")),
            P(("groups", "region", "feat", "sub")),
            P(("groups", "region", "feat"), None, None),
            P(("groups", "region", "feat"), None, None),
            P(None, ("feat", "sub"), None),
            P(("feat", "sub"), None),
            P(None, ("feat", "sub"), None),
            P(("feat", "sub"), None),
            P(),
            P(),
            P(),
            P(),
            P(),
            P(),
            P(),
            P(),
        ),
        out_specs=(
            P(("groups", "region", "feat", "sub"), None),
            P(("groups", "region", "feat"), None),
        ),
        check_vma=False,
    )
```

```python
import functools

import jax
import jax.numpy as jnp
from jax import lax
from jax.experimental import pallas as pl
from jax.experimental.pallas import tpu as pltpu
from jax.sharding import PartitionSpec as P

near_offsets = (1, 2, -1, -2)
tile_rows = 16
lanes = 128
few_parts = 8
grant = 32 << 20
chunk_rows = 64
bf16 = jnp.bfloat16
f32 = jnp.float32
vmem = pl.BlockSpec(memory_space=pltpu.VMEM)
hbm = pl.BlockSpec(memory_space=pltpu.HBM)


def in_hbm(array):
    return pltpu.with_memory_space_constraint(array, pltpu.HBM)


def in_vmem(array):
    return pltpu.with_memory_space_constraint(array, pltpu.VMEM)


def wrap(value, count):
    return jnp.where(value < 0, value + count, value)


def as_columns(rows):
    return jnp.concatenate(
        [
            jnp.transpose(jnp.broadcast_to(rows[at : at + 1], (lanes, rows.shape[1])))
            for at in range(rows.shape[0])
        ],
        axis=0,
    )


def one_hot(columns, width):
    place = lax.broadcasted_iota(jnp.int32, columns.shape, 1)
    return jnp.concatenate(
        [
            jnp.where(columns == place + start, 1.0, 0.0).astype(bf16)
            for start in range(0, width, lanes)
        ],
        axis=1,
    )


def silu(values):
    half = 0.5 * values
    return half + half * jnp.tanh(half)


def layer_norm(values, gain, offset):
    average = jnp.mean(values, axis=-1, keepdims=True)
    centred = values - average
    spread = jnp.mean(centred * centred, axis=-1, keepdims=True)
    return centred * lax.rsqrt(spread + 1e-05) * gain + offset


def my_part():
    return lax.axis_index("region") * lax.axis_size("feat") + lax.axis_index("feat")


def pick_kernel(part_count, near_cap, far_cap, far_ref, near_ref, latent_ref, out_ref, picked):
    me, sub, subs = my_part(), lax.axis_index("sub"), lax.axis_size("sub")
    half = near_cap // subs
    columns = [as_columns(near_ref[0])]
    tile_place = lax.broadcasted_iota(jnp.int32, (tile_rows, lanes), 0)
    far = as_columns(far_ref[0, 0:1])
    for slot in range(1, far_cap):
        far = jnp.where(sub == slot, as_columns(far_ref[0, slot : slot + 1]), far)
    for part in range(part_count):
        columns.append(jnp.where(tile_place == 0, far[part : part + 1], -1))
    hot = one_hot(jnp.concatenate(columns, axis=0), latent_ref.shape[0])
    picked[...] = jnp.dot(hot, latent_ref[...], preferred_element_type=f32).astype(bf16)
    for which, offset in enumerate(near_offsets):
        target = lax.rem(me + (offset + part_count), part_count)
        start = pl.multiple_of(which * near_cap + sub * half, half)
        out_ref[target, :half] = picked[pl.ds(start, half)]
    far_start = len(near_offsets) * near_cap
    for part in range(part_count):
        spot = far_start + part * tile_rows
        out_ref[part, half:] = picked[spot : spot + tile_rows][:1]


def exchange_halves(node_latent, near_rows, far_rows, part_count):
    near_cap, far_cap = near_rows.shape[2], far_rows.shape[2]
    subs = lax.axis_size("sub")
    width = node_latent.shape[1]
    block = (part_count, near_cap // subs + 1, width)
    picks = len(near_offsets) * near_cap + part_count * tile_rows
    blocks = pl.pallas_call(
        functools.partial(pick_kernel, part_count, near_cap, far_cap),
        out_shape=pltpu.HBM(block, bf16),
        in_specs=[vmem, vmem, vmem],
        out_specs=vmem,
        scratch_shapes=[pltpu.VMEM((picks, width), bf16)],
        compiler_params=pltpu.CompilerParams(vmem_limit_bytes=grant),
        cost_estimate=pl.CostEstimate(flops=0, bytes_accessed=0, transcendentals=0),
        name="pick_halo",
    )(in_hbm(jnp.transpose(far_rows, (0, 2, 1))), in_hbm(near_rows), in_hbm(node_latent))
    own = lax.all_to_all(blocks, ("region", "feat"), split_axis=0, concat_axis=0, tiled=True)
    return [own]


def exchange_all(node_latent, near_rows, far_rows, part_count):
    near_send = jnp.take(node_latent, near_rows[0], axis=0, mode="clip")
    far_send = jnp.take(node_latent, far_rows[0], axis=0, mode="clip")
    got = []
    for which, offset in enumerate(near_offsets):
        pairs = [(part, (part + offset) % part_count) for part in range(part_count)]
        got.append(lax.ppermute(near_send[which], ("region", "feat"), pairs))
    far = lax.all_to_all(far_send, ("region", "feat"), split_axis=0, concat_axis=0, tiled=True)
    got.append(far.reshape(-1, far.shape[2]))
    return got


def gather_kernel(
    near_cap,
    far_cap,
    halved,
    source_ref,
    receiver_ref,
    latent_ref,
    node_in_ref,
    node_out_ref,
    edge_hbm,
    known,
    gathered_hbm,
    pack_ref,
    gathered,
    sems,
):
    node_count, width = latent_ref.shape
    first = known.shape[0]
    edge_count = first + gathered.shape[0]
    block = first // 2
    copies = []

    def start(source, target):
        copies.append(pltpu.make_async_copy(source, target, sems.at[len(copies)]))
        copies[-1].start()

    start(edge_hbm.at[pl.ds(0, first)], known.at[:, pl.ds(0, width)])
    count = node_in_ref.shape[0]
    pack_ref[:count] = node_in_ref[...]
    pack_ref[count] = node_out_ref[...]
    latent = latent_ref[...]

    def gather(at, target, rows, begin):
        here = slice(at * (block // lanes), (at + 1) * (block // lanes))
        source = source_ref[here]
        if halved:
            far = source - (node_count + len(near_offsets) * near_cap)
            slot = lax.rem(far, far_cap)
            turned = wrap(slot - lax.axis_index("sub"), far_cap)
            source = jnp.where(far >= 0, source - slot + turned, source)
        columns = as_columns(source)
        sent = one_hot(columns, node_count)
        target[rows, begin : begin + width] = jnp.dot(
            sent, latent, preferred_element_type=f32
        ).astype(bf16)
        received = one_hot(as_columns(receiver_ref[here]), node_count)
        target[rows, begin + width : begin + 2 * width] = jnp.dot(
            received, latent, preferred_element_type=f32
        ).astype(bf16)
        slots = target.shape[1] - begin - 2 * width
        target[rows, begin + 2 * width :] = one_hot(columns - node_count, slots)

    for at in range(first // block, edge_count // block):
        begin = at * block - first
        gather(at, gathered, slice(begin, begin + block), 0)
        rows = pl.ds(begin, block)
        start(gathered.at[rows], gathered_hbm.at[rows])
    for at in range(first // block):
        gather(at, known, slice(at * block, (at + 1) * block), width)
    for copy in copies:
        copy.wait()


def place_halo(halo, part_count, near_cap, halved, got):
    subs = lax.axis_size("sub")
    far_start = len(near_offsets) * near_cap
    used = far_start
    if halved:
        half = near_cap // subs
        for which, offset in enumerate(near_offsets):
            origin = lax.rem(my_part() + (part_count - offset), part_count)
            for turn in range(subs):
                owner = wrap(lax.axis_index("sub") - turn, subs)
                start = pl.multiple_of(which * near_cap + owner * half, half)
                halo[pl.ds(start, half)] = got[turn][origin, :half]
        far = [got[turn][part, half:] for part in range(part_count) for turn in range(subs)]
        used += len(far)
        halo[far_start:used] = jnp.concatenate(
            [row.astype(f32) for row in far], axis=0
        ).astype(bf16)
    else:
        for rows in got:
            start = used - far_start if rows is not got[-1] else far_start
            halo[start : start + rows.shape[0]] = rows[...]
            used += rows.shape[0]
        used -= far_start
    if used < halo.shape[0]:
        halo[used:] = jnp.zeros((halo.shape[0] - used, halo.shape[1]), bf16)


def place_rows(whole, start, piece, owner):
    rows = piece.shape[0]
    whole[pl.ds(pl.multiple_of(start + owner * rows, rows), rows), :] = piece


def owners():
    feat, feats = lax.axis_index("feat"), lax.axis_size("feat")
    sub, subs = lax.axis_index("sub"), lax.axis_size("sub")
    own = [(0, turn) for turn in range(subs)]
    rest = [(shift, turn) for turn in range(subs) for shift in range(1, feats)]
    return [
        wrap(feat - shift, feats) * subs + wrap(sub - turn, subs) for shift, turn in own + rest
    ]


def from_feats(weight):
    feats = lax.axis_size("feat")
    return [
        lax.ppermute(weight, "feat", [(at, (at + shift) % feats) for at in range(feats)])
        for shift in range(1, feats)
    ]


def from_subs(pieces):
    subs = lax.axis_size("sub")
    return [
        lax.ppermute(piece, "sub", [(at, (at + turn) % subs) for at in range(subs)])
        for turn in range(1, subs)
        for piece in pieces
    ]


def edge_kernel(pieces_count, got_count, part_count, near_cap, halved, block, *refs):
    edge_hbm, gathered_hbm, receiver_ref, known_first = refs[:4]
    got_refs = refs[4 : 4 + got_count]
    refs = refs[4 + got_count :]
    in_pieces, out_pieces = refs[:pieces_count], refs[pieces_count : 2 * pieces_count]
    row_refs = refs[2 * pieces_count : 2 * pieces_count + 4]
    new_hbm, sum_ref = refs[2 * pieces_count + 4 : 2 * pieces_count + 6]
    known_rest, to_node, in_weight, out_weight, halo, rows, preact, hidden, output, new_ref, total, sems = (
        refs[2 * pieces_count + 6 :]
    )
    edge_count, width = new_hbm.shape
    blocks = edge_count // block
    taken = []

    def start(source, target):
        copy = pltpu.make_async_copy(source, target, sems.at[len(taken)])
        copy.start()
        taken.append(copy)
        return copy

    order = owners()
    first, later = [], []
    for which in (1, 0, 2):
        count = in_pieces[0].shape[1]
        spot = pl.ds(pl.multiple_of(which * width + order[0] * count, count), count)
        target = first if which == 1 else later
        target.append(start(in_pieces[0].at[which], in_weight.at[spot]))
    for row_ref, row in zip(row_refs, rows):
        later.append(start(row_ref, row))
    count = out_pieces[0].shape[0]
    spot = pl.ds(pl.multiple_of(order[0] * count, count), count)
    later.append(start(out_pieces[0], out_weight.at[spot]))
    in_bias, out_bias, gain, offset = rows
    rest = edge_count - block
    known_copies = [
        start(edge_hbm.at[pl.ds(block, rest)], known_rest.at[:, pl.ds(0, width)]),
        start(gathered_hbm, known_rest.at[:, pl.ds(width, known_rest.shape[1] - width)]),
    ]

    def known(at):
        return known_first if at == 0 else known_rest.at[pl.ds((at - 1) * block, block)]

    node_place = lax.broadcasted_iota(jnp.int32, (to_node.shape[0], lanes), 0)
    for row in range(edge_count // lanes):
        to_node[:, row * lanes : (row + 1) * lanes] = jnp.where(
            node_place == receiver_ref[row : row + 1], 1.0, 0.0
        ).astype(bf16)
    place_halo(halo, part_count, near_cap, halved, got_refs)
    for which in (1, 0, 2):
        for piece, owner in zip(in_pieces[1:], order[1:]):
            place_rows(in_weight, which * width, piece[which], owner)
    for piece, owner in zip(out_pieces[1:], order[1:]):
        place_rows(out_weight, 0, piece[...], owner)
    for copy in first:
        copy.wait()
    in_weight[3 * width :] = jnp.dot(
        halo[...], in_weight[width : 2 * width], preferred_element_type=f32
    ).astype(bf16)
    for copy in later:
        copy.wait()

    def in_dot(at):
        if at == 1:
            for copy in known_copies:
                copy.wait()
        preact[at][...] = jnp.dot(
            known(at)[...], in_weight[...], preferred_element_type=f32
        )

    def activate(at):
        for start_row in range(0, block, chunk_rows):
            here = slice(start_row, start_row + chunk_rows)
            hidden[at][here] = silu(preact[at][here] + in_bias[...]).astype(bf16)

    def out_dot(at):
        output[at][...] = jnp.dot(
            hidden[at][...], out_weight[...], preferred_element_type=f32
        )

    def normalise(at):
        for start_row in range(0, block, chunk_rows):
            here = slice(start_row, start_row + chunk_rows)
            there = slice(at * block + start_row, at * block + start_row + chunk_rows)
            normed = layer_norm(output[at][here] + out_bias[...], gain[...], offset[...])
            edges = known(at)[here, :width].astype(f32)
            new_ref[there] = (edges + normed).astype(bf16)
        spot = pl.ds(at * block, block)
        return start(new_ref.at[spot], new_hbm.at[spot])

    def sum_dot(at):
        spot = slice(at * block, (at + 1) * block)
        part = jnp.dot(to_node[:, spot], new_ref[spot], preferred_element_type=f32)
        if at > 0:
            part += total[...]
        if at + 1 < blocks:
            total[...] = part
        else:
            sum_ref[...] = part.astype(bf16)

    out_copies = []
    in_dot(0)
    for at in range(blocks):
        if at + 1 < blocks:
            in_dot(at + 1)
        activate(at)
        out_dot(at)
        if at > 0:
            sum_dot(at - 1)
        out_copies.append(normalise(at))
    sum_dot(blocks - 1)
    for copy in out_copies:
        copy.wait()


def node_kernel(pieces_count, *refs):
    latent_ref, own_ref, other_ref = refs[:3]
    pieces = refs[3 : 3 + pieces_count]
    in_bias, out_bias, gain, offset, new_ref, weights = refs[3 + pieces_count :]
    width = latent_ref.shape[1]
    for piece, owner in zip(pieces, owners()):
        for which in range(piece.shape[0]):
            place_rows(weights, which * width, piece[which], owner)
    latent = latent_ref[...]
    summed = (own_ref[...].astype(f32) + other_ref[...].astype(f32)).astype(bf16)
    preact = jnp.dot(
        jnp.concatenate([latent, summed], axis=1),
        weights[: 2 * width],
        preferred_element_type=f32,
    )
    hidden = silu(preact + in_bias[...]).astype(bf16)
    output = jnp.dot(hidden, weights[2 * width :], preferred_element_type=f32) + out_bias[...]
    new_ref[...] = (
        latent.astype(f32) + layer_norm(output, gain[...], offset[...])
    ).astype(bf16)


def shards(
    node_latent,
    edge_latent,
    edge_source,
    receivers,
    near_rows,
    far_rows,
    edge_in_weight,
    edge_out_weight,
    node_in_weight,
    node_out_weight,
    edge_in_bias,
    edge_out_bias,
    edge_gain,
    edge_offset,
    node_in_bias,
    node_out_bias,
    node_gain,
    node_offset,
):
    node_count, width = node_latent.shape
    edge_count = edge_latent.shape[0]
    near_cap, far_cap = near_rows.shape[2], far_rows.shape[2]
    part_count = far_rows.shape[1]
    block = edge_count // 2
    steps = edge_count // block

    far_edge = [from_feats(edge_in_weight), from_feats(edge_out_weight)]
    near_edge = [from_subs([edge_in_weight]), from_subs([edge_out_weight])]

    subs = lax.axis_size("sub")
    halved = part_count <= few_parts and far_cap == subs and near_cap % (tile_rows * subs) == 0
    exchange = exchange_halves if halved else exchange_all
    got = exchange(node_latent, near_rows, far_rows, part_count)
    halo_space = len(near_offsets) * near_cap + part_count * far_cap
    halo_space = -(-halo_space // lanes) * lanes

    source_rows = in_hbm(edge_source.reshape(-1, lanes))
    receiver_rows = in_hbm(receivers.reshape(-1, lanes))

    pack_shape = (node_in_weight.shape[0] + 1,) + node_out_weight.shape
    near_edge[1], latent_after = lax.optimization_barrier((near_edge[1], node_latent))
    gathered_width = 2 * width + halo_space
    known_width = width + gathered_width
    rest = edge_count - block
    known, gathered, node_weight = pl.pallas_call(
        functools.partial(gather_kernel, near_cap, far_cap, halved),
        out_shape=[
            pltpu.VMEM((block, known_width), bf16),
            pltpu.HBM((rest, gathered_width), bf16),
            pltpu.VMEM(pack_shape, bf16),
        ],
        in_specs=[vmem] * 5 + [hbm],
        out_specs=[vmem, hbm, vmem],
        scratch_shapes=[
            pltpu.VMEM((rest, gathered_width), bf16),
            pltpu.SemaphoreType.DMA((1 + 2 * (steps - 1),)),
        ],
        compiler_params=pltpu.CompilerParams(vmem_limit_bytes=grant),
        cost_estimate=pl.CostEstimate(flops=0, bytes_accessed=0, transcendentals=0),
        name="gather_latents",
    )(
        source_rows,
        receiver_rows,
        in_hbm(latent_after),
        in_hbm(node_in_weight),
        in_hbm(node_out_weight),
        in_hbm(edge_latent),
    )

    far_edge, got, known, gathered = lax.optimization_barrier((far_edge, got, known, gathered))
    if halved:
        got = got + from_subs(got)
    edge_in, edge_out = [
        [weight] + near + far + from_subs(far)
        for weight, near, far in zip((edge_in_weight, edge_out_weight), near_edge, far_edge)
    ]
    far_node = from_feats(node_weight)
    node_pieces = [node_weight] + from_subs([node_weight]) + far_node + from_subs(far_node)
    pieces_count = len(edge_in)

    rows = [value.reshape(1, -1) for value in (edge_in_bias, edge_out_bias, edge_gain, edge_offset)]
    edge_operands = [in_hbm(edge_latent), in_hbm(gathered), receiver_rows, in_vmem(known)]
    edge_operands += [in_vmem(blocks) for blocks in got]
    edge_specs = [hbm] * 2 + [vmem] * (2 + len(got))
    for pieces in (edge_in, edge_out):
        edge_operands += [in_hbm(pieces[0])] + [in_vmem(piece) for piece in pieces[1:]]
        edge_specs += [hbm] + [vmem] * (pieces_count - 1)
    edge_operands += [in_hbm(row) for row in rows]
    edge_specs += [hbm] * len(rows)
    copy_count = 3 + 4 + 1 + 2 + steps
    edge_new, partial_sums = pl.pallas_call(
        functools.partial(
            edge_kernel, pieces_count, len(got), part_count, near_cap, halved, block
        ),
        out_shape=[
            pltpu.HBM((edge_count, width), bf16),
            jax.ShapeDtypeStruct((node_count, width), bf16),
        ],
        in_specs=edge_specs,
        out_specs=[hbm, vmem],
        scratch_shapes=[
            pltpu.VMEM((rest, known_width), bf16),
            pltpu.VMEM((node_count, edge_count), bf16),
            pltpu.VMEM((known_width, width), bf16),
            pltpu.VMEM((width, width), bf16),
            pltpu.VMEM((halo_space, width), bf16),
            [pltpu.VMEM((1, width), f32)] * 4,
            [pltpu.VMEM((block, width), f32)] * steps,
            [pltpu.VMEM((block, width), bf16)] * steps,
            [pltpu.VMEM((block, width), f32)] * steps,
            pltpu.VMEM((edge_count, width), bf16),
            pltpu.VMEM((node_count, width), f32),
            pltpu.SemaphoreType.DMA((copy_count,)),
        ],
        compiler_params=pltpu.CompilerParams(vmem_limit_bytes=grant),
        cost_estimate=pl.CostEstimate(flops=0, bytes_accessed=0, transcendentals=0),
        name="edge_update",
    )(*edge_operands)

    subs = lax.axis_size("sub")
    other_sums = lax.ppermute(partial_sums, "sub", [(at, (at + 1) % subs) for at in range(subs)])

    rows = [value.reshape(1, -1) for value in (node_in_bias, node_out_bias, node_gain, node_offset)]
    node_new = pl.pallas_call(
        functools.partial(node_kernel, pieces_count),
        out_shape=jax.ShapeDtypeStruct((node_count, width), bf16),
        in_specs=[vmem] * (3 + pieces_count + 4),
        out_specs=vmem,
        scratch_shapes=[
            pltpu.VMEM((3 * width, width), bf16),
        ],
        compiler_params=pltpu.CompilerParams(vmem_limit_bytes=grant),
        cost_estimate=pl.CostEstimate(
            flops=2 * node_count * width * 3 * width,
            bytes_accessed=10 * node_count * width,
            transcendentals=node_count * width,
        ),
        name="node_update",
    )(node_latent, partial_sums, other_sums, *node_pieces, *rows)
    return (edge_new, node_new)


def solution(mesh):
    return jax.shard_map(
        shards,
        mesh=mesh,
        in_specs=(
            P(("groups", "region", "feat"), None),
            P(("groups", "region", "feat", "sub"), None),
            P(("groups", "region", "feat", "sub")),
            P(("groups", "region", "feat", "sub")),
            P(("groups", "region", "feat"), None, None),
            P(("groups", "region", "feat"), None, None),
            P(None, ("feat", "sub"), None),
            P(("feat", "sub"), None),
            P(None, ("feat", "sub"), None),
            P(("feat", "sub"), None),
            P(),
            P(),
            P(),
            P(),
            P(),
            P(),
            P(),
            P(),
        ),
        out_specs=(
            P(("groups", "region", "feat", "sub"), None),
            P(("groups", "region", "feat"), None),
        ),
        check_vma=False,
    )
```

```python
import functools

import jax
import jax.numpy as jnp
from jax import lax
from jax.experimental import pallas as pl
from jax.experimental.pallas import tpu as pltpu
from jax.sharding import PartitionSpec as P

near_offsets = (1, 2, -1, -2)
tile_rows = 16
lanes = 128
few_parts = 8
grant = 32 << 20
chunk_rows = 64
bf16 = jnp.bfloat16
f32 = jnp.float32
vmem = pl.BlockSpec(memory_space=pltpu.VMEM)
hbm = pl.BlockSpec(memory_space=pltpu.HBM)


def in_hbm(array):
    return pltpu.with_memory_space_constraint(array, pltpu.HBM)


def in_vmem(array):
    return pltpu.with_memory_space_constraint(array, pltpu.VMEM)


def wrap(value, count):
    return jnp.where(value < 0, value + count, value)


def as_columns(rows):
    return jnp.concatenate(
        [
            jnp.transpose(jnp.broadcast_to(rows[at : at + 1], (lanes, rows.shape[1])))
            for at in range(rows.shape[0])
        ],
        axis=0,
    )


def one_hot(columns, width):
    place = lax.broadcasted_iota(jnp.int32, columns.shape, 1)
    return jnp.concatenate(
        [
            jnp.where(columns == place + start, 1.0, 0.0).astype(bf16)
            for start in range(0, width, lanes)
        ],
        axis=1,
    )


def silu(values):
    half = 0.5 * values
    return half + half * jnp.tanh(half)


def layer_norm(values, gain, offset):
    average = jnp.mean(values, axis=-1, keepdims=True)
    centred = values - average
    spread = jnp.mean(centred * centred, axis=-1, keepdims=True)
    return centred * lax.rsqrt(spread + 1e-05) * gain + offset


def my_part():
    return lax.axis_index("region") * lax.axis_size("feat") + lax.axis_index("feat")


def pick_kernel(part_count, near_cap, far_cap, far_ref, near_ref, latent_ref, out_ref, picked):
    me, sub, subs = my_part(), lax.axis_index("sub"), lax.axis_size("sub")
    half = near_cap // subs
    columns = [as_columns(near_ref[0])]
    tile_place = lax.broadcasted_iota(jnp.int32, (tile_rows, lanes), 0)
    far = as_columns(far_ref[0, 0:1])
    for slot in range(1, far_cap):
        far = jnp.where(sub == slot, as_columns(far_ref[0, slot : slot + 1]), far)
    for part in range(part_count):
        columns.append(jnp.where(tile_place == 0, far[part : part + 1], -1))
    hot = one_hot(jnp.concatenate(columns, axis=0), latent_ref.shape[0])
    picked[...] = jnp.dot(hot, latent_ref[...], preferred_element_type=f32).astype(bf16)
    for which, offset in enumerate(near_offsets):
        target = lax.rem(me + (offset + part_count), part_count)
        start = pl.multiple_of(which * near_cap + sub * half, half)
        out_ref[target, :half] = picked[pl.ds(start, half)]
    far_start = len(near_offsets) * near_cap
    for part in range(part_count):
        spot = far_start + part * tile_rows
        out_ref[part, half:] = picked[spot : spot + tile_rows][:1]


def exchange_halves(node_latent, near_rows, far_rows, part_count):
    near_cap, far_cap = near_rows.shape[2], far_rows.shape[2]
    subs = lax.axis_size("sub")
    width = node_latent.shape[1]
    block = (part_count, near_cap // subs + 1, width)
    picks = len(near_offsets) * near_cap + part_count * tile_rows
    blocks = pl.pallas_call(
        functools.partial(pick_kernel, part_count, near_cap, far_cap),
        out_shape=pltpu.HBM(block, bf16),
        in_specs=[vmem, vmem, vmem],
        out_specs=vmem,
        scratch_shapes=[pltpu.VMEM((picks, width), bf16)],
        compiler_params=pltpu.CompilerParams(vmem_limit_bytes=grant),
        cost_estimate=pl.CostEstimate(flops=0, bytes_accessed=0, transcendentals=0),
        name="pick_halo",
    )(in_hbm(jnp.transpose(far_rows, (0, 2, 1))), in_hbm(near_rows), in_hbm(node_latent))
    own = lax.all_to_all(blocks, ("region", "feat"), split_axis=0, concat_axis=0, tiled=True)
    return [own]


def exchange_all(node_latent, near_rows, far_rows, part_count):
    near_send = jnp.take(node_latent, near_rows[0], axis=0, mode="clip")
    far_send = jnp.take(node_latent, far_rows[0], axis=0, mode="clip")
    got = []
    for which, offset in enumerate(near_offsets):
        pairs = [(part, (part + offset) % part_count) for part in range(part_count)]
        got.append(lax.ppermute(near_send[which], ("region", "feat"), pairs))
    far = lax.all_to_all(far_send, ("region", "feat"), split_axis=0, concat_axis=0, tiled=True)
    got.append(far.reshape(-1, far.shape[2]))
    return got


def gather_kernel(
    near_cap,
    far_cap,
    halved,
    source_ref,
    receiver_ref,
    latent_ref,
    node_in_ref,
    node_out_ref,
    edge_hbm,
    *refs,
):
    known, pack_ref, sems = refs[:-2], refs[-2], refs[-1]
    node_count, width = latent_ref.shape
    rows = known[0].shape[0]
    block = rows // 2
    copies = []

    def start(source, target):
        copies.append(pltpu.make_async_copy(source, target, sems.at[len(copies)]))
        copies[-1].start()

    for at, target in enumerate(known):
        start(edge_hbm.at[pl.ds(at * rows, rows)], target.at[:, pl.ds(0, width)])
    count = node_in_ref.shape[0]
    pack_ref[:count] = node_in_ref[...]
    pack_ref[count] = node_out_ref[...]
    latent = latent_ref[...]

    def gather(at, target, spot, begin):
        here = slice(at * (block // lanes), (at + 1) * (block // lanes))
        source = source_ref[here]
        if halved:
            far = source - (node_count + len(near_offsets) * near_cap)
            slot = lax.rem(far, far_cap)
            turned = wrap(slot - lax.axis_index("sub"), far_cap)
            source = jnp.where(far >= 0, source - slot + turned, source)
        columns = as_columns(source)
        sent = one_hot(columns, node_count)
        target[spot, begin : begin + width] = jnp.dot(
            sent, latent, preferred_element_type=f32
        ).astype(bf16)
        received = one_hot(as_columns(receiver_ref[here]), node_count)
        target[spot, begin + width : begin + 2 * width] = jnp.dot(
            received, latent, preferred_element_type=f32
        ).astype(bf16)
        slots = target.shape[1] - begin - 2 * width
        target[spot, begin + 2 * width :] = one_hot(columns - node_count, slots)

    for at, target in enumerate(known):
        for part in range(rows // block):
            spot = slice(part * block, (part + 1) * block)
            gather(at * (rows // block) + part, target, spot, width)
    for copy in copies:
        copy.wait()


def place_halo(halo, part_count, near_cap, halved, got):
    subs = lax.axis_size("sub")
    far_start = len(near_offsets) * near_cap
    used = far_start
    if halved:
        half = near_cap // subs
        for which, offset in enumerate(near_offsets):
            origin = lax.rem(my_part() + (part_count - offset), part_count)
            for turn in range(subs):
                owner = wrap(lax.axis_index("sub") - turn, subs)
                start = pl.multiple_of(which * near_cap + owner * half, half)
                halo[pl.ds(start, half)] = got[turn][origin, :half]
        far = [got[turn][part, half:] for part in range(part_count) for turn in range(subs)]
        used += len(far)
        halo[far_start:used] = jnp.concatenate(
            [row.astype(f32) for row in far], axis=0
        ).astype(bf16)
    else:
        for rows in got:
            start = used - far_start if rows is not got[-1] else far_start
            halo[start : start + rows.shape[0]] = rows[...]
            used += rows.shape[0]
        used -= far_start
    if used < halo.shape[0]:
        halo[used:] = jnp.zeros((halo.shape[0] - used, halo.shape[1]), bf16)


def place_rows(whole, start, piece, owner):
    rows = piece.shape[0]
    whole[pl.ds(pl.multiple_of(start + owner * rows, rows), rows), :] = piece


def owners():
    feat, feats = lax.axis_index("feat"), lax.axis_size("feat")
    sub, subs = lax.axis_index("sub"), lax.axis_size("sub")
    own = [(0, turn) for turn in range(subs)]
    rest = [(shift, turn) for turn in range(subs) for shift in range(1, feats)]
    return [
        wrap(feat - shift, feats) * subs + wrap(sub - turn, subs) for shift, turn in own + rest
    ]


def from_feats(weight):
    feats = lax.axis_size("feat")
    return [
        lax.ppermute(weight, "feat", [(at, (at + shift) % feats) for at in range(feats)])
        for shift in range(1, feats)
    ]


def from_subs(pieces):
    subs = lax.axis_size("sub")
    return [
        lax.ppermute(piece, "sub", [(at, (at + turn) % subs) for at in range(subs)])
        for turn in range(1, subs)
        for piece in pieces
    ]


def edge_kernel(pieces_count, got_count, part_count, near_cap, halved, blocks, *refs):
    receiver_ref, known = refs[0], refs[1 : 1 + blocks]
    got_refs = refs[1 + blocks : 1 + blocks + got_count]
    refs = refs[1 + blocks + got_count :]
    in_pieces, out_pieces = refs[:pieces_count], refs[pieces_count : 2 * pieces_count]
    row_refs = refs[2 * pieces_count : 2 * pieces_count + 4]
    new_hbm, sum_ref = refs[2 * pieces_count + 4 : 2 * pieces_count + 6]
    to_node, in_weight, out_weight, halo, rows, preact, hidden, output, new_ref, total, sems = (
        refs[2 * pieces_count + 6 :]
    )
    edge_count, width = new_hbm.shape
    block = edge_count // blocks
    taken = []

    def start(source, target):
        copy = pltpu.make_async_copy(source, target, sems.at[len(taken)])
        copy.start()
        taken.append(copy)
        return copy

    order = owners()
    first, later = [], []
    for which in (1, 0, 2):
        count = in_pieces[0].shape[1]
        spot = pl.ds(pl.multiple_of(which * width + order[0] * count, count), count)
        target = first if which == 1 else later
        target.append(start(in_pieces[0].at[which], in_weight.at[spot]))
    for row_ref, row in zip(row_refs, rows):
        later.append(start(row_ref, row))
    count = out_pieces[0].shape[0]
    spot = pl.ds(pl.multiple_of(order[0] * count, count), count)
    later.append(start(out_pieces[0], out_weight.at[spot]))
    in_bias, out_bias, gain, offset = rows
    node_place = lax.broadcasted_iota(jnp.int32, (to_node.shape[0], lanes), 0)
    for row in range(edge_count // lanes):
        to_node[:, row * lanes : (row + 1) * lanes] = jnp.where(
            node_place == receiver_ref[row : row + 1], 1.0, 0.0
        ).astype(bf16)
    place_halo(halo, part_count, near_cap, halved, got_refs)
    for which in (1, 0, 2):
        for piece, owner in zip(in_pieces[1:], order[1:]):
            place_rows(in_weight, which * width, piece[which], owner)
    for piece, owner in zip(out_pieces[1:], order[1:]):
        place_rows(out_weight, 0, piece[...], owner)
    for copy in first:
        copy.wait()
    in_weight[3 * width :] = jnp.dot(
        halo[...], in_weight[width : 2 * width], preferred_element_type=f32
    ).astype(bf16)
    for copy in later:
        copy.wait()

    def in_dot(at):
        preact[at][...] = jnp.dot(
            known[at][...], in_weight[...], preferred_element_type=f32
        )

    def activate(at):
        for start_row in range(0, block, chunk_rows):
            here = slice(start_row, start_row + chunk_rows)
            hidden[at][here] = silu(preact[at][here] + in_bias[...]).astype(bf16)

    def out_dot(at):
        output[at][...] = jnp.dot(
            hidden[at][...], out_weight[...], preferred_element_type=f32
        )

    def normalise(at):
        for start_row in range(0, block, chunk_rows):
            here = slice(start_row, start_row + chunk_rows)
            there = slice(at * block + start_row, at * block + start_row + chunk_rows)
            normed = layer_norm(output[at][here] + out_bias[...], gain[...], offset[...])
            edges = known[at][here, :width].astype(f32)
            new_ref[there] = (edges + normed).astype(bf16)
        spot = pl.ds(at * block, block)
        return start(new_ref.at[spot], new_hbm.at[spot])

    def sum_dot(at):
        spot = slice(at * block, (at + 1) * block)
        part = jnp.dot(to_node[:, spot], new_ref[spot], preferred_element_type=f32)
        if at > 0:
            part += total[...]
        if at + 1 < blocks:
            total[...] = part
        else:
            sum_ref[...] = part.astype(bf16)

    out_copies = []
    in_dot(0)
    for at in range(blocks):
        if at + 1 < blocks:
            in_dot(at + 1)
        activate(at)
        out_dot(at)
        if at > 0:
            sum_dot(at - 1)
        out_copies.append(normalise(at))
    sum_dot(blocks - 1)
    for copy in out_copies:
        copy.wait()


def node_kernel(pieces_count, *refs):
    latent_ref, own_ref, other_ref = refs[:3]
    pieces = refs[3 : 3 + pieces_count]
    in_bias, out_bias, gain, offset, new_ref, weights = refs[3 + pieces_count :]
    width = latent_ref.shape[1]
    for piece, owner in zip(pieces, owners()):
        for which in range(piece.shape[0]):
            place_rows(weights, which * width, piece[which], owner)
    latent = latent_ref[...]
    summed = (own_ref[...].astype(f32) + other_ref[...].astype(f32)).astype(bf16)
    preact = jnp.dot(
        jnp.concatenate([latent, summed], axis=1),
        weights[: 2 * width],
        preferred_element_type=f32,
    )
    hidden = silu(preact + in_bias[...]).astype(bf16)
    output = jnp.dot(hidden, weights[2 * width :], preferred_element_type=f32) + out_bias[...]
    new_ref[...] = (
        latent.astype(f32) + layer_norm(output, gain[...], offset[...])
    ).astype(bf16)


def shards(
    node_latent,
    edge_latent,
    edge_source,
    receivers,
    near_rows,
    far_rows,
    edge_in_weight,
    edge_out_weight,
    node_in_weight,
    node_out_weight,
    edge_in_bias,
    edge_out_bias,
    edge_gain,
    edge_offset,
    node_in_bias,
    node_out_bias,
    node_gain,
    node_offset,
):
    node_count, width = node_latent.shape
    edge_count = edge_latent.shape[0]
    near_cap, far_cap = near_rows.shape[2], far_rows.shape[2]
    part_count = far_rows.shape[1]
    block = edge_count // 2
    steps = edge_count // block

    far_edge = [from_feats(edge_in_weight), from_feats(edge_out_weight)]
    near_edge = [from_subs([edge_in_weight]), from_subs([edge_out_weight])]

    subs = lax.axis_size("sub")
    halved = part_count <= few_parts and far_cap == subs and near_cap % (tile_rows * subs) == 0
    exchange = exchange_halves if halved else exchange_all
    got = exchange(node_latent, near_rows, far_rows, part_count)
    halo_space = len(near_offsets) * near_cap + part_count * far_cap
    halo_space = -(-halo_space // lanes) * lanes

    source_rows = in_hbm(edge_source.reshape(-1, lanes))
    receiver_rows = in_hbm(receivers.reshape(-1, lanes))

    pack_shape = (node_in_weight.shape[0] + 1,) + node_out_weight.shape
    near_edge[1], latent_after = lax.optimization_barrier((near_edge[1], node_latent))
    known_width = 3 * width + halo_space
    *known, node_weight = pl.pallas_call(
        functools.partial(gather_kernel, near_cap, far_cap, halved),
        out_shape=[pltpu.VMEM((block, known_width), bf16)] * steps
        + [pltpu.HBM(pack_shape, bf16)],
        in_specs=[vmem] * 5 + [hbm],
        out_specs=[vmem] * (steps + 1),
        scratch_shapes=[pltpu.SemaphoreType.DMA((steps,))],
        compiler_params=pltpu.CompilerParams(vmem_limit_bytes=grant),
        cost_estimate=pl.CostEstimate(flops=0, bytes_accessed=0, transcendentals=0),
        name="gather_latents",
    )(
        source_rows,
        receiver_rows,
        in_hbm(latent_after),
        in_hbm(node_in_weight),
        in_hbm(node_out_weight),
        in_hbm(edge_latent),
    )

    far_edge, got, known, node_weight = lax.optimization_barrier(
        (far_edge, got, known, node_weight)
    )
    if halved:
        got = got + from_subs(got)
    edge_in, edge_out = [
        [weight] + near + far + from_subs(far)
        for weight, near, far in zip((edge_in_weight, edge_out_weight), near_edge, far_edge)
    ]
    far_node = from_feats(node_weight)
    node_pieces = [node_weight] + from_subs([node_weight]) + far_node + from_subs(far_node)
    pieces_count = len(edge_in)

    rows = [value.reshape(1, -1) for value in (edge_in_bias, edge_out_bias, edge_gain, edge_offset)]
    edge_operands = [receiver_rows] + [in_vmem(array) for array in known + got]
    edge_specs = [vmem] * len(edge_operands)
    for pieces in (edge_in, edge_out):
        edge_operands += [in_hbm(pieces[0])] + [in_vmem(piece) for piece in pieces[1:]]
        edge_specs += [hbm] + [vmem] * (pieces_count - 1)
    edge_operands += [in_hbm(row) for row in rows]
    edge_specs += [hbm] * len(rows)
    copy_count = 3 + 4 + 1 + steps
    edge_new, partial_sums = pl.pallas_call(
        functools.partial(
            edge_kernel, pieces_count, len(got), part_count, near_cap, halved, steps
        ),
        out_shape=[
            pltpu.HBM((edge_count, width), bf16),
            jax.ShapeDtypeStruct((node_count, width), bf16),
        ],
        in_specs=edge_specs,
        out_specs=[hbm, vmem],
        scratch_shapes=[
            pltpu.VMEM((node_count, edge_count), bf16),
            pltpu.VMEM((known_width, width), bf16),
            pltpu.VMEM((width, width), bf16),
            pltpu.VMEM((halo_space, width), bf16),
            [pltpu.VMEM((1, width), f32)] * 4,
            [pltpu.VMEM((block, width), f32)] * steps,
            [pltpu.VMEM((block, width), bf16)] * steps,
            [pltpu.VMEM((block, width), f32)] * steps,
            pltpu.VMEM((edge_count, width), bf16),
            pltpu.VMEM((node_count, width), f32),
            pltpu.SemaphoreType.DMA((copy_count,)),
        ],
        compiler_params=pltpu.CompilerParams(vmem_limit_bytes=grant),
        cost_estimate=pl.CostEstimate(
            flops=2 * edge_count * width * (4 * width + node_count),
            bytes_accessed=8 * edge_count * width,
            transcendentals=edge_count * width,
        ),
        name="edge_update",
    )(*edge_operands)

    subs = lax.axis_size("sub")
    other_sums = lax.ppermute(partial_sums, "sub", [(at, (at + 1) % subs) for at in range(subs)])

    rows = [value.reshape(1, -1) for value in (node_in_bias, node_out_bias, node_gain, node_offset)]
    node_new = pl.pallas_call(
        functools.partial(node_kernel, pieces_count),
        out_shape=jax.ShapeDtypeStruct((node_count, width), bf16),
        in_specs=[vmem] * (3 + pieces_count + 4),
        out_specs=vmem,
        scratch_shapes=[
            pltpu.VMEM((3 * width, width), bf16),
        ],
        compiler_params=pltpu.CompilerParams(vmem_limit_bytes=grant),
        cost_estimate=pl.CostEstimate(
            flops=2 * node_count * width * 3 * width,
            bytes_accessed=10 * node_count * width,
            transcendentals=node_count * width,
        ),
        name="node_update",
    )(node_latent, partial_sums, other_sums, *node_pieces, *rows)
    return (edge_new, node_new)


def solution(mesh):
    return jax.shard_map(
        shards,
        mesh=mesh,
        in_specs=(
            P(("groups", "region", "feat"), None),
            P(("groups", "region", "feat", "sub"), None),
            P(("groups", "region", "feat", "sub")),
            P(("groups", "region", "feat", "sub")),
            P(("groups", "region", "feat"), None, None),
            P(("groups", "region", "feat"), None, None),
            P(None, ("feat", "sub"), None),
            P(("feat", "sub"), None),
            P(None, ("feat", "sub"), None),
            P(("feat", "sub"), None),
            P(),
            P(),
            P(),
            P(),
            P(),
            P(),
            P(),
            P(),
        ),
        out_specs=(
            P(("groups", "region", "feat", "sub"), None),
            P(("groups", "region", "feat"), None),
        ),
        check_vma=False,
    )
```

```python
import functools

import jax
import jax.numpy as jnp
from jax import lax
from jax.experimental import pallas as pl
from jax.experimental.pallas import tpu as pltpu
from jax.sharding import PartitionSpec as P

near_offsets = (1, 2, -1, -2)
tile_rows = 16
lanes = 128
few_parts = 8
grant = 32 << 20
chunk_rows = 64
bf16 = jnp.bfloat16
f32 = jnp.float32
vmem = pl.BlockSpec(memory_space=pltpu.VMEM)
hbm = pl.BlockSpec(memory_space=pltpu.HBM)


def in_hbm(array):
    return pltpu.with_memory_space_constraint(array, pltpu.HBM)


def in_vmem(array):
    return pltpu.with_memory_space_constraint(array, pltpu.VMEM)


def wrap(value, count):
    return jnp.where(value < 0, value + count, value)


def as_columns(rows):
    return jnp.concatenate(
        [
            jnp.transpose(jnp.broadcast_to(rows[at : at + 1], (lanes, rows.shape[1])))
            for at in range(rows.shape[0])
        ],
        axis=0,
    )


def one_hot(columns, width):
    place = lax.broadcasted_iota(jnp.int32, columns.shape, 1)
    return jnp.concatenate(
        [
            jnp.where(columns == place + start, 1.0, 0.0).astype(bf16)
            for start in range(0, width, lanes)
        ],
        axis=1,
    )


def silu(values):
    half = 0.5 * values
    return half + half * jnp.tanh(half)


def layer_norm(values, gain, offset):
    average = jnp.mean(values, axis=-1, keepdims=True)
    centred = values - average
    spread = jnp.mean(centred * centred, axis=-1, keepdims=True)
    return centred * lax.rsqrt(spread + 1e-05) * gain + offset


def my_part():
    return lax.axis_index("region") * lax.axis_size("feat") + lax.axis_index("feat")


def pick_kernel(part_count, near_cap, far_cap, far_ref, near_ref, latent_ref, out_ref, picked):
    me, sub, subs = my_part(), lax.axis_index("sub"), lax.axis_size("sub")
    half = near_cap // subs
    columns = [as_columns(near_ref[0])]
    tile_place = lax.broadcasted_iota(jnp.int32, (tile_rows, lanes), 0)
    far = as_columns(far_ref[0, 0:1])
    for slot in range(1, far_cap):
        far = jnp.where(sub == slot, as_columns(far_ref[0, slot : slot + 1]), far)
    for part in range(part_count):
        columns.append(jnp.where(tile_place == 0, far[part : part + 1], -1))
    hot = one_hot(jnp.concatenate(columns, axis=0), latent_ref.shape[0])
    picked[...] = jnp.dot(hot, latent_ref[...], preferred_element_type=f32).astype(bf16)
    for which, offset in enumerate(near_offsets):
        target = lax.rem(me + (offset + part_count), part_count)
        start = pl.multiple_of(which * near_cap + sub * half, half)
        out_ref[target, :half] = picked[pl.ds(start, half)]
    far_start = len(near_offsets) * near_cap
    for part in range(part_count):
        spot = far_start + part * tile_rows
        out_ref[part, half:] = picked[spot : spot + tile_rows][:1]


def exchange_halves(node_latent, near_rows, far_rows, part_count):
    near_cap, far_cap = near_rows.shape[2], far_rows.shape[2]
    subs = lax.axis_size("sub")
    width = node_latent.shape[1]
    block = (part_count, near_cap // subs + 1, width)
    picks = len(near_offsets) * near_cap + part_count * tile_rows
    blocks = pl.pallas_call(
        functools.partial(pick_kernel, part_count, near_cap, far_cap),
        out_shape=pltpu.HBM(block, bf16),
        in_specs=[vmem, vmem, vmem],
        out_specs=vmem,
        scratch_shapes=[pltpu.VMEM((picks, width), bf16)],
        compiler_params=pltpu.CompilerParams(vmem_limit_bytes=grant),
        cost_estimate=pl.CostEstimate(flops=0, bytes_accessed=0, transcendentals=0),
        name="pick_halo",
    )(in_hbm(jnp.transpose(far_rows, (0, 2, 1))), in_hbm(near_rows), in_hbm(node_latent))
    own = lax.all_to_all(blocks, ("region", "feat"), split_axis=0, concat_axis=0, tiled=True)
    return [own]


def exchange_all(node_latent, near_rows, far_rows, part_count):
    near_send = jnp.take(node_latent, near_rows[0], axis=0, mode="clip")
    far_send = jnp.take(node_latent, far_rows[0], axis=0, mode="clip")
    got = []
    for which, offset in enumerate(near_offsets):
        pairs = [(part, (part + offset) % part_count) for part in range(part_count)]
        got.append(lax.ppermute(near_send[which], ("region", "feat"), pairs))
    far = lax.all_to_all(far_send, ("region", "feat"), split_axis=0, concat_axis=0, tiled=True)
    got.append(far.reshape(-1, far.shape[2]))
    return got


def gather_kernel(
    near_cap,
    far_cap,
    halved,
    source_ref,
    receiver_ref,
    latent_ref,
    node_in_ref,
    node_out_ref,
    edge_hbm,
    known,
    gathered_hbm,
    to_node_hbm,
    pack_ref,
    gathered,
    to_node,
    sems,
):
    node_count, width = latent_ref.shape
    first = known.shape[0]
    edge_count = first + gathered.shape[0]
    block = first // 2
    copies = []

    def start(source, target):
        copies.append(pltpu.make_async_copy(source, target, sems.at[len(copies)]))
        copies[-1].start()

    start(edge_hbm.at[pl.ds(0, first)], known.at[:, pl.ds(0, width)])
    count = node_in_ref.shape[0]
    pack_ref[:count] = node_in_ref[...]
    pack_ref[count] = node_out_ref[...]
    latent = latent_ref[...]

    def gather(at, target, rows, begin):
        here = slice(at * (block // lanes), (at + 1) * (block // lanes))
        source = source_ref[here]
        if halved:
            far = source - (node_count + len(near_offsets) * near_cap)
            slot = lax.rem(far, far_cap)
            turned = wrap(slot - lax.axis_index("sub"), far_cap)
            source = jnp.where(far >= 0, source - slot + turned, source)
        columns = as_columns(source)
        sent = one_hot(columns, node_count)
        target[rows, begin : begin + width] = jnp.dot(
            sent, latent, preferred_element_type=f32
        ).astype(bf16)
        received = one_hot(as_columns(receiver_ref[here]), node_count)
        target[rows, begin + width : begin + 2 * width] = jnp.dot(
            received, latent, preferred_element_type=f32
        ).astype(bf16)
        slots = target.shape[1] - begin - 2 * width
        target[rows, begin + 2 * width :] = one_hot(columns - node_count, slots)

    for at in range(first // block, edge_count // block):
        begin = at * block - first
        gather(at, gathered, slice(begin, begin + block), 0)
        rows = pl.ds(begin, block)
        start(gathered.at[rows], gathered_hbm.at[rows])
    node_place = lax.broadcasted_iota(jnp.int32, (to_node.shape[0], lanes), 0)
    for row in range(edge_count // lanes):
        to_node[:, row * lanes : (row + 1) * lanes] = jnp.where(
            node_place == receiver_ref[row : row + 1], 1.0, 0.0
        ).astype(bf16)
    start(to_node, to_node_hbm)
    for at in range(first // block):
        gather(at, known, slice(at * block, (at + 1) * block), width)
    for copy in copies:
        copy.wait()


def place_halo(halo, part_count, near_cap, halved, got):
    subs = lax.axis_size("sub")
    far_start = len(near_offsets) * near_cap
    used = far_start
    if halved:
        half = near_cap // subs
        for which, offset in enumerate(near_offsets):
            origin = lax.rem(my_part() + (part_count - offset), part_count)
            for turn in range(subs):
                owner = wrap(lax.axis_index("sub") - turn, subs)
                start = pl.multiple_of(which * near_cap + owner * half, half)
                halo[pl.ds(start, half)] = got[turn][origin, :half]
        far = [got[turn][part, half:] for part in range(part_count) for turn in range(subs)]
        used += len(far)
        halo[far_start:used] = jnp.concatenate(
            [row.astype(f32) for row in far], axis=0
        ).astype(bf16)
    else:
        for rows in got:
            start = used - far_start if rows is not got[-1] else far_start
            halo[start : start + rows.shape[0]] = rows[...]
            used += rows.shape[0]
        used -= far_start
    if used < halo.shape[0]:
        halo[used:] = jnp.zeros((halo.shape[0] - used, halo.shape[1]), bf16)


def place_rows(whole, start, piece, owner):
    rows = piece.shape[0]
    whole[pl.ds(pl.multiple_of(start + owner * rows, rows), rows), :] = piece


def owners():
    feat, feats = lax.axis_index("feat"), lax.axis_size("feat")
    sub, subs = lax.axis_index("sub"), lax.axis_size("sub")
    own = [(0, turn) for turn in range(subs)]
    rest = [(shift, turn) for turn in range(subs) for shift in range(1, feats)]
    return [
        wrap(feat - shift, feats) * subs + wrap(sub - turn, subs) for shift, turn in own + rest
    ]


def from_feats(weight):
    feats = lax.axis_size("feat")
    return [
        lax.ppermute(weight, "feat", [(at, (at + shift) % feats) for at in range(feats)])
        for shift in range(1, feats)
    ]


def from_subs(pieces):
    subs = lax.axis_size("sub")
    return [
        lax.ppermute(piece, "sub", [(at, (at + turn) % subs) for at in range(subs)])
        for turn in range(1, subs)
        for piece in pieces
    ]


def edge_kernel(pieces_count, got_count, part_count, near_cap, halved, block, *refs):
    edge_hbm, gathered_hbm, to_node_hbm, known_first = refs[:4]
    got_refs = refs[4 : 4 + got_count]
    refs = refs[4 + got_count :]
    in_pieces, out_pieces = refs[:pieces_count], refs[pieces_count : 2 * pieces_count]
    row_refs = refs[2 * pieces_count : 2 * pieces_count + 4]
    new_hbm, sum_ref = refs[2 * pieces_count + 4 : 2 * pieces_count + 6]
    known_rest, to_node, in_weight, out_weight, halo, rows, preact, hidden, output, new_ref, total, sems = (
        refs[2 * pieces_count + 6 :]
    )
    edge_count, width = new_hbm.shape
    blocks = edge_count // block
    taken = []

    def start(source, target):
        copy = pltpu.make_async_copy(source, target, sems.at[len(taken)])
        copy.start()
        taken.append(copy)
        return copy

    order = owners()
    first, later = [], []
    for which in (1, 0, 2):
        count = in_pieces[0].shape[1]
        spot = pl.ds(pl.multiple_of(which * width + order[0] * count, count), count)
        target = first if which == 1 else later
        target.append(start(in_pieces[0].at[which], in_weight.at[spot]))
    for row_ref, row in zip(row_refs, rows):
        later.append(start(row_ref, row))
    count = out_pieces[0].shape[0]
    spot = pl.ds(pl.multiple_of(order[0] * count, count), count)
    later.append(start(out_pieces[0], out_weight.at[spot]))
    in_bias, out_bias, gain, offset = rows
    rest = edge_count - block
    known_copies = [
        start(edge_hbm.at[pl.ds(block, rest)], known_rest.at[:, pl.ds(0, width)]),
        start(gathered_hbm, known_rest.at[:, pl.ds(width, known_rest.shape[1] - width)]),
        start(to_node_hbm, to_node),
    ]

    def known(at):
        return known_first if at == 0 else known_rest.at[pl.ds((at - 1) * block, block)]

    place_halo(halo, part_count, near_cap, halved, got_refs)
    for which in (1, 0, 2):
        for piece, owner in zip(in_pieces[1:], order[1:]):
            place_rows(in_weight, which * width, piece[which], owner)
    for piece, owner in zip(out_pieces[1:], order[1:]):
        place_rows(out_weight, 0, piece[...], owner)
    for copy in first:
        copy.wait()
    in_weight[3 * width :] = jnp.dot(
        halo[...], in_weight[width : 2 * width], preferred_element_type=f32
    ).astype(bf16)
    for copy in later:
        copy.wait()

    def in_dot(at):
        if at == 1:
            for copy in known_copies:
                copy.wait()
        preact[at][...] = jnp.dot(
            known(at)[...], in_weight[...], preferred_element_type=f32
        )

    def activate(at):
        for start_row in range(0, block, chunk_rows):
            here = slice(start_row, start_row + chunk_rows)
            hidden[at][here] = silu(preact[at][here] + in_bias[...]).astype(bf16)

    def out_dot(at):
        output[at][...] = jnp.dot(
            hidden[at][...], out_weight[...], preferred_element_type=f32
        )

    def normalise(at):
        for start_row in range(0, block, chunk_rows):
            here = slice(start_row, start_row + chunk_rows)
            there = slice(at * block + start_row, at * block + start_row + chunk_rows)
            normed = layer_norm(output[at][here] + out_bias[...], gain[...], offset[...])
            edges = known(at)[here, :width].astype(f32)
            new_ref[there] = (edges + normed).astype(bf16)
        spot = pl.ds(at * block, block)
        return start(new_ref.at[spot], new_hbm.at[spot])

    def sum_dot(at):
        spot = slice(at * block, (at + 1) * block)
        part = jnp.dot(to_node[:, spot], new_ref[spot], preferred_element_type=f32)
        if at > 0:
            part += total[...]
        if at + 1 < blocks:
            total[...] = part
        else:
            sum_ref[...] = part.astype(bf16)

    out_copies = []
    in_dot(0)
    for at in range(blocks):
        if at + 1 < blocks:
            in_dot(at + 1)
        activate(at)
        out_dot(at)
        if at > 0:
            sum_dot(at - 1)
        out_copies.append(normalise(at))
    sum_dot(blocks - 1)
    for copy in out_copies:
        copy.wait()


def node_kernel(pieces_count, *refs):
    latent_ref, own_ref, other_ref = refs[:3]
    pieces = refs[3 : 3 + pieces_count]
    in_bias, out_bias, gain, offset, new_ref, weights = refs[3 + pieces_count :]
    width = latent_ref.shape[1]
    for piece, owner in zip(pieces, owners()):
        for which in range(piece.shape[0]):
            place_rows(weights, which * width, piece[which], owner)
    latent = latent_ref[...]
    summed = (own_ref[...].astype(f32) + other_ref[...].astype(f32)).astype(bf16)
    preact = jnp.dot(
        jnp.concatenate([latent, summed], axis=1),
        weights[: 2 * width],
        preferred_element_type=f32,
    )
    hidden = silu(preact + in_bias[...]).astype(bf16)
    output = jnp.dot(hidden, weights[2 * width :], preferred_element_type=f32) + out_bias[...]
    new_ref[...] = (
        latent.astype(f32) + layer_norm(output, gain[...], offset[...])
    ).astype(bf16)


def shards(
    node_latent,
    edge_latent,
    edge_source,
    receivers,
    near_rows,
    far_rows,
    edge_in_weight,
    edge_out_weight,
    node_in_weight,
    node_out_weight,
    edge_in_bias,
    edge_out_bias,
    edge_gain,
    edge_offset,
    node_in_bias,
    node_out_bias,
    node_gain,
    node_offset,
):
    node_count, width = node_latent.shape
    edge_count = edge_latent.shape[0]
    near_cap, far_cap = near_rows.shape[2], far_rows.shape[2]
    part_count = far_rows.shape[1]
    block = edge_count // 2
    steps = edge_count // block

    far_edge = [from_feats(edge_in_weight), from_feats(edge_out_weight)]
    near_edge = [from_subs([edge_in_weight]), from_subs([edge_out_weight])]

    subs = lax.axis_size("sub")
    halved = part_count <= few_parts and far_cap == subs and near_cap % (tile_rows * subs) == 0
    exchange = exchange_halves if halved else exchange_all
    got = exchange(node_latent, near_rows, far_rows, part_count)
    halo_space = len(near_offsets) * near_cap + part_count * far_cap
    halo_space = -(-halo_space // lanes) * lanes

    source_rows = in_hbm(edge_source.reshape(-1, lanes))
    receiver_rows = in_hbm(receivers.reshape(-1, lanes))

    pack_shape = (node_in_weight.shape[0] + 1,) + node_out_weight.shape
    near_edge[1], latent_after = lax.optimization_barrier((near_edge[1], node_latent))
    gathered_width = 2 * width + halo_space
    known_width = width + gathered_width
    rest = edge_count - block
    known, gathered, to_node, node_weight = pl.pallas_call(
        functools.partial(gather_kernel, near_cap, far_cap, halved),
        out_shape=[
            pltpu.VMEM((block, known_width), bf16),
            pltpu.HBM((rest, gathered_width), bf16),
            pltpu.HBM((node_count, edge_count), bf16),
            pltpu.VMEM(pack_shape, bf16),
        ],
        in_specs=[vmem] * 5 + [hbm],
        out_specs=[vmem, hbm, hbm, vmem],
        scratch_shapes=[
            pltpu.VMEM((rest, gathered_width), bf16),
            pltpu.VMEM((node_count, edge_count), bf16),
            pltpu.SemaphoreType.DMA((2 + 2 * (steps - 1),)),
        ],
        compiler_params=pltpu.CompilerParams(vmem_limit_bytes=grant),
        cost_estimate=pl.CostEstimate(flops=0, bytes_accessed=0, transcendentals=0),
        name="gather_latents",
    )(
        source_rows,
        receiver_rows,
        in_hbm(latent_after),
        in_hbm(node_in_weight),
        in_hbm(node_out_weight),
        in_hbm(edge_latent),
    )

    far_edge, got, known, gathered, to_node, node_weight = lax.optimization_barrier(
        (far_edge, got, known, gathered, to_node, node_weight)
    )
    if halved:
        got = got + from_subs(got)
    edge_in, edge_out = [
        [weight] + near + far + from_subs(far)
        for weight, near, far in zip((edge_in_weight, edge_out_weight), near_edge, far_edge)
    ]
    far_node = from_feats(node_weight)
    node_pieces = [node_weight] + from_subs([node_weight]) + far_node + from_subs(far_node)
    pieces_count = len(edge_in)

    rows = [value.reshape(1, -1) for value in (edge_in_bias, edge_out_bias, edge_gain, edge_offset)]
    edge_operands = [in_hbm(edge_latent), in_hbm(gathered), in_hbm(to_node), in_vmem(known)]
    edge_operands += [in_vmem(blocks) for blocks in got]
    edge_specs = [hbm] * 3 + [vmem] * (1 + len(got))
    for pieces in (edge_in, edge_out):
        edge_operands += [in_hbm(pieces[0])] + [in_vmem(piece) for piece in pieces[1:]]
        edge_specs += [hbm] + [vmem] * (pieces_count - 1)
    edge_operands += [in_hbm(row) for row in rows]
    edge_specs += [hbm] * len(rows)
    copy_count = 3 + 4 + 1 + 3 + steps
    edge_new, partial_sums = pl.pallas_call(
        functools.partial(
            edge_kernel, pieces_count, len(got), part_count, near_cap, halved, block
        ),
        out_shape=[
            pltpu.HBM((edge_count, width), bf16),
            jax.ShapeDtypeStruct((node_count, width), bf16),
        ],
        in_specs=edge_specs,
        out_specs=[hbm, vmem],
        scratch_shapes=[
            pltpu.VMEM((rest, known_width), bf16),
            pltpu.VMEM((node_count, edge_count), bf16),
            pltpu.VMEM((known_width, width), bf16),
            pltpu.VMEM((width, width), bf16),
            pltpu.VMEM((halo_space, width), bf16),
            [pltpu.VMEM((1, width), f32)] * 4,
            [pltpu.VMEM((block, width), f32)] * steps,
            [pltpu.VMEM((block, width), bf16)] * steps,
            [pltpu.VMEM((block, width), f32)] * steps,
            pltpu.VMEM((edge_count, width), bf16),
            pltpu.VMEM((node_count, width), f32),
            pltpu.SemaphoreType.DMA((copy_count,)),
        ],
        compiler_params=pltpu.CompilerParams(vmem_limit_bytes=grant),
        cost_estimate=pl.CostEstimate(
            flops=2 * edge_count * width * (4 * width + node_count),
            bytes_accessed=8 * edge_count * width,
            transcendentals=edge_count * width,
        ),
        name="edge_update",
    )(*edge_operands)

    subs = lax.axis_size("sub")
    other_sums = lax.ppermute(partial_sums, "sub", [(at, (at + 1) % subs) for at in range(subs)])

    rows = [value.reshape(1, -1) for value in (node_in_bias, node_out_bias, node_gain, node_offset)]
    node_new = pl.pallas_call(
        functools.partial(node_kernel, pieces_count),
        out_shape=jax.ShapeDtypeStruct((node_count, width), bf16),
        in_specs=[vmem] * (3 + pieces_count + 4),
        out_specs=vmem,
        scratch_shapes=[
            pltpu.VMEM((3 * width, width), bf16),
        ],
        compiler_params=pltpu.CompilerParams(vmem_limit_bytes=grant),
        cost_estimate=pl.CostEstimate(
            flops=2 * node_count * width * 3 * width,
            bytes_accessed=10 * node_count * width,
            transcendentals=node_count * width,
        ),
        name="node_update",
    )(node_latent, partial_sums, other_sums, *node_pieces, *rows)
    return (edge_new, node_new)


def solution(mesh):
    return jax.shard_map(
        shards,
        mesh=mesh,
        in_specs=(
            P(("groups", "region", "feat"), None),
            P(("groups", "region", "feat", "sub"), None),
            P(("groups", "region", "feat", "sub")),
            P(("groups", "region", "feat", "sub")),
            P(("groups", "region", "feat"), None, None),
            P(("groups", "region", "feat"), None, None),
            P(None, ("feat", "sub"), None),
            P(("feat", "sub"), None),
            P(None, ("feat", "sub"), None),
            P(("feat", "sub"), None),
            P(),
            P(),
            P(),
            P(),
            P(),
            P(),
            P(),
            P(),
        ),
        out_specs=(
            P(("groups", "region", "feat", "sub"), None),
            P(("groups", "region", "feat"), None),
        ),
        check_vma=False,
    )
```

```python
import functools

import jax
import jax.numpy as jnp
from jax import lax
from jax.experimental import pallas as pl
from jax.experimental.pallas import tpu as pltpu
from jax.sharding import PartitionSpec as P

near_offsets = (1, 2, -1, -2)
tile_rows = 16
lanes = 128
few_parts = 8
grant = 32 << 20
chunk_rows = 64
first_rows = 512
gather_rows = 512
bf16 = jnp.bfloat16
f32 = jnp.float32
vmem = pl.BlockSpec(memory_space=pltpu.VMEM)
hbm = pl.BlockSpec(memory_space=pltpu.HBM)


def in_hbm(array):
    return pltpu.with_memory_space_constraint(array, pltpu.HBM)


def in_vmem(array):
    return pltpu.with_memory_space_constraint(array, pltpu.VMEM)


def wrap(value, count):
    return jnp.where(value < 0, value + count, value)


def as_columns(rows):
    return jnp.concatenate(
        [
            jnp.transpose(jnp.broadcast_to(rows[at : at + 1], (lanes, rows.shape[1])))
            for at in range(rows.shape[0])
        ],
        axis=0,
    )


def one_hot(columns, width):
    place = lax.broadcasted_iota(jnp.int32, columns.shape, 1)
    return jnp.concatenate(
        [
            jnp.where(columns == place + start, 1.0, 0.0).astype(bf16)
            for start in range(0, width, lanes)
        ],
        axis=1,
    )


def silu(values):
    half = 0.5 * values
    return half + half * jnp.tanh(half)


def layer_norm(values, gain, offset):
    average = jnp.mean(values, axis=-1, keepdims=True)
    centred = values - average
    spread = jnp.mean(centred * centred, axis=-1, keepdims=True)
    return centred * lax.rsqrt(spread + 1e-05) * gain + offset


def my_part():
    return lax.axis_index("region") * lax.axis_size("feat") + lax.axis_index("feat")


def pick_kernel(part_count, near_cap, far_cap, far_ref, near_ref, latent_ref, out_ref, picked):
    me, sub, subs = my_part(), lax.axis_index("sub"), lax.axis_size("sub")
    half = near_cap // subs
    columns = [as_columns(near_ref[0])]
    tile_place = lax.broadcasted_iota(jnp.int32, (tile_rows, lanes), 0)
    far = as_columns(far_ref[0, 0:1])
    for slot in range(1, far_cap):
        far = jnp.where(sub == slot, as_columns(far_ref[0, slot : slot + 1]), far)
    for part in range(part_count):
        columns.append(jnp.where(tile_place == 0, far[part : part + 1], -1))
    hot = one_hot(jnp.concatenate(columns, axis=0), latent_ref.shape[0])
    picked[...] = jnp.dot(hot, latent_ref[...], preferred_element_type=f32).astype(bf16)
    for which, offset in enumerate(near_offsets):
        target = lax.rem(me + (offset + part_count), part_count)
        start = pl.multiple_of(which * near_cap + sub * half, half)
        out_ref[target, :half] = picked[pl.ds(start, half)]
    far_start = len(near_offsets) * near_cap
    for part in range(part_count):
        spot = far_start + part * tile_rows
        out_ref[part, half:] = picked[spot : spot + tile_rows][:1]


def exchange_halves(node_latent, near_rows, far_rows, part_count):
    near_cap, far_cap = near_rows.shape[2], far_rows.shape[2]
    subs = lax.axis_size("sub")
    width = node_latent.shape[1]
    block = (part_count, near_cap // subs + 1, width)
    picks = len(near_offsets) * near_cap + part_count * tile_rows
    blocks = pl.pallas_call(
        functools.partial(pick_kernel, part_count, near_cap, far_cap),
        out_shape=pltpu.HBM(block, bf16),
        in_specs=[vmem, vmem, vmem],
        out_specs=vmem,
        scratch_shapes=[pltpu.VMEM((picks, width), bf16)],
        compiler_params=pltpu.CompilerParams(vmem_limit_bytes=grant),
        cost_estimate=pl.CostEstimate(flops=0, bytes_accessed=0, transcendentals=0),
        name="pick_halo",
    )(in_hbm(jnp.transpose(far_rows, (0, 2, 1))), in_hbm(near_rows), in_hbm(node_latent))
    own = lax.all_to_all(blocks, ("region", "feat"), split_axis=0, concat_axis=0, tiled=True)
    return [own]


def exchange_all(node_latent, near_rows, far_rows, part_count):
    near_send = jnp.take(node_latent, near_rows[0], axis=0, mode="clip")
    far_send = jnp.take(node_latent, far_rows[0], axis=0, mode="clip")
    got = []
    for which, offset in enumerate(near_offsets):
        pairs = [(part, (part + offset) % part_count) for part in range(part_count)]
        got.append(lax.ppermute(near_send[which], ("region", "feat"), pairs))
    far = lax.all_to_all(far_send, ("region", "feat"), split_axis=0, concat_axis=0, tiled=True)
    got.append(far.reshape(-1, far.shape[2]))
    return got


def gather_kernel(
    near_cap,
    far_cap,
    halved,
    source_ref,
    receiver_ref,
    latent_ref,
    node_in_ref,
    node_out_ref,
    edge_hbm,
    known,
    gathered_hbm,
    to_node,
    pack_ref,
    gathered,
    sems,
):
    node_count, width = latent_ref.shape
    first = known.shape[0]
    edge_count = first + gathered.shape[0]
    block = gather_rows
    copies = []

    def start(source, target):
        copies.append(pltpu.make_async_copy(source, target, sems.at[len(copies)]))
        copies[-1].start()

    start(edge_hbm.at[pl.ds(0, first)], known.at[:, pl.ds(0, width)])
    count = node_in_ref.shape[0]
    pack_ref[:count] = node_in_ref[...]
    pack_ref[count] = node_out_ref[...]
    latent = latent_ref[...]

    def gather(at, target, rows, begin):
        here = slice(at * (block // lanes), (at + 1) * (block // lanes))
        source = source_ref[here]
        if halved:
            far = source - (node_count + len(near_offsets) * near_cap)
            slot = lax.rem(far, far_cap)
            turned = wrap(slot - lax.axis_index("sub"), far_cap)
            source = jnp.where(far >= 0, source - slot + turned, source)
        columns = as_columns(source)
        sent = one_hot(columns, node_count)
        target[rows, begin : begin + width] = jnp.dot(
            sent, latent, preferred_element_type=f32
        ).astype(bf16)
        received = one_hot(as_columns(receiver_ref[here]), node_count)
        target[rows, begin + width : begin + 2 * width] = jnp.dot(
            received, latent, preferred_element_type=f32
        ).astype(bf16)
        slots = target.shape[1] - begin - 2 * width
        target[rows, begin + 2 * width :] = one_hot(columns - node_count, slots)

    for at in range(first // block, edge_count // block):
        begin = at * block - first
        gather(at, gathered, slice(begin, begin + block), 0)
        rows = pl.ds(begin, block)
        start(gathered.at[rows], gathered_hbm.at[rows])
    node_place = lax.broadcasted_iota(jnp.int32, (to_node.shape[0], lanes), 0)
    for row in range(edge_count // lanes):
        to_node[:, row * lanes : (row + 1) * lanes] = jnp.where(
            node_place == receiver_ref[row : row + 1], 1.0, 0.0
        ).astype(bf16)
    for at in range(first // block):
        gather(at, known, slice(at * block, (at + 1) * block), width)
    for copy in copies:
        copy.wait()


def place_halo(halo, part_count, near_cap, halved, got):
    subs = lax.axis_size("sub")
    far_start = len(near_offsets) * near_cap
    used = far_start
    if halved:
        half = near_cap // subs
        for which, offset in enumerate(near_offsets):
            origin = lax.rem(my_part() + (part_count - offset), part_count)
            for turn in range(subs):
                owner = wrap(lax.axis_index("sub") - turn, subs)
                start = pl.multiple_of(which * near_cap + owner * half, half)
                halo[pl.ds(start, half)] = got[turn][origin, :half]
        far = [got[turn][part, half:] for part in range(part_count) for turn in range(subs)]
        used += len(far)
        halo[far_start:used] = jnp.concatenate(
            [row.astype(f32) for row in far], axis=0
        ).astype(bf16)
    else:
        for rows in got:
            start = used - far_start if rows is not got[-1] else far_start
            halo[start : start + rows.shape[0]] = rows[...]
            used += rows.shape[0]
        used -= far_start
    if used < halo.shape[0]:
        halo[used:] = jnp.zeros((halo.shape[0] - used, halo.shape[1]), bf16)


def place_rows(whole, start, piece, owner):
    rows = piece.shape[0]
    whole[pl.ds(pl.multiple_of(start + owner * rows, rows), rows), :] = piece


def owners():
    feat, feats = lax.axis_index("feat"), lax.axis_size("feat")
    sub, subs = lax.axis_index("sub"), lax.axis_size("sub")
    own = [(0, turn) for turn in range(subs)]
    rest = [(shift, turn) for turn in range(subs) for shift in range(1, feats)]
    return [
        wrap(feat - shift, feats) * subs + wrap(sub - turn, subs) for shift, turn in own + rest
    ]


def from_feats(weight):
    feats = lax.axis_size("feat")
    return [
        lax.ppermute(weight, "feat", [(at, (at + shift) % feats) for at in range(feats)])
        for shift in range(1, feats)
    ]


def from_subs(pieces):
    subs = lax.axis_size("sub")
    return [
        lax.ppermute(piece, "sub", [(at, (at + turn) % subs) for at in range(subs)])
        for turn in range(1, subs)
        for piece in pieces
    ]


def edge_kernel(pieces_count, got_count, part_count, near_cap, halved, *refs):
    edge_hbm, gathered_hbm, to_node, known_first = refs[:4]
    got_refs = refs[4 : 4 + got_count]
    refs = refs[4 + got_count :]
    in_pieces, out_pieces = refs[:pieces_count], refs[pieces_count : 2 * pieces_count]
    row_refs = refs[2 * pieces_count : 2 * pieces_count + 4]
    new_hbm, sum_ref = refs[2 * pieces_count + 4 : 2 * pieces_count + 6]
    known_rest, in_weight, out_weight, halo, rows, preact, hidden, output, new_ref, total, sems = (
        refs[2 * pieces_count + 6 :]
    )
    edge_count, width = new_hbm.shape
    known = [known_first, known_rest]
    starts = [0, known_first.shape[0]]
    blocks = len(known)
    taken = []

    def start(source, target):
        copy = pltpu.make_async_copy(source, target, sems.at[len(taken)])
        copy.start()
        taken.append(copy)
        return copy

    order = owners()
    first, later = [], []
    for which in (1, 0, 2):
        count = in_pieces[0].shape[1]
        spot = pl.ds(pl.multiple_of(which * width + order[0] * count, count), count)
        target = first if which == 1 else later
        target.append(start(in_pieces[0].at[which], in_weight.at[spot]))
    for row_ref, row in zip(row_refs, rows):
        later.append(start(row_ref, row))
    count = out_pieces[0].shape[0]
    spot = pl.ds(pl.multiple_of(order[0] * count, count), count)
    later.append(start(out_pieces[0], out_weight.at[spot]))
    in_bias, out_bias, gain, offset = rows
    known_copies = [
        start(edge_hbm.at[pl.ds(starts[1], known_rest.shape[0])], known_rest.at[:, pl.ds(0, width)]),
        start(gathered_hbm, known_rest.at[:, pl.ds(width, known_rest.shape[1] - width)]),
    ]

    place_halo(halo, part_count, near_cap, halved, got_refs)
    for which in (1, 0, 2):
        for piece, owner in zip(in_pieces[1:], order[1:]):
            place_rows(in_weight, which * width, piece[which], owner)
    for piece, owner in zip(out_pieces[1:], order[1:]):
        place_rows(out_weight, 0, piece[...], owner)
    for copy in first:
        copy.wait()
    in_weight[3 * width :] = jnp.dot(
        halo[...], in_weight[width : 2 * width], preferred_element_type=f32
    ).astype(bf16)
    for copy in later:
        copy.wait()

    def in_dot(at):
        if at == 1:
            for copy in known_copies:
                copy.wait()
        preact[at][...] = jnp.dot(
            known[at][...], in_weight[...], preferred_element_type=f32
        )

    def activate(at):
        for start_row in range(0, known[at].shape[0], chunk_rows):
            here = slice(start_row, start_row + chunk_rows)
            hidden[at][here] = silu(preact[at][here] + in_bias[...]).astype(bf16)

    def out_dot(at):
        output[at][...] = jnp.dot(
            hidden[at][...], out_weight[...], preferred_element_type=f32
        )

    def normalise(at):
        for start_row in range(0, known[at].shape[0], chunk_rows):
            here = slice(start_row, start_row + chunk_rows)
            there = slice(starts[at] + start_row, starts[at] + start_row + chunk_rows)
            normed = layer_norm(output[at][here] + out_bias[...], gain[...], offset[...])
            edges = known[at][here, :width].astype(f32)
            new_ref[there] = (edges + normed).astype(bf16)
        spot = pl.ds(starts[at], known[at].shape[0])
        return start(new_ref.at[spot], new_hbm.at[spot])

    def sum_dot(at):
        spot = slice(starts[at], starts[at] + known[at].shape[0])
        part = jnp.dot(to_node[:, spot], new_ref[spot], preferred_element_type=f32)
        if at > 0:
            part += total[...]
        if at + 1 < blocks:
            total[...] = part
        else:
            sum_ref[...] = part.astype(bf16)

    out_copies = []
    in_dot(0)
    for at in range(blocks):
        if at + 1 < blocks:
            in_dot(at + 1)
        activate(at)
        out_dot(at)
        if at > 0:
            sum_dot(at - 1)
        out_copies.append(normalise(at))
    sum_dot(blocks - 1)
    for copy in out_copies:
        copy.wait()


def node_kernel(pieces_count, *refs):
    latent_ref, own_ref, other_ref = refs[:3]
    pieces = refs[3 : 3 + pieces_count]
    in_bias, out_bias, gain, offset, new_ref, weights = refs[3 + pieces_count :]
    width = latent_ref.shape[1]
    for piece, owner in zip(pieces, owners()):
        for which in range(piece.shape[0]):
            place_rows(weights, which * width, piece[which], owner)
    latent = latent_ref[...]
    summed = (own_ref[...].astype(f32) + other_ref[...].astype(f32)).astype(bf16)
    preact = jnp.dot(
        jnp.concatenate([latent, summed], axis=1),
        weights[: 2 * width],
        preferred_element_type=f32,
    )
    hidden = silu(preact + in_bias[...]).astype(bf16)
    output = jnp.dot(hidden, weights[2 * width :], preferred_element_type=f32) + out_bias[...]
    new_ref[...] = (
        latent.astype(f32) + layer_norm(output, gain[...], offset[...])
    ).astype(bf16)


def shards(
    node_latent,
    edge_latent,
    edge_source,
    receivers,
    near_rows,
    far_rows,
    edge_in_weight,
    edge_out_weight,
    node_in_weight,
    node_out_weight,
    edge_in_bias,
    edge_out_bias,
    edge_gain,
    edge_offset,
    node_in_bias,
    node_out_bias,
    node_gain,
    node_offset,
):
    node_count, width = node_latent.shape
    edge_count = edge_latent.shape[0]
    near_cap, far_cap = near_rows.shape[2], far_rows.shape[2]
    part_count = far_rows.shape[1]

    far_edge = [from_feats(edge_in_weight), from_feats(edge_out_weight)]
    near_edge = [from_subs([edge_in_weight]), from_subs([edge_out_weight])]

    subs = lax.axis_size("sub")
    halved = part_count <= few_parts and far_cap == subs and near_cap % (tile_rows * subs) == 0
    exchange = exchange_halves if halved else exchange_all
    got = exchange(node_latent, near_rows, far_rows, part_count)
    halo_space = len(near_offsets) * near_cap + part_count * far_cap
    halo_space = -(-halo_space // lanes) * lanes

    source_rows = in_hbm(edge_source.reshape(-1, lanes))
    receiver_rows = in_hbm(receivers.reshape(-1, lanes))

    pack_shape = (node_in_weight.shape[0] + 1,) + node_out_weight.shape
    near_edge[1], latent_after = lax.optimization_barrier((near_edge[1], node_latent))
    gathered_width = 2 * width + halo_space
    known_width = width + gathered_width
    sizes = [first_rows, edge_count - first_rows]
    known, gathered, to_node, node_weight = pl.pallas_call(
        functools.partial(gather_kernel, near_cap, far_cap, halved),
        out_shape=[
            pltpu.VMEM((sizes[0], known_width), bf16),
            pltpu.HBM((sizes[1], gathered_width), bf16),
            pltpu.VMEM((node_count, edge_count), bf16),
            pltpu.HBM(pack_shape, bf16),
        ],
        in_specs=[vmem] * 5 + [hbm],
        out_specs=[vmem, hbm, vmem, vmem],
        scratch_shapes=[
            pltpu.VMEM((sizes[1], gathered_width), bf16),
            pltpu.SemaphoreType.DMA((1 + sizes[1] // gather_rows,)),
        ],
        compiler_params=pltpu.CompilerParams(vmem_limit_bytes=grant),
        cost_estimate=pl.CostEstimate(flops=0, bytes_accessed=0, transcendentals=0),
        name="gather_latents",
    )(
        source_rows,
        receiver_rows,
        in_hbm(latent_after),
        in_hbm(node_in_weight),
        in_hbm(node_out_weight),
        in_hbm(edge_latent),
    )

    far_edge, got, known, gathered, to_node, node_weight = lax.optimization_barrier(
        (far_edge, got, known, gathered, to_node, node_weight)
    )
    if halved:
        got = got + from_subs(got)
    edge_in, edge_out = [
        [weight] + near + far + from_subs(far)
        for weight, near, far in zip((edge_in_weight, edge_out_weight), near_edge, far_edge)
    ]
    far_node = from_feats(node_weight)
    node_pieces = [node_weight] + from_subs([node_weight]) + far_node + from_subs(far_node)
    pieces_count = len(edge_in)

    rows = [value.reshape(1, -1) for value in (edge_in_bias, edge_out_bias, edge_gain, edge_offset)]
    edge_operands = [in_hbm(edge_latent), in_hbm(gathered), in_vmem(to_node), in_vmem(known)]
    edge_operands += [in_vmem(blocks) for blocks in got]
    edge_specs = [hbm] * 2 + [vmem] * (2 + len(got))
    for pieces in (edge_in, edge_out):
        edge_operands += [in_hbm(pieces[0])] + [in_vmem(piece) for piece in pieces[1:]]
        edge_specs += [hbm] + [vmem] * (pieces_count - 1)
    edge_operands += [in_hbm(row) for row in rows]
    edge_specs += [hbm] * len(rows)
    copy_count = 3 + 4 + 1 + 2 + len(sizes)
    edge_new, partial_sums = pl.pallas_call(
        functools.partial(edge_kernel, pieces_count, len(got), part_count, near_cap, halved),
        out_shape=[
            pltpu.HBM((edge_count, width), bf16),
            jax.ShapeDtypeStruct((node_count, width), bf16),
        ],
        in_specs=edge_specs,
        out_specs=[hbm, vmem],
        scratch_shapes=[
            pltpu.VMEM((sizes[1], known_width), bf16),
            pltpu.VMEM((known_width, width), bf16),
            pltpu.VMEM((width, width), bf16),
            pltpu.VMEM((halo_space, width), bf16),
            [pltpu.VMEM((1, width), f32)] * 4,
            [pltpu.VMEM((size, width), f32) for size in sizes],
            [pltpu.VMEM((size, width), bf16) for size in sizes],
            [pltpu.VMEM((size, width), f32) for size in sizes],
            pltpu.VMEM((edge_count, width), bf16),
            pltpu.VMEM((node_count, width), f32),
            pltpu.SemaphoreType.DMA((copy_count,)),
        ],
        compiler_params=pltpu.CompilerParams(vmem_limit_bytes=grant),
        cost_estimate=pl.CostEstimate(
            flops=2 * edge_count * width * (4 * width + node_count),
            bytes_accessed=8 * edge_count * width,
            transcendentals=edge_count * width,
        ),
        name="edge_update",
    )(*edge_operands)

    subs = lax.axis_size("sub")
    other_sums = lax.ppermute(partial_sums, "sub", [(at, (at + 1) % subs) for at in range(subs)])

    rows = [value.reshape(1, -1) for value in (node_in_bias, node_out_bias, node_gain, node_offset)]
    node_new = pl.pallas_call(
        functools.partial(node_kernel, pieces_count),
        out_shape=jax.ShapeDtypeStruct((node_count, width), bf16),
        in_specs=[vmem] * (3 + pieces_count + 4),
        out_specs=vmem,
        scratch_shapes=[
            pltpu.VMEM((3 * width, width), bf16),
        ],
        compiler_params=pltpu.CompilerParams(vmem_limit_bytes=grant),
        cost_estimate=pl.CostEstimate(
            flops=2 * node_count * width * 3 * width,
            bytes_accessed=10 * node_count * width,
            transcendentals=node_count * width,
        ),
        name="node_update",
    )(node_latent, partial_sums, other_sums, *node_pieces, *rows)
    return (edge_new, node_new)


def solution(mesh):
    return jax.shard_map(
        shards,
        mesh=mesh,
        in_specs=(
            P(("groups", "region", "feat"), None),
            P(("groups", "region", "feat", "sub"), None),
            P(("groups", "region", "feat", "sub")),
            P(("groups", "region", "feat", "sub")),
            P(("groups", "region", "feat"), None, None),
            P(("groups", "region", "feat"), None, None),
            P(None, ("feat", "sub"), None),
            P(("feat", "sub"), None),
            P(None, ("feat", "sub"), None),
            P(("feat", "sub"), None),
            P(),
            P(),
            P(),
            P(),
            P(),
            P(),
            P(),
            P(),
        ),
        out_specs=(
            P(("groups", "region", "feat", "sub"), None),
            P(("groups", "region", "feat"), None),
        ),
        check_vma=False,
    )
```

```python
import functools

import jax
import jax.numpy as jnp
from jax import lax
from jax.experimental import pallas as pl
from jax.experimental.pallas import tpu as pltpu
from jax.sharding import PartitionSpec as P

near_offsets = (1, 2, -1, -2)
tile_rows = 16
lanes = 128
few_parts = 8
grant = 32 << 20
chunk_rows = 64
block_rows = 512
bf16 = jnp.bfloat16
f32 = jnp.float32
vmem = pl.BlockSpec(memory_space=pltpu.VMEM)
hbm = pl.BlockSpec(memory_space=pltpu.HBM)


def in_hbm(array):
    return pltpu.with_memory_space_constraint(array, pltpu.HBM)


def in_vmem(array):
    return pltpu.with_memory_space_constraint(array, pltpu.VMEM)


def wrap(value, count):
    return jnp.where(value < 0, value + count, value)


def as_columns(rows):
    return jnp.concatenate(
        [
            jnp.transpose(jnp.broadcast_to(rows[at : at + 1], (lanes, rows.shape[1])))
            for at in range(rows.shape[0])
        ],
        axis=0,
    )


def one_hot(columns, width):
    place = lax.broadcasted_iota(jnp.int32, columns.shape, 1)
    return jnp.concatenate(
        [
            jnp.where(columns == place + start, 1.0, 0.0).astype(bf16)
            for start in range(0, width, lanes)
        ],
        axis=1,
    )


def silu(values):
    half = 0.5 * values
    return half + half * jnp.tanh(half)


def layer_norm(values, gain, offset):
    average = jnp.mean(values, axis=-1, keepdims=True)
    centred = values - average
    spread = jnp.mean(centred * centred, axis=-1, keepdims=True)
    return centred * lax.rsqrt(spread + 1e-05) * gain + offset


def my_part():
    return lax.axis_index("region") * lax.axis_size("feat") + lax.axis_index("feat")


def pick_kernel(part_count, near_cap, far_cap, far_ref, near_ref, latent_ref, out_ref, picked):
    me, sub, subs = my_part(), lax.axis_index("sub"), lax.axis_size("sub")
    half = near_cap // subs
    columns = [as_columns(near_ref[0])]
    tile_place = lax.broadcasted_iota(jnp.int32, (tile_rows, lanes), 0)
    far = as_columns(far_ref[0, 0:1])
    for slot in range(1, far_cap):
        far = jnp.where(sub == slot, as_columns(far_ref[0, slot : slot + 1]), far)
    for part in range(part_count):
        columns.append(jnp.where(tile_place == 0, far[part : part + 1], -1))
    hot = one_hot(jnp.concatenate(columns, axis=0), latent_ref.shape[0])
    picked[...] = jnp.dot(hot, latent_ref[...], preferred_element_type=f32).astype(bf16)
    for which, offset in enumerate(near_offsets):
        target = lax.rem(me + (offset + part_count), part_count)
        start = pl.multiple_of(which * near_cap + sub * half, half)
        out_ref[target, :half] = picked[pl.ds(start, half)]
    far_start = len(near_offsets) * near_cap
    for part in range(part_count):
        spot = far_start + part * tile_rows
        out_ref[part, half:] = picked[spot : spot + tile_rows][:1]


def exchange_halves(node_latent, near_rows, far_rows, part_count):
    near_cap, far_cap = near_rows.shape[2], far_rows.shape[2]
    subs = lax.axis_size("sub")
    width = node_latent.shape[1]
    block = (part_count, near_cap // subs + 1, width)
    picks = len(near_offsets) * near_cap + part_count * tile_rows
    blocks = pl.pallas_call(
        functools.partial(pick_kernel, part_count, near_cap, far_cap),
        out_shape=pltpu.HBM(block, bf16),
        in_specs=[vmem, vmem, vmem],
        out_specs=vmem,
        scratch_shapes=[pltpu.VMEM((picks, width), bf16)],
        compiler_params=pltpu.CompilerParams(vmem_limit_bytes=grant),
        cost_estimate=pl.CostEstimate(flops=0, bytes_accessed=0, transcendentals=0),
        name="pick_halo",
    )(in_hbm(jnp.transpose(far_rows, (0, 2, 1))), in_hbm(near_rows), in_hbm(node_latent))
    own = lax.all_to_all(blocks, ("region", "feat"), split_axis=0, concat_axis=0, tiled=True)
    return [own]


def exchange_all(node_latent, near_rows, far_rows, part_count):
    near_send = jnp.take(node_latent, near_rows[0], axis=0, mode="clip")
    far_send = jnp.take(node_latent, far_rows[0], axis=0, mode="clip")
    got = []
    for which, offset in enumerate(near_offsets):
        pairs = [(part, (part + offset) % part_count) for part in range(part_count)]
        got.append(lax.ppermute(near_send[which], ("region", "feat"), pairs))
    far = lax.all_to_all(far_send, ("region", "feat"), split_axis=0, concat_axis=0, tiled=True)
    got.append(far.reshape(-1, far.shape[2]))
    return got


def gather_kernel(
    near_cap,
    far_cap,
    halved,
    source_ref,
    receiver_ref,
    latent_ref,
    node_in_ref,
    node_out_ref,
    edge_hbm,
    known,
    gathered_hbm,
    to_node,
    pack_ref,
    gathered,
    sems,
):
    node_count, width = latent_ref.shape
    first = known.shape[0]
    edge_count = first + gathered.shape[0]
    block = block_rows
    copies = []

    def start(source, target):
        copies.append(pltpu.make_async_copy(source, target, sems.at[len(copies)]))
        copies[-1].start()

    start(edge_hbm.at[pl.ds(0, first)], known.at[:, pl.ds(0, width)])
    count = node_in_ref.shape[0]
    pack_ref[:count] = node_in_ref[...]
    pack_ref[count] = node_out_ref[...]
    latent = latent_ref[...]

    def gather(at, target, rows, begin):
        here = slice(at * (block // lanes), (at + 1) * (block // lanes))
        source = source_ref[here]
        if halved:
            far = source - (node_count + len(near_offsets) * near_cap)
            slot = lax.rem(far, far_cap)
            turned = wrap(slot - lax.axis_index("sub"), far_cap)
            source = jnp.where(far >= 0, source - slot + turned, source)
        columns = as_columns(source)
        sent = one_hot(columns, node_count)
        target[rows, begin : begin + width] = jnp.dot(
            sent, latent, preferred_element_type=f32
        ).astype(bf16)
        received = one_hot(as_columns(receiver_ref[here]), node_count)
        target[rows, begin + width : begin + 2 * width] = jnp.dot(
            received, latent, preferred_element_type=f32
        ).astype(bf16)
        slots = target.shape[1] - begin - 2 * width
        target[rows, begin + 2 * width :] = one_hot(columns - node_count, slots)

    for at in range(first // block, edge_count // block):
        begin = at * block - first
        gather(at, gathered, slice(begin, begin + block), 0)
        rows = pl.ds(begin, block)
        start(gathered.at[rows], gathered_hbm.at[rows])
    node_place = lax.broadcasted_iota(jnp.int32, (to_node.shape[0], lanes), 0)
    for row in range(edge_count // lanes):
        to_node[:, row * lanes : (row + 1) * lanes] = jnp.where(
            node_place == receiver_ref[row : row + 1], 1.0, 0.0
        ).astype(bf16)
    for at in range(first // block):
        gather(at, known, slice(at * block, (at + 1) * block), width)
    for copy in copies:
        copy.wait()


def place_halo(halo, part_count, near_cap, halved, got):
    subs = lax.axis_size("sub")
    far_start = len(near_offsets) * near_cap
    used = far_start
    if halved:
        half = near_cap // subs
        for which, offset in enumerate(near_offsets):
            origin = lax.rem(my_part() + (part_count - offset), part_count)
            for turn in range(subs):
                owner = wrap(lax.axis_index("sub") - turn, subs)
                start = pl.multiple_of(which * near_cap + owner * half, half)
                halo[pl.ds(start, half)] = got[turn][origin, :half]
        far = [got[turn][part, half:] for part in range(part_count) for turn in range(subs)]
        used += len(far)
        halo[far_start:used] = jnp.concatenate(
            [row.astype(f32) for row in far], axis=0
        ).astype(bf16)
    else:
        for rows in got:
            start = used - far_start if rows is not got[-1] else far_start
            halo[start : start + rows.shape[0]] = rows[...]
            used += rows.shape[0]
        used -= far_start
    if used < halo.shape[0]:
        halo[used:] = jnp.zeros((halo.shape[0] - used, halo.shape[1]), bf16)


def place_rows(whole, start, piece, owner):
    rows = piece.shape[0]
    whole[pl.ds(pl.multiple_of(start + owner * rows, rows), rows), :] = piece


def owners():
    feat, feats = lax.axis_index("feat"), lax.axis_size("feat")
    sub, subs = lax.axis_index("sub"), lax.axis_size("sub")
    own = [(0, turn) for turn in range(subs)]
    rest = [(shift, turn) for turn in range(subs) for shift in range(1, feats)]
    return [
        wrap(feat - shift, feats) * subs + wrap(sub - turn, subs) for shift, turn in own + rest
    ]


def from_feats(weight):
    feats = lax.axis_size("feat")
    return [
        lax.ppermute(weight, "feat", [(at, (at + shift) % feats) for at in range(feats)])
        for shift in range(1, feats)
    ]


def from_subs(pieces):
    subs = lax.axis_size("sub")
    return [
        lax.ppermute(piece, "sub", [(at, (at + turn) % subs) for at in range(subs)])
        for turn in range(1, subs)
        for piece in pieces
    ]


def edge_kernel(pieces_count, got_count, part_count, near_cap, halved, *refs):
    edge_hbm, gathered_hbm, to_node, known_first = refs[:4]
    got_refs = refs[4 : 4 + got_count]
    refs = refs[4 + got_count :]
    in_pieces, out_pieces = refs[:pieces_count], refs[pieces_count : 2 * pieces_count]
    row_refs = refs[2 * pieces_count : 2 * pieces_count + 4]
    new_hbm, sum_ref = refs[2 * pieces_count + 4 : 2 * pieces_count + 6]
    known_rest, in_weight, out_weight, halo, rows, preact, hidden, output, new_ref, total, sems = (
        refs[2 * pieces_count + 6 :]
    )
    edge_count, width = new_hbm.shape
    block = known_first.shape[0]
    blocks = edge_count // block
    known = [known_first]
    taken = []

    def start(source, target):
        copy = pltpu.make_async_copy(source, target, sems.at[len(taken)])
        copy.start()
        taken.append(copy)
        return copy

    order = owners()
    first, later = [], []
    for which in (1, 0, 2):
        count = in_pieces[0].shape[1]
        spot = pl.ds(pl.multiple_of(which * width + order[0] * count, count), count)
        target = first if which == 1 else later
        target.append(start(in_pieces[0].at[which], in_weight.at[spot]))
    for row_ref, row in zip(row_refs, rows):
        later.append(start(row_ref, row))
    count = out_pieces[0].shape[0]
    spot = pl.ds(pl.multiple_of(order[0] * count, count), count)
    later.append(start(out_pieces[0], out_weight.at[spot]))
    in_bias, out_bias, gain, offset = rows
    known_copies = [[]]
    for at in range(1, blocks):
        spot, rows_here = pl.ds(at * block, block), pl.ds((at - 1) * block, block)
        view = known_rest.at[rows_here]
        known.append(view)
        known_copies.append(
            [
                start(edge_hbm.at[spot], view.at[:, pl.ds(0, width)]),
                start(
                    gathered_hbm.at[rows_here], view.at[:, pl.ds(width, view.shape[1] - width)]
                ),
            ]
        )

    place_halo(halo, part_count, near_cap, halved, got_refs)
    for which in (1, 0, 2):
        for piece, owner in zip(in_pieces[1:], order[1:]):
            place_rows(in_weight, which * width, piece[which], owner)
    for piece, owner in zip(out_pieces[1:], order[1:]):
        place_rows(out_weight, 0, piece[...], owner)
    for copy in first:
        copy.wait()
    in_weight[3 * width :] = jnp.dot(
        halo[...], in_weight[width : 2 * width], preferred_element_type=f32
    ).astype(bf16)
    for copy in later:
        copy.wait()

    def in_dot(at):
        for copy in known_copies[at]:
            copy.wait()
        preact[at][...] = jnp.dot(
            known[at][...], in_weight[...], preferred_element_type=f32
        )

    def activate(at):
        for start_row in range(0, block, chunk_rows):
            here = slice(start_row, start_row + chunk_rows)
            hidden[at][here] = silu(preact[at][here] + in_bias[...]).astype(bf16)

    def out_dot(at):
        output[at][...] = jnp.dot(
            hidden[at][...], out_weight[...], preferred_element_type=f32
        )

    def normalise(at):
        for start_row in range(0, block, chunk_rows):
            here = slice(start_row, start_row + chunk_rows)
            there = slice(at * block + start_row, at * block + start_row + chunk_rows)
            normed = layer_norm(output[at][here] + out_bias[...], gain[...], offset[...])
            edges = known[at][here, :width].astype(f32)
            new_ref[there] = (edges + normed).astype(bf16)
        spot = pl.ds(at * block, block)
        return start(new_ref.at[spot], new_hbm.at[spot])

    def sum_dot(at):
        spot = slice(at * block, (at + 1) * block)
        part = jnp.dot(to_node[:, spot], new_ref[spot], preferred_element_type=f32)
        if at > 0:
            part += total[...]
        if at + 1 < blocks:
            total[...] = part
        else:
            sum_ref[...] = part.astype(bf16)

    out_copies = []
    in_dot(0)
    for at in range(blocks):
        if at + 1 < blocks:
            in_dot(at + 1)
        activate(at)
        out_dot(at)
        if at > 0:
            sum_dot(at - 1)
        out_copies.append(normalise(at))
    sum_dot(blocks - 1)
    for copy in out_copies:
        copy.wait()


def node_kernel(pieces_count, *refs):
    latent_ref, own_ref, other_ref = refs[:3]
    pieces = refs[3 : 3 + pieces_count]
    in_bias, out_bias, gain, offset, new_ref, weights = refs[3 + pieces_count :]
    width = latent_ref.shape[1]
    for piece, owner in zip(pieces, owners()):
        for which in range(piece.shape[0]):
            place_rows(weights, which * width, piece[which], owner)
    latent = latent_ref[...]
    summed = (own_ref[...].astype(f32) + other_ref[...].astype(f32)).astype(bf16)
    preact = jnp.dot(
        jnp.concatenate([latent, summed], axis=1),
        weights[: 2 * width],
        preferred_element_type=f32,
    )
    hidden = silu(preact + in_bias[...]).astype(bf16)
    output = jnp.dot(hidden, weights[2 * width :], preferred_element_type=f32) + out_bias[...]
    new_ref[...] = (
        latent.astype(f32) + layer_norm(output, gain[...], offset[...])
    ).astype(bf16)


def shards(
    node_latent,
    edge_latent,
    edge_source,
    receivers,
    near_rows,
    far_rows,
    edge_in_weight,
    edge_out_weight,
    node_in_weight,
    node_out_weight,
    edge_in_bias,
    edge_out_bias,
    edge_gain,
    edge_offset,
    node_in_bias,
    node_out_bias,
    node_gain,
    node_offset,
):
    node_count, width = node_latent.shape
    edge_count = edge_latent.shape[0]
    near_cap, far_cap = near_rows.shape[2], far_rows.shape[2]
    part_count = far_rows.shape[1]

    far_edge = [from_feats(edge_in_weight), from_feats(edge_out_weight)]
    near_edge = [from_subs([edge_in_weight]), from_subs([edge_out_weight])]

    subs = lax.axis_size("sub")
    halved = part_count <= few_parts and far_cap == subs and near_cap % (tile_rows * subs) == 0
    exchange = exchange_halves if halved else exchange_all
    got = exchange(node_latent, near_rows, far_rows, part_count)
    halo_space = len(near_offsets) * near_cap + part_count * far_cap
    halo_space = -(-halo_space // lanes) * lanes

    source_rows = in_hbm(edge_source.reshape(-1, lanes))
    receiver_rows = in_hbm(receivers.reshape(-1, lanes))

    pack_shape = (node_in_weight.shape[0] + 1,) + node_out_weight.shape
    near_edge[1], latent_after = lax.optimization_barrier((near_edge[1], node_latent))
    gathered_width = 2 * width + halo_space
    known_width = width + gathered_width
    steps = edge_count // block_rows
    rest = edge_count - block_rows
    known, gathered, to_node, node_weight = pl.pallas_call(
        functools.partial(gather_kernel, near_cap, far_cap, halved),
        out_shape=[
            pltpu.VMEM((block_rows, known_width), bf16),
            pltpu.HBM((rest, gathered_width), bf16),
            pltpu.VMEM((node_count, edge_count), bf16),
            pltpu.HBM(pack_shape, bf16),
        ],
        in_specs=[vmem] * 5 + [hbm],
        out_specs=[vmem, hbm, vmem, vmem],
        scratch_shapes=[
            pltpu.VMEM((rest, gathered_width), bf16),
            pltpu.SemaphoreType.DMA((steps,)),
        ],
        compiler_params=pltpu.CompilerParams(vmem_limit_bytes=grant),
        cost_estimate=pl.CostEstimate(flops=0, bytes_accessed=0, transcendentals=0),
        name="gather_latents",
    )(
        source_rows,
        receiver_rows,
        in_hbm(latent_after),
        in_hbm(node_in_weight),
        in_hbm(node_out_weight),
        in_hbm(edge_latent),
    )

    far_edge, got, known, gathered, to_node, node_weight = lax.optimization_barrier(
        (far_edge, got, known, gathered, to_node, node_weight)
    )
    if halved:
        got = got + from_subs(got)
    edge_in, edge_out = [
        [weight] + near + far + from_subs(far)
        for weight, near, far in zip((edge_in_weight, edge_out_weight), near_edge, far_edge)
    ]
    far_node = from_feats(node_weight)
    node_pieces = [node_weight] + from_subs([node_weight]) + far_node + from_subs(far_node)
    pieces_count = len(edge_in)

    rows = [value.reshape(1, -1) for value in (edge_in_bias, edge_out_bias, edge_gain, edge_offset)]
    edge_operands = [in_hbm(edge_latent), in_hbm(gathered), in_vmem(to_node), in_vmem(known)]
    edge_operands += [in_vmem(blocks) for blocks in got]
    edge_specs = [hbm] * 2 + [vmem] * (2 + len(got))
    for pieces in (edge_in, edge_out):
        edge_operands += [in_hbm(pieces[0])] + [in_vmem(piece) for piece in pieces[1:]]
        edge_specs += [hbm] + [vmem] * (pieces_count - 1)
    edge_operands += [in_hbm(row) for row in rows]
    edge_specs += [hbm] * len(rows)
    copy_count = 3 + 4 + 1 + 3 * steps
    edge_new, partial_sums = pl.pallas_call(
        functools.partial(edge_kernel, pieces_count, len(got), part_count, near_cap, halved),
        out_shape=[
            pltpu.HBM((edge_count, width), bf16),
            jax.ShapeDtypeStruct((node_count, width), bf16),
        ],
        in_specs=edge_specs,
        out_specs=[hbm, vmem],
        scratch_shapes=[
            pltpu.VMEM((rest, known_width), bf16),
            pltpu.VMEM((known_width, width), bf16),
            pltpu.VMEM((width, width), bf16),
            pltpu.VMEM((halo_space, width), bf16),
            [pltpu.VMEM((1, width), f32)] * 4,
            [pltpu.VMEM((block_rows, width), f32) for _ in range(steps)],
            [pltpu.VMEM((block_rows, width), bf16) for _ in range(steps)],
            [pltpu.VMEM((block_rows, width), f32) for _ in range(steps)],
            pltpu.VMEM((edge_count, width), bf16),
            pltpu.VMEM((node_count, width), f32),
            pltpu.SemaphoreType.DMA((copy_count,)),
        ],
        compiler_params=pltpu.CompilerParams(vmem_limit_bytes=grant),
        cost_estimate=pl.CostEstimate(
            flops=2 * edge_count * width * (4 * width + node_count),
            bytes_accessed=8 * edge_count * width,
            transcendentals=edge_count * width,
        ),
        name="edge_update",
    )(*edge_operands)

    subs = lax.axis_size("sub")
    other_sums = lax.ppermute(partial_sums, "sub", [(at, (at + 1) % subs) for at in range(subs)])

    rows = [value.reshape(1, -1) for value in (node_in_bias, node_out_bias, node_gain, node_offset)]
    node_new = pl.pallas_call(
        functools.partial(node_kernel, pieces_count),
        out_shape=jax.ShapeDtypeStruct((node_count, width), bf16),
        in_specs=[vmem] * (3 + pieces_count + 4),
        out_specs=vmem,
        scratch_shapes=[
            pltpu.VMEM((3 * width, width), bf16),
        ],
        compiler_params=pltpu.CompilerParams(vmem_limit_bytes=grant),
        cost_estimate=pl.CostEstimate(
            flops=2 * node_count * width * 3 * width,
            bytes_accessed=10 * node_count * width,
            transcendentals=node_count * width,
        ),
        name="node_update",
    )(node_latent, partial_sums, other_sums, *node_pieces, *rows)
    return (edge_new, node_new)


def solution(mesh):
    return jax.shard_map(
        shards,
        mesh=mesh,
        in_specs=(
            P(("groups", "region", "feat"), None),
            P(("groups", "region", "feat", "sub"), None),
            P(("groups", "region", "feat", "sub")),
            P(("groups", "region", "feat", "sub")),
            P(("groups", "region", "feat"), None, None),
            P(("groups", "region", "feat"), None, None),
            P(None, ("feat", "sub"), None),
            P(("feat", "sub"), None),
            P(None, ("feat", "sub"), None),
            P(("feat", "sub"), None),
            P(),
            P(),
            P(),
            P(),
            P(),
            P(),
            P(),
            P(),
        ),
        out_specs=(
            P(("groups", "region", "feat", "sub"), None),
            P(("groups", "region", "feat"), None),
        ),
        check_vma=False,
    )
```

```python
import functools

import jax
import jax.numpy as jnp
from jax import lax
from jax.experimental import pallas as pl
from jax.experimental.pallas import tpu as pltpu
from jax.sharding import PartitionSpec as P

near_offsets = (1, 2, -1, -2)
tile_rows = 16
lanes = 128
few_parts = 8
grant = 32 << 20
chunk_rows = 32
gather_rows = 512
bf16 = jnp.bfloat16
f32 = jnp.float32
vmem = pl.BlockSpec(memory_space=pltpu.VMEM)
hbm = pl.BlockSpec(memory_space=pltpu.HBM)


def in_hbm(array):
    return pltpu.with_memory_space_constraint(array, pltpu.HBM)


def in_vmem(array):
    return pltpu.with_memory_space_constraint(array, pltpu.VMEM)


def wrap(value, count):
    return jnp.where(value < 0, value + count, value)


def as_columns(rows):
    return jnp.concatenate(
        [
            jnp.transpose(jnp.broadcast_to(rows[at : at + 1], (lanes, rows.shape[1])))
            for at in range(rows.shape[0])
        ],
        axis=0,
    )


def one_hot(columns, width):
    place = lax.broadcasted_iota(jnp.int32, columns.shape, 1)
    return jnp.concatenate(
        [
            jnp.where(columns == place + start, 1.0, 0.0).astype(bf16)
            for start in range(0, width, lanes)
        ],
        axis=1,
    )


def silu(values):
    half = 0.5 * values
    return half + half * jnp.tanh(half)


def layer_norm(values, gain, offset):
    average = jnp.mean(values, axis=-1, keepdims=True)
    centred = values - average
    spread = jnp.mean(centred * centred, axis=-1, keepdims=True)
    return centred * lax.rsqrt(spread + 1e-05) * gain + offset


def my_part():
    return lax.axis_index("region") * lax.axis_size("feat") + lax.axis_index("feat")


def pick_kernel(part_count, near_cap, far_cap, far_ref, near_ref, latent_ref, out_ref, picked):
    me, sub, subs = my_part(), lax.axis_index("sub"), lax.axis_size("sub")
    half = near_cap // subs
    columns = [as_columns(near_ref[0])]
    tile_place = lax.broadcasted_iota(jnp.int32, (tile_rows, lanes), 0)
    far = as_columns(far_ref[0, 0:1])
    for slot in range(1, far_cap):
        far = jnp.where(sub == slot, as_columns(far_ref[0, slot : slot + 1]), far)
    for part in range(part_count):
        columns.append(jnp.where(tile_place == 0, far[part : part + 1], -1))
    hot = one_hot(jnp.concatenate(columns, axis=0), latent_ref.shape[0])
    picked[...] = jnp.dot(hot, latent_ref[...], preferred_element_type=f32).astype(bf16)
    for which, offset in enumerate(near_offsets):
        target = lax.rem(me + (offset + part_count), part_count)
        start = pl.multiple_of(which * near_cap + sub * half, half)
        out_ref[target, :half] = picked[pl.ds(start, half)]
    far_start = len(near_offsets) * near_cap
    for part in range(part_count):
        spot = far_start + part * tile_rows
        out_ref[part, half:] = picked[spot : spot + tile_rows][:1]


def exchange_halves(node_latent, near_rows, far_rows, part_count):
    near_cap, far_cap = near_rows.shape[2], far_rows.shape[2]
    subs = lax.axis_size("sub")
    width = node_latent.shape[1]
    block = (part_count, near_cap // subs + 1, width)
    picks = len(near_offsets) * near_cap + part_count * tile_rows
    blocks = pl.pallas_call(
        functools.partial(pick_kernel, part_count, near_cap, far_cap),
        out_shape=pltpu.HBM(block, bf16),
        in_specs=[vmem, vmem, vmem],
        out_specs=vmem,
        scratch_shapes=[pltpu.VMEM((picks, width), bf16)],
        compiler_params=pltpu.CompilerParams(vmem_limit_bytes=grant),
        cost_estimate=pl.CostEstimate(flops=0, bytes_accessed=0, transcendentals=0),
        name="pick_halo",
    )(in_hbm(jnp.transpose(far_rows, (0, 2, 1))), in_hbm(near_rows), in_hbm(node_latent))
    own = lax.all_to_all(blocks, ("region", "feat"), split_axis=0, concat_axis=0, tiled=True)
    return [own]


def exchange_all(node_latent, near_rows, far_rows, part_count):
    near_send = jnp.take(node_latent, near_rows[0], axis=0, mode="clip")
    far_send = jnp.take(node_latent, far_rows[0], axis=0, mode="clip")
    got = []
    for which, offset in enumerate(near_offsets):
        pairs = [(part, (part + offset) % part_count) for part in range(part_count)]
        got.append(lax.ppermute(near_send[which], ("region", "feat"), pairs))
    far = lax.all_to_all(far_send, ("region", "feat"), split_axis=0, concat_axis=0, tiled=True)
    got.append(far.reshape(-1, far.shape[2]))
    return got


def gather_kernel(
    near_cap,
    far_cap,
    halved,
    source_ref,
    receiver_ref,
    latent_ref,
    node_in_ref,
    node_out_ref,
    gathered_hbm,
    to_node,
    pack_ref,
    gathered,
    sems,
):
    node_count, width = latent_ref.shape
    edge_count = gathered.shape[0]
    block = gather_rows
    copies = []

    def start(source, target):
        copies.append(pltpu.make_async_copy(source, target, sems.at[len(copies)]))
        copies[-1].start()

    count = node_in_ref.shape[0]
    pack_ref[:count] = node_in_ref[...]
    pack_ref[count] = node_out_ref[...]
    latent = latent_ref[...]

    def gather(at, target, rows, begin):
        here = slice(at * (block // lanes), (at + 1) * (block // lanes))
        source = source_ref[here]
        if halved:
            far = source - (node_count + len(near_offsets) * near_cap)
            slot = lax.rem(far, far_cap)
            turned = wrap(slot - lax.axis_index("sub"), far_cap)
            source = jnp.where(far >= 0, source - slot + turned, source)
        columns = as_columns(source)
        sent = one_hot(columns, node_count)
        target[rows, begin : begin + width] = jnp.dot(
            sent, latent, preferred_element_type=f32
        ).astype(bf16)
        received = one_hot(as_columns(receiver_ref[here]), node_count)
        target[rows, begin + width : begin + 2 * width] = jnp.dot(
            received, latent, preferred_element_type=f32
        ).astype(bf16)
        slots = target.shape[1] - begin - 2 * width
        target[rows, begin + 2 * width :] = one_hot(columns - node_count, slots)

    for at in range(edge_count // block):
        gather(at, gathered, slice(at * block, (at + 1) * block), 0)
        rows = pl.ds(at * block, block)
        start(gathered.at[rows], gathered_hbm.at[rows])
    node_place = lax.broadcasted_iota(jnp.int32, (to_node.shape[0], lanes), 0)
    for row in range(edge_count // lanes):
        to_node[:, row * lanes : (row + 1) * lanes] = jnp.where(
            node_place == receiver_ref[row : row + 1], 1.0, 0.0
        ).astype(bf16)
    for copy in copies:
        copy.wait()


def place_halo(halo, part_count, near_cap, halved, got):
    subs = lax.axis_size("sub")
    far_start = len(near_offsets) * near_cap
    used = far_start
    if halved:
        half = near_cap // subs
        for which, offset in enumerate(near_offsets):
            origin = lax.rem(my_part() + (part_count - offset), part_count)
            for turn in range(subs):
                owner = wrap(lax.axis_index("sub") - turn, subs)
                start = pl.multiple_of(which * near_cap + owner * half, half)
                halo[pl.ds(start, half)] = got[turn][origin, :half]
        far = [got[turn][part, half:] for part in range(part_count) for turn in range(subs)]
        used += len(far)
        halo[far_start:used] = jnp.concatenate(
            [row.astype(f32) for row in far], axis=0
        ).astype(bf16)
    else:
        for rows in got:
            start = used - far_start if rows is not got[-1] else far_start
            halo[start : start + rows.shape[0]] = rows[...]
            used += rows.shape[0]
        used -= far_start
    if used < halo.shape[0]:
        halo[used:] = jnp.zeros((halo.shape[0] - used, halo.shape[1]), bf16)


def place_rows(whole, start, piece, owner):
    rows = piece.shape[0]
    whole[pl.ds(pl.multiple_of(start + owner * rows, rows), rows), :] = piece


def owners():
    feat, feats = lax.axis_index("feat"), lax.axis_size("feat")
    sub, subs = lax.axis_index("sub"), lax.axis_size("sub")
    own = [(0, turn) for turn in range(subs)]
    rest = [(shift, turn) for turn in range(subs) for shift in range(1, feats)]
    return [
        wrap(feat - shift, feats) * subs + wrap(sub - turn, subs) for shift, turn in own + rest
    ]


def from_feats(weight):
    feats = lax.axis_size("feat")
    return [
        lax.ppermute(weight, "feat", [(at, (at + shift) % feats) for at in range(feats)])
        for shift in range(1, feats)
    ]


def from_subs(pieces):
    subs = lax.axis_size("sub")
    return [
        lax.ppermute(piece, "sub", [(at, (at + turn) % subs) for at in range(subs)])
        for turn in range(1, subs)
        for piece in pieces
    ]


def edge_kernel(pieces_count, got_count, part_count, near_cap, halved, *refs):
    edge_hbm, gathered_hbm, to_node = refs[:3]
    got_refs = refs[3 : 3 + got_count]
    refs = refs[3 + got_count :]
    in_pieces, out_pieces = refs[:pieces_count], refs[pieces_count : 2 * pieces_count]
    row_refs = refs[2 * pieces_count : 2 * pieces_count + 4]
    new_hbm, sum_ref = refs[2 * pieces_count + 4 : 2 * pieces_count + 6]
    known_rows, in_weight, out_weight, halo, rows, preact, hidden, output, new_ref, total, sems = (
        refs[2 * pieces_count + 6 :]
    )
    edge_count, width = new_hbm.shape
    blocks = len(preact)
    block = edge_count // blocks
    known = []
    taken = []

    def start(source, target):
        copy = pltpu.make_async_copy(source, target, sems.at[len(taken)])
        copy.start()
        taken.append(copy)
        return copy

    order = owners()
    first, later = [], []
    for which in (1, 0, 2):
        count = in_pieces[0].shape[1]
        spot = pl.ds(pl.multiple_of(which * width + order[0] * count, count), count)
        target = first if which == 1 else later
        target.append(start(in_pieces[0].at[which], in_weight.at[spot]))
    for row_ref, row in zip(row_refs, rows):
        later.append(start(row_ref, row))
    count = out_pieces[0].shape[0]
    spot = pl.ds(pl.multiple_of(order[0] * count, count), count)
    later.append(start(out_pieces[0], out_weight.at[spot]))
    in_bias, out_bias, gain, offset = rows
    known_copies = []
    for at in range(blocks):
        spot = pl.ds(at * block, block)
        view = known_rows.at[spot]
        known.append(view)
        known_copies.append(
            [
                start(edge_hbm.at[spot], view.at[:, pl.ds(0, width)]),
                start(
                    gathered_hbm.at[spot], view.at[:, pl.ds(width, view.shape[1] - width)]
                ),
            ]
        )

    place_halo(halo, part_count, near_cap, halved, got_refs)
    for which in (1, 0, 2):
        for piece, owner in zip(in_pieces[1:], order[1:]):
            place_rows(in_weight, which * width, piece[which], owner)
    for piece, owner in zip(out_pieces[1:], order[1:]):
        place_rows(out_weight, 0, piece[...], owner)
    for copy in first:
        copy.wait()
    in_weight[3 * width :] = jnp.dot(
        halo[...], in_weight[width : 2 * width], preferred_element_type=f32
    ).astype(bf16)
    for copy in later:
        copy.wait()

    def in_dot(at):
        for copy in known_copies[at]:
            copy.wait()
        preact[at][...] = jnp.dot(
            known[at][...], in_weight[...], preferred_element_type=f32
        )

    def activate(at):
        for start_row in range(0, block, chunk_rows):
            here = slice(start_row, start_row + chunk_rows)
            hidden[at][here] = silu(preact[at][here] + in_bias[...]).astype(bf16)

    def out_dot(at):
        output[at][...] = jnp.dot(
            hidden[at][...], out_weight[...], preferred_element_type=f32
        )

    def normalise(at):
        for start_row in range(0, block, chunk_rows):
            here = slice(start_row, start_row + chunk_rows)
            there = slice(at * block + start_row, at * block + start_row + chunk_rows)
            normed = layer_norm(output[at][here] + out_bias[...], gain[...], offset[...])
            edges = known[at][here, :width].astype(f32)
            new_ref[there] = (edges + normed).astype(bf16)
        spot = pl.ds(at * block, block)
        return start(new_ref.at[spot], new_hbm.at[spot])

    def sum_dot(at):
        spot = slice(at * block, (at + 1) * block)
        part = jnp.dot(to_node[:, spot], new_ref[spot], preferred_element_type=f32)
        if at > 0:
            part += total[...]
        if at + 1 < blocks:
            total[...] = part
        else:
            sum_ref[...] = part.astype(bf16)

    out_copies = []
    in_dot(0)
    for at in range(blocks):
        if at + 1 < blocks:
            in_dot(at + 1)
        activate(at)
        out_dot(at)
        if at > 0:
            sum_dot(at - 1)
        out_copies.append(normalise(at))
    sum_dot(blocks - 1)
    for copy in out_copies:
        copy.wait()


def node_kernel(pieces_count, *refs):
    latent_ref, own_ref, other_ref = refs[:3]
    pieces = refs[3 : 3 + pieces_count]
    in_bias, out_bias, gain, offset, new_ref, weights = refs[3 + pieces_count :]
    width = latent_ref.shape[1]
    for piece, owner in zip(pieces, owners()):
        for which in range(piece.shape[0]):
            place_rows(weights, which * width, piece[which], owner)
    latent = latent_ref[...]
    summed = (own_ref[...].astype(f32) + other_ref[...].astype(f32)).astype(bf16)
    preact = jnp.dot(
        jnp.concatenate([latent, summed], axis=1),
        weights[: 2 * width],
        preferred_element_type=f32,
    )
    hidden = silu(preact + in_bias[...]).astype(bf16)
    output = jnp.dot(hidden, weights[2 * width :], preferred_element_type=f32) + out_bias[...]
    new_ref[...] = (
        latent.astype(f32) + layer_norm(output, gain[...], offset[...])
    ).astype(bf16)


def shards(
    node_latent,
    edge_latent,
    edge_source,
    receivers,
    near_rows,
    far_rows,
    edge_in_weight,
    edge_out_weight,
    node_in_weight,
    node_out_weight,
    edge_in_bias,
    edge_out_bias,
    edge_gain,
    edge_offset,
    node_in_bias,
    node_out_bias,
    node_gain,
    node_offset,
):
    node_count, width = node_latent.shape
    edge_count = edge_latent.shape[0]
    near_cap, far_cap = near_rows.shape[2], far_rows.shape[2]
    part_count = far_rows.shape[1]

    far_edge = [from_feats(edge_in_weight), from_feats(edge_out_weight)]
    near_edge = [from_subs([edge_in_weight]), from_subs([edge_out_weight])]

    subs = lax.axis_size("sub")
    halved = part_count <= few_parts and far_cap == subs and near_cap % (tile_rows * subs) == 0
    exchange = exchange_halves if halved else exchange_all
    got = exchange(node_latent, near_rows, far_rows, part_count)
    halo_space = len(near_offsets) * near_cap + part_count * far_cap
    halo_space = -(-halo_space // lanes) * lanes

    source_rows = in_hbm(edge_source.reshape(-1, lanes))
    receiver_rows = in_hbm(receivers.reshape(-1, lanes))

    pack_shape = (node_in_weight.shape[0] + 1,) + node_out_weight.shape
    near_edge[1], latent_after = lax.optimization_barrier((near_edge[1], node_latent))
    gathered_width = 2 * width + halo_space
    known_width = width + gathered_width
    steps = 2
    block = edge_count // steps
    gathered, to_node, node_weight = pl.pallas_call(
        functools.partial(gather_kernel, near_cap, far_cap, halved),
        out_shape=[
            pltpu.HBM((edge_count, gathered_width), bf16),
            pltpu.VMEM((node_count, edge_count), bf16),
            pltpu.HBM(pack_shape, bf16),
        ],
        in_specs=[vmem] * 5,
        out_specs=[hbm, vmem, vmem],
        scratch_shapes=[
            pltpu.VMEM((edge_count, gathered_width), bf16),
            pltpu.SemaphoreType.DMA((edge_count // gather_rows,)),
        ],
        compiler_params=pltpu.CompilerParams(vmem_limit_bytes=grant),
        cost_estimate=pl.CostEstimate(flops=0, bytes_accessed=0, transcendentals=0),
        name="gather_latents",
    )(
        source_rows,
        receiver_rows,
        in_hbm(latent_after),
        in_hbm(node_in_weight),
        in_hbm(node_out_weight),
    )

    far_edge, got, gathered, to_node, node_weight = lax.optimization_barrier(
        (far_edge, got, gathered, to_node, node_weight)
    )
    if halved:
        got = got + from_subs(got)
    edge_in, edge_out = [
        [weight] + near + far + from_subs(far)
        for weight, near, far in zip((edge_in_weight, edge_out_weight), near_edge, far_edge)
    ]
    far_node = from_feats(node_weight)
    node_pieces = [node_weight] + from_subs([node_weight]) + far_node + from_subs(far_node)
    pieces_count = len(edge_in)

    rows = [value.reshape(1, -1) for value in (edge_in_bias, edge_out_bias, edge_gain, edge_offset)]
    edge_operands = [in_hbm(edge_latent), in_hbm(gathered), in_vmem(to_node)]
    edge_operands += [in_vmem(blocks) for blocks in got]
    edge_specs = [hbm] * 2 + [vmem] * (1 + len(got))
    for pieces in (edge_in, edge_out):
        edge_operands += [in_hbm(pieces[0])] + [in_vmem(piece) for piece in pieces[1:]]
        edge_specs += [hbm] + [vmem] * (pieces_count - 1)
    edge_operands += [in_hbm(row) for row in rows]
    edge_specs += [hbm] * len(rows)
    copy_count = 3 + 4 + 1 + 3 * steps
    edge_new, partial_sums = pl.pallas_call(
        functools.partial(edge_kernel, pieces_count, len(got), part_count, near_cap, halved),
        out_shape=[
            pltpu.HBM((edge_count, width), bf16),
            jax.ShapeDtypeStruct((node_count, width), bf16),
        ],
        in_specs=edge_specs,
        out_specs=[hbm, vmem],
        scratch_shapes=[
            pltpu.VMEM((edge_count, known_width), bf16),
            pltpu.VMEM((known_width, width), bf16),
            pltpu.VMEM((width, width), bf16),
            pltpu.VMEM((halo_space, width), bf16),
            [pltpu.VMEM((1, width), f32)] * 4,
            [pltpu.VMEM((block, width), f32) for _ in range(steps)],
            [pltpu.VMEM((block, width), bf16) for _ in range(steps)],
            [pltpu.VMEM((block, width), f32) for _ in range(steps)],
            pltpu.VMEM((edge_count, width), bf16),
            pltpu.VMEM((node_count, width), f32),
            pltpu.SemaphoreType.DMA((copy_count,)),
        ],
        compiler_params=pltpu.CompilerParams(vmem_limit_bytes=grant),
        cost_estimate=pl.CostEstimate(
            flops=2 * edge_count * width * (4 * width + node_count),
            bytes_accessed=8 * edge_count * width,
            transcendentals=edge_count * width,
        ),
        name="edge_update",
    )(*edge_operands)

    subs = lax.axis_size("sub")
    other_sums = lax.ppermute(partial_sums, "sub", [(at, (at + 1) % subs) for at in range(subs)])

    rows = [value.reshape(1, -1) for value in (node_in_bias, node_out_bias, node_gain, node_offset)]
    node_new = pl.pallas_call(
        functools.partial(node_kernel, pieces_count),
        out_shape=jax.ShapeDtypeStruct((node_count, width), bf16),
        in_specs=[vmem] * (3 + pieces_count + 4),
        out_specs=vmem,
        scratch_shapes=[
            pltpu.VMEM((3 * width, width), bf16),
        ],
        compiler_params=pltpu.CompilerParams(vmem_limit_bytes=grant),
        cost_estimate=pl.CostEstimate(
            flops=2 * node_count * width * 3 * width,
            bytes_accessed=10 * node_count * width,
            transcendentals=node_count * width,
        ),
        name="node_update",
    )(node_latent, partial_sums, other_sums, *node_pieces, *rows)
    return (edge_new, node_new)


def solution(mesh):
    return jax.shard_map(
        shards,
        mesh=mesh,
        in_specs=(
            P(("groups", "region", "feat"), None),
            P(("groups", "region", "feat", "sub"), None),
            P(("groups", "region", "feat", "sub")),
            P(("groups", "region", "feat", "sub")),
            P(("groups", "region", "feat"), None, None),
            P(("groups", "region", "feat"), None, None),
            P(None, ("feat", "sub"), None),
            P(("feat", "sub"), None),
            P(None, ("feat", "sub"), None),
            P(("feat", "sub"), None),
            P(),
            P(),
            P(),
            P(),
            P(),
            P(),
            P(),
            P(),
        ),
        out_specs=(
            P(("groups", "region", "feat", "sub"), None),
            P(("groups", "region", "feat"), None),
        ),
        check_vma=False,
    )
```

```python
import functools

import jax
import jax.numpy as jnp
from jax import lax
from jax.experimental import pallas as pl
from jax.experimental.pallas import tpu as pltpu
from jax.sharding import PartitionSpec as P

near_offsets = (1, 2, -1, -2)
tile_rows = 16
lanes = 128
few_parts = 8
grant = 32 << 20
chunk_rows = 32
gather_rows = 512
bf16 = jnp.bfloat16
f32 = jnp.float32
vmem = pl.BlockSpec(memory_space=pltpu.VMEM)
hbm = pl.BlockSpec(memory_space=pltpu.HBM)


def in_hbm(array):
    return pltpu.with_memory_space_constraint(array, pltpu.HBM)


def in_vmem(array):
    return pltpu.with_memory_space_constraint(array, pltpu.VMEM)


def wrap(value, count):
    return jnp.where(value < 0, value + count, value)


def as_columns(rows):
    return jnp.concatenate(
        [
            jnp.transpose(jnp.broadcast_to(rows[at : at + 1], (lanes, rows.shape[1])))
            for at in range(rows.shape[0])
        ],
        axis=0,
    )


def one_hot(columns, width):
    place = lax.broadcasted_iota(jnp.int32, columns.shape, 1)
    return jnp.concatenate(
        [
            jnp.where(columns == place + start, 1.0, 0.0).astype(bf16)
            for start in range(0, width, lanes)
        ],
        axis=1,
    )


def silu(values):
    half = 0.5 * values
    return half + half * jnp.tanh(half)


def layer_norm(values, gain, offset):
    average = jnp.mean(values, axis=-1, keepdims=True)
    centred = values - average
    spread = jnp.mean(centred * centred, axis=-1, keepdims=True)
    return centred * lax.rsqrt(spread + 1e-05) * gain + offset


def my_part():
    return lax.axis_index("region") * lax.axis_size("feat") + lax.axis_index("feat")


def pick_kernel(part_count, near_cap, far_cap, far_ref, near_ref, latent_ref, out_ref, picked):
    me, sub, subs = my_part(), lax.axis_index("sub"), lax.axis_size("sub")
    half = near_cap // subs
    columns = [as_columns(near_ref[0])]
    tile_place = lax.broadcasted_iota(jnp.int32, (tile_rows, lanes), 0)
    far = as_columns(far_ref[0, 0:1])
    for slot in range(1, far_cap):
        far = jnp.where(sub == slot, as_columns(far_ref[0, slot : slot + 1]), far)
    for part in range(part_count):
        columns.append(jnp.where(tile_place == 0, far[part : part + 1], -1))
    hot = one_hot(jnp.concatenate(columns, axis=0), latent_ref.shape[0])
    picked[...] = jnp.dot(hot, latent_ref[...], preferred_element_type=f32).astype(bf16)
    for which, offset in enumerate(near_offsets):
        target = lax.rem(me + (offset + part_count), part_count)
        start = pl.multiple_of(which * near_cap + sub * half, half)
        out_ref[target, :half] = picked[pl.ds(start, half)]
    far_start = len(near_offsets) * near_cap
    for part in range(part_count):
        spot = far_start + part * tile_rows
        out_ref[part, half:] = picked[spot : spot + tile_rows][:1]


def exchange_halves(node_latent, near_rows, far_rows, part_count):
    near_cap, far_cap = near_rows.shape[2], far_rows.shape[2]
    subs = lax.axis_size("sub")
    width = node_latent.shape[1]
    block = (part_count, near_cap // subs + 1, width)
    picks = len(near_offsets) * near_cap + part_count * tile_rows
    blocks = pl.pallas_call(
        functools.partial(pick_kernel, part_count, near_cap, far_cap),
        out_shape=pltpu.HBM(block, bf16),
        in_specs=[vmem, vmem, vmem],
        out_specs=vmem,
        scratch_shapes=[pltpu.VMEM((picks, width), bf16)],
        compiler_params=pltpu.CompilerParams(vmem_limit_bytes=grant),
        cost_estimate=pl.CostEstimate(flops=0, bytes_accessed=0, transcendentals=0),
        name="pick_halo",
    )(in_hbm(jnp.transpose(far_rows, (0, 2, 1))), in_hbm(near_rows), in_hbm(node_latent))
    own = lax.all_to_all(blocks, ("region", "feat"), split_axis=0, concat_axis=0, tiled=True)
    return [own]


def exchange_all(node_latent, near_rows, far_rows, part_count):
    near_send = jnp.take(node_latent, near_rows[0], axis=0, mode="clip")
    far_send = jnp.take(node_latent, far_rows[0], axis=0, mode="clip")
    got = []
    for which, offset in enumerate(near_offsets):
        pairs = [(part, (part + offset) % part_count) for part in range(part_count)]
        got.append(lax.ppermute(near_send[which], ("region", "feat"), pairs))
    far = lax.all_to_all(far_send, ("region", "feat"), split_axis=0, concat_axis=0, tiled=True)
    got.append(far.reshape(-1, far.shape[2]))
    return got


def gather_kernel(
    near_cap,
    far_cap,
    halved,
    source_ref,
    receiver_ref,
    latent_ref,
    gathered_hbm,
    to_node,
    gathered,
    sems,
):
    node_count, width = latent_ref.shape
    edge_count = gathered.shape[0]
    block = gather_rows
    copies = []

    def start(source, target):
        copies.append(pltpu.make_async_copy(source, target, sems.at[len(copies)]))
        copies[-1].start()

    latent = latent_ref[...]

    def gather(at, target, rows, begin):
        here = slice(at * (block // lanes), (at + 1) * (block // lanes))
        source = source_ref[here]
        if halved:
            far = source - (node_count + len(near_offsets) * near_cap)
            slot = lax.rem(far, far_cap)
            turned = wrap(slot - lax.axis_index("sub"), far_cap)
            source = jnp.where(far >= 0, source - slot + turned, source)
        columns = as_columns(source)
        sent = one_hot(columns, node_count)
        target[rows, begin : begin + width] = jnp.dot(
            sent, latent, preferred_element_type=f32
        ).astype(bf16)
        received = one_hot(as_columns(receiver_ref[here]), node_count)
        target[rows, begin + width : begin + 2 * width] = jnp.dot(
            received, latent, preferred_element_type=f32
        ).astype(bf16)
        slots = target.shape[1] - begin - 2 * width
        target[rows, begin + 2 * width :] = one_hot(columns - node_count, slots)

    for at in range(edge_count // block):
        gather(at, gathered, slice(at * block, (at + 1) * block), 0)
        rows = pl.ds(at * block, block)
        start(gathered.at[rows], gathered_hbm.at[rows])
    node_place = lax.broadcasted_iota(jnp.int32, (to_node.shape[0], lanes), 0)
    for row in range(edge_count // lanes):
        to_node[:, row * lanes : (row + 1) * lanes] = jnp.where(
            node_place == receiver_ref[row : row + 1], 1.0, 0.0
        ).astype(bf16)
    for copy in copies:
        copy.wait()


def place_halo(halo, part_count, near_cap, halved, got):
    subs = lax.axis_size("sub")
    far_start = len(near_offsets) * near_cap
    used = far_start
    if halved:
        half = near_cap // subs
        for which, offset in enumerate(near_offsets):
            origin = lax.rem(my_part() + (part_count - offset), part_count)
            for turn in range(subs):
                owner = wrap(lax.axis_index("sub") - turn, subs)
                start = pl.multiple_of(which * near_cap + owner * half, half)
                halo[pl.ds(start, half)] = got[turn][origin, :half]
        far = [got[turn][part, half:] for part in range(part_count) for turn in range(subs)]
        used += len(far)
        halo[far_start:used] = jnp.concatenate(
            [row.astype(f32) for row in far], axis=0
        ).astype(bf16)
    else:
        for rows in got:
            start = used - far_start if rows is not got[-1] else far_start
            halo[start : start + rows.shape[0]] = rows[...]
            used += rows.shape[0]
        used -= far_start
    if used < halo.shape[0]:
        halo[used:] = jnp.zeros((halo.shape[0] - used, halo.shape[1]), bf16)


def place_rows(whole, start, piece, owner):
    rows = piece.shape[0]
    whole[pl.ds(pl.multiple_of(start + owner * rows, rows), rows), :] = piece


def owners():
    feat, feats = lax.axis_index("feat"), lax.axis_size("feat")
    sub, subs = lax.axis_index("sub"), lax.axis_size("sub")
    own = [(0, turn) for turn in range(subs)]
    rest = [(shift, turn) for turn in range(subs) for shift in range(1, feats)]
    return [
        wrap(feat - shift, feats) * subs + wrap(sub - turn, subs) for shift, turn in own + rest
    ]


def from_feats(weight):
    feats = lax.axis_size("feat")
    return [
        lax.ppermute(weight, "feat", [(at, (at + shift) % feats) for at in range(feats)])
        for shift in range(1, feats)
    ]


def from_subs(pieces):
    subs = lax.axis_size("sub")
    return [
        lax.ppermute(piece, "sub", [(at, (at + turn) % subs) for at in range(subs)])
        for turn in range(1, subs)
        for piece in pieces
    ]


def edge_kernel(pieces_count, got_count, part_count, near_cap, halved, *refs):
    edge_hbm, gathered_hbm, to_node = refs[:3]
    got_refs = refs[3 : 3 + got_count]
    refs = refs[3 + got_count :]
    in_pieces, out_pieces = refs[:pieces_count], refs[pieces_count : 2 * pieces_count]
    row_refs = refs[2 * pieces_count : 2 * pieces_count + 4]
    new_hbm, sum_ref = refs[2 * pieces_count + 4 : 2 * pieces_count + 6]
    known_rows, in_weight, out_weight, halo, rows, preact, hidden, output, new_ref, total, sems = (
        refs[2 * pieces_count + 6 :]
    )
    edge_count, width = new_hbm.shape
    blocks = len(preact)
    block = edge_count // blocks
    known = []
    taken = []

    def start(source, target):
        copy = pltpu.make_async_copy(source, target, sems.at[len(taken)])
        copy.start()
        taken.append(copy)
        return copy

    order = owners()
    first, later = [], []
    for which in (1, 0, 2):
        count = in_pieces[0].shape[1]
        spot = pl.ds(pl.multiple_of(which * width + order[0] * count, count), count)
        target = first if which == 1 else later
        target.append(start(in_pieces[0].at[which], in_weight.at[spot]))
    for row_ref, row in zip(row_refs, rows):
        later.append(start(row_ref, row))
    count = out_pieces[0].shape[0]
    spot = pl.ds(pl.multiple_of(order[0] * count, count), count)
    later.append(start(out_pieces[0], out_weight.at[spot]))
    in_bias, out_bias, gain, offset = rows
    known_copies = []
    for at in range(blocks):
        spot = pl.ds(at * block, block)
        view = known_rows.at[spot]
        known.append(view)
        known_copies.append(
            [
                start(edge_hbm.at[spot], view.at[:, pl.ds(0, width)]),
                start(
                    gathered_hbm.at[spot], view.at[:, pl.ds(width, view.shape[1] - width)]
                ),
            ]
        )

    place_halo(halo, part_count, near_cap, halved, got_refs)
    for which in (1, 0, 2):
        for piece, owner in zip(in_pieces[1:], order[1:]):
            place_rows(in_weight, which * width, piece[which], owner)
    for piece, owner in zip(out_pieces[1:], order[1:]):
        place_rows(out_weight, 0, piece[...], owner)
    for copy in first:
        copy.wait()
    in_weight[3 * width :] = jnp.dot(
        halo[...], in_weight[width : 2 * width], preferred_element_type=f32
    ).astype(bf16)
    for copy in later:
        copy.wait()

    def in_dot(at):
        for copy in known_copies[at]:
            copy.wait()
        preact[at][...] = jnp.dot(
            known[at][...], in_weight[...], preferred_element_type=f32
        )

    def activate(at):
        for start_row in range(0, block, chunk_rows):
            here = slice(start_row, start_row + chunk_rows)
            hidden[at][here] = silu(preact[at][here] + in_bias[...]).astype(bf16)

    def out_dot(at):
        output[at][...] = jnp.dot(
            hidden[at][...], out_weight[...], preferred_element_type=f32
        )

    def normalise(at):
        for start_row in range(0, block, chunk_rows):
            here = slice(start_row, start_row + chunk_rows)
            there = slice(at * block + start_row, at * block + start_row + chunk_rows)
            normed = layer_norm(output[at][here] + out_bias[...], gain[...], offset[...])
            edges = known[at][here, :width].astype(f32)
            new_ref[there] = (edges + normed).astype(bf16)
        spot = pl.ds(at * block, block)
        return start(new_ref.at[spot], new_hbm.at[spot])

    def sum_dot(at):
        spot = slice(at * block, (at + 1) * block)
        part = jnp.dot(to_node[:, spot], new_ref[spot], preferred_element_type=f32)
        if at > 0:
            part += total[...]
        if at + 1 < blocks:
            total[...] = part
        else:
            sum_ref[...] = part.astype(bf16)

    out_copies = []
    in_dot(0)
    for at in range(blocks):
        if at + 1 < blocks:
            in_dot(at + 1)
        activate(at)
        out_dot(at)
        if at > 0:
            sum_dot(at - 1)
        out_copies.append(normalise(at))
    sum_dot(blocks - 1)
    for copy in out_copies:
        copy.wait()


def node_kernel(pieces_count, *refs):
    latent_ref, own_ref, other_ref = refs[:3]
    in_pieces = refs[3 : 3 + pieces_count]
    out_pieces = refs[3 + pieces_count : 3 + 2 * pieces_count]
    in_bias, out_bias, gain, offset, new_ref, weights, known, preact, hidden, output = refs[
        3 + 2 * pieces_count :
    ]
    node_count, width = latent_ref.shape
    known[:, :width] = latent_ref[...]
    known[:, width:] = (own_ref[...].astype(f32) + other_ref[...].astype(f32)).astype(bf16)
    for in_piece, out_piece, owner in zip(in_pieces, out_pieces, owners()):
        for which in range(in_piece.shape[0]):
            place_rows(weights, which * width, in_piece[which], owner)
        place_rows(weights, 2 * width, out_piece[...], owner)
    preact[...] = jnp.dot(known[...], weights[: 2 * width], preferred_element_type=f32)
    chunks = [slice(at, at + chunk_rows) for at in range(0, node_count, chunk_rows)]
    for here in chunks:
        hidden[here] = silu(preact[here] + in_bias[...]).astype(bf16)
    output[...] = jnp.dot(hidden[...], weights[2 * width :], preferred_element_type=f32)
    for here in chunks:
        normed = layer_norm(output[here] + out_bias[...], gain[...], offset[...])
        new_ref[here] = (latent_ref[here].astype(f32) + normed).astype(bf16)


def shards(
    node_latent,
    edge_latent,
    edge_source,
    receivers,
    near_rows,
    far_rows,
    edge_in_weight,
    edge_out_weight,
    node_in_weight,
    node_out_weight,
    edge_in_bias,
    edge_out_bias,
    edge_gain,
    edge_offset,
    node_in_bias,
    node_out_bias,
    node_gain,
    node_offset,
):
    node_count, width = node_latent.shape
    edge_count = edge_latent.shape[0]
    near_cap, far_cap = near_rows.shape[2], far_rows.shape[2]
    part_count = far_rows.shape[1]

    far_edge = [from_feats(edge_in_weight), from_feats(edge_out_weight)]
    near_edge = [from_subs([edge_in_weight]), from_subs([edge_out_weight])]

    subs = lax.axis_size("sub")
    halved = part_count <= few_parts and far_cap == subs and near_cap % (tile_rows * subs) == 0
    exchange = exchange_halves if halved else exchange_all
    got = exchange(node_latent, near_rows, far_rows, part_count)
    halo_space = len(near_offsets) * near_cap + part_count * far_cap
    halo_space = -(-halo_space // lanes) * lanes

    source_rows = in_hbm(edge_source.reshape(-1, lanes))
    receiver_rows = in_hbm(receivers.reshape(-1, lanes))

    near_edge[1], latent_after = lax.optimization_barrier((near_edge[1], node_latent))
    gathered_width = 2 * width + halo_space
    known_width = width + gathered_width
    steps = 2
    block = edge_count // steps
    gathered, to_node = pl.pallas_call(
        functools.partial(gather_kernel, near_cap, far_cap, halved),
        out_shape=[
            pltpu.HBM((edge_count, gathered_width), bf16),
            pltpu.VMEM((node_count, edge_count), bf16),
        ],
        in_specs=[vmem] * 3,
        out_specs=[hbm, vmem],
        scratch_shapes=[
            pltpu.VMEM((edge_count, gathered_width), bf16),
            pltpu.SemaphoreType.DMA((edge_count // gather_rows,)),
        ],
        compiler_params=pltpu.CompilerParams(vmem_limit_bytes=grant),
        cost_estimate=pl.CostEstimate(flops=0, bytes_accessed=0, transcendentals=0),
        name="gather_latents",
    )(
        source_rows,
        receiver_rows,
        in_hbm(latent_after),
    )

    node_weights = [node_in_weight, node_out_weight]
    far_edge, got, gathered, to_node, node_weights = lax.optimization_barrier(
        (far_edge, got, gathered, to_node, node_weights)
    )
    if halved:
        got = got + from_subs(got)
    edge_in, edge_out = [
        [weight] + near + far + from_subs(far)
        for weight, near, far in zip((edge_in_weight, edge_out_weight), near_edge, far_edge)
    ]
    node_in, node_out = [
        [weight] + from_subs([weight]) + far + from_subs(far)
        for weight, far in zip(node_weights, [from_feats(weight) for weight in node_weights])
    ]
    pieces_count = len(edge_in)

    rows = [value.reshape(1, -1) for value in (edge_in_bias, edge_out_bias, edge_gain, edge_offset)]
    edge_operands = [in_hbm(edge_latent), in_hbm(gathered), in_vmem(to_node)]
    edge_operands += [in_vmem(blocks) for blocks in got]
    edge_specs = [hbm] * 2 + [vmem] * (1 + len(got))
    for pieces in (edge_in, edge_out):
        edge_operands += [in_hbm(pieces[0])] + [in_vmem(piece) for piece in pieces[1:]]
        edge_specs += [hbm] + [vmem] * (pieces_count - 1)
    edge_operands += [in_hbm(row) for row in rows]
    edge_specs += [hbm] * len(rows)
    copy_count = 3 + 4 + 1 + 3 * steps
    edge_new, partial_sums = pl.pallas_call(
        functools.partial(edge_kernel, pieces_count, len(got), part_count, near_cap, halved),
        out_shape=[
            pltpu.HBM((edge_count, width), bf16),
            jax.ShapeDtypeStruct((node_count, width), bf16),
        ],
        in_specs=edge_specs,
        out_specs=[hbm, vmem],
        scratch_shapes=[
            pltpu.VMEM((edge_count, known_width), bf16),
            pltpu.VMEM((known_width, width), bf16),
            pltpu.VMEM((width, width), bf16),
            pltpu.VMEM((halo_space, width), bf16),
            [pltpu.VMEM((1, width), f32)] * 4,
            [pltpu.VMEM((block, width), f32) for _ in range(steps)],
            [pltpu.VMEM((block, width), bf16) for _ in range(steps)],
            [pltpu.VMEM((block, width), f32) for _ in range(steps)],
            pltpu.VMEM((edge_count, width), bf16),
            pltpu.VMEM((node_count, width), f32),
            pltpu.SemaphoreType.DMA((copy_count,)),
        ],
        compiler_params=pltpu.CompilerParams(vmem_limit_bytes=grant),
        cost_estimate=pl.CostEstimate(
            flops=2 * edge_count * width * (4 * width + node_count),
            bytes_accessed=8 * edge_count * width,
            transcendentals=edge_count * width,
        ),
        name="edge_update",
    )(*edge_operands)

    subs = lax.axis_size("sub")
    other_sums = lax.ppermute(partial_sums, "sub", [(at, (at + 1) % subs) for at in range(subs)])

    rows = [value.reshape(1, -1) for value in (node_in_bias, node_out_bias, node_gain, node_offset)]
    node_new = pl.pallas_call(
        functools.partial(node_kernel, pieces_count),
        out_shape=jax.ShapeDtypeStruct((node_count, width), bf16),
        in_specs=[vmem] * (3 + 2 * pieces_count + 4),
        out_specs=vmem,
        scratch_shapes=[
            pltpu.VMEM((3 * width, width), bf16),
            pltpu.VMEM((node_count, 2 * width), bf16),
            pltpu.VMEM((node_count, width), f32),
            pltpu.VMEM((node_count, width), bf16),
            pltpu.VMEM((node_count, width), f32),
        ],
        compiler_params=pltpu.CompilerParams(vmem_limit_bytes=grant),
        cost_estimate=pl.CostEstimate(
            flops=2 * node_count * width * 3 * width,
            bytes_accessed=10 * node_count * width,
            transcendentals=node_count * width,
        ),
        name="node_update",
    )(node_latent, partial_sums, other_sums, *node_in, *node_out, *rows)
    return (edge_new, node_new)


def solution(mesh):
    return jax.shard_map(
        shards,
        mesh=mesh,
        in_specs=(
            P(("groups", "region", "feat"), None),
            P(("groups", "region", "feat", "sub"), None),
            P(("groups", "region", "feat", "sub")),
            P(("groups", "region", "feat", "sub")),
            P(("groups", "region", "feat"), None, None),
            P(("groups", "region", "feat"), None, None),
            P(None, ("feat", "sub"), None),
            P(("feat", "sub"), None),
            P(None, ("feat", "sub"), None),
            P(("feat", "sub"), None),
            P(),
            P(),
            P(),
            P(),
            P(),
            P(),
            P(),
            P(),
        ),
        out_specs=(
            P(("groups", "region", "feat", "sub"), None),
            P(("groups", "region", "feat"), None),
        ),
        check_vma=False,
    )
```

```python
import functools

import jax
import jax.numpy as jnp
from jax import lax
from jax.experimental import pallas as pl
from jax.experimental.pallas import tpu as pltpu
from jax.sharding import PartitionSpec as P

near_offsets = (1, 2, -1, -2)
tile_rows = 16
lanes = 128
few_parts = 8
grant = 32 << 20
chunk_rows = 64
bf16 = jnp.bfloat16
f32 = jnp.float32
vmem = pl.BlockSpec(memory_space=pltpu.VMEM)
hbm = pl.BlockSpec(memory_space=pltpu.HBM)


def in_hbm(array):
    return pltpu.with_memory_space_constraint(array, pltpu.HBM)


def in_vmem(array):
    return pltpu.with_memory_space_constraint(array, pltpu.VMEM)


def wrap(value, count):
    return jnp.where(value < 0, value + count, value)


def as_columns(rows):
    return jnp.concatenate(
        [
            jnp.transpose(jnp.broadcast_to(rows[at : at + 1], (lanes, rows.shape[1])))
            for at in range(rows.shape[0])
        ],
        axis=0,
    )


def one_hot(columns, width):
    place = lax.broadcasted_iota(jnp.int32, columns.shape, 1)
    return jnp.concatenate(
        [
            jnp.where(columns == place + start, 1.0, 0.0).astype(bf16)
            for start in range(0, width, lanes)
        ],
        axis=1,
    )


def silu(values):
    half = 0.5 * values
    return half + half * jnp.tanh(half)


def layer_norm(values, gain, offset):
    average = jnp.mean(values, axis=-1, keepdims=True)
    centred = values - average
    spread = jnp.mean(centred * centred, axis=-1, keepdims=True)
    return centred * lax.rsqrt(spread + 1e-05) * gain + offset


def my_part():
    return lax.axis_index("region") * lax.axis_size("feat") + lax.axis_index("feat")


def pick_kernel(part_count, near_cap, far_cap, far_ref, near_ref, latent_ref, out_ref, picked):
    me, sub, subs = my_part(), lax.axis_index("sub"), lax.axis_size("sub")
    half = near_cap // subs
    columns = [as_columns(near_ref[0])]
    tile_place = lax.broadcasted_iota(jnp.int32, (tile_rows, lanes), 0)
    far = as_columns(far_ref[0, 0:1])
    for slot in range(1, far_cap):
        far = jnp.where(sub == slot, as_columns(far_ref[0, slot : slot + 1]), far)
    for part in range(part_count):
        columns.append(jnp.where(tile_place == 0, far[part : part + 1], -1))
    hot = one_hot(jnp.concatenate(columns, axis=0), latent_ref.shape[0])
    picked[...] = jnp.dot(hot, latent_ref[...], preferred_element_type=f32).astype(bf16)
    for which, offset in enumerate(near_offsets):
        target = lax.rem(me + (offset + part_count), part_count)
        start = pl.multiple_of(which * near_cap + sub * half, half)
        out_ref[target, :half] = picked[pl.ds(start, half)]
    far_start = len(near_offsets) * near_cap
    for part in range(part_count):
        spot = far_start + part * tile_rows
        out_ref[part, half:] = picked[spot : spot + tile_rows][:1]


def exchange_halves(node_latent, near_rows, far_rows, part_count, earlier):
    near_cap, far_cap = near_rows.shape[2], far_rows.shape[2]
    subs = lax.axis_size("sub")
    width = node_latent.shape[1]
    block = (part_count, near_cap // subs + 1, width)
    picks = len(near_offsets) * near_cap + part_count * tile_rows
    blocks = pl.pallas_call(
        functools.partial(pick_kernel, part_count, near_cap, far_cap),
        out_shape=pltpu.HBM(block, bf16),
        in_specs=[vmem, vmem, vmem],
        out_specs=vmem,
        scratch_shapes=[pltpu.VMEM((picks, width), bf16)],
        compiler_params=pltpu.CompilerParams(vmem_limit_bytes=grant),
        cost_estimate=pl.CostEstimate(flops=0, bytes_accessed=0, transcendentals=0),
        name="pick_halo",
    )(in_hbm(jnp.transpose(far_rows, (0, 2, 1))), in_hbm(near_rows), in_hbm(node_latent))
    blocks, earlier = lax.optimization_barrier((blocks, earlier))
    own = lax.all_to_all(blocks, ("region", "feat"), split_axis=0, concat_axis=0, tiled=True)
    return [own], earlier


def exchange_all(node_latent, near_rows, far_rows, part_count, earlier):
    near_send = jnp.take(node_latent, near_rows[0], axis=0, mode="clip")
    far_send = jnp.take(node_latent, far_rows[0], axis=0, mode="clip")
    got = []
    for which, offset in enumerate(near_offsets):
        pairs = [(part, (part + offset) % part_count) for part in range(part_count)]
        got.append(lax.ppermute(near_send[which], ("region", "feat"), pairs))
    far = lax.all_to_all(far_send, ("region", "feat"), split_axis=0, concat_axis=0, tiled=True)
    got.append(far.reshape(-1, far.shape[2]))
    return got, earlier


def gather_kernel(
    near_cap,
    far_cap,
    halved,
    source_ref,
    receiver_ref,
    latent_ref,
    node_in_ref,
    node_out_ref,
    edge_hbm,
    known,
    gathered_hbm,
    pack_ref,
    gathered,
    sems,
):
    node_count, width = latent_ref.shape
    first = known.shape[0]
    edge_count = first + gathered.shape[0]
    block = first // 2
    copies = []

    def start(source, target):
        copies.append(pltpu.make_async_copy(source, target, sems.at[len(copies)]))
        copies[-1].start()

    start(edge_hbm.at[pl.ds(0, first)], known.at[:, pl.ds(0, width)])
    count = node_in_ref.shape[0]
    pack_ref[:count] = node_in_ref[...]
    pack_ref[count] = node_out_ref[...]
    latent = latent_ref[...]

    def gather(at, target, rows, begin):
        here = slice(at * (block // lanes), (at + 1) * (block // lanes))
        source = source_ref[here]
        if halved:
            far = source - (node_count + len(near_offsets) * near_cap)
            slot = lax.rem(far, far_cap)
            turned = wrap(slot - lax.axis_index("sub"), far_cap)
            source = jnp.where(far >= 0, source - slot + turned, source)
        columns = as_columns(source)
        sent = one_hot(columns, node_count)
        target[rows, begin : begin + width] = jnp.dot(
            sent, latent, preferred_element_type=f32
        ).astype(bf16)
        received = one_hot(as_columns(receiver_ref[here]), node_count)
        target[rows, begin + width : begin + 2 * width] = jnp.dot(
            received, latent, preferred_element_type=f32
        ).astype(bf16)
        slots = target.shape[1] - begin - 2 * width
        target[rows, begin + 2 * width :] = one_hot(columns - node_count, slots)

    for at in range(first // block, edge_count // block):
        begin = at * block - first
        gather(at, gathered, slice(begin, begin + block), 0)
        rows = pl.ds(begin, block)
        start(gathered.at[rows], gathered_hbm.at[rows])
    for at in range(first // block):
        gather(at, known, slice(at * block, (at + 1) * block), width)
    for copy in copies:
        copy.wait()


def place_halo(halo, part_count, near_cap, halved, got):
    subs = lax.axis_size("sub")
    far_start = len(near_offsets) * near_cap
    used = far_start
    if halved:
        half = near_cap // subs
        for which, offset in enumerate(near_offsets):
            origin = lax.rem(my_part() + (part_count - offset), part_count)
            for turn in range(subs):
                owner = wrap(lax.axis_index("sub") - turn, subs)
                start = pl.multiple_of(which * near_cap + owner * half, half)
                halo[pl.ds(start, half)] = got[turn][origin, :half]
        far = [got[turn][part, half:] for part in range(part_count) for turn in range(subs)]
        used += len(far)
        halo[far_start:used] = jnp.concatenate(
            [row.astype(f32) for row in far], axis=0
        ).astype(bf16)
    else:
        for rows in got:
            start = used - far_start if rows is not got[-1] else far_start
            halo[start : start + rows.shape[0]] = rows[...]
            used += rows.shape[0]
        used -= far_start
    if used < halo.shape[0]:
        halo[used:] = jnp.zeros((halo.shape[0] - used, halo.shape[1]), bf16)


def place_rows(whole, start, piece, owner):
    rows = piece.shape[0]
    whole[pl.ds(pl.multiple_of(start + owner * rows, rows), rows), :] = piece


def owners():
    feat, feats = lax.axis_index("feat"), lax.axis_size("feat")
    sub, subs = lax.axis_index("sub"), lax.axis_size("sub")
    own = [(0, turn) for turn in range(subs)]
    rest = [(shift, turn) for turn in range(subs) for shift in range(1, feats)]
    return [
        wrap(feat - shift, feats) * subs + wrap(sub - turn, subs) for shift, turn in own + rest
    ]


def from_feats(weight):
    feats = lax.axis_size("feat")
    return [
        lax.ppermute(weight, "feat", [(at, (at + shift) % feats) for at in range(feats)])
        for shift in range(1, feats)
    ]


def from_subs(pieces):
    subs = lax.axis_size("sub")
    return [
        lax.ppermute(piece, "sub", [(at, (at + turn) % subs) for at in range(subs)])
        for turn in range(1, subs)
        for piece in pieces
    ]


def edge_kernel(pieces_count, got_count, part_count, near_cap, halved, block, *refs):
    edge_hbm, gathered_hbm, receiver_ref, known_first = refs[:4]
    got_refs = refs[4 : 4 + got_count]
    refs = refs[4 + got_count :]
    in_pieces, out_pieces = refs[:pieces_count], refs[pieces_count : 2 * pieces_count]
    row_refs = refs[2 * pieces_count : 2 * pieces_count + 4]
    new_hbm, sum_ref = refs[2 * pieces_count + 4 : 2 * pieces_count + 6]
    known_rest, to_node, in_weight, out_weight, halo, rows, preact, hidden, output, new_ref, total, sems = (
        refs[2 * pieces_count + 6 :]
    )
    edge_count, width = new_hbm.shape
    blocks = edge_count // block
    taken = []

    def start(source, target):
        copy = pltpu.make_async_copy(source, target, sems.at[len(taken)])
        copy.start()
        taken.append(copy)
        return copy

    order = owners()
    first, later = [], []
    for which in (1, 0, 2):
        count = in_pieces[0].shape[1]
        spot = pl.ds(pl.multiple_of(which * width + order[0] * count, count), count)
        target = first if which == 1 else later
        target.append(start(in_pieces[0].at[which], in_weight.at[spot]))
    for row_ref, row in zip(row_refs, rows):
        later.append(start(row_ref, row))
    count = out_pieces[0].shape[0]
    spot = pl.ds(pl.multiple_of(order[0] * count, count), count)
    later.append(start(out_pieces[0], out_weight.at[spot]))
    in_bias, out_bias, gain, offset = rows
    rest = edge_count - block
    known_copies = [
        start(edge_hbm.at[pl.ds(block, rest)], known_rest.at[:, pl.ds(0, width)]),
        start(gathered_hbm, known_rest.at[:, pl.ds(width, known_rest.shape[1] - width)]),
    ]

    def known(at):
        return known_first if at == 0 else known_rest.at[pl.ds((at - 1) * block, block)]

    node_place = lax.broadcasted_iota(jnp.int32, (to_node.shape[0], lanes), 0)
    for row in range(edge_count // lanes):
        to_node[:, row * lanes : (row + 1) * lanes] = jnp.where(
            node_place == receiver_ref[row : row + 1], 1.0, 0.0
        ).astype(bf16)
    place_halo(halo, part_count, near_cap, halved, got_refs)
    for which in (1, 0, 2):
        for piece, owner in zip(in_pieces[1:], order[1:]):
            place_rows(in_weight, which * width, piece[which], owner)
    for piece, owner in zip(out_pieces[1:], order[1:]):
        place_rows(out_weight, 0, piece[...], owner)
    for copy in first:
        copy.wait()
    in_weight[3 * width :] = jnp.dot(
        halo[...], in_weight[width : 2 * width], preferred_element_type=f32
    ).astype(bf16)
    for copy in later:
        copy.wait()

    def in_dot(at):
        if at == 1:
            for copy in known_copies:
                copy.wait()
        preact[at][...] = jnp.dot(
            known(at)[...], in_weight[...], preferred_element_type=f32
        )

    def activate(at):
        for start_row in range(0, block, chunk_rows):
            here = slice(start_row, start_row + chunk_rows)
            hidden[at][here] = silu(preact[at][here] + in_bias[...]).astype(bf16)

    def out_dot(at):
        output[at][...] = jnp.dot(
            hidden[at][...], out_weight[...], preferred_element_type=f32
        )

    def normalise(at):
        for start_row in range(0, block, chunk_rows):
            here = slice(start_row, start_row + chunk_rows)
            there = slice(at * block + start_row, at * block + start_row + chunk_rows)
            normed = layer_norm(output[at][here] + out_bias[...], gain[...], offset[...])
            edges = known(at)[here, :width].astype(f32)
            new_ref[there] = (edges + normed).astype(bf16)
        spot = pl.ds(at * block, block)
        return start(new_ref.at[spot], new_hbm.at[spot])

    def sum_dot(at):
        spot = slice(at * block, (at + 1) * block)
        part = jnp.dot(to_node[:, spot], new_ref[spot], preferred_element_type=f32)
        if at > 0:
            part += total[...]
        if at + 1 < blocks:
            total[...] = part
        else:
            sum_ref[...] = part.astype(bf16)

    out_copies = []
    in_dot(0)
    for at in range(blocks):
        if at + 1 < blocks:
            in_dot(at + 1)
        activate(at)
        out_dot(at)
        if at > 0:
            sum_dot(at - 1)
        out_copies.append(normalise(at))
    sum_dot(blocks - 1)
    for copy in out_copies:
        copy.wait()


def node_kernel(pieces_count, *refs):
    latent_ref, own_ref, other_ref = refs[:3]
    pieces = refs[3 : 3 + pieces_count]
    in_bias, out_bias, gain, offset, new_ref, weights = refs[3 + pieces_count :]
    width = latent_ref.shape[1]
    for piece, owner in zip(pieces, owners()):
        for which in range(piece.shape[0]):
            place_rows(weights, which * width, piece[which], owner)
    latent = latent_ref[...]
    summed = (own_ref[...].astype(f32) + other_ref[...].astype(f32)).astype(bf16)
    preact = jnp.dot(
        jnp.concatenate([latent, summed], axis=1),
        weights[: 2 * width],
        preferred_element_type=f32,
    )
    hidden = silu(preact + in_bias[...]).astype(bf16)
    output = jnp.dot(hidden, weights[2 * width :], preferred_element_type=f32) + out_bias[...]
    new_ref[...] = (
        latent.astype(f32) + layer_norm(output, gain[...], offset[...])
    ).astype(bf16)


def shards(
    node_latent,
    edge_latent,
    edge_source,
    receivers,
    near_rows,
    far_rows,
    edge_in_weight,
    edge_out_weight,
    node_in_weight,
    node_out_weight,
    edge_in_bias,
    edge_out_bias,
    edge_gain,
    edge_offset,
    node_in_bias,
    node_out_bias,
    node_gain,
    node_offset,
):
    node_count, width = node_latent.shape
    edge_count = edge_latent.shape[0]
    near_cap, far_cap = near_rows.shape[2], far_rows.shape[2]
    part_count = far_rows.shape[1]
    block = edge_count // 2
    steps = edge_count // block

    far_edge = [from_feats(edge_in_weight), from_feats(edge_out_weight)]
    near_edge = [from_subs([edge_in_weight]), from_subs([edge_out_weight])]

    subs = lax.axis_size("sub")
    halved = part_count <= few_parts and far_cap == subs and near_cap % (tile_rows * subs) == 0
    exchange = exchange_halves if halved else exchange_all
    got, near_edge[1] = exchange(
        node_latent, near_rows, far_rows, part_count, near_edge[1]
    )
    halo_space = len(near_offsets) * near_cap + part_count * far_cap
    halo_space = -(-halo_space // lanes) * lanes

    source_rows = in_hbm(edge_source.reshape(-1, lanes))
    receiver_rows = in_hbm(receivers.reshape(-1, lanes))

    pack_shape = (node_in_weight.shape[0] + 1,) + node_out_weight.shape
    gathered_width = 2 * width + halo_space
    known_width = width + gathered_width
    rest = edge_count - block
    known, gathered, node_weight = pl.pallas_call(
        functools.partial(gather_kernel, near_cap, far_cap, halved),
        out_shape=[
            pltpu.VMEM((block, known_width), bf16),
            pltpu.HBM((rest, gathered_width), bf16),
            pltpu.VMEM(pack_shape, bf16),
        ],
        in_specs=[vmem] * 5 + [hbm],
        out_specs=[vmem, hbm, vmem],
        scratch_shapes=[
            pltpu.VMEM((rest, gathered_width), bf16),
            pltpu.SemaphoreType.DMA((1 + 2 * (steps - 1),)),
        ],
        compiler_params=pltpu.CompilerParams(vmem_limit_bytes=grant),
        cost_estimate=pl.CostEstimate(flops=0, bytes_accessed=0, transcendentals=0),
        name="gather_latents",
    )(
        source_rows,
        receiver_rows,
        in_hbm(node_latent),
        in_hbm(node_in_weight),
        in_hbm(node_out_weight),
        in_hbm(edge_latent),
    )

    far_edge, got, known, gathered, node_weight = lax.optimization_barrier(
        (far_edge, got, known, gathered, node_weight)
    )
    if halved:
        got = got + from_subs(got)
    edge_in, edge_out = [
        [weight] + near + far + from_subs(far)
        for weight, near, far in zip((edge_in_weight, edge_out_weight), near_edge, far_edge)
    ]
    far_node = from_feats(node_weight)
    node_pieces = [node_weight] + from_subs([node_weight]) + far_node + from_subs(far_node)
    pieces_count = len(edge_in)

    rows = [value.reshape(1, -1) for value in (edge_in_bias, edge_out_bias, edge_gain, edge_offset)]
    edge_operands = [in_hbm(edge_latent), in_hbm(gathered), receiver_rows, in_vmem(known)]
    edge_operands += [in_vmem(blocks) for blocks in got]
    edge_specs = [hbm] * 2 + [vmem] * (2 + len(got))
    for pieces in (edge_in, edge_out):
        edge_operands += [in_hbm(pieces[0])] + [in_vmem(piece) for piece in pieces[1:]]
        edge_specs += [hbm] + [vmem] * (pieces_count - 1)
    edge_operands += [in_hbm(row) for row in rows]
    edge_specs += [hbm] * len(rows)
    copy_count = 3 + 4 + 1 + 2 + steps
    edge_new, partial_sums = pl.pallas_call(
        functools.partial(
            edge_kernel, pieces_count, len(got), part_count, near_cap, halved, block
        ),
        out_shape=[
            pltpu.HBM((edge_count, width), bf16),
            jax.ShapeDtypeStruct((node_count, width), bf16),
        ],
        in_specs=edge_specs,
        out_specs=[hbm, vmem],
        scratch_shapes=[
            pltpu.VMEM((rest, known_width), bf16),
            pltpu.VMEM((node_count, edge_count), bf16),
            pltpu.VMEM((known_width, width), bf16),
            pltpu.VMEM((width, width), bf16),
            pltpu.VMEM((halo_space, width), bf16),
            [pltpu.VMEM((1, width), f32)] * 4,
            [pltpu.VMEM((block, width), f32)] * steps,
            [pltpu.VMEM((block, width), bf16)] * steps,
            [pltpu.VMEM((block, width), f32)] * steps,
            pltpu.VMEM((edge_count, width), bf16),
            pltpu.VMEM((node_count, width), f32),
            pltpu.SemaphoreType.DMA((copy_count,)),
        ],
        compiler_params=pltpu.CompilerParams(vmem_limit_bytes=grant),
        cost_estimate=pl.CostEstimate(
            flops=2 * edge_count * width * (4 * width + node_count),
            bytes_accessed=8 * edge_count * width,
            transcendentals=edge_count * width,
        ),
        name="edge_update",
    )(*edge_operands)

    subs = lax.axis_size("sub")
    other_sums = lax.ppermute(partial_sums, "sub", [(at, (at + 1) % subs) for at in range(subs)])

    rows = [value.reshape(1, -1) for value in (node_in_bias, node_out_bias, node_gain, node_offset)]
    node_new = pl.pallas_call(
        functools.partial(node_kernel, pieces_count),
        out_shape=jax.ShapeDtypeStruct((node_count, width), bf16),
        in_specs=[vmem] * (3 + pieces_count + 4),
        out_specs=vmem,
        scratch_shapes=[
            pltpu.VMEM((3 * width, width), bf16),
        ],
        compiler_params=pltpu.CompilerParams(vmem_limit_bytes=grant),
        cost_estimate=pl.CostEstimate(
            flops=2 * node_count * width * 3 * width,
            bytes_accessed=10 * node_count * width,
            transcendentals=node_count * width,
        ),
        name="node_update",
    )(node_latent, partial_sums, other_sums, *node_pieces, *rows)
    return (edge_new, node_new)


def solution(mesh):
    return jax.shard_map(
        shards,
        mesh=mesh,
        in_specs=(
            P(("groups", "region", "feat"), None),
            P(("groups", "region", "feat", "sub"), None),
            P(("groups", "region", "feat", "sub")),
            P(("groups", "region", "feat", "sub")),
            P(("groups", "region", "feat"), None, None),
            P(("groups", "region", "feat"), None, None),
            P(None, ("feat", "sub"), None),
            P(("feat", "sub"), None),
            P(None, ("feat", "sub"), None),
            P(("feat", "sub"), None),
            P(),
            P(),
            P(),
            P(),
            P(),
            P(),
            P(),
            P(),
        ),
        out_specs=(
            P(("groups", "region", "feat", "sub"), None),
            P(("groups", "region", "feat"), None),
        ),
        check_vma=False,
    )
```

```python
import functools

import jax
import jax.numpy as jnp
from jax import lax
from jax.experimental import pallas as pl
from jax.experimental.pallas import tpu as pltpu
from jax.sharding import PartitionSpec as P

near_offsets = (1, 2, -1, -2)
tile_rows = 16
lanes = 128
few_parts = 8
grant = 32 << 20
chunk_rows = 64
first_rows = 512
gather_rows = 512
bf16 = jnp.bfloat16
f32 = jnp.float32
vmem = pl.BlockSpec(memory_space=pltpu.VMEM)
hbm = pl.BlockSpec(memory_space=pltpu.HBM)


def in_hbm(array):
    return pltpu.with_memory_space_constraint(array, pltpu.HBM)


def in_vmem(array):
    return pltpu.with_memory_space_constraint(array, pltpu.VMEM)


def wrap(value, count):
    return jnp.where(value < 0, value + count, value)


def as_columns(rows):
    return jnp.concatenate(
        [
            jnp.transpose(jnp.broadcast_to(rows[at : at + 1], (lanes, rows.shape[1])))
            for at in range(rows.shape[0])
        ],
        axis=0,
    )


def one_hot(columns, width):
    place = lax.broadcasted_iota(jnp.int32, columns.shape, 1)
    return jnp.concatenate(
        [
            jnp.where(columns == place + start, 1.0, 0.0).astype(bf16)
            for start in range(0, width, lanes)
        ],
        axis=1,
    )


def silu(values):
    half = 0.5 * values
    return half + half * jnp.tanh(half)


def layer_norm(values, gain, offset):
    average = jnp.mean(values, axis=-1, keepdims=True)
    centred = values - average
    spread = jnp.mean(centred * centred, axis=-1, keepdims=True)
    return centred * lax.rsqrt(spread + 1e-05) * gain + offset


def my_part():
    return lax.axis_index("region") * lax.axis_size("feat") + lax.axis_index("feat")


def pick_kernel(part_count, near_cap, far_cap, far_ref, near_ref, latent_ref, out_ref, picked):
    me, sub, subs = my_part(), lax.axis_index("sub"), lax.axis_size("sub")
    half, width = near_cap // subs, latent_ref.shape[1]
    columns = [as_columns(near_ref[0])]
    tile_place = lax.broadcasted_iota(jnp.int32, (tile_rows, lanes), 0)
    far = as_columns(far_ref[0, 0:1])
    for slot in range(1, far_cap):
        far = jnp.where(sub == slot, as_columns(far_ref[0, slot : slot + 1]), far)
    for part in range(part_count):
        columns.append(jnp.where(tile_place == 0, far[part : part + 1], -1))
    hot = one_hot(jnp.concatenate(columns, axis=0), latent_ref.shape[0])
    rows = jnp.dot(hot, latent_ref[...], preferred_element_type=f32)
    far_start = len(near_offsets) * near_cap
    picked[...] = rows[:far_start].astype(bf16)
    for which, offset in enumerate(near_offsets):
        target = lax.rem(me + (offset + part_count), part_count)
        start = pl.multiple_of(which * near_cap + sub * half, half)
        out_ref[target, :, :width] = picked[pl.ds(start, half)]
    for part in range(part_count):
        spot = far_start + part * tile_rows
        far_row = rows[spot : spot + 1]
        pieces = [far_row[:, at : at + lanes] for at in range(0, width, lanes)]
        pieces.append(jnp.zeros((half - len(pieces), lanes), f32))
        out_ref[part, :, width:] = jnp.concatenate(pieces, axis=0).astype(bf16)


def exchange_halves(node_latent, near_rows, far_rows, part_count):
    near_cap, far_cap = near_rows.shape[2], far_rows.shape[2]
    subs = lax.axis_size("sub")
    width = node_latent.shape[1]
    block = (part_count, near_cap // subs, width + lanes)
    picks = len(near_offsets) * near_cap
    blocks = pl.pallas_call(
        functools.partial(pick_kernel, part_count, near_cap, far_cap),
        out_shape=pltpu.HBM(block, bf16),
        in_specs=[vmem, vmem, vmem],
        out_specs=vmem,
        scratch_shapes=[pltpu.VMEM((picks, width), bf16)],
        compiler_params=pltpu.CompilerParams(vmem_limit_bytes=grant),
        cost_estimate=pl.CostEstimate(flops=0, bytes_accessed=0, transcendentals=0),
        name="pick_halo",
    )(in_hbm(jnp.transpose(far_rows, (0, 2, 1))), in_hbm(near_rows), in_hbm(node_latent))
    own = lax.all_to_all(blocks, ("region", "feat"), split_axis=0, concat_axis=0, tiled=True)
    return [own]


def exchange_all(node_latent, near_rows, far_rows, part_count):
    near_send = jnp.take(node_latent, near_rows[0], axis=0, mode="clip")
    far_send = jnp.take(node_latent, far_rows[0], axis=0, mode="clip")
    got = []
    for which, offset in enumerate(near_offsets):
        pairs = [(part, (part + offset) % part_count) for part in range(part_count)]
        got.append(lax.ppermute(near_send[which], ("region", "feat"), pairs))
    far = lax.all_to_all(far_send, ("region", "feat"), split_axis=0, concat_axis=0, tiled=True)
    got.append(far.reshape(-1, far.shape[2]))
    return got


def gather_kernel(
    near_cap,
    far_cap,
    halved,
    source_ref,
    receiver_ref,
    latent_ref,
    node_in_ref,
    node_out_ref,
    edge_hbm,
    known,
    gathered_hbm,
    to_node,
    pack_ref,
    gathered,
    sems,
):
    node_count, width = latent_ref.shape
    first = known.shape[0]
    edge_count = first + gathered.shape[0]
    block = gather_rows
    copies = []

    def start(source, target):
        copies.append(pltpu.make_async_copy(source, target, sems.at[len(copies)]))
        copies[-1].start()

    start(edge_hbm.at[pl.ds(0, first)], known.at[:, pl.ds(0, width)])
    count = node_in_ref.shape[0]
    pack_ref[:count] = node_in_ref[...]
    pack_ref[count] = node_out_ref[...]
    latent = latent_ref[...]

    def gather(at, target, rows, begin):
        here = slice(at * (block // lanes), (at + 1) * (block // lanes))
        source = source_ref[here]
        if halved:
            far = source - (node_count + len(near_offsets) * near_cap)
            slot = lax.rem(far, far_cap)
            turned = wrap(slot - lax.axis_index("sub"), far_cap)
            source = jnp.where(far >= 0, source - slot + turned, source)
        columns = as_columns(source)
        sent = one_hot(columns, node_count)
        target[rows, begin : begin + width] = jnp.dot(
            sent, latent, preferred_element_type=f32
        ).astype(bf16)
        received = one_hot(as_columns(receiver_ref[here]), node_count)
        target[rows, begin + width : begin + 2 * width] = jnp.dot(
            received, latent, preferred_element_type=f32
        ).astype(bf16)
        slots = target.shape[1] - begin - 2 * width
        target[rows, begin + 2 * width :] = one_hot(columns - node_count, slots)

    for at in range(first // block, edge_count // block):
        begin = at * block - first
        gather(at, gathered, slice(begin, begin + block), 0)
        rows = pl.ds(begin, block)
        start(gathered.at[rows], gathered_hbm.at[rows])
    node_place = lax.broadcasted_iota(jnp.int32, (to_node.shape[0], lanes), 0)
    for row in range(edge_count // lanes):
        to_node[:, row * lanes : (row + 1) * lanes] = jnp.where(
            node_place == receiver_ref[row : row + 1], 1.0, 0.0
        ).astype(bf16)
    for at in range(first // block):
        gather(at, known, slice(at * block, (at + 1) * block), width)
    for copy in copies:
        copy.wait()


def place_halo(halo, part_count, near_cap, halved, got):
    subs, width = lax.axis_size("sub"), halo.shape[1]
    far_start = len(near_offsets) * near_cap
    used = far_start
    if halved:
        half = near_cap // subs
        for which, offset in enumerate(near_offsets):
            origin = lax.rem(my_part() + (part_count - offset), part_count)
            for turn in range(subs):
                owner = wrap(lax.axis_index("sub") - turn, subs)
                start = pl.multiple_of(which * near_cap + owner * half, half)
                halo[pl.ds(start, half)] = got[turn][origin, :, :width]
        far = []
        for part in range(part_count):
            for turn in range(subs):
                tile = got[turn][part, :, width:].astype(f32)
                pieces = [tile[at : at + 1] for at in range(width // lanes)]
                far.append(jnp.concatenate(pieces, axis=1))
        used += len(far)
        halo[far_start:used] = jnp.concatenate(far, axis=0).astype(bf16)
    else:
        for rows in got:
            start = used - far_start if rows is not got[-1] else far_start
            halo[start : start + rows.shape[0]] = rows[...]
            used += rows.shape[0]
        used -= far_start
    if used < halo.shape[0]:
        halo[used:] = jnp.zeros((halo.shape[0] - used, halo.shape[1]), bf16)


def place_rows(whole, start, piece, owner):
    rows = piece.shape[0]
    whole[pl.ds(pl.multiple_of(start + owner * rows, rows), rows), :] = piece


def owners():
    feat, feats = lax.axis_index("feat"), lax.axis_size("feat")
    sub, subs = lax.axis_index("sub"), lax.axis_size("sub")
    own = [(0, turn) for turn in range(subs)]
    rest = [(shift, turn) for turn in range(subs) for shift in range(1, feats)]
    return [
        wrap(feat - shift, feats) * subs + wrap(sub - turn, subs) for shift, turn in own + rest
    ]


def from_feats(weight):
    feats = lax.axis_size("feat")
    return [
        lax.ppermute(weight, "feat", [(at, (at + shift) % feats) for at in range(feats)])
        for shift in range(1, feats)
    ]


def from_subs(pieces):
    subs = lax.axis_size("sub")
    return [
        lax.ppermute(piece, "sub", [(at, (at + turn) % subs) for at in range(subs)])
        for turn in range(1, subs)
        for piece in pieces
    ]


def edge_kernel(pieces_count, got_count, part_count, near_cap, halved, *refs):
    edge_hbm, gathered_hbm, to_node, known_first = refs[:4]
    got_refs = refs[4 : 4 + got_count]
    refs = refs[4 + got_count :]
    in_pieces, out_pieces = refs[:pieces_count], refs[pieces_count : 2 * pieces_count]
    row_refs = refs[2 * pieces_count : 2 * pieces_count + 4]
    new_hbm, sum_ref = refs[2 * pieces_count + 4 : 2 * pieces_count + 6]
    known_rest, in_weight, out_weight, halo, rows, preact, hidden, output, new_ref, total, sems = (
        refs[2 * pieces_count + 6 :]
    )
    edge_count, width = new_hbm.shape
    known = [known_first, known_rest]
    starts = [0, known_first.shape[0]]
    blocks = len(known)
    taken = []

    def start(source, target):
        copy = pltpu.make_async_copy(source, target, sems.at[len(taken)])
        copy.start()
        taken.append(copy)
        return copy

    order = owners()
    first, later = [], []
    for which in (1, 0, 2):
        count = in_pieces[0].shape[1]
        spot = pl.ds(pl.multiple_of(which * width + order[0] * count, count), count)
        target = first if which == 1 else later
        target.append(start(in_pieces[0].at[which], in_weight.at[spot]))
    for row_ref, row in zip(row_refs, rows):
        later.append(start(row_ref, row))
    count = out_pieces[0].shape[0]
    spot = pl.ds(pl.multiple_of(order[0] * count, count), count)
    later.append(start(out_pieces[0], out_weight.at[spot]))
    in_bias, out_bias, gain, offset = rows
    known_copies = [
        start(edge_hbm.at[pl.ds(starts[1], known_rest.shape[0])], known_rest.at[:, pl.ds(0, width)]),
        start(gathered_hbm, known_rest.at[:, pl.ds(width, known_rest.shape[1] - width)]),
    ]

    place_halo(halo, part_count, near_cap, halved, got_refs)
    for which in (1, 0, 2):
        for piece, owner in zip(in_pieces[1:], order[1:]):
            place_rows(in_weight, which * width, piece[which], owner)
    for piece, owner in zip(out_pieces[1:], order[1:]):
        place_rows(out_weight, 0, piece[...], owner)
    for copy in first:
        copy.wait()
    in_weight[3 * width :] = jnp.dot(
        halo[...], in_weight[width : 2 * width], preferred_element_type=f32
    ).astype(bf16)
    for copy in later:
        copy.wait()

    def in_dot(at):
        if at == 1:
            for copy in known_copies:
                copy.wait()
        preact[at][...] = jnp.dot(
            known[at][...], in_weight[...], preferred_element_type=f32
        )

    def activate(at):
        for start_row in range(0, known[at].shape[0], chunk_rows):
            here = slice(start_row, start_row + chunk_rows)
            hidden[at][here] = silu(preact[at][here] + in_bias[...]).astype(bf16)

    def out_dot(at):
        output[at][...] = jnp.dot(
            hidden[at][...], out_weight[...], preferred_element_type=f32
        )

    def normalise(at):
        for start_row in range(0, known[at].shape[0], chunk_rows):
            here = slice(start_row, start_row + chunk_rows)
            there = slice(starts[at] + start_row, starts[at] + start_row + chunk_rows)
            normed = layer_norm(output[at][here] + out_bias[...], gain[...], offset[...])
            edges = known[at][here, :width].astype(f32)
            new_ref[there] = (edges + normed).astype(bf16)
        spot = pl.ds(starts[at], known[at].shape[0])
        return start(new_ref.at[spot], new_hbm.at[spot])

    def sum_dot(at):
        spot = slice(starts[at], starts[at] + known[at].shape[0])
        part = jnp.dot(to_node[:, spot], new_ref[spot], preferred_element_type=f32)
        if at > 0:
            part += total[...]
        if at + 1 < blocks:
            total[...] = part
        else:
            sum_ref[...] = part.astype(bf16)

    out_copies = []
    in_dot(0)
    for at in range(blocks):
        if at + 1 < blocks:
            in_dot(at + 1)
        activate(at)
        out_dot(at)
        if at > 0:
            sum_dot(at - 1)
        out_copies.append(normalise(at))
    sum_dot(blocks - 1)
    for copy in out_copies:
        copy.wait()


def node_kernel(pieces_count, *refs):
    latent_ref, own_ref, other_ref = refs[:3]
    pieces = refs[3 : 3 + pieces_count]
    in_bias, out_bias, gain, offset, new_ref, weights = refs[3 + pieces_count :]
    width = latent_ref.shape[1]
    for piece, owner in zip(pieces, owners()):
        for which in range(piece.shape[0]):
            place_rows(weights, which * width, piece[which], owner)
    latent = latent_ref[...]
    summed = (own_ref[...].astype(f32) + other_ref[...].astype(f32)).astype(bf16)
    preact = jnp.dot(
        jnp.concatenate([latent, summed], axis=1),
        weights[: 2 * width],
        preferred_element_type=f32,
    )
    hidden = silu(preact + in_bias[...]).astype(bf16)
    output = jnp.dot(hidden, weights[2 * width :], preferred_element_type=f32) + out_bias[...]
    new_ref[...] = (
        latent.astype(f32) + layer_norm(output, gain[...], offset[...])
    ).astype(bf16)


def shards(
    node_latent,
    edge_latent,
    edge_source,
    receivers,
    near_rows,
    far_rows,
    edge_in_weight,
    edge_out_weight,
    node_in_weight,
    node_out_weight,
    edge_in_bias,
    edge_out_bias,
    edge_gain,
    edge_offset,
    node_in_bias,
    node_out_bias,
    node_gain,
    node_offset,
):
    node_count, width = node_latent.shape
    edge_count = edge_latent.shape[0]
    near_cap, far_cap = near_rows.shape[2], far_rows.shape[2]
    part_count = far_rows.shape[1]

    far_edge = [from_feats(edge_in_weight), from_feats(edge_out_weight)]
    near_edge = [from_subs([edge_in_weight]), from_subs([edge_out_weight])]

    subs = lax.axis_size("sub")
    halved = part_count <= few_parts and far_cap == subs and near_cap % (tile_rows * subs) == 0
    exchange = exchange_halves if halved else exchange_all
    got = exchange(node_latent, near_rows, far_rows, part_count)
    halo_space = len(near_offsets) * near_cap + part_count * far_cap
    halo_space = -(-halo_space // lanes) * lanes

    source_rows = in_hbm(edge_source.reshape(-1, lanes))
    receiver_rows = in_hbm(receivers.reshape(-1, lanes))

    pack_shape = (node_in_weight.shape[0] + 1,) + node_out_weight.shape
    near_edge[1], latent_after = lax.optimization_barrier((near_edge[1], node_latent))
    gathered_width = 2 * width + halo_space
    known_width = width + gathered_width
    sizes = [first_rows, edge_count - first_rows]
    known, gathered, to_node, node_weight = pl.pallas_call(
        functools.partial(gather_kernel, near_cap, far_cap, halved),
        out_shape=[
            pltpu.VMEM((sizes[0], known_width), bf16),
            pltpu.HBM((sizes[1], gathered_width), bf16),
            pltpu.VMEM((node_count, edge_count), bf16),
            pltpu.HBM(pack_shape, bf16),
        ],
        in_specs=[vmem] * 5 + [hbm],
        out_specs=[vmem, hbm, vmem, vmem],
        scratch_shapes=[
            pltpu.VMEM((sizes[1], gathered_width), bf16),
            pltpu.SemaphoreType.DMA((1 + sizes[1] // gather_rows,)),
        ],
        compiler_params=pltpu.CompilerParams(vmem_limit_bytes=grant),
        cost_estimate=pl.CostEstimate(flops=0, bytes_accessed=0, transcendentals=0),
        name="gather_latents",
    )(
        source_rows,
        receiver_rows,
        in_hbm(latent_after),
        in_hbm(node_in_weight),
        in_hbm(node_out_weight),
        in_hbm(edge_latent),
    )

    far_edge, got, known, gathered, to_node, node_weight = lax.optimization_barrier(
        (far_edge, got, known, gathered, to_node, node_weight)
    )
    if halved:
        got = got + from_subs(got)
    edge_in, edge_out = [
        [weight] + near + far + from_subs(far)
        for weight, near, far in zip((edge_in_weight, edge_out_weight), near_edge, far_edge)
    ]
    far_node = from_feats(node_weight)
    node_pieces = [node_weight] + from_subs([node_weight]) + far_node + from_subs(far_node)
    pieces_count = len(edge_in)

    rows = [value.reshape(1, -1) for value in (edge_in_bias, edge_out_bias, edge_gain, edge_offset)]
    edge_operands = [in_hbm(edge_latent), in_hbm(gathered), in_vmem(to_node), in_vmem(known)]
    edge_operands += [in_vmem(blocks) for blocks in got]
    edge_specs = [hbm] * 2 + [vmem] * (2 + len(got))
    for pieces in (edge_in, edge_out):
        edge_operands += [in_hbm(pieces[0])] + [in_vmem(piece) for piece in pieces[1:]]
        edge_specs += [hbm] + [vmem] * (pieces_count - 1)
    edge_operands += [in_hbm(row) for row in rows]
    edge_specs += [hbm] * len(rows)
    copy_count = 3 + 4 + 1 + 2 + len(sizes)
    edge_new, partial_sums = pl.pallas_call(
        functools.partial(edge_kernel, pieces_count, len(got), part_count, near_cap, halved),
        out_shape=[
            pltpu.HBM((edge_count, width), bf16),
            jax.ShapeDtypeStruct((node_count, width), bf16),
        ],
        in_specs=edge_specs,
        out_specs=[hbm, vmem],
        scratch_shapes=[
            pltpu.VMEM((sizes[1], known_width), bf16),
            pltpu.VMEM((known_width, width), bf16),
            pltpu.VMEM((width, width), bf16),
            pltpu.VMEM((halo_space, width), bf16),
            [pltpu.VMEM((1, width), f32)] * 4,
            [pltpu.VMEM((size, width), f32) for size in sizes],
            [pltpu.VMEM((size, width), bf16) for size in sizes],
            [pltpu.VMEM((size, width), f32) for size in sizes],
            pltpu.VMEM((edge_count, width), bf16),
            pltpu.VMEM((node_count, width), f32),
            pltpu.SemaphoreType.DMA((copy_count,)),
        ],
        compiler_params=pltpu.CompilerParams(vmem_limit_bytes=grant),
        cost_estimate=pl.CostEstimate(
            flops=2 * edge_count * width * (4 * width + node_count),
            bytes_accessed=8 * edge_count * width,
            transcendentals=edge_count * width,
        ),
        name="edge_update",
    )(*edge_operands)

    subs = lax.axis_size("sub")
    other_sums = lax.ppermute(partial_sums, "sub", [(at, (at + 1) % subs) for at in range(subs)])

    rows = [value.reshape(1, -1) for value in (node_in_bias, node_out_bias, node_gain, node_offset)]
    node_new = pl.pallas_call(
        functools.partial(node_kernel, pieces_count),
        out_shape=jax.ShapeDtypeStruct((node_count, width), bf16),
        in_specs=[vmem] * (3 + pieces_count + 4),
        out_specs=vmem,
        scratch_shapes=[
            pltpu.VMEM((3 * width, width), bf16),
        ],
        compiler_params=pltpu.CompilerParams(vmem_limit_bytes=grant),
        cost_estimate=pl.CostEstimate(
            flops=2 * node_count * width * 3 * width,
            bytes_accessed=10 * node_count * width,
            transcendentals=node_count * width,
        ),
        name="node_update",
    )(node_latent, partial_sums, other_sums, *node_pieces, *rows)
    return (edge_new, node_new)


def solution(mesh):
    return jax.shard_map(
        shards,
        mesh=mesh,
        in_specs=(
            P(("groups", "region", "feat"), None),
            P(("groups", "region", "feat", "sub"), None),
            P(("groups", "region", "feat", "sub")),
            P(("groups", "region", "feat", "sub")),
            P(("groups", "region", "feat"), None, None),
            P(("groups", "region", "feat"), None, None),
            P(None, ("feat", "sub"), None),
            P(("feat", "sub"), None),
            P(None, ("feat", "sub"), None),
            P(("feat", "sub"), None),
            P(),
            P(),
            P(),
            P(),
            P(),
            P(),
            P(),
            P(),
        ),
        out_specs=(
            P(("groups", "region", "feat", "sub"), None),
            P(("groups", "region", "feat"), None),
        ),
        check_vma=False,
    )
```

```python
import functools

import jax
import jax.numpy as jnp
from jax import lax
from jax.experimental import pallas as pl
from jax.experimental.pallas import tpu as pltpu
from jax.sharding import PartitionSpec as P

near_offsets = (1, 2, -1, -2)
tile_rows = 16
lanes = 128
few_parts = 8
grant = 32 << 20
chunk_rows = 64
bf16 = jnp.bfloat16
f32 = jnp.float32
vmem = pl.BlockSpec(memory_space=pltpu.VMEM)
hbm = pl.BlockSpec(memory_space=pltpu.HBM)


def in_hbm(array):
    return pltpu.with_memory_space_constraint(array, pltpu.HBM)


def in_vmem(array):
    return pltpu.with_memory_space_constraint(array, pltpu.VMEM)


def wrap(value, count):
    return jnp.where(value < 0, value + count, value)


def as_columns(rows):
    return jnp.concatenate(
        [
            jnp.transpose(jnp.broadcast_to(rows[at : at + 1], (lanes, rows.shape[1])))
            for at in range(rows.shape[0])
        ],
        axis=0,
    )


def one_hot(columns, width):
    place = lax.broadcasted_iota(jnp.int32, columns.shape, 1)
    return jnp.concatenate(
        [
            jnp.where(columns == place + start, 1.0, 0.0).astype(bf16)
            for start in range(0, width, lanes)
        ],
        axis=1,
    )


def silu(values):
    half = 0.5 * values
    return half + half * jnp.tanh(half)


def layer_norm(values, gain, offset):
    average = jnp.mean(values, axis=-1, keepdims=True)
    centred = values - average
    spread = jnp.mean(centred * centred, axis=-1, keepdims=True)
    return centred * lax.rsqrt(spread + 1e-05) * gain + offset


def my_part():
    return lax.axis_index("region") * lax.axis_size("feat") + lax.axis_index("feat")


def pick_kernel(part_count, near_cap, far_cap, far_ref, near_ref, latent_ref, out_ref, picked):
    me, sub, subs = my_part(), lax.axis_index("sub"), lax.axis_size("sub")
    half, width = near_cap // subs, latent_ref.shape[1]
    columns = [as_columns(near_ref[0])]
    tile_place = lax.broadcasted_iota(jnp.int32, (tile_rows, lanes), 0)
    far = as_columns(far_ref[0, 0:1])
    for slot in range(1, far_cap):
        far = jnp.where(sub == slot, as_columns(far_ref[0, slot : slot + 1]), far)
    for part in range(part_count):
        columns.append(jnp.where(tile_place == 0, far[part : part + 1], -1))
    hot = one_hot(jnp.concatenate(columns, axis=0), latent_ref.shape[0])
    rows = jnp.dot(hot, latent_ref[...], preferred_element_type=f32)
    far_start = len(near_offsets) * near_cap
    picked[...] = rows[:far_start].astype(bf16)
    for which, offset in enumerate(near_offsets):
        target = lax.rem(me + (offset + part_count), part_count)
        start = pl.multiple_of(which * near_cap + sub * half, half)
        out_ref[target, :, :width] = picked[pl.ds(start, half)]
    for part in range(part_count):
        spot = far_start + part * tile_rows
        far_row = rows[spot : spot + 1]
        pieces = [far_row[:, at : at + lanes] for at in range(0, width, lanes)]
        pieces.append(jnp.zeros((half - len(pieces), lanes), f32))
        out_ref[part, :, width:] = jnp.concatenate(pieces, axis=0).astype(bf16)


def exchange_halves(node_latent, near_rows, far_rows, part_count, earlier):
    near_cap, far_cap = near_rows.shape[2], far_rows.shape[2]
    subs = lax.axis_size("sub")
    width = node_latent.shape[1]
    block = (part_count, near_cap // subs, width + lanes)
    picks = len(near_offsets) * near_cap
    blocks = pl.pallas_call(
        functools.partial(pick_kernel, part_count, near_cap, far_cap),
        out_shape=pltpu.HBM(block, bf16),
        in_specs=[vmem, vmem, vmem],
        out_specs=vmem,
        scratch_shapes=[pltpu.VMEM((picks, width), bf16)],
        compiler_params=pltpu.CompilerParams(vmem_limit_bytes=grant),
        cost_estimate=pl.CostEstimate(flops=0, bytes_accessed=0, transcendentals=0),
        name="pick_halo",
    )(in_hbm(jnp.transpose(far_rows, (0, 2, 1))), in_hbm(near_rows), in_hbm(node_latent))
    blocks, earlier = lax.optimization_barrier((blocks, earlier))
    own = lax.all_to_all(blocks, ("region", "feat"), split_axis=0, concat_axis=0, tiled=True)
    return [own], earlier


def exchange_all(node_latent, near_rows, far_rows, part_count, earlier):
    near_send = jnp.take(node_latent, near_rows[0], axis=0, mode="clip")
    far_send = jnp.take(node_latent, far_rows[0], axis=0, mode="clip")
    got = []
    for which, offset in enumerate(near_offsets):
        pairs = [(part, (part + offset) % part_count) for part in range(part_count)]
        got.append(lax.ppermute(near_send[which], ("region", "feat"), pairs))
    far = lax.all_to_all(far_send, ("region", "feat"), split_axis=0, concat_axis=0, tiled=True)
    got.append(far.reshape(-1, far.shape[2]))
    return got, earlier


def gather_kernel(
    near_cap,
    far_cap,
    halved,
    source_ref,
    receiver_ref,
    latent_ref,
    node_in_ref,
    node_out_ref,
    edge_hbm,
    known,
    gathered_hbm,
    pack_ref,
    gathered,
    sems,
):
    node_count, width = latent_ref.shape
    first = known.shape[0]
    edge_count = first + gathered.shape[0]
    block = first // 2
    copies = []

    def start(source, target):
        copies.append(pltpu.make_async_copy(source, target, sems.at[len(copies)]))
        copies[-1].start()

    start(edge_hbm.at[pl.ds(0, first)], known.at[:, pl.ds(0, width)])
    count = node_in_ref.shape[0]
    pack_ref[:count] = node_in_ref[...]
    pack_ref[count] = node_out_ref[...]
    latent = latent_ref[...]

    def gather(at, target, rows, begin):
        here = slice(at * (block // lanes), (at + 1) * (block // lanes))
        source = source_ref[here]
        if halved:
            far = source - (node_count + len(near_offsets) * near_cap)
            slot = lax.rem(far, far_cap)
            turned = wrap(slot - lax.axis_index("sub"), far_cap)
            source = jnp.where(far >= 0, source - slot + turned, source)
        columns = as_columns(source)
        sent = one_hot(columns, node_count)
        target[rows, begin : begin + width] = jnp.dot(
            sent, latent, preferred_element_type=f32
        ).astype(bf16)
        received = one_hot(as_columns(receiver_ref[here]), node_count)
        target[rows, begin + width : begin + 2 * width] = jnp.dot(
            received, latent, preferred_element_type=f32
        ).astype(bf16)
        slots = target.shape[1] - begin - 2 * width
        target[rows, begin + 2 * width :] = one_hot(columns - node_count, slots)

    for at in range(first // block, edge_count // block):
        begin = at * block - first
        gather(at, gathered, slice(begin, begin + block), 0)
        rows = pl.ds(begin, block)
        start(gathered.at[rows], gathered_hbm.at[rows])
    for at in range(first // block):
        gather(at, known, slice(at * block, (at + 1) * block), width)
    for copy in copies:
        copy.wait()


def place_halo(halo, part_count, near_cap, halved, got):
    subs, width = lax.axis_size("sub"), halo.shape[1]
    far_start = len(near_offsets) * near_cap
    used = far_start
    if halved:
        half = near_cap // subs
        for which, offset in enumerate(near_offsets):
            origin = lax.rem(my_part() + (part_count - offset), part_count)
            for turn in range(subs):
                owner = wrap(lax.axis_index("sub") - turn, subs)
                start = pl.multiple_of(which * near_cap + owner * half, half)
                halo[pl.ds(start, half)] = got[turn][origin, :, :width]
        far = []
        for part in range(part_count):
            for turn in range(subs):
                tile = got[turn][part, :, width:].astype(f32)
                pieces = [tile[at : at + 1] for at in range(width // lanes)]
                far.append(jnp.concatenate(pieces, axis=1))
        used += len(far)
        halo[far_start:used] = jnp.concatenate(far, axis=0).astype(bf16)
    else:
        for rows in got:
            start = used - far_start if rows is not got[-1] else far_start
            halo[start : start + rows.shape[0]] = rows[...]
            used += rows.shape[0]
        used -= far_start
    if used < halo.shape[0]:
        halo[used:] = jnp.zeros((halo.shape[0] - used, halo.shape[1]), bf16)


def place_rows(whole, start, piece, owner):
    rows = piece.shape[0]
    whole[pl.ds(pl.multiple_of(start + owner * rows, rows), rows), :] = piece


def owners():
    feat, feats = lax.axis_index("feat"), lax.axis_size("feat")
    sub, subs = lax.axis_index("sub"), lax.axis_size("sub")
    own = [(0, turn) for turn in range(subs)]
    rest = [(shift, turn) for turn in range(subs) for shift in range(1, feats)]
    return [
        wrap(feat - shift, feats) * subs + wrap(sub - turn, subs) for shift, turn in own + rest
    ]


def from_feats(weight):
    feats = lax.axis_size("feat")
    return [
        lax.ppermute(weight, "feat", [(at, (at + shift) % feats) for at in range(feats)])
        for shift in range(1, feats)
    ]


def from_subs(pieces):
    subs = lax.axis_size("sub")
    return [
        lax.ppermute(piece, "sub", [(at, (at + turn) % subs) for at in range(subs)])
        for turn in range(1, subs)
        for piece in pieces
    ]


def edge_kernel(pieces_count, got_count, part_count, near_cap, halved, block, *refs):
    edge_hbm, gathered_hbm, receiver_ref, known_first = refs[:4]
    got_refs = refs[4 : 4 + got_count]
    refs = refs[4 + got_count :]
    in_pieces, out_pieces = refs[:pieces_count], refs[pieces_count : 2 * pieces_count]
    row_refs = refs[2 * pieces_count : 2 * pieces_count + 4]
    new_hbm, sum_ref = refs[2 * pieces_count + 4 : 2 * pieces_count + 6]
    known_rest, to_node, in_weight, out_weight, halo, rows, preact, hidden, output, new_ref, total, sems = (
        refs[2 * pieces_count + 6 :]
    )
    edge_count, width = new_hbm.shape
    blocks = edge_count // block
    taken = []

    def start(source, target):
        copy = pltpu.make_async_copy(source, target, sems.at[len(taken)])
        copy.start()
        taken.append(copy)
        return copy

    order = owners()
    first, later = [], []
    for which in (1, 0, 2):
        count = in_pieces[0].shape[1]
        spot = pl.ds(pl.multiple_of(which * width + order[0] * count, count), count)
        target = first if which == 1 else later
        target.append(start(in_pieces[0].at[which], in_weight.at[spot]))
    for row_ref, row in zip(row_refs, rows):
        later.append(start(row_ref, row))
    count = out_pieces[0].shape[0]
    spot = pl.ds(pl.multiple_of(order[0] * count, count), count)
    later.append(start(out_pieces[0], out_weight.at[spot]))
    in_bias, out_bias, gain, offset = rows
    rest = edge_count - block
    known_copies = [
        start(edge_hbm.at[pl.ds(block, rest)], known_rest.at[:, pl.ds(0, width)]),
        start(gathered_hbm, known_rest.at[:, pl.ds(width, known_rest.shape[1] - width)]),
    ]

    def known(at):
        return known_first if at == 0 else known_rest.at[pl.ds((at - 1) * block, block)]

    node_place = lax.broadcasted_iota(jnp.int32, (to_node.shape[0], lanes), 0)
    for row in range(edge_count // lanes):
        to_node[:, row * lanes : (row + 1) * lanes] = jnp.where(
            node_place == receiver_ref[row : row + 1], 1.0, 0.0
        ).astype(bf16)
    place_halo(halo, part_count, near_cap, halved, got_refs)
    for which in (1, 0, 2):
        for piece, owner in zip(in_pieces[1:], order[1:]):
            place_rows(in_weight, which * width, piece[which], owner)
    for piece, owner in zip(out_pieces[1:], order[1:]):
        place_rows(out_weight, 0, piece[...], owner)
    for copy in first:
        copy.wait()
    in_weight[3 * width :] = jnp.dot(
        halo[...], in_weight[width : 2 * width], preferred_element_type=f32
    ).astype(bf16)
    for copy in later:
        copy.wait()

    def in_dot(at):
        if at == 1:
            for copy in known_copies:
                copy.wait()
        preact[at][...] = jnp.dot(
            known(at)[...], in_weight[...], preferred_element_type=f32
        )

    def activate(at):
        for start_row in range(0, block, chunk_rows):
            here = slice(start_row, start_row + chunk_rows)
            hidden[at][here] = silu(preact[at][here] + in_bias[...]).astype(bf16)

    def out_dot(at):
        output[at][...] = jnp.dot(
            hidden[at][...], out_weight[...], preferred_element_type=f32
        )

    def normalise(at):
        for start_row in range(0, block, chunk_rows):
            here = slice(start_row, start_row + chunk_rows)
            there = slice(at * block + start_row, at * block + start_row + chunk_rows)
            normed = layer_norm(output[at][here] + out_bias[...], gain[...], offset[...])
            edges = known(at)[here, :width].astype(f32)
            new_ref[there] = (edges + normed).astype(bf16)
        spot = pl.ds(at * block, block)
        return start(new_ref.at[spot], new_hbm.at[spot])

    def sum_dot(at):
        spot = slice(at * block, (at + 1) * block)
        part = jnp.dot(to_node[:, spot], new_ref[spot], preferred_element_type=f32)
        if at > 0:
            part += total[...]
        if at + 1 < blocks:
            total[...] = part
        else:
            sum_ref[...] = part.astype(bf16)

    out_copies = []
    in_dot(0)
    for at in range(blocks):
        if at + 1 < blocks:
            in_dot(at + 1)
        activate(at)
        out_dot(at)
        if at > 0:
            sum_dot(at - 1)
        out_copies.append(normalise(at))
    sum_dot(blocks - 1)
    for copy in out_copies:
        copy.wait()


def node_kernel(pieces_count, *refs):
    latent_ref, own_ref, other_ref = refs[:3]
    pieces = refs[3 : 3 + pieces_count]
    in_bias, out_bias, gain, offset, new_ref, weights = refs[3 + pieces_count :]
    width = latent_ref.shape[1]
    for piece, owner in zip(pieces, owners()):
        for which in range(piece.shape[0]):
            place_rows(weights, which * width, piece[which], owner)
    latent = latent_ref[...]
    summed = (own_ref[...].astype(f32) + other_ref[...].astype(f32)).astype(bf16)
    preact = jnp.dot(
        jnp.concatenate([latent, summed], axis=1),
        weights[: 2 * width],
        preferred_element_type=f32,
    )
    hidden = silu(preact + in_bias[...]).astype(bf16)
    output = jnp.dot(hidden, weights[2 * width :], preferred_element_type=f32) + out_bias[...]
    new_ref[...] = (
        latent.astype(f32) + layer_norm(output, gain[...], offset[...])
    ).astype(bf16)


def shards(
    node_latent,
    edge_latent,
    edge_source,
    receivers,
    near_rows,
    far_rows,
    edge_in_weight,
    edge_out_weight,
    node_in_weight,
    node_out_weight,
    edge_in_bias,
    edge_out_bias,
    edge_gain,
    edge_offset,
    node_in_bias,
    node_out_bias,
    node_gain,
    node_offset,
):
    node_count, width = node_latent.shape
    edge_count = edge_latent.shape[0]
    near_cap, far_cap = near_rows.shape[2], far_rows.shape[2]
    part_count = far_rows.shape[1]
    block = edge_count // 2
    steps = edge_count // block

    far_edge = [from_feats(edge_in_weight), from_feats(edge_out_weight)]
    near_edge = [from_subs([edge_in_weight]), from_subs([edge_out_weight])]

    subs = lax.axis_size("sub")
    halved = part_count <= few_parts and far_cap == subs and near_cap % (tile_rows * subs) == 0
    exchange = exchange_halves if halved else exchange_all
    got, near_edge[1] = exchange(
        node_latent, near_rows, far_rows, part_count, near_edge[1]
    )
    halo_space = len(near_offsets) * near_cap + part_count * far_cap
    halo_space = -(-halo_space // lanes) * lanes

    source_rows = in_hbm(edge_source.reshape(-1, lanes))
    receiver_rows = in_hbm(receivers.reshape(-1, lanes))

    pack_shape = (node_in_weight.shape[0] + 1,) + node_out_weight.shape
    gathered_width = 2 * width + halo_space
    known_width = width + gathered_width
    rest = edge_count - block
    known, gathered, node_weight = pl.pallas_call(
        functools.partial(gather_kernel, near_cap, far_cap, halved),
        out_shape=[
            pltpu.VMEM((block, known_width), bf16),
            pltpu.HBM((rest, gathered_width), bf16),
            pltpu.VMEM(pack_shape, bf16),
        ],
        in_specs=[vmem] * 5 + [hbm],
        out_specs=[vmem, hbm, vmem],
        scratch_shapes=[
            pltpu.VMEM((rest, gathered_width), bf16),
            pltpu.SemaphoreType.DMA((1 + 2 * (steps - 1),)),
        ],
        compiler_params=pltpu.CompilerParams(vmem_limit_bytes=grant),
        cost_estimate=pl.CostEstimate(flops=0, bytes_accessed=0, transcendentals=0),
        name="gather_latents",
    )(
        source_rows,
        receiver_rows,
        in_hbm(node_latent),
        in_hbm(node_in_weight),
        in_hbm(node_out_weight),
        in_hbm(edge_latent),
    )

    far_edge, got, known, gathered, node_weight = lax.optimization_barrier(
        (far_edge, got, known, gathered, node_weight)
    )
    if halved:
        got = got + from_subs(got)
    edge_in, edge_out = [
        [weight] + near + far + from_subs(far)
        for weight, near, far in zip((edge_in_weight, edge_out_weight), near_edge, far_edge)
    ]
    far_node = from_feats(node_weight)
    node_pieces = [node_weight] + from_subs([node_weight]) + far_node + from_subs(far_node)
    pieces_count = len(edge_in)

    rows = [value.reshape(1, -1) for value in (edge_in_bias, edge_out_bias, edge_gain, edge_offset)]
    edge_operands = [in_hbm(edge_latent), in_hbm(gathered), receiver_rows, in_vmem(known)]
    edge_operands += [in_vmem(blocks) for blocks in got]
    edge_specs = [hbm] * 2 + [vmem] * (2 + len(got))
    for pieces in (edge_in, edge_out):
        edge_operands += [in_hbm(pieces[0])] + [in_vmem(piece) for piece in pieces[1:]]
        edge_specs += [hbm] + [vmem] * (pieces_count - 1)
    edge_operands += [in_hbm(row) for row in rows]
    edge_specs += [hbm] * len(rows)
    copy_count = 3 + 4 + 1 + 2 + steps
    edge_new, partial_sums = pl.pallas_call(
        functools.partial(
            edge_kernel, pieces_count, len(got), part_count, near_cap, halved, block
        ),
        out_shape=[
            pltpu.HBM((edge_count, width), bf16),
            jax.ShapeDtypeStruct((node_count, width), bf16),
        ],
        in_specs=edge_specs,
        out_specs=[hbm, vmem],
        scratch_shapes=[
            pltpu.VMEM((rest, known_width), bf16),
            pltpu.VMEM((node_count, edge_count), bf16),
            pltpu.VMEM((known_width, width), bf16),
            pltpu.VMEM((width, width), bf16),
            pltpu.VMEM((halo_space, width), bf16),
            [pltpu.VMEM((1, width), f32)] * 4,
            [pltpu.VMEM((block, width), f32)] * steps,
            [pltpu.VMEM((block, width), bf16)] * steps,
            [pltpu.VMEM((block, width), f32)] * steps,
            pltpu.VMEM((edge_count, width), bf16),
            pltpu.VMEM((node_count, width), f32),
            pltpu.SemaphoreType.DMA((copy_count,)),
        ],
        compiler_params=pltpu.CompilerParams(vmem_limit_bytes=grant),
        cost_estimate=pl.CostEstimate(
            flops=2 * edge_count * width * (4 * width + node_count),
            bytes_accessed=8 * edge_count * width,
            transcendentals=edge_count * width,
        ),
        name="edge_update",
    )(*edge_operands)

    subs = lax.axis_size("sub")
    other_sums = lax.ppermute(partial_sums, "sub", [(at, (at + 1) % subs) for at in range(subs)])

    rows = [value.reshape(1, -1) for value in (node_in_bias, node_out_bias, node_gain, node_offset)]
    node_new = pl.pallas_call(
        functools.partial(node_kernel, pieces_count),
        out_shape=jax.ShapeDtypeStruct((node_count, width), bf16),
        in_specs=[vmem] * (3 + pieces_count + 4),
        out_specs=vmem,
        scratch_shapes=[
            pltpu.VMEM((3 * width, width), bf16),
        ],
        compiler_params=pltpu.CompilerParams(vmem_limit_bytes=grant),
        cost_estimate=pl.CostEstimate(
            flops=2 * node_count * width * 3 * width,
            bytes_accessed=10 * node_count * width,
            transcendentals=node_count * width,
        ),
        name="node_update",
    )(node_latent, partial_sums, other_sums, *node_pieces, *rows)
    return (edge_new, node_new)


def solution(mesh):
    return jax.shard_map(
        shards,
        mesh=mesh,
        in_specs=(
            P(("groups", "region", "feat"), None),
            P(("groups", "region", "feat", "sub"), None),
            P(("groups", "region", "feat", "sub")),
            P(("groups", "region", "feat", "sub")),
            P(("groups", "region", "feat"), None, None),
            P(("groups", "region", "feat"), None, None),
            P(None, ("feat", "sub"), None),
            P(("feat", "sub"), None),
            P(None, ("feat", "sub"), None),
            P(("feat", "sub"), None),
            P(),
            P(),
            P(),
            P(),
            P(),
            P(),
            P(),
            P(),
        ),
        out_specs=(
            P(("groups", "region", "feat", "sub"), None),
            P(("groups", "region", "feat"), None),
        ),
        check_vma=False,
    )
```

```python
import functools

import jax
import jax.numpy as jnp
from jax import lax
from jax.experimental import pallas as pl
from jax.experimental.pallas import tpu as pltpu
from jax.sharding import PartitionSpec as P

near_offsets = (1, 2, -1, -2)
tile_rows = 16
lanes = 128
few_parts = 8
grant = 32 << 20
chunk_rows = 64
first_rows = 512
gather_rows = 512
bf16 = jnp.bfloat16
f32 = jnp.float32
vmem = pl.BlockSpec(memory_space=pltpu.VMEM)
hbm = pl.BlockSpec(memory_space=pltpu.HBM)


def in_hbm(array):
    return pltpu.with_memory_space_constraint(array, pltpu.HBM)


def in_vmem(array):
    return pltpu.with_memory_space_constraint(array, pltpu.VMEM)


def wrap(value, count):
    return jnp.where(value < 0, value + count, value)


def as_columns(rows):
    return jnp.concatenate(
        [
            jnp.transpose(jnp.broadcast_to(rows[at : at + 1], (lanes, rows.shape[1])))
            for at in range(rows.shape[0])
        ],
        axis=0,
    )


def one_hot(columns, width):
    place = lax.broadcasted_iota(jnp.int32, columns.shape, 1)
    return jnp.concatenate(
        [
            jnp.where(columns == place + start, 1.0, 0.0).astype(bf16)
            for start in range(0, width, lanes)
        ],
        axis=1,
    )


def silu(values):
    half = 0.5 * values
    return half + half * jnp.tanh(half)


def layer_norm(values, gain, offset):
    average = jnp.mean(values, axis=-1, keepdims=True)
    centred = values - average
    spread = jnp.mean(centred * centred, axis=-1, keepdims=True)
    return centred * lax.rsqrt(spread + 1e-05) * gain + offset


def my_part():
    return lax.axis_index("region") * lax.axis_size("feat") + lax.axis_index("feat")


def pick_kernel(part_count, near_cap, far_cap, far_ref, near_ref, latent_ref, out_ref, picked):
    me, sub, subs = my_part(), lax.axis_index("sub"), lax.axis_size("sub")
    half, width = near_cap // subs, latent_ref.shape[1]
    columns = [as_columns(near_ref[0])]
    tile_place = lax.broadcasted_iota(jnp.int32, (tile_rows, lanes), 0)
    far = as_columns(far_ref[0, 0:1])
    for slot in range(1, far_cap):
        far = jnp.where(sub == slot, as_columns(far_ref[0, slot : slot + 1]), far)
    for part in range(part_count):
        columns.append(jnp.where(tile_place == 0, far[part : part + 1], -1))
    hot = one_hot(jnp.concatenate(columns, axis=0), latent_ref.shape[0])
    rows = jnp.dot(hot, latent_ref[...], preferred_element_type=f32)
    far_start = len(near_offsets) * near_cap
    picked[...] = rows[:far_start].astype(bf16)
    for which, offset in enumerate(near_offsets):
        target = lax.rem(me + (offset + part_count), part_count)
        start = pl.multiple_of(which * near_cap + sub * half, half)
        out_ref[target, :, :width] = picked[pl.ds(start, half)]
    for part in range(part_count):
        spot = far_start + part * tile_rows
        far_row = rows[spot : spot + 1]
        pieces = [far_row[:, at : at + lanes] for at in range(0, width, lanes)]
        pieces.append(jnp.zeros((half - len(pieces), lanes), f32))
        out_ref[part, :, width:] = jnp.concatenate(pieces, axis=0).astype(bf16)


def exchange_halves(node_latent, near_rows, far_rows, part_count):
    near_cap, far_cap = near_rows.shape[2], far_rows.shape[2]
    subs = lax.axis_size("sub")
    width = node_latent.shape[1]
    block = (part_count, near_cap // subs, width + lanes)
    picks = len(near_offsets) * near_cap
    blocks = pl.pallas_call(
        functools.partial(pick_kernel, part_count, near_cap, far_cap),
        out_shape=pltpu.HBM(block, bf16),
        in_specs=[vmem, vmem, vmem],
        out_specs=vmem,
        scratch_shapes=[pltpu.VMEM((picks, width), bf16)],
        compiler_params=pltpu.CompilerParams(vmem_limit_bytes=grant),
        cost_estimate=pl.CostEstimate(flops=0, bytes_accessed=0, transcendentals=0),
        name="pick_halo",
    )(in_hbm(jnp.transpose(far_rows, (0, 2, 1))), in_hbm(near_rows), in_hbm(node_latent))
    own = lax.all_to_all(blocks, ("region", "feat"), split_axis=0, concat_axis=0, tiled=True)
    return [own]


def exchange_all(node_latent, near_rows, far_rows, part_count):
    near_send = jnp.take(node_latent, near_rows[0], axis=0, mode="clip")
    far_send = jnp.take(node_latent, far_rows[0], axis=0, mode="clip")
    got = []
    for which, offset in enumerate(near_offsets):
        pairs = [(part, (part + offset) % part_count) for part in range(part_count)]
        got.append(lax.ppermute(near_send[which], ("region", "feat"), pairs))
    far = lax.all_to_all(far_send, ("region", "feat"), split_axis=0, concat_axis=0, tiled=True)
    got.append(far.reshape(-1, far.shape[2]))
    return got


def gather_kernel(
    near_cap,
    far_cap,
    halved,
    source_ref,
    receiver_ref,
    latent_ref,
    node_in_ref,
    node_out_ref,
    edge_hbm,
    known,
    gathered_hbm,
    to_node,
    pack_ref,
    gathered,
    sems,
):
    node_count, width = latent_ref.shape
    first = known.shape[0]
    edge_count = first + gathered.shape[0]
    block = gather_rows
    copies = []

    def start(source, target):
        copies.append(pltpu.make_async_copy(source, target, sems.at[len(copies)]))
        copies[-1].start()

    start(edge_hbm.at[pl.ds(0, first)], known.at[:, pl.ds(0, width)])
    count = node_in_ref.shape[0]
    pack_ref[:count] = node_in_ref[...]
    pack_ref[count] = node_out_ref[...]
    latent = latent_ref[...]

    def gather(at, target, rows, begin):
        here = slice(at * (block // lanes), (at + 1) * (block // lanes))
        source = source_ref[here]
        if halved:
            far = source - (node_count + len(near_offsets) * near_cap)
            slot = lax.rem(far, far_cap)
            turned = wrap(slot - lax.axis_index("sub"), far_cap)
            source = jnp.where(far >= 0, source - slot + turned, source)
        columns = as_columns(source)
        sent = one_hot(columns, node_count)
        target[rows, begin : begin + width] = jnp.dot(
            sent, latent, preferred_element_type=f32
        ).astype(bf16)
        received = one_hot(as_columns(receiver_ref[here]), node_count)
        target[rows, begin + width : begin + 2 * width] = jnp.dot(
            received, latent, preferred_element_type=f32
        ).astype(bf16)
        slots = target.shape[1] - begin - 2 * width
        target[rows, begin + 2 * width :] = one_hot(columns - node_count, slots)

    for at in range(first // block, edge_count // block):
        begin = at * block - first
        gather(at, gathered, slice(begin, begin + block), 0)
        rows = pl.ds(begin, block)
        start(gathered.at[rows], gathered_hbm.at[rows])
    node_place = lax.broadcasted_iota(jnp.int32, (to_node.shape[0], lanes), 0)
    for row in range(edge_count // lanes):
        to_node[:, row * lanes : (row + 1) * lanes] = jnp.where(
            node_place == receiver_ref[row : row + 1], 1.0, 0.0
        ).astype(bf16)
    for at in range(first // block):
        gather(at, known, slice(at * block, (at + 1) * block), width)
    for copy in copies:
        copy.wait()


def place_halo(halo, part_count, near_cap, halved, got):
    subs, width = lax.axis_size("sub"), halo.shape[1]
    far_start = len(near_offsets) * near_cap
    used = far_start
    if halved:
        half = near_cap // subs
        for which, offset in enumerate(near_offsets):
            origin = lax.rem(my_part() + (part_count - offset), part_count)
            for turn in range(subs):
                owner = wrap(lax.axis_index("sub") - turn, subs)
                start = pl.multiple_of(which * near_cap + owner * half, half)
                halo[pl.ds(start, half)] = got[turn][origin, :, :width]
        far = []
        for part in range(part_count):
            for turn in range(subs):
                tile = got[turn][part, :, width:].astype(f32)
                pieces = [tile[at : at + 1] for at in range(width // lanes)]
                far.append(jnp.concatenate(pieces, axis=1))
        used += len(far)
        halo[far_start:used] = jnp.concatenate(far, axis=0).astype(bf16)
    else:
        for rows in got:
            start = used - far_start if rows is not got[-1] else far_start
            halo[start : start + rows.shape[0]] = rows[...]
            used += rows.shape[0]
        used -= far_start
    if used < halo.shape[0]:
        halo[used:] = jnp.zeros((halo.shape[0] - used, halo.shape[1]), bf16)


def place_rows(whole, start, piece, owner):
    rows = piece.shape[0]
    whole[pl.ds(pl.multiple_of(start + owner * rows, rows), rows), :] = piece


def owners():
    feat, feats = lax.axis_index("feat"), lax.axis_size("feat")
    sub, subs = lax.axis_index("sub"), lax.axis_size("sub")
    own = [(0, turn) for turn in range(subs)]
    rest = [(shift, turn) for turn in range(subs) for shift in range(1, feats)]
    return [
        wrap(feat - shift, feats) * subs + wrap(sub - turn, subs) for shift, turn in own + rest
    ]


def from_feats(weight):
    feats = lax.axis_size("feat")
    return [
        lax.ppermute(weight, "feat", [(at, (at + shift) % feats) for at in range(feats)])
        for shift in range(1, feats)
    ]


def from_subs(pieces):
    subs = lax.axis_size("sub")
    return [
        lax.ppermute(piece, "sub", [(at, (at + turn) % subs) for at in range(subs)])
        for turn in range(1, subs)
        for piece in pieces
    ]


def edge_kernel(pieces_count, got_count, part_count, near_cap, halved, *refs):
    edge_hbm, gathered_hbm, to_node, known_first = refs[:4]
    got_refs = refs[4 : 4 + got_count]
    refs = refs[4 + got_count :]
    in_pieces, out_pieces = refs[:pieces_count], refs[pieces_count : 2 * pieces_count]
    row_refs = refs[2 * pieces_count : 2 * pieces_count + 4]
    new_hbm, sum_ref = refs[2 * pieces_count + 4 : 2 * pieces_count + 6]
    known_rest, in_weight, out_weight, halo, rows, preact, hidden, output, new_ref, total, sems = (
        refs[2 * pieces_count + 6 :]
    )
    edge_count, width = new_hbm.shape
    known = [known_first, known_rest]
    starts = [0, known_first.shape[0]]
    blocks = len(known)
    taken = []

    def start(source, target):
        copy = pltpu.make_async_copy(source, target, sems.at[len(taken)])
        copy.start()
        taken.append(copy)
        return copy

    order = owners()
    first, later = [], []
    for which in (1, 0, 2):
        count = in_pieces[0].shape[1]
        spot = pl.ds(pl.multiple_of(which * width + order[0] * count, count), count)
        target = first if which == 1 else later
        target.append(start(in_pieces[0].at[which], in_weight.at[spot]))
    for row_ref, row in zip(row_refs, rows):
        later.append(start(row_ref, row))
    count = out_pieces[0].shape[0]
    spot = pl.ds(pl.multiple_of(order[0] * count, count), count)
    later.append(start(out_pieces[0], out_weight.at[spot]))
    in_bias, out_bias, gain, offset = rows
    known_copies = [
        start(edge_hbm.at[pl.ds(starts[1], known_rest.shape[0])], known_rest.at[:, pl.ds(0, width)]),
        start(gathered_hbm, known_rest.at[:, pl.ds(width, known_rest.shape[1] - width)]),
    ]

    place_halo(halo, part_count, near_cap, halved, got_refs)
    for which in (1, 0, 2):
        for piece, owner in zip(in_pieces[1:], order[1:]):
            place_rows(in_weight, which * width, piece[which], owner)
    for piece, owner in zip(out_pieces[1:], order[1:]):
        place_rows(out_weight, 0, piece[...], owner)
    for copy in first:
        copy.wait()
    in_weight[3 * width :] = jnp.dot(
        halo[...], in_weight[width : 2 * width], preferred_element_type=f32
    ).astype(bf16)
    for copy in later:
        copy.wait()

    def in_dot(at):
        if at == 1:
            for copy in known_copies:
                copy.wait()
        preact[at][...] = jnp.dot(
            known[at][...], in_weight[...], preferred_element_type=f32
        )

    def activate(at):
        for start_row in range(0, known[at].shape[0], chunk_rows):
            here = slice(start_row, start_row + chunk_rows)
            hidden[at][here] = silu(preact[at][here] + in_bias[...]).astype(bf16)

    def out_dot(at):
        output[at][...] = jnp.dot(
            hidden[at][...], out_weight[...], preferred_element_type=f32
        )

    def normalise(at):
        for start_row in range(0, known[at].shape[0], chunk_rows):
            here = slice(start_row, start_row + chunk_rows)
            there = slice(starts[at] + start_row, starts[at] + start_row + chunk_rows)
            normed = layer_norm(output[at][here] + out_bias[...], gain[...], offset[...])
            edges = known[at][here, :width].astype(f32)
            new_ref[there] = (edges + normed).astype(bf16)
        spot = pl.ds(starts[at], known[at].shape[0])
        return start(new_ref.at[spot], new_hbm.at[spot])

    def sum_dot(at):
        spot = slice(starts[at], starts[at] + known[at].shape[0])
        part = jnp.dot(to_node[:, spot], new_ref[spot], preferred_element_type=f32)
        if at > 0:
            part += total[...]
        if at + 1 < blocks:
            total[...] = part
        else:
            sum_ref[...] = part.astype(bf16)

    out_copies = []
    in_dot(0)
    for at in range(blocks):
        if at + 1 < blocks:
            in_dot(at + 1)
        activate(at)
        out_dot(at)
        if at > 0:
            sum_dot(at - 1)
        out_copies.append(normalise(at))
    sum_dot(blocks - 1)
    for copy in out_copies:
        copy.wait()


def node_kernel(pieces_count, *refs):
    latent_ref, own_ref, other_ref = refs[:3]
    pieces = refs[3 : 3 + pieces_count]
    in_bias, out_bias, gain, offset, new_hbm, weights, made, sems = refs[3 + pieces_count :]
    width = latent_ref.shape[1]
    for piece, owner in zip(pieces, owners()):
        for which in range(piece.shape[0]):
            place_rows(weights, which * width, piece[which], owner)
    latent = latent_ref[...]
    summed = (own_ref[...].astype(f32) + other_ref[...].astype(f32)).astype(bf16)
    preact = jnp.dot(
        jnp.concatenate([latent, summed], axis=1),
        weights[: 2 * width],
        preferred_element_type=f32,
    )
    hidden = silu(preact + in_bias[...]).astype(bf16)
    output = jnp.dot(hidden, weights[2 * width :], preferred_element_type=f32) + out_bias[...]
    third = latent.shape[0] // 3
    copies = []
    for part in range(3):
        here = slice(part * third, (part + 1) * third)
        normed = layer_norm(output[here], gain[...], offset[...])
        made[here] = (latent[here].astype(f32) + normed).astype(bf16)
        spot = pl.ds(part * third, third)
        copies.append(pltpu.make_async_copy(made.at[spot], new_hbm.at[spot], sems.at[part]))
        copies[-1].start()
    for copy in copies:
        copy.wait()


def shards(
    node_latent,
    edge_latent,
    edge_source,
    receivers,
    near_rows,
    far_rows,
    edge_in_weight,
    edge_out_weight,
    node_in_weight,
    node_out_weight,
    edge_in_bias,
    edge_out_bias,
    edge_gain,
    edge_offset,
    node_in_bias,
    node_out_bias,
    node_gain,
    node_offset,
):
    node_count, width = node_latent.shape
    edge_count = edge_latent.shape[0]
    near_cap, far_cap = near_rows.shape[2], far_rows.shape[2]
    part_count = far_rows.shape[1]

    far_edge = [from_feats(edge_in_weight), from_feats(edge_out_weight)]
    near_edge = [from_subs([edge_in_weight]), from_subs([edge_out_weight])]

    subs = lax.axis_size("sub")
    halved = part_count <= few_parts and far_cap == subs and near_cap % (tile_rows * subs) == 0
    exchange = exchange_halves if halved else exchange_all
    got = exchange(node_latent, near_rows, far_rows, part_count)
    halo_space = len(near_offsets) * near_cap + part_count * far_cap
    halo_space = -(-halo_space // lanes) * lanes

    source_rows = in_hbm(edge_source.reshape(-1, lanes))
    receiver_rows = in_hbm(receivers.reshape(-1, lanes))

    pack_shape = (node_in_weight.shape[0] + 1,) + node_out_weight.shape
    near_edge[1], latent_after = lax.optimization_barrier((near_edge[1], node_latent))
    gathered_width = 2 * width + halo_space
    known_width = width + gathered_width
    sizes = [first_rows, edge_count - first_rows]
    known, gathered, to_node, node_weight = pl.pallas_call(
        functools.partial(gather_kernel, near_cap, far_cap, halved),
        out_shape=[
            pltpu.VMEM((sizes[0], known_width), bf16),
            pltpu.HBM((sizes[1], gathered_width), bf16),
            pltpu.VMEM((node_count, edge_count), bf16),
            pltpu.HBM(pack_shape, bf16),
        ],
        in_specs=[vmem] * 5 + [hbm],
        out_specs=[vmem, hbm, vmem, vmem],
        scratch_shapes=[
            pltpu.VMEM((sizes[1], gathered_width), bf16),
            pltpu.SemaphoreType.DMA((1 + sizes[1] // gather_rows,)),
        ],
        compiler_params=pltpu.CompilerParams(vmem_limit_bytes=grant),
        cost_estimate=pl.CostEstimate(flops=0, bytes_accessed=0, transcendentals=0),
        name="gather_latents",
    )(
        source_rows,
        receiver_rows,
        in_hbm(latent_after),
        in_hbm(node_in_weight),
        in_hbm(node_out_weight),
        in_hbm(edge_latent),
    )

    far_edge, got, known, gathered, to_node, node_weight = lax.optimization_barrier(
        (far_edge, got, known, gathered, to_node, node_weight)
    )
    if halved:
        got = got + from_subs(got)
    edge_in, edge_out = [
        [weight] + near + far + from_subs(far)
        for weight, near, far in zip((edge_in_weight, edge_out_weight), near_edge, far_edge)
    ]
    far_node = from_feats(node_weight)
    node_pieces = [node_weight] + from_subs([node_weight]) + far_node + from_subs(far_node)
    pieces_count = len(edge_in)

    rows = [value.reshape(1, -1) for value in (edge_in_bias, edge_out_bias, edge_gain, edge_offset)]
    edge_operands = [in_hbm(edge_latent), in_hbm(gathered), in_vmem(to_node), in_vmem(known)]
    edge_operands += [in_vmem(blocks) for blocks in got]
    edge_specs = [hbm] * 2 + [vmem] * (2 + len(got))
    for pieces in (edge_in, edge_out):
        edge_operands += [in_hbm(pieces[0])] + [in_vmem(piece) for piece in pieces[1:]]
        edge_specs += [hbm] + [vmem] * (pieces_count - 1)
    edge_operands += [in_hbm(row) for row in rows]
    edge_specs += [hbm] * len(rows)
    copy_count = 3 + 4 + 1 + 2 + len(sizes)
    edge_new, partial_sums = pl.pallas_call(
        functools.partial(edge_kernel, pieces_count, len(got), part_count, near_cap, halved),
        out_shape=[
            pltpu.HBM((edge_count, width), bf16),
            jax.ShapeDtypeStruct((node_count, width), bf16),
        ],
        in_specs=edge_specs,
        out_specs=[hbm, vmem],
        scratch_shapes=[
            pltpu.VMEM((sizes[1], known_width), bf16),
            pltpu.VMEM((known_width, width), bf16),
            pltpu.VMEM((width, width), bf16),
            pltpu.VMEM((halo_space, width), bf16),
            [pltpu.VMEM((1, width), f32)] * 4,
            [pltpu.VMEM((size, width), f32) for size in sizes],
            [pltpu.VMEM((size, width), bf16) for size in sizes],
            [pltpu.VMEM((size, width), f32) for size in sizes],
            pltpu.VMEM((edge_count, width), bf16),
            pltpu.VMEM((node_count, width), f32),
            pltpu.SemaphoreType.DMA((copy_count,)),
        ],
        compiler_params=pltpu.CompilerParams(vmem_limit_bytes=grant),
        cost_estimate=pl.CostEstimate(
            flops=2 * edge_count * width * (4 * width + node_count),
            bytes_accessed=8 * edge_count * width,
            transcendentals=edge_count * width,
        ),
        name="edge_update",
    )(*edge_operands)

    subs = lax.axis_size("sub")
    other_sums = lax.ppermute(partial_sums, "sub", [(at, (at + 1) % subs) for at in range(subs)])

    rows = [value.reshape(1, -1) for value in (node_in_bias, node_out_bias, node_gain, node_offset)]
    node_new = pl.pallas_call(
        functools.partial(node_kernel, pieces_count),
        out_shape=pltpu.HBM((node_count, width), bf16),
        in_specs=[vmem] * (3 + pieces_count + 4),
        out_specs=hbm,
        scratch_shapes=[
            pltpu.VMEM((3 * width, width), bf16),
            pltpu.VMEM((node_count, width), bf16),
            pltpu.SemaphoreType.DMA((3,)),
        ],
        compiler_params=pltpu.CompilerParams(vmem_limit_bytes=grant),
        cost_estimate=pl.CostEstimate(
            flops=2 * node_count * width * 3 * width,
            bytes_accessed=10 * node_count * width,
            transcendentals=node_count * width,
        ),
        name="node_update",
    )(node_latent, partial_sums, other_sums, *node_pieces, *rows)
    return (edge_new, node_new)


def solution(mesh):
    return jax.shard_map(
        shards,
        mesh=mesh,
        in_specs=(
            P(("groups", "region", "feat"), None),
            P(("groups", "region", "feat", "sub"), None),
            P(("groups", "region", "feat", "sub")),
            P(("groups", "region", "feat", "sub")),
            P(("groups", "region", "feat"), None, None),
            P(("groups", "region", "feat"), None, None),
            P(None, ("feat", "sub"), None),
            P(("feat", "sub"), None),
            P(None, ("feat", "sub"), None),
            P(("feat", "sub"), None),
            P(),
            P(),
            P(),
            P(),
            P(),
            P(),
            P(),
            P(),
        ),
        out_specs=(
            P(("groups", "region", "feat", "sub"), None),
            P(("groups", "region", "feat"), None),
        ),
        check_vma=False,
    )
```
